32 devices in a mesh: snap: 4 (over y, x), dom: 8 (over z, core).
Axes of the slice: x: 2, y: 2, z: 4, core: 2. Of those that a mesh axis runs over, the one named last changes fastest.
Arguments:
- readings: bfloat16 [4, 2, 4096], P('snap', None, 'dom'), may hold values from -6 to 6
- previous: bfloat16 [4, 64, 4096], P('snap', None, 'dom'), may hold values from -3 to 3
- upstream: bfloat16 [4, 64, 4096], P('snap', None, 'dom'), may hold values from -6 to 6
- gate_weight: bfloat16 [128, 330], replicated, may hold values from -0.3125 to 0.3125
- gate_bias: float32 [128], replicated, may hold values from -4 to 4
- cand_weight: bfloat16 [64, 330], replicated, may hold values from -0.3125 to 0.3125
- cand_bias: float32 [64], replicated, may hold values from -3 to 3
- neighbours: int32 [4, 4096], P(None, 'dom'), may hold values from 0 to 543, as said below
- edge_weight: float32 [4, 4096], P(None, 'dom'), may hold values from 0.1 to 1
- send_rows: int32 [8, 32], P('dom'), may hold values from 0 to 511, as said below
Outputs:
- state_grad: bfloat16 [4, 64, 4096], P('snap', None, 'dom')
- gate_weight_grad: float32 [128, 330], replicated
- gate_bias_grad: float32 [128], replicated
- cand_weight_grad: float32 [64, 330], replicated
- cand_bias_grad: float32 [64], replicated
The draws below stay inside these ranges and needn't reach their ends.
Inputs may be any that keep to these rules, and one draw needn't show every extreme that they name: Value v of neighbours[d, i] below 512 is a row of segment i's own partition; v = 512 + q * 4 + s names slot s of what partition q sends to segment i's partition. Row d = 0 names each row of a partition exactly once, and in every partition every value from 512 to 543 appears. `send_rows`: row q holds rows of partition q; slots p * 4 to p * 4 + 3 are those sent to partition p; rows may repeat.
All inputs are finite; a program needn't handle non-finite values.
Results may differ from the reference program's by a relative error of at most 0.006.
Values may be sent and summed in bfloat16 or wider, within the bound.
No kernel may reach another device: no remote copies, remote signals or barrier semaphores. Data moves between devices by JAX's collectives and lax.ppermute only.
A program may use at most 64 MiB of HBM per device.

```python
import math
import jax
import jax.numpy as jnp
from jax import lax

FIN = 2
H = 64
M = 5
DEG = 4
SEG_DEV = 512
CAP = 4
SNAPS = 4
SEGMENTS = 4096
HALO = 32
N_DOM = 8


def draw_neighbours(key, part):
    keys = jax.random.split(jax.random.fold_in(key, 11), N_DOM)

    def one_part(part_key):
        first_key, order_key, local_key, remote_key, pick_key = jax.random.split(part_key, 5)
        first = jax.random.permutation(first_key, SEG_DEV).astype(jnp.int32)
        order = jax.random.permutation(order_key, SEG_DEV).astype(jnp.int32)
        covered = jnp.zeros((SEG_DEV,), jnp.int32).at[order[:HALO]].set(SEG_DEV + jnp.arange(HALO, dtype=jnp.int32))
        marked = jnp.zeros((SEG_DEV,), jnp.int32).at[order[:HALO]].set(1)
        local = jax.random.randint(local_key, (DEG - 1, SEG_DEV), 0, SEG_DEV, dtype=jnp.int32)
        remote = jax.random.randint(remote_key, (DEG - 1, SEG_DEV), SEG_DEV, SEG_DEV + HALO, dtype=jnp.int32)
        picked = jax.random.randint(pick_key, (DEG - 1, SEG_DEV), 0, 10, dtype=jnp.int32)
        rest = jnp.where(picked == 0, remote, local)
        head = jnp.where(marked == 1, covered, rest[0])
        return jnp.concatenate([first[None, :], head[None, :], rest[1:]], axis=0)
    blocks = jax.vmap(one_part)(keys)
    return jnp.transpose(blocks, (1, 0, 2)).reshape(DEG, SEG_DEV * N_DOM)


def draw_send_rows(key, part):
    rows_key, high_key, low_key = jax.random.split(jax.random.fold_in(key, 7), 3)
    rows = jax.random.randint(rows_key, (N_DOM, HALO), 0, SEG_DEV, dtype=jnp.int32)
    high_spot = jax.random.randint(high_key, (N_DOM,), 0, HALO, dtype=jnp.int32)
    low_spot = (high_spot + 1 + jax.random.randint(low_key, (N_DOM,), 0, HALO - 1, dtype=jnp.int32)) % HALO
    column = jnp.arange(HALO, dtype=jnp.int32)[None, :]
    rows = jnp.where(column == high_spot[:, None], SEG_DEV - 1, rows)
    rows = jnp.where(column == low_spot[:, None], 0, rows)
    return rows.astype(jnp.int32)


def level_of(key, shape, pieces, low, top_value):
    factor_of, own = 1.0, jax.random.fold_in(key, 6)
    for dim, shards_of in pieces:
        draws = jnp.exp(jax.random.uniform(jax.random.fold_in(own, dim), (shards_of,), jnp.float32, low / len(pieces), top_value / len(pieces)))
        factor_of = factor_of * jnp.repeat(draws, shape[dim] // shards_of).reshape([-1 if axis == dim else 1 for axis in range(len(shape))])
    return factor_of


def bell_draw(own_key, shape, width, limit, pieces=(), kind=jnp.bfloat16):
    gain = level_of(own_key, shape, pieces, -0.22, 0.18) if pieces else 1.0
    entries = jax.random.normal(own_key, shape, jnp.float32) * width * gain
    return jnp.minimum(jnp.maximum(entries, -limit), limit).astype(kind)


def setup_inputs(seed: int = 0) -> dict:
    splits = jax.random.split(jax.random.key(seed), 11)
    return {
        "readings": bell_draw(splits[0], (SNAPS, FIN, SEGMENTS), 1.0, 6.0, ((0, 4), (2, 8))),
        "previous": bell_draw(splits[1], (SNAPS, H, SEGMENTS), 0.5, 3.0, ((0, 4), (2, 8))),
        "upstream": bell_draw(splits[2], (SNAPS, H, SEGMENTS), 1.0, 6.0, ((0, 4), (2, 8))),
        "gate_weight": bell_draw(splits[3], (2 * H, M * (FIN + H)), (M * (FIN + H)) ** -0.5, 0.3125),
        "gate_bias": bell_draw(splits[4], (2 * H,), 1.0, 4.0, (), jnp.float32),
        "cand_weight": bell_draw(splits[5], (H, M * (FIN + H)), (M * (FIN + H)) ** -0.5, 0.3125),
        "cand_bias": bell_draw(splits[6], (H,), 0.5, 3.0, (), jnp.float32),
        "neighbours": draw_neighbours(jax.random.fold_in(splits[10], 71), 0),
        "edge_weight": jnp.clip(jnp.exp(math.log(1.0) - 2.3025851 * jax.random.uniform(splits[8], (DEG, SEGMENTS), jnp.float32) ** level_of(splits[8], (DEG, SEGMENTS), ((1, 8),), -0.2, 0.2)), 0.1, 1.0),
        "send_rows": draw_send_rows(jax.random.fold_in(splits[10], 71), 0),
    }


def global_sources(neighbours, send_rows):
    total = neighbours.shape[1]
    node = jnp.arange(total, dtype=jnp.int32)
    owner = (node // SEG_DEV).astype(jnp.int32)
    halo_index = jnp.clip(neighbours - SEG_DEV, 0, HALO - 1).astype(jnp.int32)
    peer = (halo_index // CAP).astype(jnp.int32)
    position = (halo_index % CAP).astype(jnp.int32)
    remote_row = send_rows[peer, owner[None, :] * CAP + position]
    local_src = owner[None, :] * SEG_DEV + neighbours
    remote_src = peer * SEG_DEV + remote_row
    return jnp.where(neighbours < SEG_DEV, local_src, remote_src).astype(jnp.int32)

def collect(values, weights, sources):
    total = jnp.zeros(values.shape, jnp.float32)
    for slot in range(sources.shape[0]):
        total = total + values[:, sources[slot]].astype(jnp.float32) * weights[slot][None, :]
    return total

def spread(values, weights, sources):
    total = jnp.zeros(values.shape, jnp.float32)
    for slot in range(sources.shape[0]):
        total = total.at[:, sources[slot]].add(values.astype(jnp.float32) * weights[slot][None, :])
    return total

def reference(readings, previous, upstream, gate_weight, gate_bias, cand_weight, cand_bias, neighbours, edge_weight, send_rows):
    sources = global_sources(neighbours, send_rows)
    total_rows = neighbours.shape[1]
    in_degree = lax.optimization_barrier(jnp.sum(edge_weight, axis=0))
    out_degree = jnp.zeros((total_rows,), jnp.float32)
    for slot in range(sources.shape[0]):
        out_degree = out_degree.at[sources[slot]].add(edge_weight[slot])
    walk_in = edge_weight / in_degree[None, :]
    walk_out = edge_weight / out_degree[sources]

    def diffuse(base):
        lower = base.astype(jnp.float32)
        first_out = spread(base, walk_out, sources).astype(jnp.bfloat16)
        second_out = (2.0 * spread(first_out, walk_out, sources) - lower).astype(jnp.bfloat16)
        first_in = collect(base, walk_in, sources).astype(jnp.bfloat16)
        second_in = (2.0 * collect(first_in, walk_in, sources) - lower).astype(jnp.bfloat16)
        return jnp.concatenate([base, first_out, second_out, first_in, second_in], axis=0)

    def adjoint(grads):
        pulled = collect(grads[2], walk_out, sources)
        pushed = spread(grads[4], walk_in, sources)
        turned_out = (grads[1].astype(jnp.float32) + 2.0 * pulled).astype(jnp.bfloat16)
        turned_in = (grads[3].astype(jnp.float32) + 2.0 * pushed).astype(jnp.bfloat16)
        direct = grads[0].astype(jnp.float32) - grads[2].astype(jnp.float32) - grads[4].astype(jnp.float32)
        return direct + collect(turned_out, walk_out, sources) + spread(turned_in, walk_in, sources)
    chans = FIN + H
    cand_rows = cand_weight.reshape(H, M, chans)[:, :, FIN:].reshape(H, M * H)
    gate_rows = gate_weight.reshape(2 * H, M, chans)[:, :, FIN:].reshape(2 * H, M * H)
    grad_wru = jnp.zeros((2 * H, M * chans), jnp.float32)
    grad_bru = jnp.zeros((2 * H,), jnp.float32)
    grad_wc = jnp.zeros((H, M * chans), jnp.float32)
    grad_bc = jnp.zeros((H,), jnp.float32)
    results = []
    for snap in range(SNAPS):
        upward = upstream[snap].astype(jnp.float32)
        held = previous[snap].astype(jnp.float32)
        states = diffuse(jnp.concatenate([readings[snap], previous[snap]], axis=0))
        gates = jnp.dot(gate_weight, states, preferred_element_type=jnp.float32) + gate_bias[:, None]
        reset = jax.nn.sigmoid(gates[:H])
        update = jax.nn.sigmoid(gates[H:])
        scaled = (reset * held).astype(jnp.bfloat16)
        mixed = diffuse(jnp.concatenate([readings[snap], scaled], axis=0))
        cand = jnp.tanh(jnp.dot(cand_weight, mixed, preferred_element_type=jnp.float32) + cand_bias[:, None])
        cand_grad = (upward * (1.0 - update) * (1.0 - cand * cand)).astype(jnp.bfloat16)
        grad_wc = grad_wc + jnp.dot(cand_grad, mixed.T, preferred_element_type=jnp.float32)
        grad_bc = grad_bc + lax.optimization_barrier(jnp.sum(cand_grad.astype(jnp.float32), axis=1))
        back_c = jnp.dot(cand_rows.T, cand_grad, preferred_element_type=jnp.float32).astype(jnp.bfloat16).reshape(M, H, total_rows)
        scaled_grad = adjoint(back_c)
        reset_part = scaled_grad * held * reset * (1.0 - reset)
        update_part = upward * (held - cand) * update * (1.0 - update)
        gate_grad = jnp.concatenate([reset_part, update_part], axis=0).astype(jnp.bfloat16)
        grad_wru = grad_wru + jnp.dot(gate_grad, states.T, preferred_element_type=jnp.float32)
        grad_bru = grad_bru + lax.optimization_barrier(jnp.sum(gate_grad.astype(jnp.float32), axis=1))
        back_g = jnp.dot(gate_rows.T, gate_grad, preferred_element_type=jnp.float32).astype(jnp.bfloat16).reshape(M, H, total_rows)
        state_part = adjoint(back_g)
        results.append((upward * update + scaled_grad * reset + state_part).astype(jnp.bfloat16))
    factor = 1.0 / math.sqrt(SNAPS * SEGMENTS)
    state_grad = jnp.stack(results, axis=0)
    return (state_grad, grad_wru * factor, grad_bru * factor, grad_wc * factor, grad_bc * factor)
```

```python
import functools
import math

import jax
import jax.numpy as jnp
from jax import lax
from jax.experimental import pallas as pl
from jax.experimental.pallas import tpu as pltpu
from jax.sharding import PartitionSpec as P

F32 = jnp.float32
BF16 = jnp.bfloat16
LANES = 128


def nn(a, b):
    return lax.dot_general(a, b, (((1,), (0,)), ((), ())), preferred_element_type=F32)


def nt(a, b):
    return lax.dot_general(a, b, (((1,), (1,)), ((), ())), preferred_element_type=F32)


def tn(a, b):
    return lax.dot_general(a, b, (((0,), (0,)), ((), ())), preferred_element_type=F32)


def iota(shape, axis):
    return lax.broadcasted_iota(jnp.int32, shape, axis)


def column(row):
    k = row.shape[1]
    spread = jnp.broadcast_to(row.astype(F32), (k, k))
    return jnp.sum(jnp.where(iota((k, k), 0) == iota((k, k), 1), spread, 0.0), axis=1, keepdims=True)


def run(kernel, name, outs, *args, scratch=(), flops=20_000_000):
    whole = pl.BlockSpec(memory_space=pltpu.VMEM)
    return pl.pallas_call(
        kernel,
        name=name,
        out_shape=[jax.ShapeDtypeStruct(shape, kind) for shape, kind in outs],
        in_specs=[whole] * len(args),
        out_specs=[whole] * len(outs),
        scratch_shapes=list(scratch),
        compiler_params=pltpu.CompilerParams(vmem_limit_bytes=24 * 1024 * 1024),
        cost_estimate=pl.CostEstimate(flops=flops, bytes_accessed=2_000_000, transcendentals=0),
    )(*args)


def prep_kernel(cap, nb, w, rows, readings, previous, e, s, b, pay):
    degree, n = nb.shape
    nh = s.shape[0]
    hid = previous.shape[1]
    fin = readings.shape[1]
    step = 32
    for at in range(0, n + nh, step):
        node = iota((step, n), 0) + at
        total = jnp.zeros((step, n), F32)
        for d in range(degree):
            total = total + jnp.where(node == nb[d : d + 1, :], w[d : d + 1, :], 0.0)
        e[at : at + step, :] = total.astype(BF16)
    sent = column(rows[...]).astype(jnp.int32)
    s[...] = jnp.where(iota((nh, n), 1) == sent, 1.0, 0.0).astype(BF16)
    b[:hid, :] = previous[0]
    rest = b.shape[0] - hid
    row = iota((rest, n), 0)
    tail = jnp.where(row == fin, 1.0, 0.0)
    for f in range(fin):
        tail = jnp.where(row == f, readings[0, f : f + 1, :].astype(F32), tail)
    b[hid:, :] = tail.astype(BF16)
    base = b[...]
    chans = base.shape[0]
    bound = nt(s[...], base)
    halo = nt(e[n:, :], base)
    for p in range(nh // cap):
        pay[p, :, :chans] = bound[p * cap : (p + 1) * cap, :]
        pay[p, :, LANES : LANES + chans] = halo[p * cap : (p + 1) * cap, :]


def order_matrix(shape, chans, hid, fin, block):
    k = iota(shape, 0)
    col = iota(shape, 1)
    m = lax.div(col, jnp.int32(block))
    c = col - m * block
    source = jnp.where(c < hid, m * chans + fin + c, jnp.where(c < hid + fin, m * chans + c - hid, -1))
    return jnp.where(k == source, 1.0, 0.0).astype(BF16)


def mid_a_kernel(hid, fin, orders, e, b, gw, cw, fa, ra, gw_o, cw_o):
    n = e.shape[1]
    a = e[:n, :]
    base = b[...]
    fa[...] = nt(base, a)
    ra[...] = nn(base, a)
    block = base.shape[0]
    order = order_matrix((gw.shape[1], orders * block), hid + fin, hid, fin, block)
    gw_o[...] = nn(gw[...], order).astype(BF16)
    cw_o[...] = nn(cw[...], order).astype(BF16)


def post_a_kernel(one, cap, recv, e, s, fa, ra, f1, r1, ro, ri, pay, flat):
    n = e.shape[1]
    nh = s.shape[0]
    chans = fa.shape[0]
    for p in range(nh // cap):
        flat[p * cap : (p + 1) * cap, :] = recv[p]
    h = e[n:, :]
    sel = s[...]
    seen = flat[:, :chans].astype(BF16)
    back = flat[:, LANES : LANES + chans]
    back_degree = flat[:, LANES + one : LANES + one + 1]
    out_degree = fa[one : one + 1, :] + jnp.sum(sel.astype(F32) * back_degree, axis=0, keepdims=True)
    pulled = ra[...] + tn(seen, h)
    inv_o = 1.0 / out_degree
    inv_i = 1.0 / pulled[one : one + 1, :]
    ro[...] = inv_o
    ri[...] = inv_i
    first_out = ((fa[...] + tn(back.astype(BF16), sel)) * inv_o).astype(BF16)
    first_in = (pulled * inv_i).astype(BF16)
    f1[...] = first_out
    r1[...] = first_in
    bound = nt(sel, first_in)
    halo = nt(h, first_out)
    hi, ho = scaled(h, inv_i), scaled(h, inv_o)
    si, so = scaled(sel, inv_i), scaled(sel, inv_o)
    coefs = (nt(sel, hi), nt(h, so), nt(sel, ho), nt(h, si))
    for p in range(nh // cap):
        at = slice(p * cap, (p + 1) * cap)
        pay[p, :, :chans] = bound[at, :]
        pay[p, :, LANES : LANES + chans] = halo[at, :]
        for k, coef in enumerate(coefs):
            pay[p, :, 2 * LANES + k * nh : 2 * LANES + (k + 1) * nh] = coef[at, :]


def scaled(rows, factor):
    return (rows.astype(F32) * factor).astype(BF16)


def mid_b_kernel(e, s, f1, r1, ro, ri, f2l, r2l, kc, ke, ka):
    n = e.shape[1]
    a = e[:n, :]
    h = e[n:, :]
    sel = s[...]
    nh = sel.shape[0]
    chans = f1.shape[0]
    inv_o, inv_i = ro[...], ri[...]
    outs = nt(jnp.concatenate([f1[...], scaled(sel, inv_o), scaled(sel, inv_i)], axis=0), a)
    ins = nn(jnp.concatenate([r1[...], scaled(h, inv_i), scaled(h, inv_o)], axis=0), a)
    f2l[...] = outs[:chans]
    r2l[...] = ins[:chans]
    kc[:nh, :] = ins[chans : chans + nh].astype(BF16)
    kc[nh:, :] = h
    ke[:nh, :] = outs[chans : chans + nh].astype(BF16)
    ke[nh:, :] = sel
    ka[:nh, :] = (2.0 * ins[chans + nh :]).astype(BF16)
    ka[nh : 2 * nh, :] = h
    ka[2 * nh : 3 * nh, :] = (2.0 * outs[chans + nh :]).astype(BF16)
    ka[3 * nh :, :] = sel


def send(pay, cap, left, right, left_two, right_two):
    nh = left.shape[0]
    rows = jnp.concatenate([left, right], axis=1)
    rows_two = jnp.concatenate([left_two, right_two], axis=1)
    both = jnp.concatenate([rows, rows_two], axis=0).astype(BF16)
    k = iota((2 * nh, 2 * nh), 0)
    part = lax.div(k, jnp.int32(2 * cap))
    spot = k - part * (2 * cap)
    source = jnp.where(spot < cap, part * cap + spot, nh + part * cap + spot - cap)
    mine = nn(jnp.where(iota((2 * nh, 2 * nh), 1) == source, 1.0, 0.0).astype(BF16), both)
    for p in range(nh // cap):
        own = mine[p * 2 * cap : (p + 1) * 2 * cap, :]
        pay[p] = jnp.concatenate([rows, own], axis=0).astype(BF16)


def post_b_kernel(cap, one, recv, e, s, b, f1, r1, f2l, r2l, ro, ri, gw, gb, states, reset, update, y, f1l, r1l, pay, flat):
    n = e.shape[1]
    nh = s.shape[0]
    hid = y.shape[0]
    chans = b.shape[0]
    for p in range(nh // cap):
        flat[p * cap : (p + 1) * cap, :] = recv[p, :, : 2 * LANES]
    a = e[:n, :]
    h = e[n:, :]
    sel = s[...]
    inv_o, inv_i = ro[...], ri[...]
    base = b[...].astype(F32)
    seen = flat[:, :chans].astype(BF16)
    back = flat[:, LANES : LANES + chans].astype(BF16)
    f2 = 2.0 * (f2l[...] + tn(back, sel)) * inv_o - base
    r2 = 2.0 * (r2l[...] + tn(seen, h)) * inv_i - base
    states[:chans, :] = b[...]
    states[chans : 2 * chans, :] = f1[...]
    states[2 * chans : 3 * chans, :] = f2.astype(BF16)
    states[3 * chans : 4 * chans, :] = r1[...]
    states[4 * chans :, :] = r2.astype(BF16)
    gates = jax.nn.sigmoid(nn(gw[...], states[...]) + column(gb[...]))
    reset[...] = gates[:hid]
    update[...] = gates[hid:]
    now = (gates[:hid] * base[:hid]).astype(BF16)
    y[...] = now
    local_out = nt(now, a) * inv_o
    local_in = nn(now, a) * inv_i
    f1l[...] = local_out
    r1l[...] = local_in
    bound = nt(sel, jnp.concatenate([now, local_in.astype(BF16)], axis=0))
    halo = nt(h, jnp.concatenate([now, local_out.astype(BF16)], axis=0))
    send(pay, cap, bound[:, :hid], halo[:, :hid], bound[:, hid:], halo[:, hid:])


def gather_matrix(coef, out, nd, cap, per, first, factor):
    nh = nd * cap
    width = nd * per
    k = iota((nh, width), 0)
    col = iota((nh, width), 1)
    r = lax.div(col, jnp.int32(per))
    u = col - r * per
    p = lax.div(u, jnp.int32(cap))
    spot = u - p * cap
    here = lax.div(k, jnp.int32(cap))
    slot = k - here * cap
    inside = u < nh
    place = jnp.where((k == r * cap + spot) & inside, 1.0, 0.0).astype(BF16)
    keep = (here == p) & inside
    for i in range(2):
        wide = nn(coef[:, (first + i) * nh : (first + i + 1) * nh].astype(BF16), place)
        own = (r == here) & (u == nh + cap + slot)
        out[(i + 1) * nh : (i + 2) * nh, :] = jnp.where(keep, factor * wide, jnp.where(own, 1.0, 0.0)).astype(BF16)
    out[:nh, :] = jnp.where((r == here) & (u == nh + slot), 1.0, 0.0).astype(BF16)


def mid_c_kernel(nd, cap, per, fused, recv, e, f1l, r1l, f2l, r2l, *rest):
    n = e.shape[1]
    a = e[:n, :]
    f2l[...] = nt(f1l[...].astype(BF16), a)
    r2l[...] = nn(r1l[...].astype(BF16), a)
    if fused:
        gd, ga, flat = rest
        for p in range(nd):
            flat[p * cap : (p + 1) * cap, :] = recv[p, :, 2 * LANES :]
        gather_matrix(flat, gd, nd, cap, per, 0, 1.0)
        gather_matrix(flat, ga, nd, cap, per, 2, 2.0)


def arrived(fused, hid, nh, g, recv):
    if fused:
        halo = nn(g[...], recv[...].reshape(recv.shape[0] * recv.shape[1], recv.shape[2]))
        two = halo[nh : 2 * nh, :hid], halo[2 * nh :, hid:]
    else:
        halo = recv[...]
        two = halo[nh:, :hid], halo[nh:, hid:]
    one = halo[:nh]
    return one[:, :hid], one[:, hid:], two[0], two[1]


def back_and_send(cap, hid, g, a, h, sel, inv_o, inv_i, z1, z2, pay):
    g0, g1, g2, g3, g4 = (g[m * hid : (m + 1) * hid, :].astype(BF16).astype(F32) for m in range(5))
    y1 = (g2 * inv_o).astype(BF16)
    y2 = (g4 * inv_i).astype(BF16)
    now1 = ((g1 + 2.0 * nn(y1, a)) * inv_o).astype(BF16)
    now2 = ((g3 + 2.0 * nt(y2, a)) * inv_i).astype(BF16)
    z1[...] = now1
    z2[...] = now2
    bound = nt(sel, jnp.concatenate([y1, now1], axis=0))
    halo = nt(h, jnp.concatenate([y2, now2], axis=0))
    send(pay, cap, bound[:, :hid], halo[:, :hid], bound[:, hid:], halo[:, hid:])
    return g0 - g2 - g4


def hidden_weights(w, hid, block, orders):
    return jnp.concatenate([w[:, m * block : m * block + hid] for m in range(orders)], axis=1)


def post_c_kernel(fused, cap, orders, g, recv, e, s, kc, ke, y, f1l, r1l, f2l, r2l, ro, ri, states, cw, cb, upstream, update,
                  mixed, cand_grad, gate_update, z1, z2, direct, pay):
    n = e.shape[1]
    nh = s.shape[0]
    hid = y.shape[0]
    block = states.shape[0] // orders
    a = e[:n, :]
    h = e[n:, :]
    sel = s[...]
    inv_o, inv_i = ro[...], ri[...]
    c1, e1, c2, e2 = arrived(fused, hid, nh, g, recv)
    base = y[...].astype(F32)
    c1, e1 = c1.astype(BF16), e1.astype(BF16)
    cc = jnp.concatenate([c1, c2.astype(BF16)], axis=0)
    ee = jnp.concatenate([e1, e2.astype(BF16)], axis=0)
    f1 = f1l[...] + tn(e1, sel) * inv_o
    f2 = 2.0 * (f2l[...] + tn(ee, ke[...])) * inv_o - base
    r1 = r1l[...] + tn(c1, h) * inv_i
    r2 = 2.0 * (r2l[...] + tn(cc, kc[...])) * inv_i - base
    for m, value in enumerate((y[...], f1, f2, r1, r2)):
        mixed[m * block : m * block + hid, :] = value.astype(BF16)
        mixed[m * block + hid : (m + 1) * block, :] = states[m * block + hid : (m + 1) * block, :]
    weights = cw[...]
    cand = jnp.tanh(nn(weights, mixed[...]) + column(cb[...]))
    up = upstream[0].astype(F32)
    gate = update[...]
    grad = (up * (1.0 - gate) * (1.0 - cand * cand)).astype(BF16)
    cand_grad[...] = grad
    held = states[:hid, :].astype(F32)
    gate_update[...] = (up * (held - cand) * gate * (1.0 - gate)).astype(BF16)
    back = tn(hidden_weights(weights, hid, block, orders), grad)
    direct[...] = back_and_send(cap, hid, back, a, h, sel, inv_o, inv_i, z1, z2, pay)


def weight_part(grad, features, orders, chans, hid, fin):
    block = features.shape[0] // orders
    width = -(-(orders * chans + 1) // LANES) * LANES
    shape = (width, orders * block)
    k = iota(shape, 0)
    col = iota(shape, 1)
    m = lax.div(col, jnp.int32(block))
    c = col - m * block
    source = jnp.where(c < hid, m * chans + fin + c, jnp.where(c < hid + fin, m * chans + c - hid, -1))
    source = jnp.where(col == hid + fin, orders * chans, source)
    order = jnp.where(k == source, 1.0, 0.0).astype(BF16)
    return nt(nt(grad, features).astype(BF16), order)


def mid_d_kernel(orders, fin, e, z1, z2, direct, cand_grad, mixed, gate_update, states, base, part):
    n = e.shape[1]
    a = e[:n, :]
    hid = z1.shape[0]
    base[...] = direct[...] + nn(z1[...], a) + nt(z2[...], a)
    part[:hid, :] = weight_part(gate_update[...], states[...], orders, hid + fin, hid, fin).astype(BF16)
    part[hid:, :] = weight_part(cand_grad[...], mixed[...], orders, hid + fin, hid, fin).astype(BF16)


def add_halo(fused, g, recv, ka, base):
    hid = base.shape[0]
    nh = ka.shape[0] // 4
    c1, e1, c2, e2 = arrived(fused, hid, nh, g, recv)
    return base[...] + tn(jnp.concatenate([c1, c2, e1, e2], axis=0).astype(BF16), ka[...])


def post_d_kernel(fused, cap, orders, g, recv, e, s, ka, base, ro, ri, states, gw, upstream, reset, update, gate_update,
                  gate_reset, z1, z2, direct, pay):
    n = e.shape[1]
    hid = base.shape[0]
    block = states.shape[0] // orders
    scaled_grad = add_halo(fused, g, recv, ka, base)
    held = states[:hid, :].astype(F32)
    gate = reset[...]
    grad = (scaled_grad * held * gate * (1.0 - gate)).astype(BF16)
    gate_reset[...] = grad
    weights = hidden_weights(gw[...], hid, block, orders)
    back = tn(weights, jnp.concatenate([grad, gate_update[...]], axis=0))
    rest = back_and_send(cap, hid, back, e[:n, :], e[n:, :], s[...], ro[...], ri[...], z1, z2, pay)
    direct[...] = rest + upstream[0].astype(F32) * update[...] + scaled_grad * gate


def mid_e_kernel(orders, fin, rows, e, z1, z2, direct, gate_reset, states, part, base, grads):
    n = e.shape[1]
    a = e[:n, :]
    hid = z1.shape[0]
    base[...] = direct[...] + nn(z1[...], a) + nt(z2[...], a)
    first = weight_part(gate_reset[...], states[...], orders, hid + fin, hid, fin)
    both = jnp.concatenate([first, part[...].astype(F32)], axis=0)
    for k in range(grads.shape[0]):
        if k * rows < both.shape[0]:
            grads[k] = both[k * rows : (k + 1) * rows, :].astype(BF16)
        else:
            grads[k] = jnp.zeros(grads.shape[1:], BF16)


def post_e_kernel(fused, g, recv, ka, base, out):
    out[0] = add_halo(fused, g, recv, ka, base).astype(BF16)


def add_kernel(recv, out):
    total = recv[0].astype(F32)
    for k in range(1, recv.shape[0]):
        total = total + recv[k].astype(F32)
    for k in range(out.shape[0]):
        out[k] = total.astype(BF16)


def finish_kernel(hid, factor, recv, gw, gb, cw, cb):
    rows = recv.shape[1]
    features = gw.shape[1]
    total = gw.shape[0] + cw.shape[0]
    for k in range(total // rows):
        part = recv[k].astype(F32)[:, :features] * factor
        at = k * rows
        if at < 2 * hid:
            gw[at : at + rows, :] = part
        else:
            cw[at - 2 * hid : at - 2 * hid + rows, :] = part
    flat = jnp.concatenate([recv[k].astype(F32) for k in range(total // rows)], axis=0)
    pick = jnp.where(iota((8, flat.shape[1]), 1) == features, 1.0, 0.0).astype(BF16)
    bias = nt(pick, flat.astype(BF16))[:1] * factor
    gb[...] = bias[:, : 2 * hid]
    cb[...] = bias[:, 2 * hid :]


def body(
    readings,
    previous,
    upstream,
    gate_weight,
    gate_bias,
    cand_weight,
    cand_bias,
    neighbours,
    edge_weight,
    send_rows,
):
    fin, hid = readings.shape[1], previous.shape[1]
    chans = fin + hid
    orders = gate_weight.shape[1] // chans
    n = readings.shape[2]
    nd = lax.axis_size("dom")
    devices = nd * lax.axis_size("snap")
    nh = send_rows.shape[1]
    cap = nh // nd
    block = hid + 16 * (-(-(fin + 1) // 16))
    one = hid + fin
    per = nh + 2 * cap
    fused = 3 * nh * nd * per <= 1 << 18
    move = functools.partial(lax.all_to_all, axis_name="dom", split_axis=0, concat_axis=0, tiled=True)

    e, s, b, pay = run(
        functools.partial(prep_kernel, cap), "prep",
        [((n + nh, n), BF16), ((nh, n), BF16), ((block, n), BF16), ((nd, cap, 2 * LANES), F32)],
        neighbours, edge_weight, send_rows, readings, previous,
    )
    recv = move(pay)
    fa, ra, gw, cw = run(
        functools.partial(mid_a_kernel, hid, fin, orders), "mid_a",
        [((block, n), F32), ((block, n), F32), ((2 * hid, orders * block), BF16), ((hid, orders * block), BF16)],
        e, b, gate_weight, cand_weight,
    )
    wide = 2 * LANES + 4 * nh
    f1, r1, ro, ri, pay = run(
        functools.partial(post_a_kernel, one, cap), "post_a",
        [((block, n), BF16), ((block, n), BF16), ((1, n), F32), ((1, n), F32), ((nd, cap, wide), F32)],
        recv, e, s, fa, ra, scratch=[pltpu.VMEM((nh, 2 * LANES), F32)],
    )
    recv_b = move(pay)
    f2l, r2l, kc, ke, ka = run(
        mid_b_kernel, "mid_b",
        [((block, n), F32), ((block, n), F32), ((2 * nh, n), BF16), ((2 * nh, n), BF16), ((4 * nh, n), BF16)],
        e, s, f1, r1, ro, ri,
    )
    pay_kind = ((nd, per, 2 * hid), BF16)
    field, field16 = ((hid, n), F32), ((hid, n), BF16)
    states, reset, update, y, f1l, r1l, pay = run(
        functools.partial(post_b_kernel, cap, one), "post_b",
        [((orders * block, n), BF16), field, field, field16, field, field, pay_kind],
        recv_b, e, s, b, f1, r1, f2l, r2l, ro, ri, gw, gate_bias[None, :],
        scratch=[pltpu.VMEM((nh, 2 * LANES), F32)],
    )
    recv = move(pay)
    table = ((3 * nh, nd * per), BF16)
    f2l, r2l, *tables = run(
        functools.partial(mid_c_kernel, nd, cap, per, fused), "mid_c",
        [field, field] + [table] * (2 if fused else 0),
        recv_b, e, f1l, r1l, scratch=[pltpu.VMEM((nh, 4 * nh), F32)] if fused else [],
    )
    if fused:
        inward, outward = tables
        halo_of = lambda got, first, factor: got
    else:
        inward = outward = jnp.zeros((8, LANES), BF16)
        coefs = recv_b[:, :, 2 * LANES :].reshape(nd, cap, 4, nd, cap)

        def halo_of(got, first, factor):
            rows = got[:, :nh].reshape(nd, nd, cap, 2, hid).astype(F32)
            two = jnp.einsum("psgrt,rptgk->psgk", coefs[:, :, first : first + 2], rows)
            two = factor * two.reshape(nh, 2 * hid) + got[:, nh + cap :].reshape(nh, 2 * hid).astype(F32)
            return jnp.concatenate([got[:, nh : nh + cap].reshape(nh, 2 * hid).astype(F32), two], axis=0)

    mixed, cand_grad, gate_update, z1, z2, direct, pay = run(
        functools.partial(post_c_kernel, fused, cap, orders), "post_c",
        [((orders * block, n), BF16), field16, field16, field16, field16, field, pay_kind],
        inward, halo_of(recv, 0, 1.0), e, s, kc, ke, y, f1l, r1l, f2l, r2l, ro, ri, states, cw, cand_bias[None, :], upstream, update,
    )
    recv = move(pay)
    width = -(-(orders * chans + 1) // LANES) * LANES
    base, part = run(
        functools.partial(mid_d_kernel, orders, fin), "mid_d", [field, ((2 * hid, width), BF16)],
        e, z1, z2, direct, cand_grad, mixed, gate_update, states,
    )
    gate_reset, z1, z2, direct, pay = run(
        functools.partial(post_d_kernel, fused, cap, orders), "post_d",
        [field16, field16, field16, field, pay_kind],
        outward, halo_of(recv, 2, 2.0), e, s, ka, base, ro, ri, states, gw, upstream, reset, update, gate_update,
    )
    recv = move(pay)
    rows = 8 * (-(-3 * hid // (8 * devices)))
    base, grads = run(
        functools.partial(mid_e_kernel, orders, fin, rows), "mid_e", [field, ((devices, rows, width), BF16)],
        e, z1, z2, direct, gate_reset, states, part,
    )
    (state_grad,) = run(
        functools.partial(post_e_kernel, fused), "post_e", [((1, hid, n), BF16)],
        outward, halo_of(recv, 2, 2.0), ka, base,
    )
    both = ("snap", "dom")
    grads = lax.all_to_all(grads, both, 0, 0, tiled=True)
    (grads,) = run(add_kernel, "add", [((devices, rows, width), BF16)], grads)
    grads = lax.all_to_all(grads, both, 0, 0, tiled=True)
    factor = 1.0 / math.sqrt(readings.shape[0] * lax.axis_size("snap") * n * nd)
    feats = orders * chans
    grad_gw, grad_gb, grad_cw, grad_cb = run(
        functools.partial(finish_kernel, hid, factor), "finish",
        [((2 * hid, feats), F32), ((1, 2 * hid), F32), ((hid, feats), F32), ((1, hid), F32)],
        grads,
    )
    return state_grad, grad_gw, grad_gb[0], grad_cw, grad_cb[0]


def solution(mesh):
    in_specs = (
        P("snap", None, "dom"),
        P("snap", None, "dom"),
        P("snap", None, "dom"),
        P(),
        P(),
        P(),
        P(),
        P(None, "dom"),
        P(None, "dom"),
        P("dom", None),
    )
    out_specs = (P("snap", None, "dom"), P(), P(), P(), P())
    return jax.shard_map(body, mesh=mesh, in_specs=in_specs, out_specs=out_specs, check_vma=False)
```

```python
import functools
import math

import jax
import jax.numpy as jnp
from jax import lax
from jax.experimental import pallas as pl
from jax.experimental.pallas import tpu as pltpu
from jax.sharding import PartitionSpec as P

F32 = jnp.float32
BF16 = jnp.bfloat16
LANES = 128


def nn(a, b):
    return lax.dot_general(a, b, (((1,), (0,)), ((), ())), preferred_element_type=F32)


def nt(a, b):
    return lax.dot_general(a, b, (((1,), (1,)), ((), ())), preferred_element_type=F32)


def tn(a, b):
    return lax.dot_general(a, b, (((0,), (0,)), ((), ())), preferred_element_type=F32)


def iota(shape, axis):
    return lax.broadcasted_iota(jnp.int32, shape, axis)


def column(row):
    k = row.shape[1]
    spread = jnp.broadcast_to(row.astype(F32), (k, k))
    return jnp.sum(jnp.where(iota((k, k), 0) == iota((k, k), 1), spread, 0.0), axis=1, keepdims=True)


def run(kernel, name, outs, *args, scratch=(), flops=20_000_000, vmem=24):
    whole = pl.BlockSpec(memory_space=pltpu.VMEM)
    return pl.pallas_call(
        kernel,
        name=name,
        out_shape=[jax.ShapeDtypeStruct(shape, kind) for shape, kind in outs],
        in_specs=[whole] * len(args),
        out_specs=[whole] * len(outs),
        scratch_shapes=list(scratch),
        compiler_params=pltpu.CompilerParams(vmem_limit_bytes=vmem * 1024 * 1024),
        cost_estimate=pl.CostEstimate(flops=flops, bytes_accessed=2_000_000, transcendentals=0),
    )(*args)


def prep_kernel(cap, nb, w, rows, readings, previous, e, s, b, pay):
    degree, n = nb.shape
    nh = s.shape[0]
    hid = previous.shape[1]
    fin = readings.shape[1]
    step = 32
    for at in range(0, n + nh, step):
        node = iota((step, n), 0) + at
        total = jnp.zeros((step, n), F32)
        for d in range(degree):
            total = total + jnp.where(node == nb[d : d + 1, :], w[d : d + 1, :], 0.0)
        e[at : at + step, :] = total.astype(BF16)
    sent = column(rows[...]).astype(jnp.int32)
    s[...] = jnp.where(iota((nh, n), 1) == sent, 1.0, 0.0).astype(BF16)
    b[:hid, :] = previous[0]
    rest = b.shape[0] - hid
    row = iota((rest, n), 0)
    tail = jnp.where(row == fin, 1.0, 0.0)
    for f in range(fin):
        tail = jnp.where(row == f, readings[0, f : f + 1, :].astype(F32), tail)
    b[hid:, :] = tail.astype(BF16)
    base = b[...]
    chans = base.shape[0]
    bound = nt(s[...], base)
    halo = nt(e[n:, :], base)
    for p in range(nh // cap):
        pay[p, :, :chans] = bound[p * cap : (p + 1) * cap, :]
        pay[p, :, LANES : LANES + chans] = halo[p * cap : (p + 1) * cap, :]


def order_matrix(shape, chans, hid, fin, block):
    k = iota(shape, 0)
    col = iota(shape, 1)
    m = lax.div(col, jnp.int32(block))
    c = col - m * block
    source = jnp.where(c < hid, m * chans + fin + c, jnp.where(c < hid + fin, m * chans + c - hid, -1))
    return jnp.where(k == source, 1.0, 0.0).astype(BF16)


def mid_a_kernel(hid, fin, orders, e, b, gw, cw, fa, ra, gw_o, cw_o):
    n = e.shape[1]
    a = e[:n, :]
    base = b[...]
    fa[...] = nt(base, a)
    ra[...] = nn(base, a)
    block = base.shape[0]
    order = order_matrix((gw.shape[1], orders * block), hid + fin, hid, fin, block)
    gw_o[...] = nn(gw[...], order).astype(BF16)
    cw_o[...] = nn(cw[...], order).astype(BF16)


def post_a_kernel(one, cap, recv, e, s, fa, ra, f1, r1, ro, ri, pay, flat):
    n = e.shape[1]
    nh = s.shape[0]
    chans = fa.shape[0]
    for p in range(nh // cap):
        flat[p * cap : (p + 1) * cap, :] = recv[p]
    h = e[n:, :]
    sel = s[...]
    seen = flat[:, :chans].astype(BF16)
    back = flat[:, LANES : LANES + chans]
    back_degree = flat[:, LANES + one : LANES + one + 1]
    out_degree = fa[one : one + 1, :] + jnp.sum(sel.astype(F32) * back_degree, axis=0, keepdims=True)
    pulled = ra[...] + tn(seen, h)
    inv_o = 1.0 / out_degree
    inv_i = 1.0 / pulled[one : one + 1, :]
    ro[...] = inv_o
    ri[...] = inv_i
    first_out = ((fa[...] + tn(back.astype(BF16), sel)) * inv_o).astype(BF16)
    first_in = (pulled * inv_i).astype(BF16)
    f1[...] = first_out
    r1[...] = first_in
    bound = nt(sel, first_in)
    halo = nt(h, first_out)
    hi, ho = scaled(h, inv_i), scaled(h, inv_o)
    si, so = scaled(sel, inv_i), scaled(sel, inv_o)
    coefs = (nt(sel, hi), nt(h, so), nt(sel, ho), nt(h, si))
    for p in range(nh // cap):
        at = slice(p * cap, (p + 1) * cap)
        pay[p, :, :chans] = bound[at, :]
        pay[p, :, LANES : LANES + chans] = halo[at, :]
        for k, coef in enumerate(coefs):
            pay[p, :, 2 * LANES + k * nh : 2 * LANES + (k + 1) * nh] = coef[at, :]


def scaled(rows, factor):
    return (rows.astype(F32) * factor).astype(BF16)


def mid_b_kernel(e, s, f1, r1, ro, ri, f2l, r2l, kc, ke, ka):
    n = e.shape[1]
    a = e[:n, :]
    h = e[n:, :]
    sel = s[...]
    nh = sel.shape[0]
    chans = f1.shape[0]
    inv_o, inv_i = ro[...], ri[...]
    outs = nt(jnp.concatenate([f1[...], scaled(sel, inv_o), scaled(sel, inv_i)], axis=0), a)
    ins = nn(jnp.concatenate([r1[...], scaled(h, inv_i), scaled(h, inv_o)], axis=0), a)
    f2l[...] = outs[:chans]
    r2l[...] = ins[:chans]
    kc[:nh, :] = ins[chans : chans + nh].astype(BF16)
    kc[nh:, :] = h
    ke[:nh, :] = outs[chans : chans + nh].astype(BF16)
    ke[nh:, :] = sel
    ka[:nh, :] = (2.0 * ins[chans + nh :]).astype(BF16)
    ka[nh : 2 * nh, :] = h
    ka[2 * nh : 3 * nh, :] = (2.0 * outs[chans + nh :]).astype(BF16)
    ka[3 * nh :, :] = sel


def send(pay, cap, left, right, left_two, right_two):
    nh = left.shape[0]
    rows = jnp.concatenate([left, right], axis=1)
    rows_two = jnp.concatenate([left_two, right_two], axis=1)
    both = jnp.concatenate([rows, rows_two], axis=0).astype(BF16)
    k = iota((2 * nh, 2 * nh), 0)
    part = lax.div(k, jnp.int32(2 * cap))
    spot = k - part * (2 * cap)
    source = jnp.where(spot < cap, part * cap + spot, nh + part * cap + spot - cap)
    mine = nn(jnp.where(iota((2 * nh, 2 * nh), 1) == source, 1.0, 0.0).astype(BF16), both)
    for p in range(nh // cap):
        own = mine[p * 2 * cap : (p + 1) * 2 * cap, :]
        pay[p] = jnp.concatenate([rows, own], axis=0).astype(BF16)


def post_b_kernel(cap, one, recv, e, s, b, f1, r1, f2l, r2l, ro, ri, gw, gb, states, reset, update, y, f1l, r1l, pay, flat):
    n = e.shape[1]
    nh = s.shape[0]
    hid = y.shape[0]
    chans = b.shape[0]
    for p in range(nh // cap):
        flat[p * cap : (p + 1) * cap, :] = recv[p, :, : 2 * LANES]
    a = e[:n, :]
    h = e[n:, :]
    sel = s[...]
    inv_o, inv_i = ro[...], ri[...]
    base = b[...].astype(F32)
    seen = flat[:, :chans].astype(BF16)
    back = flat[:, LANES : LANES + chans].astype(BF16)
    f2 = 2.0 * (f2l[...] + tn(back, sel)) * inv_o - base
    r2 = 2.0 * (r2l[...] + tn(seen, h)) * inv_i - base
    states[:chans, :] = b[...]
    states[chans : 2 * chans, :] = f1[...]
    states[2 * chans : 3 * chans, :] = f2.astype(BF16)
    states[3 * chans : 4 * chans, :] = r1[...]
    states[4 * chans :, :] = r2.astype(BF16)
    gates = jax.nn.sigmoid(nn(gw[...], states[...]) + column(gb[...]))
    reset[...] = gates[:hid]
    update[...] = gates[hid:]
    now = (gates[:hid] * base[:hid]).astype(BF16)
    y[...] = now
    local_out = nt(now, a) * inv_o
    local_in = nn(now, a) * inv_i
    f1l[...] = local_out
    r1l[...] = local_in
    bound = nt(sel, jnp.concatenate([now, local_in.astype(BF16)], axis=0))
    halo = nt(h, jnp.concatenate([now, local_out.astype(BF16)], axis=0))
    send(pay, cap, bound[:, :hid], halo[:, :hid], bound[:, hid:], halo[:, hid:])


def gather_matrix(coef, out, nd, cap, per, first, factor):
    nh = nd * cap
    width = nd * per
    k = iota((nh, width), 0)
    col = iota((nh, width), 1)
    r = lax.div(col, jnp.int32(per))
    u = col - r * per
    p = lax.div(u, jnp.int32(cap))
    spot = u - p * cap
    here = lax.div(k, jnp.int32(cap))
    slot = k - here * cap
    inside = u < nh
    place = jnp.where((k == r * cap + spot) & inside, 1.0, 0.0).astype(BF16)
    keep = (here == p) & inside
    for i in range(2):
        wide = nn(coef[:, (first + i) * nh : (first + i + 1) * nh].astype(BF16), place)
        own = (r == here) & (u == nh + cap + slot)
        out[(i + 1) * nh : (i + 2) * nh, :] = jnp.where(keep, factor * wide, jnp.where(own, 1.0, 0.0)).astype(BF16)
    out[:nh, :] = jnp.where((r == here) & (u == nh + slot), 1.0, 0.0).astype(BF16)


def mid_c_kernel(nd, cap, per, fused, recv, e, f1l, r1l, f2l, r2l, *rest):
    n = e.shape[1]
    a = e[:n, :]
    f2l[...] = nt(f1l[...].astype(BF16), a)
    r2l[...] = nn(r1l[...].astype(BF16), a)
    if fused:
        gd, ga, flat = rest
        for p in range(nd):
            flat[p * cap : (p + 1) * cap, :] = recv[p, :, 2 * LANES :]
        gather_matrix(flat, gd, nd, cap, per, 0, 1.0)
        gather_matrix(flat, ga, nd, cap, per, 2, 2.0)


def arrived(fused, hid, nh, g, recv):
    if fused:
        halo = nn(g[...], recv[...].reshape(recv.shape[0] * recv.shape[1], recv.shape[2]))
        two = halo[nh : 2 * nh, :hid], halo[2 * nh :, hid:]
    else:
        halo = recv[...]
        two = halo[nh:, :hid], halo[nh:, hid:]
    one = halo[:nh]
    return one[:, :hid], one[:, hid:], two[0], two[1]


def back_and_send(cap, hid, g, a, h, sel, inv_o, inv_i, z1, z2, pay):
    g0, g1, g2, g3, g4 = (g[m * hid : (m + 1) * hid, :].astype(BF16).astype(F32) for m in range(5))
    y1 = (g2 * inv_o).astype(BF16)
    y2 = (g4 * inv_i).astype(BF16)
    now1 = ((g1 + 2.0 * nn(y1, a)) * inv_o).astype(BF16)
    now2 = ((g3 + 2.0 * nt(y2, a)) * inv_i).astype(BF16)
    z1[...] = now1
    z2[...] = now2
    bound = nt(sel, jnp.concatenate([y1, now1], axis=0))
    halo = nt(h, jnp.concatenate([y2, now2], axis=0))
    send(pay, cap, bound[:, :hid], halo[:, :hid], bound[:, hid:], halo[:, hid:])
    return g0 - g2 - g4


def hidden_weights(w, hid, block, orders):
    return jnp.concatenate([w[:, m * block : m * block + hid] for m in range(orders)], axis=1)


def post_c_kernel(fused, cap, orders, g, recv, e, s, kc, ke, y, f1l, r1l, f2l, r2l, ro, ri, states, cw, cb, upstream, update,
                  mixed, cand_grad, gate_update, z1, z2, direct, pay):
    n = e.shape[1]
    nh = s.shape[0]
    hid = y.shape[0]
    block = states.shape[0] // orders
    a = e[:n, :]
    h = e[n:, :]
    sel = s[...]
    inv_o, inv_i = ro[...], ri[...]
    c1, e1, c2, e2 = arrived(fused, hid, nh, g, recv)
    base = y[...].astype(F32)
    c1, e1 = c1.astype(BF16), e1.astype(BF16)
    cc = jnp.concatenate([c1, c2.astype(BF16)], axis=0)
    ee = jnp.concatenate([e1, e2.astype(BF16)], axis=0)
    f1 = f1l[...] + tn(e1, sel) * inv_o
    f2 = 2.0 * (f2l[...] + tn(ee, ke[...])) * inv_o - base
    r1 = r1l[...] + tn(c1, h) * inv_i
    r2 = 2.0 * (r2l[...] + tn(cc, kc[...])) * inv_i - base
    for m, value in enumerate((y[...], f1, f2, r1, r2)):
        mixed[m * block : m * block + hid, :] = value.astype(BF16)
        mixed[m * block + hid : (m + 1) * block, :] = states[m * block + hid : (m + 1) * block, :]
    weights = cw[...]
    cand = jnp.tanh(nn(weights, mixed[...]) + column(cb[...]))
    up = upstream[0].astype(F32)
    gate = update[...]
    grad = (up * (1.0 - gate) * (1.0 - cand * cand)).astype(BF16)
    cand_grad[...] = grad
    held = states[:hid, :].astype(F32)
    gate_update[...] = (up * (held - cand) * gate * (1.0 - gate)).astype(BF16)
    back = tn(hidden_weights(weights, hid, block, orders), grad)
    direct[...] = back_and_send(cap, hid, back, a, h, sel, inv_o, inv_i, z1, z2, pay)


def weight_part(grad, features, orders, chans, hid, fin):
    block = features.shape[0] // orders
    width = -(-(orders * chans + 1) // LANES) * LANES
    shape = (width, orders * block)
    k = iota(shape, 0)
    col = iota(shape, 1)
    m = lax.div(col, jnp.int32(block))
    c = col - m * block
    source = jnp.where(c < hid, m * chans + fin + c, jnp.where(c < hid + fin, m * chans + c - hid, -1))
    source = jnp.where(col == hid + fin, orders * chans, source)
    order = jnp.where(k == source, 1.0, 0.0).astype(BF16)
    return nt(nt(grad, features).astype(BF16), order)


def mid_d_kernel(orders, fin, e, z1, z2, direct, cand_grad, mixed, gate_update, states, base, part):
    n = e.shape[1]
    a = e[:n, :]
    hid = z1.shape[0]
    base[...] = direct[...] + nn(z1[...], a) + nt(z2[...], a)
    part[:hid, :] = weight_part(gate_update[...], states[...], orders, hid + fin, hid, fin).astype(BF16)
    part[hid:, :] = weight_part(cand_grad[...], mixed[...], orders, hid + fin, hid, fin).astype(BF16)


def add_halo(fused, g, recv, ka, base):
    hid = base.shape[0]
    nh = ka.shape[0] // 4
    c1, e1, c2, e2 = arrived(fused, hid, nh, g, recv)
    return base[...] + tn(jnp.concatenate([c1, c2, e1, e2], axis=0).astype(BF16), ka[...])


def post_d_kernel(fused, cap, orders, g, recv, e, s, ka, base, ro, ri, states, gw, upstream, reset, update, gate_update,
                  gate_reset, z1, z2, direct, pay):
    n = e.shape[1]
    hid = base.shape[0]
    block = states.shape[0] // orders
    scaled_grad = add_halo(fused, g, recv, ka, base)
    held = states[:hid, :].astype(F32)
    gate = reset[...]
    grad = (scaled_grad * held * gate * (1.0 - gate)).astype(BF16)
    gate_reset[...] = grad
    weights = hidden_weights(gw[...], hid, block, orders)
    back = tn(weights, jnp.concatenate([grad, gate_update[...]], axis=0))
    rest = back_and_send(cap, hid, back, e[:n, :], e[n:, :], s[...], ro[...], ri[...], z1, z2, pay)
    direct[...] = rest + upstream[0].astype(F32) * update[...] + scaled_grad * gate


def mid_e_kernel(orders, fin, rows, e, z1, z2, direct, gate_reset, states, part, base, grads):
    n = e.shape[1]
    a = e[:n, :]
    hid = z1.shape[0]
    base[...] = direct[...] + nn(z1[...], a) + nt(z2[...], a)
    first = weight_part(gate_reset[...], states[...], orders, hid + fin, hid, fin)
    both = jnp.concatenate([first, part[...].astype(F32)], axis=0)
    for k in range(grads.shape[0]):
        if k * rows < both.shape[0]:
            grads[k] = both[k * rows : (k + 1) * rows, :].astype(BF16)
        else:
            grads[k] = jnp.zeros(grads.shape[1:], BF16)


def post_e_kernel(fused, g, recv, ka, base, out):
    out[0] = add_halo(fused, g, recv, ka, base).astype(BF16)


def add_kernel(recv, out):
    total = recv[0].astype(F32)
    for k in range(1, recv.shape[0]):
        total = total + recv[k].astype(F32)
    for k in range(out.shape[0]):
        out[k] = total.astype(BF16)


def finish_kernel(hid, factor, recv, gw, gb, cw, cb):
    rows = recv.shape[1]
    features = gw.shape[1]
    total = gw.shape[0] + cw.shape[0]
    for k in range(total // rows):
        part = recv[k].astype(F32)[:, :features] * factor
        at = k * rows
        if at < 2 * hid:
            gw[at : at + rows, :] = part
        else:
            cw[at - 2 * hid : at - 2 * hid + rows, :] = part
    flat = jnp.concatenate([recv[k].astype(F32) for k in range(total // rows)], axis=0)
    pick = jnp.where(iota((8, flat.shape[1]), 1) == features, 1.0, 0.0).astype(BF16)
    bias = nt(pick, flat.astype(BF16))[:1] * factor
    gb[...] = bias[:, : 2 * hid]
    cb[...] = bias[:, 2 * hid :]


def spread_body(
    readings,
    previous,
    upstream,
    gate_weight,
    gate_bias,
    cand_weight,
    cand_bias,
    neighbours,
    edge_weight,
    send_rows,
):
    fin, hid = readings.shape[1], previous.shape[1]
    chans = fin + hid
    orders = gate_weight.shape[1] // chans
    n = readings.shape[2]
    nd = lax.axis_size("dom")
    devices = nd * lax.axis_size("snap")
    nh = send_rows.shape[1]
    cap = nh // nd
    block = hid + 16 * (-(-(fin + 1) // 16))
    one = hid + fin
    per = nh + 2 * cap
    fused = 3 * nh * nd * per <= 1 << 18
    move = functools.partial(lax.all_to_all, axis_name="dom", split_axis=0, concat_axis=0, tiled=True)

    e, s, b, pay = run(
        functools.partial(prep_kernel, cap), "prep",
        [((n + nh, n), BF16), ((nh, n), BF16), ((block, n), BF16), ((nd, cap, 2 * LANES), F32)],
        neighbours, edge_weight, send_rows, readings, previous,
    )
    recv = move(pay)
    fa, ra, gw, cw = run(
        functools.partial(mid_a_kernel, hid, fin, orders), "mid_a",
        [((block, n), F32), ((block, n), F32), ((2 * hid, orders * block), BF16), ((hid, orders * block), BF16)],
        e, b, gate_weight, cand_weight,
    )
    wide = 2 * LANES + 4 * nh
    f1, r1, ro, ri, pay = run(
        functools.partial(post_a_kernel, one, cap), "post_a",
        [((block, n), BF16), ((block, n), BF16), ((1, n), F32), ((1, n), F32), ((nd, cap, wide), F32)],
        recv, e, s, fa, ra, scratch=[pltpu.VMEM((nh, 2 * LANES), F32)],
    )
    recv_b = move(pay)
    f2l, r2l, kc, ke, ka = run(
        mid_b_kernel, "mid_b",
        [((block, n), F32), ((block, n), F32), ((2 * nh, n), BF16), ((2 * nh, n), BF16), ((4 * nh, n), BF16)],
        e, s, f1, r1, ro, ri,
    )
    pay_kind = ((nd, per, 2 * hid), BF16)
    field, field16 = ((hid, n), F32), ((hid, n), BF16)
    states, reset, update, y, f1l, r1l, pay = run(
        functools.partial(post_b_kernel, cap, one), "post_b",
        [((orders * block, n), BF16), field, field, field16, field, field, pay_kind],
        recv_b, e, s, b, f1, r1, f2l, r2l, ro, ri, gw, gate_bias[None, :],
        scratch=[pltpu.VMEM((nh, 2 * LANES), F32)],
    )
    recv = move(pay)
    table = ((3 * nh, nd * per), BF16)
    f2l, r2l, *tables = run(
        functools.partial(mid_c_kernel, nd, cap, per, fused), "mid_c",
        [field, field] + [table] * (2 if fused else 0),
        recv_b, e, f1l, r1l, scratch=[pltpu.VMEM((nh, 4 * nh), F32)] if fused else [],
    )
    if fused:
        inward, outward = tables
        halo_of = lambda got, first, factor: got
    else:
        inward = outward = jnp.zeros((8, LANES), BF16)
        coefs = recv_b[:, :, 2 * LANES :].reshape(nd, cap, 4, nd, cap)

        def halo_of(got, first, factor):
            rows = got[:, :nh].reshape(nd, nd, cap, 2, hid).astype(F32)
            two = jnp.einsum("psgrt,rptgk->psgk", coefs[:, :, first : first + 2], rows)
            two = factor * two.reshape(nh, 2 * hid) + got[:, nh + cap :].reshape(nh, 2 * hid).astype(F32)
            return jnp.concatenate([got[:, nh : nh + cap].reshape(nh, 2 * hid).astype(F32), two], axis=0)

    mixed, cand_grad, gate_update, z1, z2, direct, pay = run(
        functools.partial(post_c_kernel, fused, cap, orders), "post_c",
        [((orders * block, n), BF16), field16, field16, field16, field16, field, pay_kind],
        inward, halo_of(recv, 0, 1.0), e, s, kc, ke, y, f1l, r1l, f2l, r2l, ro, ri, states, cw, cand_bias[None, :], upstream, update,
    )
    recv = move(pay)
    width = -(-(orders * chans + 1) // LANES) * LANES
    base, part = run(
        functools.partial(mid_d_kernel, orders, fin), "mid_d", [field, ((2 * hid, width), BF16)],
        e, z1, z2, direct, cand_grad, mixed, gate_update, states,
    )
    gate_reset, z1, z2, direct, pay = run(
        functools.partial(post_d_kernel, fused, cap, orders), "post_d",
        [field16, field16, field16, field, pay_kind],
        outward, halo_of(recv, 2, 2.0), e, s, ka, base, ro, ri, states, gw, upstream, reset, update, gate_update,
    )
    recv = move(pay)
    rows = 8 * (-(-3 * hid // (8 * devices)))
    base, grads = run(
        functools.partial(mid_e_kernel, orders, fin, rows), "mid_e", [field, ((devices, rows, width), BF16)],
        e, z1, z2, direct, gate_reset, states, part,
    )
    (state_grad,) = run(
        functools.partial(post_e_kernel, fused), "post_e", [((1, hid, n), BF16)],
        outward, halo_of(recv, 2, 2.0), ka, base,
    )
    both = ("snap", "dom")
    grads = lax.all_to_all(grads, both, 0, 0, tiled=True)
    (grads,) = run(add_kernel, "add", [((devices, rows, width), BF16)], grads)
    grads = lax.all_to_all(grads, both, 0, 0, tiled=True)
    factor = 1.0 / math.sqrt(readings.shape[0] * lax.axis_size("snap") * n * nd)
    feats = orders * chans
    grad_gw, grad_gb, grad_cw, grad_cb = run(
        functools.partial(finish_kernel, hid, factor), "finish",
        [((2 * hid, feats), F32), ((1, 2 * hid), F32), ((hid, feats), F32), ((1, hid), F32)],
        grads,
    )
    return state_grad, grad_gw, grad_gb[0], grad_cw, grad_cb[0]


def pack_kernel(own, nb, w, rows, readings, previous, tail):
    degree = nb.shape[0]
    nh = rows.shape[1]
    hid = previous.shape[1]
    fin = readings.shape[1]
    tail[...] = jnp.zeros_like(tail)
    tail[:fin, :] = readings[0].astype(F32)
    high = lax.shift_right_logical(nb[...], 5)
    tail[fin : fin + degree, :] = high.astype(F32)
    tail[fin + degree : fin + 2 * degree, :] = (nb[...] - high * 32).astype(F32)
    tail[fin + 2 * degree : fin + 3 * degree, :] = w[...]
    at = fin + 3 * degree
    high = lax.shift_right_logical(rows[...], 5)
    tail[at : at + 1, :nh] = high.astype(F32)
    tail[at + 1 : at + 2, :nh] = (rows[...] - high * 32).astype(F32)
    own[:hid, :] = previous[0]
    own[hid:, :] = tail[...].astype(BF16)


def pack_entry(nb, w, rows, readings, previous, own, tail):
    pack_kernel(own, nb, w, rows, readings, previous, tail)


def exchange(first, second, e, sx, pay):
    n = e.shape[2]
    count = first[0].shape[0]
    bound = sum(nt(first[p], sx[p]) for p in range(len(first)))
    halo = sum(nt(second[p], e[p, n:, :]) for p in range(len(second)))
    pay[:count, :] = bound.astype(BF16)
    pay[count:, :] = halo.astype(BF16)


def merged(mine, got):
    half = mine.shape[1] // 2
    value = jnp.where(iota(mine.shape, 1) < half, mine[...].astype(F32), got[...].astype(F32)).astype(BF16)
    count = mine.shape[0] // 2
    return value[:count, :], value[count:, :]


def build_kernel(cap, hid, fin, degree, parts, *refs):
    blocks_in, (e, sx, b, pay, blocks) = refs[:parts], refs[parts:]
    n = e.shape[2]
    slots = sx.shape[1]
    half = slots // 2
    nh = 2 * parts * cap
    me = lax.axis_index("dom")
    z = lax.shift_right_logical(me, 1)
    core = me - 2 * z
    for k in range(parts):
        blocks[lax.bitwise_xor(z, jnp.int32(k))] = blocks_in[k][...]
    lane = iota((slots, n), 1)
    slot = iota((slots, 1), 0)
    rel = lax.div(slot, jnp.int32(half))
    rest = slot - rel * half
    dest = lax.div(rest, jnp.int32(parts * cap))
    rest = rest - dest * (parts * cap)
    source = lax.div(rest, jnp.int32(cap))
    t = rest - source * cap
    other = lax.bitwise_xor(rel, core)
    spot = (dest * 2 + other) * cap + t
    width = -(-nh // LANES) * LANES
    step = parts * cap
    row = iota((32, n), 0).astype(F32)
    for p in range(parts):
        tail = blocks[p, hid:, :].astype(F32)
        high, low = tail[fin : fin + degree], tail[fin + degree : fin + 2 * degree]
        w = tail[fin + 2 * degree : fin + 3 * degree]
        at = fin + 3 * degree
        sent = tail[at : at + 1] * 32.0 + tail[at + 1 : at + 2]
        low_is = [jnp.where(low[d : d + 1] == row, 1.0, 0.0).astype(BF16) for d in range(degree)]
        for chunk in range(n // 32):
            total = None
            for d in range(degree):
                term = low_is[d] * jnp.where(high[d : d + 1] == float(chunk), w[d : d + 1], 0.0).astype(BF16)
                total = term if total is None else total + term
            e[p, chunk * 32 : (chunk + 1) * 32, :] = total
        names = high * 32.0 + low
        e[p, n:, :] = jnp.zeros((slots, n), BF16)
        line = iota((step, n), 0)
        src = lax.div(line, jnp.int32(cap))
        for r in range(2):
            node = (n + (src * 2 + lax.bitwise_xor(jnp.int32(r), core)) * cap + line - src * cap).astype(F32)
            total = jnp.zeros((step, n), F32)
            for d in range(degree):
                total = total + jnp.where(names[d : d + 1] == node, w[d : d + 1], 0.0)
            start = n + r * half + p * step
            e[p, start : start + step, :] = total.astype(BF16)
        named = jnp.where(iota((slots, width), 1) == spot, sent[:, :width], 0.0)
        target = jnp.sum(named, axis=1, keepdims=True).astype(jnp.int32)
        target = jnp.where(source == p, target, -1)
        sx[p] = jnp.where(lane == target, 1.0, 0.0).astype(BF16)
        b[p, :hid, :] = blocks[p, :hid, :]
        line = iota(tail.shape, 0)
        b[p, hid:, :] = jnp.where(line < fin, tail, jnp.where(line == fin, 1.0, 0.0)).astype(BF16)
    base = [b[p] for p in range(parts)]
    exchange(base, base, e, sx, pay)


def order_kernel(hid, fin, orders, block, gw, cw, own, gw_o, cw_o):
    order = order_matrix((cw.shape[1], orders * block), hid + fin, hid, fin, block)
    gw_o[...] = tn(gw[...], order).astype(BF16)
    cw_o[...] = nn(cw[...], order).astype(BF16)


def local_kernel(e, x1, x2, l1, l2):
    n = e.shape[2]
    for p in range(e.shape[0]):
        l1[p] = nn(x1[p], e[p, :n, :])
        l2[p] = nt(x2[p], e[p, :n, :])


def chip_a_kernel(one, mine, got, e, sx, l1, l2, f1, r1, ro, ri, pay):
    n = e.shape[2]
    top, low = merged(mine, got)
    firsts, seconds = [], []
    for p in range(e.shape[0]):
        pulled = l1[p] + nn(top, e[p, n:, :])
        pushed = l2[p] + nn(low, sx[p])
        inv_o = 1.0 / pushed[one : one + 1, :]
        inv_i = 1.0 / pulled[one : one + 1, :]
        ro[p] = inv_o
        ri[p] = inv_i
        out = (pushed * inv_o).astype(BF16)
        into = (pulled * inv_i).astype(BF16)
        f1[p] = out
        r1[p] = into
        firsts.append(into)
        seconds.append(out)
    exchange(firsts, seconds, e, sx, pay)


def chip_b_kernel(mine, got, e, sx, b, f1, r1, l1, l2, ro, ri, gw, gb, states, reset, update, y, pay):
    n = e.shape[2]
    hid = y.shape[1]
    chans = b.shape[1]
    top, low = merged(mine, got)
    bias = column(gb[...])
    fields = []
    for p in range(e.shape[0]):
        base = b[p].astype(F32)
        r2 = 2.0 * (l1[p] + nn(top, e[p, n:, :])) * ri[p] - base
        f2 = 2.0 * (l2[p] + nn(low, sx[p])) * ro[p] - base
        states[p, :chans, :] = b[p]
        states[p, chans : 2 * chans, :] = f1[p]
        states[p, 2 * chans : 3 * chans, :] = f2.astype(BF16)
        states[p, 3 * chans : 4 * chans, :] = r1[p]
        states[p, 4 * chans :, :] = r2.astype(BF16)
        gates = jax.nn.sigmoid(nn(gw[...], states[p]) + bias)
        reset[p] = gates[:hid]
        update[p] = gates[hid:]
        now = (gates[:hid] * base[:hid]).astype(BF16)
        y[p] = now
        fields.append(now)
    exchange(fields, fields, e, sx, pay)


def chip_c1_kernel(mine, got, e, sx, l1, l2, ro, ri, f1, r1, pay):
    n = e.shape[2]
    top, low = merged(mine, got)
    firsts, seconds = [], []
    for p in range(e.shape[0]):
        into = ((l1[p] + nn(top, e[p, n:, :])) * ri[p]).astype(BF16)
        out = ((l2[p] + nn(low, sx[p])) * ro[p]).astype(BF16)
        f1[p] = out
        r1[p] = into
        firsts.append(into)
        seconds.append(out)
    exchange(firsts, seconds, e, sx, pay)


def split_back(back, hid, inv_o, inv_i, y1, y2, g1, g3):
    parts = [back[m * hid : (m + 1) * hid, :].astype(BF16) for m in range(5)]
    y1[...] = (parts[2].astype(F32) * inv_o).astype(BF16)
    y2[...] = (parts[4].astype(F32) * inv_i).astype(BF16)
    g1[...] = parts[1]
    g3[...] = parts[3]
    return parts[0].astype(F32) - parts[2].astype(F32) - parts[4].astype(F32)


def chip_c2_kernel(orders, parts, *refs):
    ups, refs = refs[:parts], refs[parts:]
    mine, got, e, sx, y, f1, r1, l1, l2, ro, ri, states, cw, cb, update = refs[:15]
    mixed, cand_grad, gate_update, y1, y2, g1, g3, upstream, direct, pay = refs[15:]
    n = e.shape[2]
    hid = y.shape[1]
    block = states.shape[1] // orders
    z = lax.shift_right_logical(lax.axis_index("dom"), 1)
    for k in range(parts):
        upstream[lax.bitwise_xor(z, jnp.int32(k))] = ups[k][0]
    top, low = merged(mine, got)
    bias = column(cb[...])
    hidden = hidden_weights(cw[...], hid, block, orders)
    for p in range(e.shape[0]):
        base = y[p].astype(F32)
        r2 = 2.0 * (l1[p] + nn(top, e[p, n:, :])) * ri[p] - base
        f2 = 2.0 * (l2[p] + nn(low, sx[p])) * ro[p] - base
        for m, value in enumerate((y[p], f1[p], f2, r1[p], r2)):
            mixed[p, m * block : m * block + hid, :] = value.astype(BF16)
            mixed[p, m * block + hid : (m + 1) * block, :] = states[p, m * block + hid : (m + 1) * block, :]
        cand = jnp.tanh(nn(cw[...], mixed[p]) + bias)
        up = upstream[p].astype(F32)
        gate = update[p]
        grad = (up * (1.0 - gate) * (1.0 - cand * cand)).astype(BF16)
        cand_grad[p] = grad
        gate_update[p] = (up * (states[p, :hid, :].astype(F32) - cand) * gate * (1.0 - gate)).astype(BF16)
        direct[p] = split_back(tn(hidden, grad), hid, ro[p], ri[p], y1.at[p], y2.at[p], g1.at[p], g3.at[p])
    parts = range(e.shape[0])
    exchange([y1[p] for p in parts], [y2[p] for p in parts], e, sx, pay)


def chip_part(grads, features, orders, chans, hid, fin):
    block = features.shape[1] // orders
    width = -(-(orders * chans + 1) // LANES) * LANES
    shape = (width, orders * block)
    k = iota(shape, 0)
    col = iota(shape, 1)
    m = lax.div(col, jnp.int32(block))
    c = col - m * block
    source = jnp.where(c < hid, m * chans + fin + c, jnp.where(c < hid + fin, m * chans + c - hid, -1))
    source = jnp.where(col == hid + fin, orders * chans, source)
    order = jnp.where(k == source, 1.0, 0.0).astype(BF16)
    total = sum(nt(grads[p], features[p]) for p in range(grads.shape[0]))
    return nt(total.astype(BF16), order)


def local_d_kernel(orders, fin, e, y1, y2, cand_grad, mixed, gate_update, states, l1, l2, part):
    hid = y1.shape[1]
    local_kernel(e, y1, y2, l1, l2)
    part[:hid, :] = chip_part(gate_update, states, orders, hid + fin, hid, fin).astype(BF16)
    part[hid:, :] = chip_part(cand_grad, mixed, orders, hid + fin, hid, fin).astype(BF16)


def chip_e1_kernel(after, *refs):
    chip_d1_kernel(*refs)


def chip_d1_kernel(mine, got, e, sx, l1, l2, g1, g3, ro, ri, z1, z2, pay):
    n = e.shape[2]
    top, low = merged(mine, got)
    firsts, seconds = [], []
    for p in range(e.shape[0]):
        one = ((g1[p].astype(F32) + 2.0 * (l1[p] + nn(top, e[p, n:, :]))) * ro[p]).astype(BF16)
        two = ((g3[p].astype(F32) + 2.0 * (l2[p] + nn(low, sx[p]))) * ri[p]).astype(BF16)
        z1[p] = one
        z2[p] = two
        firsts.append(one)
        seconds.append(two)
    exchange(firsts, seconds, e, sx, pay)


def local_d2_kernel(e, z1, z2, direct, base):
    n = e.shape[2]
    for p in range(e.shape[0]):
        base[p] = direct[p] + nn(z1[p], e[p, :n, :]) + nt(z2[p], e[p, :n, :])


def chip_d2_kernel(orders, mine, got, e, sx, base, ro, ri, states, gw, upstream, reset, update, gate_update,
                   gate_reset, y1, y2, g1, g3, direct, pay):
    n = e.shape[2]
    hid = base.shape[1]
    block = states.shape[1] // orders
    top, low = merged(mine, got)
    hidden = hidden_weights(gw[...], hid, block, orders)
    for p in range(e.shape[0]):
        scaled_grad = base[p] + nn(top, e[p, n:, :]) + nn(low, sx[p])
        gate = reset[p]
        grad = (scaled_grad * states[p, :hid, :].astype(F32) * gate * (1.0 - gate)).astype(BF16)
        gate_reset[p] = grad
        back = tn(hidden, jnp.concatenate([grad, gate_update[p]], axis=0))
        rest = split_back(back, hid, ro[p], ri[p], y1.at[p], y2.at[p], g1.at[p], g3.at[p])
        direct[p] = rest + upstream[p].astype(F32) * update[p] + scaled_grad * gate
    parts = range(e.shape[0])
    exchange([y1[p] for p in parts], [y2[p] for p in parts], e, sx, pay)


def grads_kernel(orders, fin, gate_reset, states, part, keep, give, flat):
    hid = gate_reset.shape[1]
    half = keep.shape[0]
    core = lax.rem(lax.axis_index("dom"), 2)
    flat[:hid, :] = chip_part(gate_reset, states, orders, hid + fin, hid, fin)
    flat[hid:, :] = part[...].astype(F32)
    keep[...] = flat[pl.ds(pl.multiple_of(core * half, 8), half), :].astype(BF16)
    give[...] = flat[pl.ds(pl.multiple_of((1 - core) * half, 8), half), :].astype(BF16)


def local_e_kernel(e, z1, z2, direct, base):
    n = e.shape[2]
    z = lax.shift_right_logical(lax.axis_index("dom"), 1)
    a = e[z, :n, :]
    base[...] = direct[z] + nn(z1[z], a) + nt(z2[z], a)


def chip_e_kernel(mine, got, e, sx, base, out):
    n = e.shape[2]
    z = lax.shift_right_logical(lax.axis_index("dom"), 1)
    top, low = merged(mine, got)
    out[0] = (base[...] + nn(top, e[z, n:, :]) + nn(low, sx[z])).astype(BF16)


def sum_kernel(*refs):
    values = [ref[...].astype(F32) for ref in refs[:-1]]
    while len(values) > 1:
        values = [values[k] + values[k + 1] for k in range(0, len(values), 2)]
    refs[-1][...] = values[0].astype(BF16)


def end_kernel(factor, mine, got, gw, gb, cw, cb, flat):
    half = mine.shape[0]
    core = lax.rem(lax.axis_index("dom"), 2)
    flat[pl.ds(pl.multiple_of(core * half, 8), half), :] = mine[...].astype(F32)
    flat[pl.ds(pl.multiple_of((1 - core) * half, 8), half), :] = got[...].astype(F32)
    features, rows = gw.shape
    same = jnp.where(iota((features, flat.shape[1]), 0) == iota((features, flat.shape[1]), 1), 1.0, 0.0).astype(BF16)
    gw[...] = nt(same, flat[:rows, :].astype(BF16)) * factor
    cw[...] = flat[rows:, :features] * factor
    pick = jnp.where(iota((8, flat.shape[1]), 1) == features, 1.0, 0.0).astype(BF16)
    bias = nt(pick, flat[...].astype(BF16))[:1] * factor
    gb[...] = bias[:, :rows]
    cb[...] = bias[:, rows:]


def chip_body(
    readings,
    previous,
    upstream,
    gate_weight,
    gate_bias,
    cand_weight,
    cand_bias,
    neighbours,
    edge_weight,
    send_rows,
):
    fin, hid = readings.shape[1], previous.shape[1]
    chans = fin + hid
    orders = gate_weight.shape[1] // chans
    degree = neighbours.shape[0]
    n = readings.shape[2]
    nd = lax.axis_size("dom")
    snaps = lax.axis_size("snap")
    parts = nd // 2
    cap = send_rows.shape[1] // nd
    block = hid + 16 * (-(-(fin + 3 * degree + 2) // 16))
    slots = 2 * parts * parts * cap

    def swap(array, k, axis="dom", size=nd):
        return lax.ppermute(array, axis, [(i, i ^ k) for i in range(size)])

    (own,) = run(
        pack_entry, "pack", [((block, n), BF16)], neighbours, edge_weight, send_rows, readings, previous,
        scratch=[pltpu.VMEM((block - hid, n), F32)], vmem=56,
    )
    blocks = [own] + [swap(own, 2 * k) for k in range(1, parts)]
    ups = [upstream] + [swap(upstream, 2 * k) for k in range(1, parts)]
    gw, cw = run(
        functools.partial(order_kernel, hid, fin, orders, block), "order",
        [((2 * hid, orders * block), BF16), ((hid, orders * block), BF16)], gate_weight.T, cand_weight, own,
    )
    wide, wide16, wide_pay = ((parts, block, n), F32), ((parts, block, n), BF16), ((2 * block, slots), BF16)
    field, field16, pay_kind = ((parts, hid, n), F32), ((parts, hid, n), BF16), ((2 * hid, slots), BF16)
    line = ((parts, 1, n), F32)
    e, sx, b, pay = run(
        functools.partial(build_kernel, cap, hid, fin, degree, parts), "build",
        [((parts, n + slots, n), BF16), ((parts, slots, n), BF16), wide16, wide_pay],
        *blocks, scratch=[pltpu.VMEM((parts, block, n), BF16)],
    )
    got = swap(pay, 1)
    l1, l2 = run(local_kernel, "local_a", [wide, wide], e, b, b)
    f1, r1, ro, ri, pay = run(
        functools.partial(chip_a_kernel, hid + fin), "chip_a", [wide16, wide16, line, line, wide_pay],
        pay, got, e, sx, l1, l2,
    )
    got = swap(pay, 1)
    l1, l2 = run(local_kernel, "local_b", [wide, wide], e, r1, f1)
    states, reset, update, y, pay = run(
        chip_b_kernel, "chip_b", [((parts, orders * block, n), BF16), field, field, field16, pay_kind],
        pay, got, e, sx, b, f1, r1, l1, l2, ro, ri, gw, gate_bias[None, :],
    )
    got = swap(pay, 1)
    l1, l2 = run(local_kernel, "local_c1", [field, field], e, y, y)
    f1, r1, pay = run(
        chip_c1_kernel, "chip_c1", [field16, field16, pay_kind], pay, got, e, sx, l1, l2, ro, ri
    )
    got = swap(pay, 1)
    l1, l2 = run(local_kernel, "local_c2", [field, field], e, r1, f1)
    mixed, cand_grad, gate_update, y1, y2, g1, g3, up, direct, pay = run(
        functools.partial(chip_c2_kernel, orders, parts), "chip_c2",
        [((parts, orders * block, n), BF16)] + [field16] * 7 + [field, pay_kind],
        *ups, pay, got, e, sx, y, f1, r1, l1, l2, ro, ri, states, cw, cand_bias[None, :], update,
    )
    got = swap(pay, 1)
    width = -(-(orders * chans + 1) // LANES) * LANES
    l1, l2, part = run(
        functools.partial(local_d_kernel, orders, fin), "local_d1", [field, field, ((2 * hid, width), BF16)],
        e, y1, y2, cand_grad, mixed, gate_update, states,
    )
    z1, z2, pay = run(
        chip_d1_kernel, "chip_d1", [field16, field16, pay_kind], pay, got, e, sx, l1, l2, g1, g3, ro, ri
    )
    got = swap(pay, 1)
    (base,) = run(local_d2_kernel, "local_d2", [field], e, z1, z2, direct)
    gate_reset, y1, y2, g1, g3, direct, pay = run(
        functools.partial(chip_d2_kernel, orders), "chip_d2", [field16] * 5 + [field, pay_kind],
        pay, got, e, sx, base, ro, ri, states, gw, up, reset, update, gate_update,
    )
    got = swap(pay, 1)
    half = ((3 * hid // 2, width), BF16)
    keep, give = run(
        functools.partial(grads_kernel, orders, fin), "grads", [half, half], gate_reset, states, part,
        scratch=[pltpu.VMEM((3 * hid, width), F32)],
    )
    (mine,) = run(sum_kernel, "sum_core", [half], keep, swap(give, 1))
    every = [mine] + [swap(mine, k, "snap", snaps) for k in range(1, snaps)]
    l1, l2 = run(local_kernel, "local_e1", [field, field], e, y1, y2)
    z1, z2, pay = run(
        chip_e1_kernel, "chip_e1", [field16, field16, pay_kind], mine, pay, got, e, sx, l1, l2, g1, g3, ro, ri
    )
    got = swap(pay, 1)
    (base,) = run(local_e_kernel, "local_e2", [((hid, n), F32)], e, z1, z2, direct)
    (state_grad,) = run(chip_e_kernel, "chip_e2", [((1, hid, n), BF16)], pay, got, e, sx, base)
    (mine,) = run(sum_kernel, "sum_snap", [half], *every)
    factor = 1.0 / math.sqrt(readings.shape[0] * snaps * n * nd)
    feats = orders * chans
    grad_gw, grad_gb, grad_cw, grad_cb = run(
        functools.partial(end_kernel, factor), "end",
        [((feats, 2 * hid), F32), ((1, 2 * hid), F32), ((hid, feats), F32), ((1, hid), F32)],
        mine, swap(mine, 1), scratch=[pltpu.VMEM((3 * hid, width), F32)],
    )
    return state_grad, grad_gw.T, grad_gb[0], grad_cw, grad_cb[0]


def body(*args):
    neighbours, send_rows = args[7], args[9]
    n = neighbours.shape[1]
    nd, snaps = lax.axis_size("dom"), lax.axis_size("snap")
    parts = nd // 2
    slots = 2 * parts * parts * (send_rows.shape[1] // nd)
    powers = nd & (nd - 1) == 0 and snaps & (snaps - 1) == 0 and nd > 1
    if powers and parts * (n + slots) * n * 2 <= 4 << 20:
        return chip_body(*args)
    return spread_body(*args)


def solution(mesh):
    in_specs = (
        P("snap", None, "dom"),
        P("snap", None, "dom"),
        P("snap", None, "dom"),
        P(),
        P(),
        P(),
        P(),
        P(None, "dom"),
        P(None, "dom"),
        P("dom", None),
    )
    out_specs = (P("snap", None, "dom"), P(), P(), P(), P())
    return jax.shard_map(body, mesh=mesh, in_specs=in_specs, out_specs=out_specs, check_vma=False)
```

```python
import functools
import math

import jax
import jax.numpy as jnp
from jax import lax
from jax.experimental import pallas as pl
from jax.experimental.pallas import tpu as pltpu
from jax.sharding import PartitionSpec as P

F32 = jnp.float32
BF16 = jnp.bfloat16
LANES = 128


def nn(a, b):
    return lax.dot_general(a, b, (((1,), (0,)), ((), ())), preferred_element_type=F32)


def nt(a, b):
    return lax.dot_general(a, b, (((1,), (1,)), ((), ())), preferred_element_type=F32)


def tn(a, b):
    return lax.dot_general(a, b, (((0,), (0,)), ((), ())), preferred_element_type=F32)


def iota(shape, axis):
    return lax.broadcasted_iota(jnp.int32, shape, axis)


def column(row):
    k = row.shape[1]
    spread = jnp.broadcast_to(row.astype(F32), (k, k))
    return jnp.sum(jnp.where(iota((k, k), 0) == iota((k, k), 1), spread, 0.0), axis=1, keepdims=True)


def run(kernel, name, outs, *args, scratch=(), flops=20_000_000, vmem=24, after=()):
    whole = pl.BlockSpec(memory_space=pltpu.VMEM)
    return pl.pallas_call(
        lambda *refs: kernel(*refs[len(after) :]),
        name=name,
        out_shape=[jax.ShapeDtypeStruct(shape, kind) for shape, kind in outs],
        in_specs=[pl.BlockSpec(memory_space=pl.ANY)] * len(after) + [whole] * len(args),
        out_specs=[whole] * len(outs),
        scratch_shapes=list(scratch),
        compiler_params=pltpu.CompilerParams(vmem_limit_bytes=vmem * 1024 * 1024),
        cost_estimate=pl.CostEstimate(flops=flops, bytes_accessed=2_000_000, transcendentals=0),
    )(*after, *args)


def prep_kernel(cap, nb, w, rows, readings, previous, e, s, b, pay):
    degree, n = nb.shape
    nh = s.shape[0]
    hid = previous.shape[1]
    fin = readings.shape[1]
    step = 32
    for at in range(0, n + nh, step):
        node = iota((step, n), 0) + at
        total = jnp.zeros((step, n), F32)
        for d in range(degree):
            total = total + jnp.where(node == nb[d : d + 1, :], w[d : d + 1, :], 0.0)
        e[at : at + step, :] = total.astype(BF16)
    sent = column(rows[...]).astype(jnp.int32)
    s[...] = jnp.where(iota((nh, n), 1) == sent, 1.0, 0.0).astype(BF16)
    b[:hid, :] = previous[0]
    rest = b.shape[0] - hid
    row = iota((rest, n), 0)
    tail = jnp.where(row == fin, 1.0, 0.0)
    for f in range(fin):
        tail = jnp.where(row == f, readings[0, f : f + 1, :].astype(F32), tail)
    b[hid:, :] = tail.astype(BF16)
    base = b[...]
    chans = base.shape[0]
    bound = nt(s[...], base)
    halo = nt(e[n:, :], base)
    for p in range(nh // cap):
        pay[p, :, :chans] = bound[p * cap : (p + 1) * cap, :]
        pay[p, :, LANES : LANES + chans] = halo[p * cap : (p + 1) * cap, :]


def order_matrix(shape, chans, hid, fin, block):
    k = iota(shape, 0)
    col = iota(shape, 1)
    m = lax.div(col, jnp.int32(block))
    c = col - m * block
    source = jnp.where(c < hid, m * chans + fin + c, jnp.where(c < hid + fin, m * chans + c - hid, -1))
    return jnp.where(k == source, 1.0, 0.0).astype(BF16)


def mid_a_kernel(hid, fin, orders, e, b, gw, cw, fa, ra, gw_o, cw_o):
    n = e.shape[1]
    a = e[:n, :]
    base = b[...]
    fa[...] = nt(base, a)
    ra[...] = nn(base, a)
    block = base.shape[0]
    order = order_matrix((gw.shape[1], orders * block), hid + fin, hid, fin, block)
    gw_o[...] = nn(gw[...], order).astype(BF16)
    cw_o[...] = nn(cw[...], order).astype(BF16)


def post_a_kernel(one, cap, recv, e, s, fa, ra, f1, r1, ro, ri, pay, flat):
    n = e.shape[1]
    nh = s.shape[0]
    chans = fa.shape[0]
    for p in range(nh // cap):
        flat[p * cap : (p + 1) * cap, :] = recv[p]
    h = e[n:, :]
    sel = s[...]
    seen = flat[:, :chans].astype(BF16)
    back = flat[:, LANES : LANES + chans]
    back_degree = flat[:, LANES + one : LANES + one + 1]
    out_degree = fa[one : one + 1, :] + jnp.sum(sel.astype(F32) * back_degree, axis=0, keepdims=True)
    pulled = ra[...] + tn(seen, h)
    inv_o = 1.0 / out_degree
    inv_i = 1.0 / pulled[one : one + 1, :]
    ro[...] = inv_o
    ri[...] = inv_i
    first_out = ((fa[...] + tn(back.astype(BF16), sel)) * inv_o).astype(BF16)
    first_in = (pulled * inv_i).astype(BF16)
    f1[...] = first_out
    r1[...] = first_in
    bound = nt(sel, first_in)
    halo = nt(h, first_out)
    hi, ho = scaled(h, inv_i), scaled(h, inv_o)
    si, so = scaled(sel, inv_i), scaled(sel, inv_o)
    coefs = (nt(sel, hi), nt(h, so), nt(sel, ho), nt(h, si))
    for p in range(nh // cap):
        at = slice(p * cap, (p + 1) * cap)
        pay[p, :, :chans] = bound[at, :]
        pay[p, :, LANES : LANES + chans] = halo[at, :]
        for k, coef in enumerate(coefs):
            pay[p, :, 2 * LANES + k * nh : 2 * LANES + (k + 1) * nh] = coef[at, :]


def scaled(rows, factor):
    return (rows.astype(F32) * factor).astype(BF16)


def mid_b_kernel(e, s, f1, r1, ro, ri, f2l, r2l, kc, ke, ka):
    n = e.shape[1]
    a = e[:n, :]
    h = e[n:, :]
    sel = s[...]
    nh = sel.shape[0]
    chans = f1.shape[0]
    inv_o, inv_i = ro[...], ri[...]
    outs = nt(jnp.concatenate([f1[...], scaled(sel, inv_o), scaled(sel, inv_i)], axis=0), a)
    ins = nn(jnp.concatenate([r1[...], scaled(h, inv_i), scaled(h, inv_o)], axis=0), a)
    f2l[...] = outs[:chans]
    r2l[...] = ins[:chans]
    kc[:nh, :] = ins[chans : chans + nh].astype(BF16)
    kc[nh:, :] = h
    ke[:nh, :] = outs[chans : chans + nh].astype(BF16)
    ke[nh:, :] = sel
    ka[:nh, :] = (2.0 * ins[chans + nh :]).astype(BF16)
    ka[nh : 2 * nh, :] = h
    ka[2 * nh : 3 * nh, :] = (2.0 * outs[chans + nh :]).astype(BF16)
    ka[3 * nh :, :] = sel


def send(pay, cap, left, right, left_two, right_two):
    nh = left.shape[0]
    rows = jnp.concatenate([left, right], axis=1)
    rows_two = jnp.concatenate([left_two, right_two], axis=1)
    both = jnp.concatenate([rows, rows_two], axis=0).astype(BF16)
    k = iota((2 * nh, 2 * nh), 0)
    part = lax.div(k, jnp.int32(2 * cap))
    spot = k - part * (2 * cap)
    source = jnp.where(spot < cap, part * cap + spot, nh + part * cap + spot - cap)
    mine = nn(jnp.where(iota((2 * nh, 2 * nh), 1) == source, 1.0, 0.0).astype(BF16), both)
    for p in range(nh // cap):
        own = mine[p * 2 * cap : (p + 1) * 2 * cap, :]
        pay[p] = jnp.concatenate([rows, own], axis=0).astype(BF16)


def post_b_kernel(cap, one, recv, e, s, b, f1, r1, f2l, r2l, ro, ri, gw, gb, states, reset, update, y, f1l, r1l, pay, flat):
    n = e.shape[1]
    nh = s.shape[0]
    hid = y.shape[0]
    chans = b.shape[0]
    for p in range(nh // cap):
        flat[p * cap : (p + 1) * cap, :] = recv[p, :, : 2 * LANES]
    a = e[:n, :]
    h = e[n:, :]
    sel = s[...]
    inv_o, inv_i = ro[...], ri[...]
    base = b[...].astype(F32)
    seen = flat[:, :chans].astype(BF16)
    back = flat[:, LANES : LANES + chans].astype(BF16)
    f2 = 2.0 * (f2l[...] + tn(back, sel)) * inv_o - base
    r2 = 2.0 * (r2l[...] + tn(seen, h)) * inv_i - base
    states[:chans, :] = b[...]
    states[chans : 2 * chans, :] = f1[...]
    states[2 * chans : 3 * chans, :] = f2.astype(BF16)
    states[3 * chans : 4 * chans, :] = r1[...]
    states[4 * chans :, :] = r2.astype(BF16)
    gates = jax.nn.sigmoid(nn(gw[...], states[...]) + column(gb[...]))
    reset[...] = gates[:hid]
    update[...] = gates[hid:]
    now = (gates[:hid] * base[:hid]).astype(BF16)
    y[...] = now
    local_out = nt(now, a) * inv_o
    local_in = nn(now, a) * inv_i
    f1l[...] = local_out
    r1l[...] = local_in
    bound = nt(sel, jnp.concatenate([now, local_in.astype(BF16)], axis=0))
    halo = nt(h, jnp.concatenate([now, local_out.astype(BF16)], axis=0))
    send(pay, cap, bound[:, :hid], halo[:, :hid], bound[:, hid:], halo[:, hid:])


def gather_matrix(coef, out, nd, cap, per, first, factor):
    nh = nd * cap
    width = nd * per
    k = iota((nh, width), 0)
    col = iota((nh, width), 1)
    r = lax.div(col, jnp.int32(per))
    u = col - r * per
    p = lax.div(u, jnp.int32(cap))
    spot = u - p * cap
    here = lax.div(k, jnp.int32(cap))
    slot = k - here * cap
    inside = u < nh
    place = jnp.where((k == r * cap + spot) & inside, 1.0, 0.0).astype(BF16)
    keep = (here == p) & inside
    for i in range(2):
        wide = nn(coef[:, (first + i) * nh : (first + i + 1) * nh].astype(BF16), place)
        own = (r == here) & (u == nh + cap + slot)
        out[(i + 1) * nh : (i + 2) * nh, :] = jnp.where(keep, factor * wide, jnp.where(own, 1.0, 0.0)).astype(BF16)
    out[:nh, :] = jnp.where((r == here) & (u == nh + slot), 1.0, 0.0).astype(BF16)


def mid_c_kernel(nd, cap, per, fused, recv, e, f1l, r1l, f2l, r2l, *rest):
    n = e.shape[1]
    a = e[:n, :]
    f2l[...] = nt(f1l[...].astype(BF16), a)
    r2l[...] = nn(r1l[...].astype(BF16), a)
    if fused:
        gd, ga, flat = rest
        for p in range(nd):
            flat[p * cap : (p + 1) * cap, :] = recv[p, :, 2 * LANES :]
        gather_matrix(flat, gd, nd, cap, per, 0, 1.0)
        gather_matrix(flat, ga, nd, cap, per, 2, 2.0)


def arrived(fused, hid, nh, g, recv):
    if fused:
        halo = nn(g[...], recv[...].reshape(recv.shape[0] * recv.shape[1], recv.shape[2]))
        two = halo[nh : 2 * nh, :hid], halo[2 * nh :, hid:]
    else:
        halo = recv[...]
        two = halo[nh:, :hid], halo[nh:, hid:]
    one = halo[:nh]
    return one[:, :hid], one[:, hid:], two[0], two[1]


def back_and_send(cap, hid, g, a, h, sel, inv_o, inv_i, z1, z2, pay):
    g0, g1, g2, g3, g4 = (g[m * hid : (m + 1) * hid, :].astype(BF16).astype(F32) for m in range(5))
    y1 = (g2 * inv_o).astype(BF16)
    y2 = (g4 * inv_i).astype(BF16)
    now1 = ((g1 + 2.0 * nn(y1, a)) * inv_o).astype(BF16)
    now2 = ((g3 + 2.0 * nt(y2, a)) * inv_i).astype(BF16)
    z1[...] = now1
    z2[...] = now2
    bound = nt(sel, jnp.concatenate([y1, now1], axis=0))
    halo = nt(h, jnp.concatenate([y2, now2], axis=0))
    send(pay, cap, bound[:, :hid], halo[:, :hid], bound[:, hid:], halo[:, hid:])
    return g0 - g2 - g4


def hidden_weights(w, hid, block, orders):
    return jnp.concatenate([w[:, m * block : m * block + hid] for m in range(orders)], axis=1)


def post_c_kernel(fused, cap, orders, g, recv, e, s, kc, ke, y, f1l, r1l, f2l, r2l, ro, ri, states, cw, cb, upstream, update,
                  mixed, cand_grad, gate_update, z1, z2, direct, pay):
    n = e.shape[1]
    nh = s.shape[0]
    hid = y.shape[0]
    block = states.shape[0] // orders
    a = e[:n, :]
    h = e[n:, :]
    sel = s[...]
    inv_o, inv_i = ro[...], ri[...]
    c1, e1, c2, e2 = arrived(fused, hid, nh, g, recv)
    base = y[...].astype(F32)
    c1, e1 = c1.astype(BF16), e1.astype(BF16)
    cc = jnp.concatenate([c1, c2.astype(BF16)], axis=0)
    ee = jnp.concatenate([e1, e2.astype(BF16)], axis=0)
    f1 = f1l[...] + tn(e1, sel) * inv_o
    f2 = 2.0 * (f2l[...] + tn(ee, ke[...])) * inv_o - base
    r1 = r1l[...] + tn(c1, h) * inv_i
    r2 = 2.0 * (r2l[...] + tn(cc, kc[...])) * inv_i - base
    for m, value in enumerate((y[...], f1, f2, r1, r2)):
        mixed[m * block : m * block + hid, :] = value.astype(BF16)
        mixed[m * block + hid : (m + 1) * block, :] = states[m * block + hid : (m + 1) * block, :]
    weights = cw[...]
    cand = jnp.tanh(nn(weights, mixed[...]) + column(cb[...]))
    up = upstream[0].astype(F32)
    gate = update[...]
    grad = (up * (1.0 - gate) * (1.0 - cand * cand)).astype(BF16)
    cand_grad[...] = grad
    held = states[:hid, :].astype(F32)
    gate_update[...] = (up * (held - cand) * gate * (1.0 - gate)).astype(BF16)
    back = tn(hidden_weights(weights, hid, block, orders), grad)
    direct[...] = back_and_send(cap, hid, back, a, h, sel, inv_o, inv_i, z1, z2, pay)


def weight_part(grad, features, orders, chans, hid, fin):
    block = features.shape[0] // orders
    width = -(-(orders * chans + 1) // LANES) * LANES
    shape = (width, orders * block)
    k = iota(shape, 0)
    col = iota(shape, 1)
    m = lax.div(col, jnp.int32(block))
    c = col - m * block
    source = jnp.where(c < hid, m * chans + fin + c, jnp.where(c < hid + fin, m * chans + c - hid, -1))
    source = jnp.where(col == hid + fin, orders * chans, source)
    order = jnp.where(k == source, 1.0, 0.0).astype(BF16)
    return nt(nt(grad, features).astype(BF16), order)


def mid_d_kernel(orders, fin, e, z1, z2, direct, cand_grad, mixed, gate_update, states, base, part):
    n = e.shape[1]
    a = e[:n, :]
    hid = z1.shape[0]
    base[...] = direct[...] + nn(z1[...], a) + nt(z2[...], a)
    part[:hid, :] = weight_part(gate_update[...], states[...], orders, hid + fin, hid, fin).astype(BF16)
    part[hid:, :] = weight_part(cand_grad[...], mixed[...], orders, hid + fin, hid, fin).astype(BF16)


def add_halo(fused, g, recv, ka, base):
    hid = base.shape[0]
    nh = ka.shape[0] // 4
    c1, e1, c2, e2 = arrived(fused, hid, nh, g, recv)
    return base[...] + tn(jnp.concatenate([c1, c2, e1, e2], axis=0).astype(BF16), ka[...])


def post_d_kernel(fused, cap, orders, g, recv, e, s, ka, base, ro, ri, states, gw, upstream, reset, update, gate_update,
                  gate_reset, z1, z2, direct, pay):
    n = e.shape[1]
    hid = base.shape[0]
    block = states.shape[0] // orders
    scaled_grad = add_halo(fused, g, recv, ka, base)
    held = states[:hid, :].astype(F32)
    gate = reset[...]
    grad = (scaled_grad * held * gate * (1.0 - gate)).astype(BF16)
    gate_reset[...] = grad
    weights = hidden_weights(gw[...], hid, block, orders)
    back = tn(weights, jnp.concatenate([grad, gate_update[...]], axis=0))
    rest = back_and_send(cap, hid, back, e[:n, :], e[n:, :], s[...], ro[...], ri[...], z1, z2, pay)
    direct[...] = rest + upstream[0].astype(F32) * update[...] + scaled_grad * gate


def mid_e_kernel(orders, fin, rows, e, z1, z2, direct, gate_reset, states, part, base, grads):
    n = e.shape[1]
    a = e[:n, :]
    hid = z1.shape[0]
    base[...] = direct[...] + nn(z1[...], a) + nt(z2[...], a)
    first = weight_part(gate_reset[...], states[...], orders, hid + fin, hid, fin)
    both = jnp.concatenate([first, part[...].astype(F32)], axis=0)
    for k in range(grads.shape[0]):
        if k * rows < both.shape[0]:
            grads[k] = both[k * rows : (k + 1) * rows, :].astype(BF16)
        else:
            grads[k] = jnp.zeros(grads.shape[1:], BF16)


def post_e_kernel(fused, g, recv, ka, base, out):
    out[0] = add_halo(fused, g, recv, ka, base).astype(BF16)


def add_kernel(recv, out):
    total = recv[0].astype(F32)
    for k in range(1, recv.shape[0]):
        total = total + recv[k].astype(F32)
    for k in range(out.shape[0]):
        out[k] = total.astype(BF16)


def finish_kernel(hid, factor, recv, gw, gb, cw, cb):
    rows = recv.shape[1]
    features = gw.shape[1]
    total = gw.shape[0] + cw.shape[0]
    for k in range(total // rows):
        part = recv[k].astype(F32)[:, :features] * factor
        at = k * rows
        if at < 2 * hid:
            gw[at : at + rows, :] = part
        else:
            cw[at - 2 * hid : at - 2 * hid + rows, :] = part
    flat = jnp.concatenate([recv[k].astype(F32) for k in range(total // rows)], axis=0)
    pick = jnp.where(iota((8, flat.shape[1]), 1) == features, 1.0, 0.0).astype(BF16)
    bias = nt(pick, flat.astype(BF16))[:1] * factor
    gb[...] = bias[:, : 2 * hid]
    cb[...] = bias[:, 2 * hid :]


def spread_body(
    readings,
    previous,
    upstream,
    gate_weight,
    gate_bias,
    cand_weight,
    cand_bias,
    neighbours,
    edge_weight,
    send_rows,
):
    fin, hid = readings.shape[1], previous.shape[1]
    chans = fin + hid
    orders = gate_weight.shape[1] // chans
    n = readings.shape[2]
    nd = lax.axis_size("dom")
    devices = nd * lax.axis_size("snap")
    nh = send_rows.shape[1]
    cap = nh // nd
    block = hid + 16 * (-(-(fin + 1) // 16))
    one = hid + fin
    per = nh + 2 * cap
    fused = 3 * nh * nd * per <= 1 << 18
    move = functools.partial(lax.all_to_all, axis_name="dom", split_axis=0, concat_axis=0, tiled=True)

    e, s, b, pay = run(
        functools.partial(prep_kernel, cap), "prep",
        [((n + nh, n), BF16), ((nh, n), BF16), ((block, n), BF16), ((nd, cap, 2 * LANES), F32)],
        neighbours, edge_weight, send_rows, readings, previous,
    )
    recv = move(pay)
    fa, ra, gw, cw = run(
        functools.partial(mid_a_kernel, hid, fin, orders), "mid_a",
        [((block, n), F32), ((block, n), F32), ((2 * hid, orders * block), BF16), ((hid, orders * block), BF16)],
        e, b, gate_weight, cand_weight,
    )
    wide = 2 * LANES + 4 * nh
    f1, r1, ro, ri, pay = run(
        functools.partial(post_a_kernel, one, cap), "post_a",
        [((block, n), BF16), ((block, n), BF16), ((1, n), F32), ((1, n), F32), ((nd, cap, wide), F32)],
        recv, e, s, fa, ra, scratch=[pltpu.VMEM((nh, 2 * LANES), F32)],
    )
    recv_b = move(pay)
    f2l, r2l, kc, ke, ka = run(
        mid_b_kernel, "mid_b",
        [((block, n), F32), ((block, n), F32), ((2 * nh, n), BF16), ((2 * nh, n), BF16), ((4 * nh, n), BF16)],
        e, s, f1, r1, ro, ri,
    )
    pay_kind = ((nd, per, 2 * hid), BF16)
    field, field16 = ((hid, n), F32), ((hid, n), BF16)
    states, reset, update, y, f1l, r1l, pay = run(
        functools.partial(post_b_kernel, cap, one), "post_b",
        [((orders * block, n), BF16), field, field, field16, field, field, pay_kind],
        recv_b, e, s, b, f1, r1, f2l, r2l, ro, ri, gw, gate_bias[None, :],
        scratch=[pltpu.VMEM((nh, 2 * LANES), F32)],
    )
    recv = move(pay)
    table = ((3 * nh, nd * per), BF16)
    f2l, r2l, *tables = run(
        functools.partial(mid_c_kernel, nd, cap, per, fused), "mid_c",
        [field, field] + [table] * (2 if fused else 0),
        recv_b, e, f1l, r1l, scratch=[pltpu.VMEM((nh, 4 * nh), F32)] if fused else [],
    )
    if fused:
        inward, outward = tables
        halo_of = lambda got, first, factor: got
    else:
        inward = outward = jnp.zeros((8, LANES), BF16)
        coefs = recv_b[:, :, 2 * LANES :].reshape(nd, cap, 4, nd, cap)

        def halo_of(got, first, factor):
            rows = got[:, :nh].reshape(nd, nd, cap, 2, hid).astype(F32)
            two = jnp.einsum("psgrt,rptgk->psgk", coefs[:, :, first : first + 2], rows)
            two = factor * two.reshape(nh, 2 * hid) + got[:, nh + cap :].reshape(nh, 2 * hid).astype(F32)
            return jnp.concatenate([got[:, nh : nh + cap].reshape(nh, 2 * hid).astype(F32), two], axis=0)

    mixed, cand_grad, gate_update, z1, z2, direct, pay = run(
        functools.partial(post_c_kernel, fused, cap, orders), "post_c",
        [((orders * block, n), BF16), field16, field16, field16, field16, field, pay_kind],
        inward, halo_of(recv, 0, 1.0), e, s, kc, ke, y, f1l, r1l, f2l, r2l, ro, ri, states, cw, cand_bias[None, :], upstream, update,
    )
    recv = move(pay)
    width = -(-(orders * chans + 1) // LANES) * LANES
    base, part = run(
        functools.partial(mid_d_kernel, orders, fin), "mid_d", [field, ((2 * hid, width), BF16)],
        e, z1, z2, direct, cand_grad, mixed, gate_update, states,
    )
    gate_reset, z1, z2, direct, pay = run(
        functools.partial(post_d_kernel, fused, cap, orders), "post_d",
        [field16, field16, field16, field, pay_kind],
        outward, halo_of(recv, 2, 2.0), e, s, ka, base, ro, ri, states, gw, upstream, reset, update, gate_update,
    )
    recv = move(pay)
    rows = 8 * (-(-3 * hid // (8 * devices)))
    base, grads = run(
        functools.partial(mid_e_kernel, orders, fin, rows), "mid_e", [field, ((devices, rows, width), BF16)],
        e, z1, z2, direct, gate_reset, states, part,
    )
    (state_grad,) = run(
        functools.partial(post_e_kernel, fused), "post_e", [((1, hid, n), BF16)],
        outward, halo_of(recv, 2, 2.0), ka, base,
    )
    both = ("snap", "dom")
    grads = lax.all_to_all(grads, both, 0, 0, tiled=True)
    (grads,) = run(add_kernel, "add", [((devices, rows, width), BF16)], grads)
    grads = lax.all_to_all(grads, both, 0, 0, tiled=True)
    factor = 1.0 / math.sqrt(readings.shape[0] * lax.axis_size("snap") * n * nd)
    feats = orders * chans
    grad_gw, grad_gb, grad_cw, grad_cb = run(
        functools.partial(finish_kernel, hid, factor), "finish",
        [((2 * hid, feats), F32), ((1, 2 * hid), F32), ((hid, feats), F32), ((1, hid), F32)],
        grads,
    )
    return state_grad, grad_gw, grad_gb[0], grad_cw, grad_cb[0]


def pack_kernel(own, nb, w, rows, readings, previous, tail):
    degree = nb.shape[0]
    nh = rows.shape[1]
    hid = previous.shape[1]
    fin = readings.shape[1]
    tail[...] = jnp.zeros_like(tail)
    tail[:fin, :] = readings[0].astype(F32)
    high = lax.shift_right_logical(nb[...], 5)
    tail[fin : fin + degree, :] = high.astype(F32)
    tail[fin + degree : fin + 2 * degree, :] = (nb[...] - high * 32).astype(F32)
    tail[fin + 2 * degree : fin + 3 * degree, :] = w[...]
    at = fin + 3 * degree
    high = lax.shift_right_logical(rows[...], 5)
    tail[at : at + 1, :nh] = high.astype(F32)
    tail[at + 1 : at + 2, :nh] = (rows[...] - high * 32).astype(F32)
    own[:hid, :] = previous[0]
    own[hid:, :] = tail[...].astype(BF16)


def pack_entry(nb, w, rows, readings, previous, own, sent, tail):
    pack_kernel(own, nb, w, rows, readings, previous, tail)
    sent[...] = own[...]


def exchange(first, second, hc, sc, pay):
    count = first[0].shape[0]
    parts = len(first)
    pay[:count, :] = jnp.concatenate([nt(first[p], sc[p]).astype(BF16) for p in range(parts)], axis=1)
    pay[count:, :] = jnp.concatenate([nt(second[p], hc[p]).astype(BF16) for p in range(parts)], axis=1)


def merged(parts, mine, got):
    step = mine.shape[1] // (2 * parts)
    here = lax.rem(lax.div(iota(mine.shape, 1), jnp.int32(step)), jnp.int32(2)) == 0
    value = jnp.where(here, mine[...].astype(F32), got[...].astype(F32)).astype(BF16)
    count = mine.shape[0] // 2
    return value[:count, :], value[count:, :]


def build_kernel(cap, hid, fin, degree, parts, *refs):
    blocks_in, (a, at, hc, hx, sc, sx, b, pay, blocks) = refs[:parts], refs[parts:]
    n = a.shape[2]
    slots = sx.shape[1]
    nh = 2 * parts * cap
    half = parts * cap
    me = lax.axis_index("dom")
    z = lax.shift_right_logical(me, 1)
    core = me - 2 * z
    for k in range(parts):
        blocks[lax.bitwise_xor(z, jnp.int32(k))] = blocks_in[k][...]
    line = iota((nh, 1), 0)
    rel = lax.div(line, jnp.int32(half))
    k = lax.div(line - rel * half, jnp.int32(cap))
    t = line - rel * half - k * cap
    spot = (k * 2 + lax.bitwise_xor(rel, core)) * cap + t
    node = (n + spot).astype(F32)
    width = -(-nh // LANES) * LANES
    slot = iota((slots, nh), 0)
    outer = lax.div(slot, jnp.int32(nh))
    rest = slot - outer * nh
    slot_rel = lax.div(rest, jnp.int32(half))
    rest = rest - slot_rel * half
    inner = lax.div(rest, jnp.int32(cap))
    filled = iota((slots, nh), 1) == slot_rel * half + outer * cap + rest - inner * cap
    row = iota((32, n), 0).astype(F32)
    for p in range(parts):
        tail = blocks[p, hid:, :].astype(F32)
        high, low = tail[fin : fin + degree], tail[fin + degree : fin + 2 * degree]
        w = tail[fin + 2 * degree : fin + 3 * degree]
        start = fin + 3 * degree
        sent = tail[start : start + 1] * 32.0 + tail[start + 1 : start + 2]
        low_is = [jnp.where(low[d : d + 1] == row, 1.0, 0.0).astype(BF16) for d in range(degree)]
        for chunk in range(n // 32):
            total = None
            for d in range(degree):
                term = low_is[d] * jnp.where(high[d : d + 1] == float(chunk), w[d : d + 1], 0.0).astype(BF16)
                total = term if total is None else total + term
            a[p, chunk * 32 : (chunk + 1) * 32, :] = total
        at[p] = a[p].T
        names = high * 32.0 + low
        total = jnp.zeros((nh, n), F32)
        for d in range(degree):
            total = total + jnp.where(names[d : d + 1] == node, w[d : d + 1], 0.0)
        halo = total.astype(BF16)
        hc[p] = halo
        named = jnp.where(iota((nh, width), 1) == spot, sent[:, :width], 0.0)
        target = jnp.sum(named, axis=1, keepdims=True).astype(jnp.int32)
        picked = jnp.where(iota((nh, n), 1) == target, 1.0, 0.0).astype(BF16)
        sc[p] = picked
        place = jnp.where(filled & (inner == p), 1.0, 0.0).astype(BF16)
        hx[p] = nn(place, halo).astype(BF16)
        sx[p] = nn(place, picked).astype(BF16)
        b[p, :hid, :] = blocks[p, :hid, :]
        line = iota(tail.shape, 0)
        b[p, hid:, :] = jnp.where(line < fin, tail, jnp.where(line == fin, 1.0, 0.0)).astype(BF16)
    base = [b[p] for p in range(parts)]
    exchange(base, base, hc, sc, pay)


def order_kernel(hid, fin, orders, block, gw, cw, gw_o, cw_o):
    order = order_matrix((cw.shape[1], orders * block), hid + fin, hid, fin, block)
    gw_o[...] = tn(gw[...], order).astype(BF16)
    cw_o[...] = nn(cw[...], order).astype(BF16)


def local_kernel(a, at, x1, x2, l1, l2):
    for p in range(a.shape[0]):
        l1[p] = nn(x1[p], a[p])
        l2[p] = nn(x2[p], at[p])


def chip_a_kernel(one, mine, got, hc, hx, sc, sx, l1, l2, f1, r1, ro, ri, pay):
    top, low = merged(sx.shape[0], mine, got)
    firsts, seconds = [], []
    for p in range(sx.shape[0]):
        pulled = l1[p] + nn(top, hx[p])
        pushed = l2[p] + nn(low, sx[p])
        inv_o = 1.0 / pushed[one : one + 1, :]
        inv_i = 1.0 / pulled[one : one + 1, :]
        ro[p] = inv_o
        ri[p] = inv_i
        out = (pushed * inv_o).astype(BF16)
        into = (pulled * inv_i).astype(BF16)
        f1[p] = out
        r1[p] = into
        firsts.append(into)
        seconds.append(out)
    exchange(firsts, seconds, hc, sc, pay)


def chip_b_kernel(mine, got, hc, hx, sc, sx, b, f1, r1, l1, l2, ro, ri, gw, gb, states, reset, update, y, pay):
    hid = y.shape[1]
    chans = b.shape[1]
    top, low = merged(sx.shape[0], mine, got)
    bias = column(gb[...])
    fields = []
    for p in range(sx.shape[0]):
        base = b[p].astype(F32)
        r2 = 2.0 * (l1[p] + nn(top, hx[p])) * ri[p] - base
        f2 = 2.0 * (l2[p] + nn(low, sx[p])) * ro[p] - base
        states[p, :chans, :] = b[p]
        states[p, chans : 2 * chans, :] = f1[p]
        states[p, 2 * chans : 3 * chans, :] = f2.astype(BF16)
        states[p, 3 * chans : 4 * chans, :] = r1[p]
        states[p, 4 * chans :, :] = r2.astype(BF16)
        gates = jax.nn.sigmoid(nn(gw[...], states[p]) + bias)
        reset[p] = gates[:hid]
        update[p] = gates[hid:]
        now = (gates[:hid] * base[:hid]).astype(BF16)
        y[p] = now
        fields.append(now)
    exchange(fields, fields, hc, sc, pay)


def chip_c1_kernel(mine, got, hc, hx, sc, sx, l1, l2, ro, ri, f1, r1, pay):
    top, low = merged(sx.shape[0], mine, got)
    firsts, seconds = [], []
    for p in range(sx.shape[0]):
        into = ((l1[p] + nn(top, hx[p])) * ri[p]).astype(BF16)
        out = ((l2[p] + nn(low, sx[p])) * ro[p]).astype(BF16)
        f1[p] = out
        r1[p] = into
        firsts.append(into)
        seconds.append(out)
    exchange(firsts, seconds, hc, sc, pay)


def split_back(back, hid, inv_o, inv_i, y1, y2, g1, g3):
    parts = [back[m * hid : (m + 1) * hid, :].astype(BF16) for m in range(5)]
    y1[...] = (parts[2].astype(F32) * inv_o).astype(BF16)
    y2[...] = (parts[4].astype(F32) * inv_i).astype(BF16)
    g1[...] = parts[1]
    g3[...] = parts[3]
    return parts[0].astype(F32) - parts[2].astype(F32) - parts[4].astype(F32)


def chip_c2_kernel(orders, parts, *refs):
    ups, refs = refs[:parts], refs[parts:]
    mine, got, hc, hx, sc, sx, y, f1, r1, l1, l2, ro, ri, states, cw, cb, update = refs[:17]
    mixed, cand_grad, gate_update, y1, y2, g1, g3, upstream, direct, pay = refs[17:]
    hid = y.shape[1]
    block = states.shape[1] // orders
    z = lax.shift_right_logical(lax.axis_index("dom"), 1)
    for k in range(parts):
        upstream[lax.bitwise_xor(z, jnp.int32(k))] = ups[k][0]
    top, low = merged(sx.shape[0], mine, got)
    bias = column(cb[...])
    hidden = hidden_weights(cw[...], hid, block, orders)
    for p in range(sx.shape[0]):
        base = y[p].astype(F32)
        r2 = 2.0 * (l1[p] + nn(top, hx[p])) * ri[p] - base
        f2 = 2.0 * (l2[p] + nn(low, sx[p])) * ro[p] - base
        for m, value in enumerate((y[p], f1[p], f2, r1[p], r2)):
            mixed[p, m * block : m * block + hid, :] = value.astype(BF16)
            mixed[p, m * block + hid : (m + 1) * block, :] = states[p, m * block + hid : (m + 1) * block, :]
        cand = jnp.tanh(nn(cw[...], mixed[p]) + bias)
        up = upstream[p].astype(F32)
        gate = update[p]
        grad = (up * (1.0 - gate) * (1.0 - cand * cand)).astype(BF16)
        cand_grad[p] = grad
        gate_update[p] = (up * (states[p, :hid, :].astype(F32) - cand) * gate * (1.0 - gate)).astype(BF16)
        direct[p] = split_back(tn(hidden, grad), hid, ro[p], ri[p], y1.at[p], y2.at[p], g1.at[p], g3.at[p])
    parts = range(sx.shape[0])
    exchange([y1[p] for p in parts], [y2[p] for p in parts], hc, sc, pay)


def chip_part(grads, features, orders, chans, hid, fin):
    block = features.shape[1] // orders
    width = -(-(orders * chans + 1) // LANES) * LANES
    shape = (width, orders * block)
    k = iota(shape, 0)
    col = iota(shape, 1)
    m = lax.div(col, jnp.int32(block))
    c = col - m * block
    source = jnp.where(c < hid, m * chans + fin + c, jnp.where(c < hid + fin, m * chans + c - hid, -1))
    source = jnp.where(col == hid + fin, orders * chans, source)
    order = jnp.where(k == source, 1.0, 0.0).astype(BF16)
    total = sum(nt(grads[p], features[p]) for p in range(features.shape[0]))
    return nt(total.astype(BF16), order)


def local_d_kernel(orders, fin, a, at, y1, y2, cand_grad, mixed, l1, l2, part):
    hid = y1.shape[1]
    local_kernel(a, at, y1, y2, l1, l2)
    part[...] = chip_part(cand_grad, mixed, orders, hid + fin, hid, fin).astype(BF16)


def chip_d1_kernel(mine, got, hc, hx, sc, sx, l1, l2, g1, g3, ro, ri, z1, z2, pay):
    top, low = merged(sx.shape[0], mine, got)
    firsts, seconds = [], []
    for p in range(sx.shape[0]):
        one = ((g1[p].astype(F32) + 2.0 * (l1[p] + nn(top, hx[p]))) * ro[p]).astype(BF16)
        two = ((g3[p].astype(F32) + 2.0 * (l2[p] + nn(low, sx[p]))) * ri[p]).astype(BF16)
        z1[p] = one
        z2[p] = two
        firsts.append(one)
        seconds.append(two)
    exchange(firsts, seconds, hc, sc, pay)


def local_d2_kernel(a, at, z1, z2, direct, base):
    for p in range(a.shape[0]):
        base[p] = direct[p] + nn(z1[p], a[p]) + nn(z2[p], at[p])


def chip_d2_kernel(orders, mine, got, hc, hx, sc, sx, base, ro, ri, states, gw, upstream, reset, update, gate_update,
                   gate_grad, y1, y2, g1, g3, direct, pay):
    hid = base.shape[1]
    block = states.shape[1] // orders
    top, low = merged(sx.shape[0], mine, got)
    hidden = hidden_weights(gw[...], hid, block, orders)
    for p in range(sx.shape[0]):
        scaled_grad = base[p] + nn(top, hx[p]) + nn(low, sx[p])
        gate = reset[p]
        grad = (scaled_grad * states[p, :hid, :].astype(F32) * gate * (1.0 - gate)).astype(BF16)
        gate_grad[p, :hid, :] = grad
        gate_grad[p, hid:, :] = gate_update[p]
        back = tn(hidden, gate_grad[p])
        rest = split_back(back, hid, ro[p], ri[p], y1.at[p], y2.at[p], g1.at[p], g3.at[p])
        direct[p] = rest + upstream[p].astype(F32) * update[p] + scaled_grad * gate
    parts = range(sx.shape[0])
    exchange([y1[p] for p in parts], [y2[p] for p in parts], hc, sc, pay)


def grads_kernel(orders, fin, gate_grad, states, part, keep, give, flat):
    both = gate_grad.shape[1]
    hid = both // 2
    half = keep.shape[0]
    core = lax.rem(lax.axis_index("dom"), 2)
    flat[:both, :] = chip_part(gate_grad, states, orders, hid + fin, hid, fin)
    flat[both:, :] = part[...].astype(F32)
    keep[...] = flat[pl.ds(pl.multiple_of(core * half, 8), half), :].astype(BF16)
    give[...] = flat[pl.ds(pl.multiple_of((1 - core) * half, 8), half), :].astype(BF16)


def local_e_kernel(a, at, z1, z2, direct, base):
    z = lax.shift_right_logical(lax.axis_index("dom"), 1)
    base[...] = direct[z] + nn(z1[z], a[z]) + nn(z2[z], at[z])


def chip_e_kernel(mine, got, hc, hx, sc, sx, base, out):
    z = lax.shift_right_logical(lax.axis_index("dom"), 1)
    top, low = merged(sx.shape[0], mine, got)
    out[0] = (base[...] + nn(top, hx[z]) + nn(low, sx[z])).astype(BF16)


def sum_kernel(*refs):
    values = [ref[...].astype(F32) for ref in refs[:-2]]
    while len(values) > 1:
        values = [values[k] + values[k + 1] for k in range(0, len(values), 2)]
    refs[-1][...] = values[0].astype(BF16)
    refs[-2][...] = values[0].astype(BF16)


def end_kernel(factor, mine, got, gw, gb, cw, cb, flat):
    half = mine.shape[0]
    core = lax.rem(lax.axis_index("dom"), 2)
    flat[pl.ds(pl.multiple_of(core * half, 8), half), :] = mine[...].astype(F32)
    flat[pl.ds(pl.multiple_of((1 - core) * half, 8), half), :] = got[...].astype(F32)
    features, rows = gw.shape
    same = jnp.where(iota((features, flat.shape[1]), 0) == iota((features, flat.shape[1]), 1), 1.0, 0.0).astype(BF16)
    gw[...] = nt(same, flat[:rows, :].astype(BF16)) * factor
    cw[...] = flat[rows:, :features] * factor
    pick = jnp.where(iota((8, flat.shape[1]), 1) == features, 1.0, 0.0).astype(BF16)
    bias = nt(pick, flat[...].astype(BF16))[:1] * factor
    gb[...] = bias[:, :rows]
    cb[...] = bias[:, rows:]


def chip_body(
    readings,
    previous,
    upstream,
    gate_weight,
    gate_bias,
    cand_weight,
    cand_bias,
    neighbours,
    edge_weight,
    send_rows,
):
    fin, hid = readings.shape[1], previous.shape[1]
    chans = fin + hid
    orders = gate_weight.shape[1] // chans
    degree = neighbours.shape[0]
    n = readings.shape[2]
    nd = lax.axis_size("dom")
    snaps = lax.axis_size("snap")
    parts = nd // 2
    cap = send_rows.shape[1] // nd
    block = hid + 16 * (-(-(fin + 3 * degree + 2) // 16))
    slots = 2 * parts * parts * cap

    def swap(array, k, axis="dom", size=nd):
        return lax.ppermute(array, axis, [(i, i ^ k) for i in range(size)])

    own, sent = run(
        pack_entry, "pack", [((block, n), BF16)] * 2, neighbours, edge_weight, send_rows, readings, previous,
        scratch=[pltpu.VMEM((block - hid, n), F32)], vmem=56,
    )
    blocks = [own] + [swap(sent, 2 * k) for k in range(1, parts)]
    ups = [upstream] + [swap(upstream, 2 * k) for k in range(1, parts)]
    gw, cw = run(
        functools.partial(order_kernel, hid, fin, orders, block), "order",
        [((2 * hid, orders * block), BF16), ((hid, orders * block), BF16)], gate_weight.T, cand_weight, after=[own],
    )
    wide, wide16, wide_pay = ((parts, block, n), F32), ((parts, block, n), BF16), ((2 * block, slots), BF16)
    field, field16, pay_kind = ((parts, hid, n), F32), ((parts, hid, n), BF16), ((2 * hid, slots), BF16)
    line = ((parts, 1, n), F32)
    a, at, hc, hx, sc, sx, b, pay = run(
        functools.partial(build_kernel, cap, hid, fin, degree, parts), "build",
        [((parts, n, n), BF16)] * 2 + [((parts, rows, n), BF16) for rows in (2 * parts * cap, slots)] * 2 + [wide16, wide_pay],
        *blocks, scratch=[pltpu.VMEM((parts, block, n), BF16)], after=[gw],
    )
    edges = (hc, hx, sc, sx)
    got = swap(pay, 1)
    l1, l2 = run(local_kernel, "local_a", [wide, wide], a, at, b, b)
    f1, r1, ro, ri, pay = run(
        functools.partial(chip_a_kernel, hid + fin), "chip_a", [wide16, wide16, line, line, wide_pay],
        pay, got, *edges, l1, l2, after=ups[1:],
    )
    got = swap(pay, 1)
    l1, l2 = run(local_kernel, "local_b", [wide, wide], a, at, r1, f1)
    states, reset, update, y, pay = run(
        chip_b_kernel, "chip_b", [((parts, orders * block, n), BF16), field, field, field16, pay_kind],
        pay, got, *edges, b, f1, r1, l1, l2, ro, ri, gw, gate_bias[None, :],
    )
    got = swap(pay, 1)
    l1, l2 = run(local_kernel, "local_c1", [field, field], a, at, y, y)
    f1, r1, pay = run(
        chip_c1_kernel, "chip_c1", [field16, field16, pay_kind], pay, got, *edges, l1, l2, ro, ri
    )
    got = swap(pay, 1)
    l1, l2 = run(local_kernel, "local_c2", [field, field], a, at, r1, f1)
    mixed, cand_grad, gate_update, y1, y2, g1, g3, up, direct, pay = run(
        functools.partial(chip_c2_kernel, orders, parts), "chip_c2",
        [((parts, orders * block, n), BF16)] + [field16] * 7 + [field, pay_kind],
        *ups, pay, got, *edges, y, f1, r1, l1, l2, ro, ri, states, cw, cand_bias[None, :], update,
    )
    got = swap(pay, 1)
    width = -(-(orders * chans + 1) // LANES) * LANES
    l1, l2, part = run(
        functools.partial(local_d_kernel, orders, fin), "local_d1", [field, field, ((hid, width), BF16)],
        a, at, y1, y2, cand_grad, mixed,
    )
    z1, z2, pay = run(
        chip_d1_kernel, "chip_d1", [field16, field16, pay_kind], pay, got, *edges, l1, l2, g1, g3, ro, ri
    )
    got = swap(pay, 1)
    (base,) = run(local_d2_kernel, "local_d2", [field], a, at, z1, z2, direct)
    gate_grad, y1, y2, g1, g3, direct, pay = run(
        functools.partial(chip_d2_kernel, orders), "chip_d2",
        [((parts, 2 * hid, n), BF16)] + [field16] * 4 + [field, pay_kind],
        pay, got, *edges, base, ro, ri, states, gw, up, reset, update, gate_update,
    )
    got = swap(pay, 1)
    half = ((3 * hid // 2, width), BF16)
    keep, give = run(
        functools.partial(grads_kernel, orders, fin), "grads", [half, half], gate_grad, states, part,
        scratch=[pltpu.VMEM((3 * hid, width), F32)],
    )
    l1, l2 = run(local_kernel, "local_e1", [field, field], a, at, y1, y2)
    mine, sent = run(sum_kernel, "sum_core", [half] * 2, keep, swap(give, 1), after=[l1, got])
    every = [mine] + [swap(sent, k, "snap", snaps) for k in range(1, snaps)]
    z1, z2, pay = run(
        chip_d1_kernel, "chip_e1", [field16, field16, pay_kind], pay, got, *edges, l1, l2, g1, g3, ro, ri, after=[mine],
    )
    got = swap(pay, 1)
    (base,) = run(local_e_kernel, "local_e2", [((hid, n), F32)], a, at, z1, z2, direct)
    (state_grad,) = run(chip_e_kernel, "chip_e2", [((1, hid, n), BF16)], pay, got, *edges, base)
    mine, sent = run(sum_kernel, "sum_snap", [half] * 2, *every, after=[state_grad])
    factor = 1.0 / math.sqrt(readings.shape[0] * snaps * n * nd)
    feats = orders * chans
    grad_gw, grad_gb, grad_cw, grad_cb = run(
        functools.partial(end_kernel, factor), "end",
        [((feats, 2 * hid), F32), ((1, 2 * hid), F32), ((hid, feats), F32), ((1, hid), F32)],
        mine, swap(sent, 1), scratch=[pltpu.VMEM((3 * hid, width), F32)],
    )
    return state_grad, grad_gw.T, grad_gb[0], grad_cw, grad_cb[0]


def body(*args):
    neighbours, send_rows = args[7], args[9]
    n = neighbours.shape[1]
    nd, snaps = lax.axis_size("dom"), lax.axis_size("snap")
    parts = nd // 2
    slots = 2 * parts * parts * (send_rows.shape[1] // nd)
    powers = nd & (nd - 1) == 0 and snaps & (snaps - 1) == 0 and nd > 1
    if powers and parts * (n + slots) * n * 2 <= 4 << 20:
        return chip_body(*args)
    return spread_body(*args)


def solution(mesh):
    in_specs = (
        P("snap", None, "dom"),
        P("snap", None, "dom"),
        P("snap", None, "dom"),
        P(),
        P(),
        P(),
        P(),
        P(None, "dom"),
        P(None, "dom"),
        P("dom", None),
    )
    out_specs = (P("snap", None, "dom"), P(), P(), P(), P())
    return jax.shard_map(body, mesh=mesh, in_specs=in_specs, out_specs=out_specs, check_vma=False)
```

```python
import functools
import math

import jax
import jax.numpy as jnp
from jax import lax
from jax.experimental import pallas as pl
from jax.experimental.pallas import tpu as pltpu
from jax.sharding import PartitionSpec as P

F32 = jnp.float32
BF16 = jnp.bfloat16
LANES = 128


def nn(a, b):
    return lax.dot_general(a, b, (((1,), (0,)), ((), ())), preferred_element_type=F32)


def nt(a, b):
    return lax.dot_general(a, b, (((1,), (1,)), ((), ())), preferred_element_type=F32)


def tn(a, b):
    return lax.dot_general(a, b, (((0,), (0,)), ((), ())), preferred_element_type=F32)


def iota(shape, axis):
    return lax.broadcasted_iota(jnp.int32, shape, axis)


def column(row):
    k = row.shape[1]
    spread = jnp.broadcast_to(row.astype(F32), (k, k))
    return jnp.sum(jnp.where(iota((k, k), 0) == iota((k, k), 1), spread, 0.0), axis=1, keepdims=True)


def run(kernel, name, outs, *args, scratch=(), flops=20_000_000, vmem=24, after=()):
    whole = pl.BlockSpec(memory_space=pltpu.VMEM)
    return pl.pallas_call(
        lambda *refs: kernel(*refs[len(after) :]),
        name=name,
        out_shape=[jax.ShapeDtypeStruct(shape, kind) for shape, kind in outs],
        in_specs=[pl.BlockSpec(memory_space=pl.ANY)] * len(after) + [whole] * len(args),
        out_specs=[whole] * len(outs),
        scratch_shapes=list(scratch),
        compiler_params=pltpu.CompilerParams(vmem_limit_bytes=vmem * 1024 * 1024),
        cost_estimate=pl.CostEstimate(flops=flops, bytes_accessed=2_000_000, transcendentals=0),
    )(*after, *args)


def prep_kernel(cap, nb, w, rows, readings, previous, e, s, b, pay):
    degree, n = nb.shape
    nh = s.shape[0]
    hid = previous.shape[1]
    fin = readings.shape[1]
    step = 32
    for at in range(0, n + nh, step):
        node = iota((step, n), 0) + at
        total = jnp.zeros((step, n), F32)
        for d in range(degree):
            total = total + jnp.where(node == nb[d : d + 1, :], w[d : d + 1, :], 0.0)
        e[at : at + step, :] = total.astype(BF16)
    sent = column(rows[...]).astype(jnp.int32)
    s[...] = jnp.where(iota((nh, n), 1) == sent, 1.0, 0.0).astype(BF16)
    b[:hid, :] = previous[0]
    rest = b.shape[0] - hid
    row = iota((rest, n), 0)
    tail = jnp.where(row == fin, 1.0, 0.0)
    for f in range(fin):
        tail = jnp.where(row == f, readings[0, f : f + 1, :].astype(F32), tail)
    b[hid:, :] = tail.astype(BF16)
    base = b[...]
    chans = base.shape[0]
    bound = nt(s[...], base)
    halo = nt(e[n:, :], base)
    for p in range(nh // cap):
        pay[p, :, :chans] = bound[p * cap : (p + 1) * cap, :]
        pay[p, :, LANES : LANES + chans] = halo[p * cap : (p + 1) * cap, :]


def order_matrix(shape, chans, hid, fin, block):
    k = iota(shape, 0)
    col = iota(shape, 1)
    m = lax.div(col, jnp.int32(block))
    c = col - m * block
    source = jnp.where(c < hid, m * chans + fin + c, jnp.where(c < hid + fin, m * chans + c - hid, -1))
    return jnp.where(k == source, 1.0, 0.0).astype(BF16)


def mid_a_kernel(hid, fin, orders, e, b, gw, cw, fa, ra, gw_o, cw_o):
    n = e.shape[1]
    a = e[:n, :]
    base = b[...]
    fa[...] = nt(base, a)
    ra[...] = nn(base, a)
    block = base.shape[0]
    order = order_matrix((gw.shape[1], orders * block), hid + fin, hid, fin, block)
    gw_o[...] = nn(gw[...], order).astype(BF16)
    cw_o[...] = nn(cw[...], order).astype(BF16)


def post_a_kernel(one, cap, recv, e, s, fa, ra, f1, r1, ro, ri, pay, flat):
    n = e.shape[1]
    nh = s.shape[0]
    chans = fa.shape[0]
    for p in range(nh // cap):
        flat[p * cap : (p + 1) * cap, :] = recv[p]
    h = e[n:, :]
    sel = s[...]
    seen = flat[:, :chans].astype(BF16)
    back = flat[:, LANES : LANES + chans]
    back_degree = flat[:, LANES + one : LANES + one + 1]
    out_degree = fa[one : one + 1, :] + jnp.sum(sel.astype(F32) * back_degree, axis=0, keepdims=True)
    pulled = ra[...] + tn(seen, h)
    inv_o = 1.0 / out_degree
    inv_i = 1.0 / pulled[one : one + 1, :]
    ro[...] = inv_o
    ri[...] = inv_i
    first_out = ((fa[...] + tn(back.astype(BF16), sel)) * inv_o).astype(BF16)
    first_in = (pulled * inv_i).astype(BF16)
    f1[...] = first_out
    r1[...] = first_in
    bound = nt(sel, first_in)
    halo = nt(h, first_out)
    hi, ho = scaled(h, inv_i), scaled(h, inv_o)
    si, so = scaled(sel, inv_i), scaled(sel, inv_o)
    coefs = (nt(sel, hi), nt(h, so), nt(sel, ho), nt(h, si))
    for p in range(nh // cap):
        at = slice(p * cap, (p + 1) * cap)
        pay[p, :, :chans] = bound[at, :]
        pay[p, :, LANES : LANES + chans] = halo[at, :]
        for k, coef in enumerate(coefs):
            pay[p, :, 2 * LANES + k * nh : 2 * LANES + (k + 1) * nh] = coef[at, :]


def scaled(rows, factor):
    return (rows.astype(F32) * factor).astype(BF16)


def mid_b_kernel(e, s, f1, r1, ro, ri, f2l, r2l, kc, ke, ka):
    n = e.shape[1]
    a = e[:n, :]
    h = e[n:, :]
    sel = s[...]
    nh = sel.shape[0]
    chans = f1.shape[0]
    inv_o, inv_i = ro[...], ri[...]
    outs = nt(jnp.concatenate([f1[...], scaled(sel, inv_o), scaled(sel, inv_i)], axis=0), a)
    ins = nn(jnp.concatenate([r1[...], scaled(h, inv_i), scaled(h, inv_o)], axis=0), a)
    f2l[...] = outs[:chans]
    r2l[...] = ins[:chans]
    kc[:nh, :] = ins[chans : chans + nh].astype(BF16)
    kc[nh:, :] = h
    ke[:nh, :] = outs[chans : chans + nh].astype(BF16)
    ke[nh:, :] = sel
    ka[:nh, :] = (2.0 * ins[chans + nh :]).astype(BF16)
    ka[nh : 2 * nh, :] = h
    ka[2 * nh : 3 * nh, :] = (2.0 * outs[chans + nh :]).astype(BF16)
    ka[3 * nh :, :] = sel


def send(pay, cap, left, right, left_two, right_two):
    nh = left.shape[0]
    rows = jnp.concatenate([left, right], axis=1)
    rows_two = jnp.concatenate([left_two, right_two], axis=1)
    both = jnp.concatenate([rows, rows_two], axis=0).astype(BF16)
    k = iota((2 * nh, 2 * nh), 0)
    part = lax.div(k, jnp.int32(2 * cap))
    spot = k - part * (2 * cap)
    source = jnp.where(spot < cap, part * cap + spot, nh + part * cap + spot - cap)
    mine = nn(jnp.where(iota((2 * nh, 2 * nh), 1) == source, 1.0, 0.0).astype(BF16), both)
    for p in range(nh // cap):
        own = mine[p * 2 * cap : (p + 1) * 2 * cap, :]
        pay[p] = jnp.concatenate([rows, own], axis=0).astype(BF16)


def post_b_kernel(cap, one, recv, e, s, b, f1, r1, f2l, r2l, ro, ri, gw, gb, states, reset, update, y, f1l, r1l, pay, flat):
    n = e.shape[1]
    nh = s.shape[0]
    hid = y.shape[0]
    chans = b.shape[0]
    for p in range(nh // cap):
        flat[p * cap : (p + 1) * cap, :] = recv[p, :, : 2 * LANES]
    a = e[:n, :]
    h = e[n:, :]
    sel = s[...]
    inv_o, inv_i = ro[...], ri[...]
    base = b[...].astype(F32)
    seen = flat[:, :chans].astype(BF16)
    back = flat[:, LANES : LANES + chans].astype(BF16)
    f2 = 2.0 * (f2l[...] + tn(back, sel)) * inv_o - base
    r2 = 2.0 * (r2l[...] + tn(seen, h)) * inv_i - base
    states[:chans, :] = b[...]
    states[chans : 2 * chans, :] = f1[...]
    states[2 * chans : 3 * chans, :] = f2.astype(BF16)
    states[3 * chans : 4 * chans, :] = r1[...]
    states[4 * chans :, :] = r2.astype(BF16)
    gates = jax.nn.sigmoid(nn(gw[...], states[...]) + column(gb[...]))
    reset[...] = gates[:hid]
    update[...] = gates[hid:]
    now = (gates[:hid] * base[:hid]).astype(BF16)
    y[...] = now
    local_out = nt(now, a) * inv_o
    local_in = nn(now, a) * inv_i
    f1l[...] = local_out
    r1l[...] = local_in
    bound = nt(sel, jnp.concatenate([now, local_in.astype(BF16)], axis=0))
    halo = nt(h, jnp.concatenate([now, local_out.astype(BF16)], axis=0))
    send(pay, cap, bound[:, :hid], halo[:, :hid], bound[:, hid:], halo[:, hid:])


def gather_matrix(coef, out, nd, cap, per, first, factor):
    nh = nd * cap
    width = nd * per
    k = iota((nh, width), 0)
    col = iota((nh, width), 1)
    r = lax.div(col, jnp.int32(per))
    u = col - r * per
    p = lax.div(u, jnp.int32(cap))
    spot = u - p * cap
    here = lax.div(k, jnp.int32(cap))
    slot = k - here * cap
    inside = u < nh
    place = jnp.where((k == r * cap + spot) & inside, 1.0, 0.0).astype(BF16)
    keep = (here == p) & inside
    for i in range(2):
        wide = nn(coef[:, (first + i) * nh : (first + i + 1) * nh].astype(BF16), place)
        own = (r == here) & (u == nh + cap + slot)
        out[(i + 1) * nh : (i + 2) * nh, :] = jnp.where(keep, factor * wide, jnp.where(own, 1.0, 0.0)).astype(BF16)
    out[:nh, :] = jnp.where((r == here) & (u == nh + slot), 1.0, 0.0).astype(BF16)


def mid_c_kernel(nd, cap, per, fused, recv, e, f1l, r1l, f2l, r2l, *rest):
    n = e.shape[1]
    a = e[:n, :]
    f2l[...] = nt(f1l[...].astype(BF16), a)
    r2l[...] = nn(r1l[...].astype(BF16), a)
    if fused:
        gd, ga, flat = rest
        for p in range(nd):
            flat[p * cap : (p + 1) * cap, :] = recv[p, :, 2 * LANES :]
        gather_matrix(flat, gd, nd, cap, per, 0, 1.0)
        gather_matrix(flat, ga, nd, cap, per, 2, 2.0)


def arrived(fused, hid, nh, g, recv):
    if fused:
        halo = nn(g[...], recv[...].reshape(recv.shape[0] * recv.shape[1], recv.shape[2]))
        two = halo[nh : 2 * nh, :hid], halo[2 * nh :, hid:]
    else:
        halo = recv[...]
        two = halo[nh:, :hid], halo[nh:, hid:]
    one = halo[:nh]
    return one[:, :hid], one[:, hid:], two[0], two[1]


def back_and_send(cap, hid, g, a, h, sel, inv_o, inv_i, z1, z2, pay):
    g0, g1, g2, g3, g4 = (g[m * hid : (m + 1) * hid, :].astype(BF16).astype(F32) for m in range(5))
    y1 = (g2 * inv_o).astype(BF16)
    y2 = (g4 * inv_i).astype(BF16)
    now1 = ((g1 + 2.0 * nn(y1, a)) * inv_o).astype(BF16)
    now2 = ((g3 + 2.0 * nt(y2, a)) * inv_i).astype(BF16)
    z1[...] = now1
    z2[...] = now2
    bound = nt(sel, jnp.concatenate([y1, now1], axis=0))
    halo = nt(h, jnp.concatenate([y2, now2], axis=0))
    send(pay, cap, bound[:, :hid], halo[:, :hid], bound[:, hid:], halo[:, hid:])
    return g0 - g2 - g4


def hidden_weights(w, hid, block, orders):
    return jnp.concatenate([w[:, m * block : m * block + hid] for m in range(orders)], axis=1)


def post_c_kernel(fused, cap, orders, g, recv, e, s, kc, ke, y, f1l, r1l, f2l, r2l, ro, ri, states, cw, cb, upstream, update,
                  mixed, cand_grad, gate_update, z1, z2, direct, pay):
    n = e.shape[1]
    nh = s.shape[0]
    hid = y.shape[0]
    block = states.shape[0] // orders
    a = e[:n, :]
    h = e[n:, :]
    sel = s[...]
    inv_o, inv_i = ro[...], ri[...]
    c1, e1, c2, e2 = arrived(fused, hid, nh, g, recv)
    base = y[...].astype(F32)
    c1, e1 = c1.astype(BF16), e1.astype(BF16)
    cc = jnp.concatenate([c1, c2.astype(BF16)], axis=0)
    ee = jnp.concatenate([e1, e2.astype(BF16)], axis=0)
    f1 = f1l[...] + tn(e1, sel) * inv_o
    f2 = 2.0 * (f2l[...] + tn(ee, ke[...])) * inv_o - base
    r1 = r1l[...] + tn(c1, h) * inv_i
    r2 = 2.0 * (r2l[...] + tn(cc, kc[...])) * inv_i - base
    for m, value in enumerate((y[...], f1, f2, r1, r2)):
        mixed[m * block : m * block + hid, :] = value.astype(BF16)
        mixed[m * block + hid : (m + 1) * block, :] = states[m * block + hid : (m + 1) * block, :]
    weights = cw[...]
    cand = jnp.tanh(nn(weights, mixed[...]) + column(cb[...]))
    up = upstream[0].astype(F32)
    gate = update[...]
    grad = (up * (1.0 - gate) * (1.0 - cand * cand)).astype(BF16)
    cand_grad[...] = grad
    held = states[:hid, :].astype(F32)
    gate_update[...] = (up * (held - cand) * gate * (1.0 - gate)).astype(BF16)
    back = tn(hidden_weights(weights, hid, block, orders), grad)
    direct[...] = back_and_send(cap, hid, back, a, h, sel, inv_o, inv_i, z1, z2, pay)


def weight_part(grad, features, orders, chans, hid, fin):
    block = features.shape[0] // orders
    width = -(-(orders * chans + 1) // LANES) * LANES
    shape = (width, orders * block)
    k = iota(shape, 0)
    col = iota(shape, 1)
    m = lax.div(col, jnp.int32(block))
    c = col - m * block
    source = jnp.where(c < hid, m * chans + fin + c, jnp.where(c < hid + fin, m * chans + c - hid, -1))
    source = jnp.where(col == hid + fin, orders * chans, source)
    order = jnp.where(k == source, 1.0, 0.0).astype(BF16)
    return nt(nt(grad, features).astype(BF16), order)


def mid_d_kernel(orders, fin, e, z1, z2, direct, cand_grad, mixed, gate_update, states, base, part):
    n = e.shape[1]
    a = e[:n, :]
    hid = z1.shape[0]
    base[...] = direct[...] + nn(z1[...], a) + nt(z2[...], a)
    part[:hid, :] = weight_part(gate_update[...], states[...], orders, hid + fin, hid, fin).astype(BF16)
    part[hid:, :] = weight_part(cand_grad[...], mixed[...], orders, hid + fin, hid, fin).astype(BF16)


def add_halo(fused, g, recv, ka, base):
    hid = base.shape[0]
    nh = ka.shape[0] // 4
    c1, e1, c2, e2 = arrived(fused, hid, nh, g, recv)
    return base[...] + tn(jnp.concatenate([c1, c2, e1, e2], axis=0).astype(BF16), ka[...])


def post_d_kernel(fused, cap, orders, g, recv, e, s, ka, base, ro, ri, states, gw, upstream, reset, update, gate_update,
                  gate_reset, z1, z2, direct, pay):
    n = e.shape[1]
    hid = base.shape[0]
    block = states.shape[0] // orders
    scaled_grad = add_halo(fused, g, recv, ka, base)
    held = states[:hid, :].astype(F32)
    gate = reset[...]
    grad = (scaled_grad * held * gate * (1.0 - gate)).astype(BF16)
    gate_reset[...] = grad
    weights = hidden_weights(gw[...], hid, block, orders)
    back = tn(weights, jnp.concatenate([grad, gate_update[...]], axis=0))
    rest = back_and_send(cap, hid, back, e[:n, :], e[n:, :], s[...], ro[...], ri[...], z1, z2, pay)
    direct[...] = rest + upstream[0].astype(F32) * update[...] + scaled_grad * gate


def mid_e_kernel(orders, fin, rows, e, z1, z2, direct, gate_reset, states, part, base, grads):
    n = e.shape[1]
    a = e[:n, :]
    hid = z1.shape[0]
    base[...] = direct[...] + nn(z1[...], a) + nt(z2[...], a)
    first = weight_part(gate_reset[...], states[...], orders, hid + fin, hid, fin)
    both = jnp.concatenate([first, part[...].astype(F32)], axis=0)
    for k in range(grads.shape[0]):
        if k * rows < both.shape[0]:
            grads[k] = both[k * rows : (k + 1) * rows, :].astype(BF16)
        else:
            grads[k] = jnp.zeros(grads.shape[1:], BF16)


def post_e_kernel(fused, g, recv, ka, base, out):
    out[0] = add_halo(fused, g, recv, ka, base).astype(BF16)


def add_kernel(recv, out):
    total = recv[0].astype(F32)
    for k in range(1, recv.shape[0]):
        total = total + recv[k].astype(F32)
    for k in range(out.shape[0]):
        out[k] = total.astype(BF16)


def finish_kernel(hid, factor, recv, gw, gb, cw, cb):
    rows = recv.shape[1]
    features = gw.shape[1]
    total = gw.shape[0] + cw.shape[0]
    for k in range(total // rows):
        part = recv[k].astype(F32)[:, :features] * factor
        at = k * rows
        if at < 2 * hid:
            gw[at : at + rows, :] = part
        else:
            cw[at - 2 * hid : at - 2 * hid + rows, :] = part
    flat = jnp.concatenate([recv[k].astype(F32) for k in range(total // rows)], axis=0)
    pick = jnp.where(iota((8, flat.shape[1]), 1) == features, 1.0, 0.0).astype(BF16)
    bias = nt(pick, flat.astype(BF16))[:1] * factor
    gb[...] = bias[:, : 2 * hid]
    cb[...] = bias[:, 2 * hid :]


def spread_body(
    readings,
    previous,
    upstream,
    gate_weight,
    gate_bias,
    cand_weight,
    cand_bias,
    neighbours,
    edge_weight,
    send_rows,
):
    fin, hid = readings.shape[1], previous.shape[1]
    chans = fin + hid
    orders = gate_weight.shape[1] // chans
    n = readings.shape[2]
    nd = lax.axis_size("dom")
    devices = nd * lax.axis_size("snap")
    nh = send_rows.shape[1]
    cap = nh // nd
    block = hid + 16 * (-(-(fin + 1) // 16))
    one = hid + fin
    per = nh + 2 * cap
    fused = 3 * nh * nd * per <= 1 << 18
    move = functools.partial(lax.all_to_all, axis_name="dom", split_axis=0, concat_axis=0, tiled=True)

    e, s, b, pay = run(
        functools.partial(prep_kernel, cap), "prep",
        [((n + nh, n), BF16), ((nh, n), BF16), ((block, n), BF16), ((nd, cap, 2 * LANES), F32)],
        neighbours, edge_weight, send_rows, readings, previous,
    )
    recv = move(pay)
    fa, ra, gw, cw = run(
        functools.partial(mid_a_kernel, hid, fin, orders), "mid_a",
        [((block, n), F32), ((block, n), F32), ((2 * hid, orders * block), BF16), ((hid, orders * block), BF16)],
        e, b, gate_weight, cand_weight,
    )
    wide = 2 * LANES + 4 * nh
    f1, r1, ro, ri, pay = run(
        functools.partial(post_a_kernel, one, cap), "post_a",
        [((block, n), BF16), ((block, n), BF16), ((1, n), F32), ((1, n), F32), ((nd, cap, wide), F32)],
        recv, e, s, fa, ra, scratch=[pltpu.VMEM((nh, 2 * LANES), F32)],
    )
    recv_b = move(pay)
    f2l, r2l, kc, ke, ka = run(
        mid_b_kernel, "mid_b",
        [((block, n), F32), ((block, n), F32), ((2 * nh, n), BF16), ((2 * nh, n), BF16), ((4 * nh, n), BF16)],
        e, s, f1, r1, ro, ri,
    )
    pay_kind = ((nd, per, 2 * hid), BF16)
    field, field16 = ((hid, n), F32), ((hid, n), BF16)
    states, reset, update, y, f1l, r1l, pay = run(
        functools.partial(post_b_kernel, cap, one), "post_b",
        [((orders * block, n), BF16), field, field, field16, field, field, pay_kind],
        recv_b, e, s, b, f1, r1, f2l, r2l, ro, ri, gw, gate_bias[None, :],
        scratch=[pltpu.VMEM((nh, 2 * LANES), F32)],
    )
    recv = move(pay)
    table = ((3 * nh, nd * per), BF16)
    f2l, r2l, *tables = run(
        functools.partial(mid_c_kernel, nd, cap, per, fused), "mid_c",
        [field, field] + [table] * (2 if fused else 0),
        recv_b, e, f1l, r1l, scratch=[pltpu.VMEM((nh, 4 * nh), F32)] if fused else [],
    )
    if fused:
        inward, outward = tables
        halo_of = lambda got, first, factor: got
    else:
        inward = outward = jnp.zeros((8, LANES), BF16)
        coefs = recv_b[:, :, 2 * LANES :].reshape(nd, cap, 4, nd, cap)

        def halo_of(got, first, factor):
            rows = got[:, :nh].reshape(nd, nd, cap, 2, hid).astype(F32)
            two = jnp.einsum("psgrt,rptgk->psgk", coefs[:, :, first : first + 2], rows)
            two = factor * two.reshape(nh, 2 * hid) + got[:, nh + cap :].reshape(nh, 2 * hid).astype(F32)
            return jnp.concatenate([got[:, nh : nh + cap].reshape(nh, 2 * hid).astype(F32), two], axis=0)

    mixed, cand_grad, gate_update, z1, z2, direct, pay = run(
        functools.partial(post_c_kernel, fused, cap, orders), "post_c",
        [((orders * block, n), BF16), field16, field16, field16, field16, field, pay_kind],
        inward, halo_of(recv, 0, 1.0), e, s, kc, ke, y, f1l, r1l, f2l, r2l, ro, ri, states, cw, cand_bias[None, :], upstream, update,
    )
    recv = move(pay)
    width = -(-(orders * chans + 1) // LANES) * LANES
    base, part = run(
        functools.partial(mid_d_kernel, orders, fin), "mid_d", [field, ((2 * hid, width), BF16)],
        e, z1, z2, direct, cand_grad, mixed, gate_update, states,
    )
    gate_reset, z1, z2, direct, pay = run(
        functools.partial(post_d_kernel, fused, cap, orders), "post_d",
        [field16, field16, field16, field, pay_kind],
        outward, halo_of(recv, 2, 2.0), e, s, ka, base, ro, ri, states, gw, upstream, reset, update, gate_update,
    )
    recv = move(pay)
    rows = 8 * (-(-3 * hid // (8 * devices)))
    base, grads = run(
        functools.partial(mid_e_kernel, orders, fin, rows), "mid_e", [field, ((devices, rows, width), BF16)],
        e, z1, z2, direct, gate_reset, states, part,
    )
    (state_grad,) = run(
        functools.partial(post_e_kernel, fused), "post_e", [((1, hid, n), BF16)],
        outward, halo_of(recv, 2, 2.0), ka, base,
    )
    both = ("snap", "dom")
    grads = lax.all_to_all(grads, both, 0, 0, tiled=True)
    (grads,) = run(add_kernel, "add", [((devices, rows, width), BF16)], grads)
    grads = lax.all_to_all(grads, both, 0, 0, tiled=True)
    factor = 1.0 / math.sqrt(readings.shape[0] * lax.axis_size("snap") * n * nd)
    feats = orders * chans
    grad_gw, grad_gb, grad_cw, grad_cb = run(
        functools.partial(finish_kernel, hid, factor), "finish",
        [((2 * hid, feats), F32), ((1, 2 * hid), F32), ((hid, feats), F32), ((1, hid), F32)],
        grads,
    )
    return state_grad, grad_gw, grad_gb[0], grad_cw, grad_cb[0]


def pack_kernel(own, nb, w, rows, readings, previous, tail):
    degree = nb.shape[0]
    nh = rows.shape[1]
    hid = previous.shape[1]
    fin = readings.shape[1]
    tail[...] = jnp.zeros_like(tail)
    tail[:fin, :] = readings[0].astype(F32)
    high = lax.shift_right_logical(nb[...], 5)
    tail[fin : fin + degree, :] = high.astype(F32)
    tail[fin + degree : fin + 2 * degree, :] = (nb[...] - high * 32).astype(F32)
    tail[fin + 2 * degree : fin + 3 * degree, :] = w[...]
    at = fin + 3 * degree
    high = lax.shift_right_logical(rows[...], 5)
    tail[at : at + 1, :nh] = high.astype(F32)
    tail[at + 1 : at + 2, :nh] = (rows[...] - high * 32).astype(F32)
    own[:hid, :] = previous[0]
    own[hid:, :] = tail[...].astype(BF16)


def pack_entry(nb, w, rows, readings, previous, own, sent, tail):
    pack_kernel(own, nb, w, rows, readings, previous, tail)
    sent[...] = own[...]


def exchange(first, second, hc, sc, pay):
    count = first[0].shape[0]
    parts = len(first)
    pay[:count, :] = jnp.concatenate([nt(first[p], sc[p]).astype(BF16) for p in range(parts)], axis=1)
    pay[count:, :] = jnp.concatenate([nt(second[p], hc[p]).astype(BF16) for p in range(parts)], axis=1)


def merged(parts, mine, got):
    step = mine.shape[1] // (2 * parts)
    here = lax.rem(lax.div(iota(mine.shape, 1), jnp.int32(step)), jnp.int32(2)) == 0
    value = jnp.where(here, mine[...].astype(F32), got[...].astype(F32)).astype(BF16)
    count = mine.shape[0] // 2
    return value[:count, :], value[count:, :]


def build_part(cap, hid, fin, degree, parts, p, block, a, at, hc, hx, sc, sx, b):
    n = a.shape[1]
    slots = sx.shape[0]
    nh = 2 * parts * cap
    half = parts * cap
    core = lax.rem(lax.axis_index("dom"), 2)
    line = iota((nh, 1), 0)
    rel = lax.div(line, jnp.int32(half))
    k = lax.div(line - rel * half, jnp.int32(cap))
    t = line - rel * half - k * cap
    spot = (k * 2 + lax.bitwise_xor(rel, core)) * cap + t
    node = (n + spot).astype(F32)
    width = -(-nh // LANES) * LANES
    slot = iota((slots, nh), 0)
    outer = lax.div(slot, jnp.int32(nh))
    rest = slot - outer * nh
    slot_rel = lax.div(rest, jnp.int32(half))
    rest = rest - slot_rel * half
    inner = lax.div(rest, jnp.int32(cap))
    filled = iota((slots, nh), 1) == slot_rel * half + outer * cap + rest - inner * cap
    row = iota((32, n), 0).astype(F32)
    edges = hid + fin + 3 * degree + 2
    tail = block[hid : hid + 16 * (-(-(edges - hid) // 16)), :].astype(F32)
    high, low = tail[fin : fin + degree], tail[fin + degree : fin + 2 * degree]
    w = tail[fin + 2 * degree : fin + 3 * degree]
    start = fin + 3 * degree
    sent = tail[start : start + 1] * 32.0 + tail[start + 1 : start + 2]
    low_is = [jnp.where(low[d : d + 1] == row, 1.0, 0.0).astype(BF16) for d in range(degree)]
    for chunk in range(n // 32):
        total = None
        for d in range(degree):
            term = low_is[d] * jnp.where(high[d : d + 1] == float(chunk), w[d : d + 1], 0.0).astype(BF16)
            total = term if total is None else total + term
        a[chunk * 32 : (chunk + 1) * 32, :] = total
    at[...] = a[...].T
    names = high * 32.0 + low
    total = jnp.zeros((nh, n), F32)
    for d in range(degree):
        total = total + jnp.where(names[d : d + 1] == node, w[d : d + 1], 0.0)
    halo = total.astype(BF16)
    hc[...] = halo
    named = jnp.where(iota((nh, width), 1) == spot, sent[:, :width], 0.0)
    target = jnp.sum(named, axis=1, keepdims=True).astype(jnp.int32)
    picked = jnp.where(iota((nh, n), 1) == target, 1.0, 0.0).astype(BF16)
    sc[...] = picked
    place = jnp.where(filled & (inner == p), 1.0, 0.0).astype(BF16)
    hx[...] = nn(place, halo).astype(BF16)
    sx[...] = nn(place, picked).astype(BF16)
    b[:hid, :] = block[:hid, :]
    line = iota(tail.shape, 0)
    b[hid:, :] = jnp.where(line < fin, tail, jnp.where(line == fin, 1.0, 0.0)).astype(BF16)


def build_early_kernel(cap, hid, fin, degree, parts, *refs):
    count = parts - 1
    z = lax.shift_right_logical(lax.axis_index("dom"), 1)
    for k in range(count):
        p = lax.bitwise_xor(z, jnp.int32(k))
        build_part(cap, hid, fin, degree, parts, p, refs[k], *(ref.at[k] for ref in refs[count:]))


def build_late_kernel(cap, hid, fin, degree, parts, last, *refs):
    early, outs, pay = refs[:7], refs[7:14], refs[14]
    z = lax.shift_right_logical(lax.axis_index("dom"), 1)
    for k in range(parts - 1):
        p = lax.bitwise_xor(z, jnp.int32(k))
        for source, to in zip(early, outs):
            to[p] = source[k]
    p = lax.bitwise_xor(z, jnp.int32(parts - 1))
    build_part(cap, hid, fin, degree, parts, p, last, *(ref.at[p] for ref in outs))
    hc, sc, b = outs[2], outs[4], outs[6]
    base = [b[p] for p in range(parts)]
    exchange(base, base, hc, sc, pay)


def chip_source(col, chans, hid, fin, block):
    m = lax.div(col, jnp.int32(block))
    c = col - m * block
    m = jnp.where(m == 2, 3, jnp.where(m == 3, 2, m))
    return m, c, jnp.where(c < hid, m * chans + fin + c, jnp.where(c < hid + fin, m * chans + c - hid, -1))


def order_kernel(hid, fin, orders, block, gw, cw, gw_o, cw_o, gw_b, cw_b, order):
    chans = hid + fin
    feats = cw.shape[1]
    shape = (feats, orders * block)
    source = chip_source(iota(shape, 1), chans, hid, fin, block)[2]
    pick = jnp.where(iota(shape, 0) == source, 1.0, 0.0).astype(BF16)
    gw_o[...] = tn(gw[...], pick).astype(BF16)
    cw_o[...] = nn(cw[...], pick).astype(BF16)
    shape = (orders * hid, feats)
    line = iota(shape, 0)
    m = lax.div(line, jnp.int32(hid))
    pick = jnp.where(iota(shape, 1) == m * chans + fin + line - m * hid, 1.0, 0.0).astype(BF16)
    gw_b[...] = nn(pick, gw[...]).astype(BF16)
    cw_b[...] = nt(pick, cw[...]).astype(BF16)
    m, c, source = chip_source(iota(order.shape, 0), chans, hid, fin, block)
    source = jnp.where((m == 0) & (c == hid + fin), feats, source)
    order[...] = jnp.where(iota(order.shape, 1) == source, 1.0, 0.0).astype(BF16)


def local_kernel(a, at, x1, x2, l1, l2):
    for p in range(a.shape[0]):
        l1[p] = nn(x1[p], a[p])
        l2[p] = nn(x2[p], at[p])


def arrive(sx, hx, mine, got, l1, l2):
    parts = range(sx.shape[0])
    top, low = merged(sx.shape[0], mine, got)
    pulled = [l1[p] + nn(top, hx[p]) for p in parts]
    pushed = [l2[p] + nn(low, sx[p]) for p in parts]
    return parts, pulled, pushed


def chip_a_kernel(one, mine, got, hc, hx, sc, sx, b, l1, l2, sa, ro, ri, pay):
    chans = b.shape[1]
    parts, pulled, pushed = arrive(sx, hx, mine, got, l1, l2)
    inv_o = [1.0 / pushed[p][one : one + 1, :] for p in parts]
    inv_i = [1.0 / pulled[p][one : one + 1, :] for p in parts]
    outs = [(pushed[p] * inv_o[p]).astype(BF16) for p in parts]
    ins = [(pulled[p] * inv_i[p]).astype(BF16) for p in parts]
    for p in parts:
        ro[p] = inv_o[p]
        ri[p] = inv_i[p]
        sa[p, :chans, :] = b[p]
        sa[p, chans : 2 * chans, :] = outs[p]
        sa[p, 2 * chans :, :] = ins[p]
    exchange(ins, outs, hc, sc, pay)


def local_b_kernel(a, at, sa, gw, l1, l2, gp):
    chans = l1.shape[1]
    weights = gw[:, : 3 * chans]
    for p in range(a.shape[0]):
        l1[p] = nn(sa[p, 2 * chans :, :], a[p])
        l2[p] = nn(sa[p, chans : 2 * chans, :], at[p])
        gp[p] = nn(weights, sa[p])


def chip_b_kernel(mine, got, hc, hx, sc, sx, sa, l1, l2, ro, ri, gw, gb, gp, sb, reset, update, y, pay):
    hid = y.shape[1]
    chans = l1.shape[1]
    bias = column(gb[...])
    weights = gw[:, 3 * chans :]
    parts, pulled, pushed = arrive(sx, hx, mine, got, l1, l2)
    base = [sa[p, :chans, :].astype(F32) for p in parts]
    r2 = [(pulled[p] * (2.0 * ri[p]) - base[p]).astype(BF16) for p in parts]
    f2 = [(pushed[p] * (2.0 * ro[p]) - base[p]).astype(BF16) for p in parts]
    second = [jnp.concatenate([f2[p], r2[p]], axis=0) for p in parts]
    gates = [jax.nn.sigmoid(gp[p] + nn(weights, second[p]) + bias) for p in parts]
    now = [(gates[p][:hid] * base[p][:hid]).astype(BF16) for p in parts]
    for p in parts:
        sb[p] = second[p]
        reset[p] = gates[p][:hid]
        update[p] = gates[p][hid:]
        y[p] = now[p]
    exchange(now, now, hc, sc, pay)


def chip_c1_kernel(mine, got, hc, hx, sc, sx, y, sa, l1, l2, ro, ri, ma, pay):
    hid = y.shape[1]
    chans = ma.shape[1] // 3
    parts, pulled, pushed = arrive(sx, hx, mine, got, l1, l2)
    ins = [(pulled[p] * ri[p]).astype(BF16) for p in parts]
    outs = [(pushed[p] * ro[p]).astype(BF16) for p in parts]
    exchange(ins, outs, hc, sc, pay)
    for p in parts:
        for m, value in enumerate((y[p], outs[p], ins[p])):
            ma[p, m * chans : m * chans + hid, :] = value
            ma[p, m * chans + hid : (m + 1) * chans, :] = sa[p, m * chans + hid : (m + 1) * chans, :]


def local_c2_kernel(a, at, ma, cw, l1, l2, cp):
    hid = l1.shape[1]
    chans = ma.shape[1] // 3
    weights = cw[:, : 3 * chans]
    for p in range(a.shape[0]):
        l1[p] = nn(ma[p, 2 * chans : 2 * chans + hid, :], a[p])
        l2[p] = nn(ma[p, chans : chans + hid, :], at[p])
        cp[p] = nn(weights, ma[p])


def split_back(back, hid, ro, ri, y1, y2, g1, g3, direct):
    parts = range(len(back))
    blocks = [[back[p][m * hid : (m + 1) * hid, :] for m in range(5)] for p in parts]
    one = [(blocks[p][2] * (2.0 * ro[p])).astype(BF16) for p in parts]
    two = [(blocks[p][4] * (2.0 * ri[p])).astype(BF16) for p in parts]
    for p in parts:
        y1[p] = one[p]
        y2[p] = two[p]
        g1[p] = blocks[p][1].astype(BF16)
        g3[p] = blocks[p][3].astype(BF16)
        direct[p] = blocks[p][0] - blocks[p][2] - blocks[p][4]
    return one, two


def chip_c2_kernel(parts, *refs):
    ups, refs = refs[:parts], refs[parts:]
    mine, got, hc, hx, sc, sx, ma, sa, sb, l1, l2, ro, ri, cw, cw_b, cb, cp, update = refs[:18]
    mb, cand_grad, gate_update, y1, y2, g1, g3, upstream, direct, pay = refs[18:]
    hid = l1.shape[1]
    chans = ma.shape[1] // 3
    z = lax.shift_right_logical(lax.axis_index("dom"), 1)
    for k in range(parts):
        upstream[lax.bitwise_xor(z, jnp.int32(k))] = ups[k][0]
    bias = column(cb[...])
    weights = cw[:, 3 * chans :]
    parts, pulled, pushed = arrive(sx, hx, mine, got, l1, l2)
    base = [ma[p, :hid, :].astype(F32) for p in parts]
    r2 = [(pulled[p] * (2.0 * ri[p]) - base[p]).astype(BF16) for p in parts]
    f2 = [(pushed[p] * (2.0 * ro[p]) - base[p]).astype(BF16) for p in parts]
    second = [
        jnp.concatenate([f2[p], sb[p, hid:chans, :], r2[p], sb[p, chans + hid :, :]], axis=0) for p in parts
    ]
    cand = [jnp.tanh(cp[p] + nn(weights, second[p]) + bias) for p in parts]
    rest = [upstream[p].astype(F32) * (1.0 - update[p]) for p in parts]
    grad = [(rest[p] - rest[p] * cand[p] * cand[p]).astype(BF16) for p in parts]
    back = [nn(cw_b[...], grad[p]) for p in parts]
    for p in parts:
        mb[p] = second[p]
        cand_grad[p] = grad[p]
        gate_update[p] = ((sa[p, :hid, :].astype(F32) - cand[p]) * (rest[p] * update[p])).astype(BF16)
    one, two = split_back(back, hid, ro, ri, y1, y2, g1, g3, direct)
    exchange(one, two, hc, sc, pay)


def chip_part(grads, first, second, order):
    parts = range(first.shape[0])
    split = first.shape[1]
    one = sum(nt(grads[p], first[p]) for p in parts).astype(BF16)
    two = sum(nt(grads[p], second[p]) for p in parts).astype(BF16)
    return nn(one, order[:split, :]) + nn(two, order[split:, :])


def local_d_kernel(a, at, y1, y2, cand_grad, ma, mb, order, l1, l2, part):
    local_kernel(a, at, y1, y2, l1, l2)
    part[...] = chip_part(cand_grad, ma, mb, order).astype(BF16)


def chip_d1_kernel(mine, got, hc, hx, sc, sx, l1, l2, g1, g3, ro, ri, z1, z2, pay):
    parts, pulled, pushed = arrive(sx, hx, mine, got, l1, l2)
    one = [((g1[p].astype(F32) + pulled[p]) * ro[p]).astype(BF16) for p in parts]
    two = [((g3[p].astype(F32) + pushed[p]) * ri[p]).astype(BF16) for p in parts]
    exchange(one, two, hc, sc, pay)
    for p in parts:
        z1[p] = one[p]
        z2[p] = two[p]


def local_d2_kernel(a, at, z1, z2, direct, base):
    for p in range(a.shape[0]):
        base[p] = direct[p] + nn(z1[p], a[p]) + nn(z2[p], at[p])


def chip_d2_kernel(mine, got, hc, hx, sc, sx, base, ro, ri, sa, gw_b, upstream, reset, update, gate_update,
                   gate_grad, y1, y2, g1, g3, direct, pay):
    hid = base.shape[1]
    parts = range(sx.shape[0])
    top, low = merged(sx.shape[0], mine, got)
    scaled_grad = [base[p] + nn(top, hx[p]) + nn(low, sx[p]) for p in parts]
    kept = [scaled_grad[p] * reset[p] for p in parts]
    grad = [
        jnp.concatenate([(sa[p, :hid, :].astype(F32) * (kept[p] - kept[p] * reset[p])).astype(BF16), gate_update[p]], axis=0)
        for p in parts
    ]
    back = [nn(gw_b[...], grad[p]) for p in parts]
    one, two = split_back(back, hid, ro, ri, y1, y2, g1, g3, direct)
    for p in parts:
        gate_grad[p] = grad[p]
        direct[p] = direct[p] + upstream[p].astype(F32) * update[p] + kept[p]
    exchange(one, two, hc, sc, pay)


def grads_kernel(gate_grad, sa, sb, order, part, keep, give, flat):
    both = gate_grad.shape[1]
    half = keep.shape[0]
    core = lax.rem(lax.axis_index("dom"), 2)
    flat[:both, :] = chip_part(gate_grad, sa, sb, order)
    flat[both:, :] = part[...].astype(F32)
    keep[...] = flat[pl.ds(pl.multiple_of(core * half, 8), half), :].astype(BF16)
    give[...] = flat[pl.ds(pl.multiple_of((1 - core) * half, 8), half), :].astype(BF16)


def local_e_kernel(a, at, z1, z2, direct, base):
    z = lax.shift_right_logical(lax.axis_index("dom"), 1)
    base[...] = direct[z] + nn(z1[z], a[z]) + nn(z2[z], at[z])


def chip_e_kernel(mine, got, hc, hx, sc, sx, base, out, done):
    done[...] = jnp.zeros_like(done)
    z = lax.shift_right_logical(lax.axis_index("dom"), 1)
    top, low = merged(sx.shape[0], mine, got)
    out[0] = (base[...] + nn(top, hx[z]) + nn(low, sx[z])).astype(BF16)


def sum_kernel(*refs):
    values = [ref[...].astype(F32) for ref in refs[:-2]]
    while len(values) > 1:
        values = [values[k] + values[k + 1] for k in range(0, len(values), 2)]
    refs[-1][...] = values[0].astype(BF16)
    refs[-2][...] = values[0].astype(BF16)


def end_kernel(factor, mine, got, gw, gb, cw, cb, flat):
    half = mine.shape[0]
    core = lax.rem(lax.axis_index("dom"), 2)
    flat[pl.ds(pl.multiple_of(core * half, 8), half), :] = mine[...].astype(F32)
    flat[pl.ds(pl.multiple_of((1 - core) * half, 8), half), :] = got[...].astype(F32)
    features, rows = gw.shape
    same = jnp.where(iota((features, flat.shape[1]), 0) == iota((features, flat.shape[1]), 1), 1.0, 0.0).astype(BF16)
    gw[...] = nt(same, flat[:rows, :].astype(BF16)) * factor
    cw[...] = flat[rows:, :features] * factor
    pick = jnp.where(iota((8, flat.shape[1]), 1) == features, 1.0, 0.0).astype(BF16)
    bias = nt(pick, flat[...].astype(BF16))[:1] * factor
    gb[...] = bias[:, :rows]
    cb[...] = bias[:, rows:]


def chip_body(
    readings,
    previous,
    upstream,
    gate_weight,
    gate_bias,
    cand_weight,
    cand_bias,
    neighbours,
    edge_weight,
    send_rows,
):
    fin, hid = readings.shape[1], previous.shape[1]
    chans = fin + hid
    orders = gate_weight.shape[1] // chans
    degree = neighbours.shape[0]
    n = readings.shape[2]
    nd = lax.axis_size("dom")
    snaps = lax.axis_size("snap")
    parts = nd // 2
    cap = send_rows.shape[1] // nd
    block = hid + 16 * (-(-(fin + 3 * degree + 2) // 16))
    slots = 2 * parts * parts * cap

    def swap(array, k, axis="dom", size=nd):
        return lax.ppermute(array, axis, [(i, i ^ k) for i in range(size)])

    own, sent = run(
        pack_entry, "pack", [((block, n), BF16)] * 2, neighbours, edge_weight, send_rows, readings, previous,
        scratch=[pltpu.VMEM((block - hid, n), F32)], vmem=56,
    )
    blocks = [own] + [swap(sent, 2 * k) for k in range(1, parts - 1)]
    relay = blocks[-1] if parts > 2 else sent
    ups = [upstream] + [swap(upstream, 2 * k) for k in range(1, parts - 1)]
    ups.append(swap(ups[-1], 2))
    width = -(-(orders * chans + 1) // LANES) * LANES
    gw, cw, gw_b, cw_b, order = run(
        functools.partial(order_kernel, hid, fin, orders, block), "order",
        [((2 * hid, orders * block), BF16), ((hid, orders * block), BF16), ((orders * hid, 2 * hid), BF16), ((orders * hid, hid), BF16),
         ((orders * block, width), BF16)],
        gate_weight.T, cand_weight, after=[own],
    )
    relay, gw = lax.optimization_barrier((relay, gw))
    wide, wide16, wide_pay = ((parts, block, n), F32), ((parts, block, n), BF16), ((2 * block, slots), BF16)
    field, field16, pay_kind = ((parts, hid, n), F32), ((parts, hid, n), BF16), ((2 * hid, slots), BF16)
    first, second = ((parts, 3 * block, n), BF16), ((parts, 2 * block, n), BF16)
    line = ((parts, 1, n), F32)
    built = [((n, n), BF16)] * 2 + [((rows, n), BF16) for rows in (2 * parts * cap, slots)] * 2 + [((block, n), BF16)]
    early = run(
        functools.partial(build_early_kernel, cap, hid, fin, degree, parts), "build_early",
        [((parts - 1, *shape), kind) for shape, kind in built], *blocks[:-1], relay if parts > 2 else own,
    )
    a, at, hc, hx, sc, sx, b, pay = run(
        functools.partial(build_late_kernel, cap, hid, fin, degree, parts), "build_late",
        [((parts, *shape), kind) for shape, kind in built] + [wide_pay], swap(relay, 2), *early,
    )
    edges = (hc, hx, sc, sx)
    got = swap(pay, 1)
    l1, l2 = run(local_kernel, "local_a", [wide, wide], a, at, b, b)
    sa, ro, ri, pay = run(
        functools.partial(chip_a_kernel, hid + fin), "chip_a", [first, line, line, wide_pay],
        pay, got, *edges, b, l1, l2, after=ups[1:],
    )
    got = swap(pay, 1)
    l1, l2, gp = run(local_b_kernel, "local_b", [wide, wide, ((parts, 2 * hid, n), F32)], a, at, sa, gw)
    sb, reset, update, y, pay = run(
        chip_b_kernel, "chip_b", [second, field, field, field16, pay_kind],
        pay, got, *edges, sa, l1, l2, ro, ri, gw, gate_bias[None, :], gp,
    )
    got = swap(pay, 1)
    l1, l2 = run(local_kernel, "local_c1", [field, field], a, at, y, y)
    ma, pay = run(chip_c1_kernel, "chip_c1", [first, pay_kind], pay, got, *edges, y, sa, l1, l2, ro, ri)
    got = swap(pay, 1)
    l1, l2, cp = run(local_c2_kernel, "local_c2", [field, field, field], a, at, ma, cw)
    mb, cand_grad, gate_update, y1, y2, g1, g3, up, direct, pay = run(
        functools.partial(chip_c2_kernel, parts), "chip_c2", [second] + [field16] * 7 + [field, pay_kind],
        *ups, pay, got, *edges, ma, sa, sb, l1, l2, ro, ri, cw, cw_b, cand_bias[None, :], cp, update,
    )
    got = swap(pay, 1)
    l1, l2, part = run(
        local_d_kernel, "local_d1", [field, field, ((hid, width), BF16)], a, at, y1, y2, cand_grad, ma, mb, order
    )
    z1, z2, pay = run(
        chip_d1_kernel, "chip_d1", [field16, field16, pay_kind], pay, got, *edges, l1, l2, g1, g3, ro, ri
    )
    got = swap(pay, 1)
    (base,) = run(local_d2_kernel, "local_d2", [field], a, at, z1, z2, direct)
    gate_grad, y1, y2, g1, g3, direct, pay = run(
        chip_d2_kernel, "chip_d2", [((parts, 2 * hid, n), BF16)] + [field16] * 4 + [field, pay_kind],
        pay, got, *edges, base, ro, ri, sa, gw_b, up, reset, update, gate_update,
    )
    got = swap(pay, 1)
    half = ((3 * hid // 2, width), BF16)
    keep, give = run(
        grads_kernel, "grads", [half, half], gate_grad, sa, sb, order, part, scratch=[pltpu.VMEM((3 * hid, width), F32)]
    )
    l1, l2 = run(local_kernel, "local_e1", [field, field], a, at, y1, y2)
    mine, sent = run(sum_kernel, "sum_core", [half] * 2, keep, swap(give, 1), after=[l1, got])
    every = [mine] + [swap(sent, k, "snap", snaps) for k in range(1, snaps)]
    z1, z2, pay = run(
        chip_d1_kernel, "chip_e1", [field16, field16, pay_kind], pay, got, *edges, l1, l2, g1, g3, ro, ri, after=[mine],
    )
    got = swap(pay, 1)
    (base,) = run(local_e_kernel, "local_e2", [((hid, n), F32)], a, at, z1, z2, direct)
    state_grad, done = run(
        chip_e_kernel, "chip_e2", [((1, hid, n), BF16), ((8, LANES), F32)], pay, got, *edges, base
    )
    mine, sent = run(sum_kernel, "sum_snap", [half] * 2, *every, after=[done])
    factor = 1.0 / math.sqrt(readings.shape[0] * snaps * n * nd)
    feats = orders * chans
    grad_gw, grad_gb, grad_cw, grad_cb = run(
        functools.partial(end_kernel, factor), "end",
        [((feats, 2 * hid), F32), ((1, 2 * hid), F32), ((hid, feats), F32), ((1, hid), F32)],
        mine, swap(sent, 1), scratch=[pltpu.VMEM((3 * hid, width), F32)],
    )
    return state_grad, grad_gw.T, grad_gb[0], grad_cw, grad_cb[0]


def body(*args):
    neighbours, send_rows = args[7], args[9]
    n = neighbours.shape[1]
    nd, snaps = lax.axis_size("dom"), lax.axis_size("snap")
    parts = nd // 2
    slots = 2 * parts * parts * (send_rows.shape[1] // nd)
    powers = nd & (nd - 1) == 0 and snaps & (snaps - 1) == 0 and nd > 2
    if powers and parts * (n + slots) * n * 2 <= 4 << 20:
        return chip_body(*args)
    return spread_body(*args)


def solution(mesh):
    in_specs = (
        P("snap", None, "dom"),
        P("snap", None, "dom"),
        P("snap", None, "dom"),
        P(),
        P(),
        P(),
        P(),
        P(None, "dom"),
        P(None, "dom"),
        P("dom", None),
    )
    out_specs = (P("snap", None, "dom"), P(), P(), P(), P())
    return jax.shard_map(body, mesh=mesh, in_specs=in_specs, out_specs=out_specs, check_vma=False)
```

```python
import functools
import math

import jax
import jax.numpy as jnp
from jax import lax
from jax.experimental import pallas as pl
from jax.experimental.pallas import tpu as pltpu
from jax.sharding import PartitionSpec as P

F32 = jnp.float32
BF16 = jnp.bfloat16
LANES = 128


def nn(a, b):
    return lax.dot_general(a, b, (((1,), (0,)), ((), ())), preferred_element_type=F32)


def nt(a, b):
    return lax.dot_general(a, b, (((1,), (1,)), ((), ())), preferred_element_type=F32)


def tn(a, b):
    return lax.dot_general(a, b, (((0,), (0,)), ((), ())), preferred_element_type=F32)


def iota(shape, axis):
    return lax.broadcasted_iota(jnp.int32, shape, axis)


def column(row):
    k = row.shape[1]
    spread = jnp.broadcast_to(row.astype(F32), (k, k))
    return jnp.sum(jnp.where(iota((k, k), 0) == iota((k, k), 1), spread, 0.0), axis=1, keepdims=True)


def run(kernel, name, outs, *args, scratch=(), flops=20_000_000, vmem=24, after=()):
    return pl.pallas_call(
        lambda *refs: kernel(*refs[len(after) :]),
        name=name,
        out_shape=[jax.ShapeDtypeStruct(shape, kind) for shape, kind in outs],
        in_specs=[pl.BlockSpec(memory_space=pl.ANY)] * len(after) + [pl.BlockSpec(memory_space=pltpu.VMEM)] * len(args),
        out_specs=[pl.BlockSpec(memory_space=pltpu.VMEM)] * len(outs),
        scratch_shapes=list(scratch),
        compiler_params=pltpu.CompilerParams(vmem_limit_bytes=vmem * 1024 * 1024),
        cost_estimate=pl.CostEstimate(flops=flops, bytes_accessed=2_000_000, transcendentals=0),
    )(*after, *args)


def prep_kernel(cap, nb, w, rows, readings, previous, e, s, b, pay):
    degree, n = nb.shape
    nh = s.shape[0]
    hid = previous.shape[1]
    fin = readings.shape[1]
    step = 32
    for at in range(0, n + nh, step):
        node = iota((step, n), 0) + at
        total = jnp.zeros((step, n), F32)
        for d in range(degree):
            total = total + jnp.where(node == nb[d : d + 1, :], w[d : d + 1, :], 0.0)
        e[at : at + step, :] = total.astype(BF16)
    sent = column(rows[...]).astype(jnp.int32)
    s[...] = jnp.where(iota((nh, n), 1) == sent, 1.0, 0.0).astype(BF16)
    b[:hid, :] = previous[0]
    rest = b.shape[0] - hid
    row = iota((rest, n), 0)
    tail = jnp.where(row == fin, 1.0, 0.0)
    for f in range(fin):
        tail = jnp.where(row == f, readings[0, f : f + 1, :].astype(F32), tail)
    b[hid:, :] = tail.astype(BF16)
    base = b[...]
    chans = base.shape[0]
    bound = nt(s[...], base)
    halo = nt(e[n:, :], base)
    for p in range(nh // cap):
        pay[p, :, :chans] = bound[p * cap : (p + 1) * cap, :]
        pay[p, :, LANES : LANES + chans] = halo[p * cap : (p + 1) * cap, :]


def order_matrix(shape, chans, hid, fin, block):
    k = iota(shape, 0)
    col = iota(shape, 1)
    m = lax.div(col, jnp.int32(block))
    c = col - m * block
    source = jnp.where(c < hid, m * chans + fin + c, jnp.where(c < hid + fin, m * chans + c - hid, -1))
    return jnp.where(k == source, 1.0, 0.0).astype(BF16)


def mid_a_kernel(hid, fin, orders, e, b, gw, cw, fa, ra, gw_o, cw_o):
    n = e.shape[1]
    a = e[:n, :]
    base = b[...]
    fa[...] = nt(base, a)
    ra[...] = nn(base, a)
    block = base.shape[0]
    order = order_matrix((gw.shape[1], orders * block), hid + fin, hid, fin, block)
    gw_o[...] = nn(gw[...], order).astype(BF16)
    cw_o[...] = nn(cw[...], order).astype(BF16)


def post_a_kernel(one, cap, recv, e, s, fa, ra, f1, r1, ro, ri, pay, flat):
    n = e.shape[1]
    nh = s.shape[0]
    chans = fa.shape[0]
    for p in range(nh // cap):
        flat[p * cap : (p + 1) * cap, :] = recv[p]
    h = e[n:, :]
    sel = s[...]
    seen = flat[:, :chans].astype(BF16)
    back = flat[:, LANES : LANES + chans]
    back_degree = flat[:, LANES + one : LANES + one + 1]
    out_degree = fa[one : one + 1, :] + jnp.sum(sel.astype(F32) * back_degree, axis=0, keepdims=True)
    pulled = ra[...] + tn(seen, h)
    inv_o = 1.0 / out_degree
    inv_i = 1.0 / pulled[one : one + 1, :]
    ro[...] = inv_o
    ri[...] = inv_i
    first_out = ((fa[...] + tn(back.astype(BF16), sel)) * inv_o).astype(BF16)
    first_in = (pulled * inv_i).astype(BF16)
    f1[...] = first_out
    r1[...] = first_in
    bound = nt(sel, first_in)
    halo = nt(h, first_out)
    hi, ho = scaled(h, inv_i), scaled(h, inv_o)
    si, so = scaled(sel, inv_i), scaled(sel, inv_o)
    coefs = (nt(sel, hi), nt(h, so), nt(sel, ho), nt(h, si))
    for p in range(nh // cap):
        at = slice(p * cap, (p + 1) * cap)
        pay[p, :, :chans] = bound[at, :]
        pay[p, :, LANES : LANES + chans] = halo[at, :]
        for k, coef in enumerate(coefs):
            pay[p, :, 2 * LANES + k * nh : 2 * LANES + (k + 1) * nh] = coef[at, :]


def scaled(rows, factor):
    return (rows.astype(F32) * factor).astype(BF16)


def mid_b_kernel(e, s, f1, r1, ro, ri, f2l, r2l, kc, ke, ka):
    n = e.shape[1]
    a = e[:n, :]
    h = e[n:, :]
    sel = s[...]
    nh = sel.shape[0]
    chans = f1.shape[0]
    inv_o, inv_i = ro[...], ri[...]
    outs = nt(jnp.concatenate([f1[...], scaled(sel, inv_o), scaled(sel, inv_i)], axis=0), a)
    ins = nn(jnp.concatenate([r1[...], scaled(h, inv_i), scaled(h, inv_o)], axis=0), a)
    f2l[...] = outs[:chans]
    r2l[...] = ins[:chans]
    kc[:nh, :] = ins[chans : chans + nh].astype(BF16)
    kc[nh:, :] = h
    ke[:nh, :] = outs[chans : chans + nh].astype(BF16)
    ke[nh:, :] = sel
    ka[:nh, :] = (2.0 * ins[chans + nh :]).astype(BF16)
    ka[nh : 2 * nh, :] = h
    ka[2 * nh : 3 * nh, :] = (2.0 * outs[chans + nh :]).astype(BF16)
    ka[3 * nh :, :] = sel


def send(pay, cap, left, right, left_two, right_two):
    nh = left.shape[0]
    rows = jnp.concatenate([left, right], axis=1)
    rows_two = jnp.concatenate([left_two, right_two], axis=1)
    both = jnp.concatenate([rows, rows_two], axis=0).astype(BF16)
    k = iota((2 * nh, 2 * nh), 0)
    part = lax.div(k, jnp.int32(2 * cap))
    spot = k - part * (2 * cap)
    source = jnp.where(spot < cap, part * cap + spot, nh + part * cap + spot - cap)
    mine = nn(jnp.where(iota((2 * nh, 2 * nh), 1) == source, 1.0, 0.0).astype(BF16), both)
    for p in range(nh // cap):
        own = mine[p * 2 * cap : (p + 1) * 2 * cap, :]
        pay[p] = jnp.concatenate([rows, own], axis=0).astype(BF16)


def post_b_kernel(cap, one, recv, e, s, b, f1, r1, f2l, r2l, ro, ri, gw, gb, states, reset, update, y, f1l, r1l, pay, flat):
    n = e.shape[1]
    nh = s.shape[0]
    hid = y.shape[0]
    chans = b.shape[0]
    for p in range(nh // cap):
        flat[p * cap : (p + 1) * cap, :] = recv[p, :, : 2 * LANES]
    a = e[:n, :]
    h = e[n:, :]
    sel = s[...]
    inv_o, inv_i = ro[...], ri[...]
    base = b[...].astype(F32)
    seen = flat[:, :chans].astype(BF16)
    back = flat[:, LANES : LANES + chans].astype(BF16)
    f2 = 2.0 * (f2l[...] + tn(back, sel)) * inv_o - base
    r2 = 2.0 * (r2l[...] + tn(seen, h)) * inv_i - base
    states[:chans, :] = b[...]
    states[chans : 2 * chans, :] = f1[...]
    states[2 * chans : 3 * chans, :] = f2.astype(BF16)
    states[3 * chans : 4 * chans, :] = r1[...]
    states[4 * chans :, :] = r2.astype(BF16)
    gates = jax.nn.sigmoid(nn(gw[...], states[...]) + column(gb[...]))
    reset[...] = gates[:hid]
    update[...] = gates[hid:]
    now = (gates[:hid] * base[:hid]).astype(BF16)
    y[...] = now
    local_out = nt(now, a) * inv_o
    local_in = nn(now, a) * inv_i
    f1l[...] = local_out
    r1l[...] = local_in
    bound = nt(sel, jnp.concatenate([now, local_in.astype(BF16)], axis=0))
    halo = nt(h, jnp.concatenate([now, local_out.astype(BF16)], axis=0))
    send(pay, cap, bound[:, :hid], halo[:, :hid], bound[:, hid:], halo[:, hid:])


def gather_matrix(coef, out, nd, cap, per, first, factor):
    nh = nd * cap
    width = nd * per
    k = iota((nh, width), 0)
    col = iota((nh, width), 1)
    r = lax.div(col, jnp.int32(per))
    u = col - r * per
    p = lax.div(u, jnp.int32(cap))
    spot = u - p * cap
    here = lax.div(k, jnp.int32(cap))
    slot = k - here * cap
    inside = u < nh
    place = jnp.where((k == r * cap + spot) & inside, 1.0, 0.0).astype(BF16)
    keep = (here == p) & inside
    for i in range(2):
        wide = nn(coef[:, (first + i) * nh : (first + i + 1) * nh].astype(BF16), place)
        own = (r == here) & (u == nh + cap + slot)
        out[(i + 1) * nh : (i + 2) * nh, :] = jnp.where(keep, factor * wide, jnp.where(own, 1.0, 0.0)).astype(BF16)
    out[:nh, :] = jnp.where((r == here) & (u == nh + slot), 1.0, 0.0).astype(BF16)


def mid_c_kernel(nd, cap, per, fused, recv, e, f1l, r1l, f2l, r2l, *rest):
    n = e.shape[1]
    a = e[:n, :]
    f2l[...] = nt(f1l[...].astype(BF16), a)
    r2l[...] = nn(r1l[...].astype(BF16), a)
    if fused:
        gd, ga, flat = rest
        for p in range(nd):
            flat[p * cap : (p + 1) * cap, :] = recv[p, :, 2 * LANES :]
        gather_matrix(flat, gd, nd, cap, per, 0, 1.0)
        gather_matrix(flat, ga, nd, cap, per, 2, 2.0)


def arrived(fused, hid, nh, g, recv):
    if fused:
        halo = nn(g[...], recv[...].reshape(recv.shape[0] * recv.shape[1], recv.shape[2]))
        two = halo[nh : 2 * nh, :hid], halo[2 * nh :, hid:]
    else:
        halo = recv[...]
        two = halo[nh:, :hid], halo[nh:, hid:]
    one = halo[:nh]
    return one[:, :hid], one[:, hid:], two[0], two[1]


def back_and_send(cap, hid, g, a, h, sel, inv_o, inv_i, z1, z2, pay):
    g0, g1, g2, g3, g4 = (g[m * hid : (m + 1) * hid, :].astype(BF16).astype(F32) for m in range(5))
    y1 = (g2 * inv_o).astype(BF16)
    y2 = (g4 * inv_i).astype(BF16)
    now1 = ((g1 + 2.0 * nn(y1, a)) * inv_o).astype(BF16)
    now2 = ((g3 + 2.0 * nt(y2, a)) * inv_i).astype(BF16)
    z1[...] = now1
    z2[...] = now2
    bound = nt(sel, jnp.concatenate([y1, now1], axis=0))
    halo = nt(h, jnp.concatenate([y2, now2], axis=0))
    send(pay, cap, bound[:, :hid], halo[:, :hid], bound[:, hid:], halo[:, hid:])
    return g0 - g2 - g4


def hidden_weights(w, hid, block, orders):
    return jnp.concatenate([w[:, m * block : m * block + hid] for m in range(orders)], axis=1)


def post_c_kernel(fused, cap, orders, g, recv, e, s, kc, ke, y, f1l, r1l, f2l, r2l, ro, ri, states, cw, cb, upstream, update,
                  mixed, cand_grad, gate_update, z1, z2, direct, pay):
    n = e.shape[1]
    nh = s.shape[0]
    hid = y.shape[0]
    block = states.shape[0] // orders
    a = e[:n, :]
    h = e[n:, :]
    sel = s[...]
    inv_o, inv_i = ro[...], ri[...]
    c1, e1, c2, e2 = arrived(fused, hid, nh, g, recv)
    base = y[...].astype(F32)
    c1, e1 = c1.astype(BF16), e1.astype(BF16)
    cc = jnp.concatenate([c1, c2.astype(BF16)], axis=0)
    ee = jnp.concatenate([e1, e2.astype(BF16)], axis=0)
    f1 = f1l[...] + tn(e1, sel) * inv_o
    f2 = 2.0 * (f2l[...] + tn(ee, ke[...])) * inv_o - base
    r1 = r1l[...] + tn(c1, h) * inv_i
    r2 = 2.0 * (r2l[...] + tn(cc, kc[...])) * inv_i - base
    for m, value in enumerate((y[...], f1, f2, r1, r2)):
        mixed[m * block : m * block + hid, :] = value.astype(BF16)
        mixed[m * block + hid : (m + 1) * block, :] = states[m * block + hid : (m + 1) * block, :]
    weights = cw[...]
    cand = jnp.tanh(nn(weights, mixed[...]) + column(cb[...]))
    up = upstream[0].astype(F32)
    gate = update[...]
    grad = (up * (1.0 - gate) * (1.0 - cand * cand)).astype(BF16)
    cand_grad[...] = grad
    held = states[:hid, :].astype(F32)
    gate_update[...] = (up * (held - cand) * gate * (1.0 - gate)).astype(BF16)
    back = tn(hidden_weights(weights, hid, block, orders), grad)
    direct[...] = back_and_send(cap, hid, back, a, h, sel, inv_o, inv_i, z1, z2, pay)


def weight_part(grad, features, orders, chans, hid, fin):
    block = features.shape[0] // orders
    width = -(-(orders * chans + 1) // LANES) * LANES
    shape = (width, orders * block)
    k = iota(shape, 0)
    col = iota(shape, 1)
    m = lax.div(col, jnp.int32(block))
    c = col - m * block
    source = jnp.where(c < hid, m * chans + fin + c, jnp.where(c < hid + fin, m * chans + c - hid, -1))
    source = jnp.where(col == hid + fin, orders * chans, source)
    order = jnp.where(k == source, 1.0, 0.0).astype(BF16)
    return nt(nt(grad, features).astype(BF16), order)


def mid_d_kernel(orders, fin, e, z1, z2, direct, cand_grad, mixed, gate_update, states, base, part):
    n = e.shape[1]
    a = e[:n, :]
    hid = z1.shape[0]
    base[...] = direct[...] + nn(z1[...], a) + nt(z2[...], a)
    part[:hid, :] = weight_part(gate_update[...], states[...], orders, hid + fin, hid, fin).astype(BF16)
    part[hid:, :] = weight_part(cand_grad[...], mixed[...], orders, hid + fin, hid, fin).astype(BF16)


def add_halo(fused, g, recv, ka, base):
    hid = base.shape[0]
    nh = ka.shape[0] // 4
    c1, e1, c2, e2 = arrived(fused, hid, nh, g, recv)
    return base[...] + tn(jnp.concatenate([c1, c2, e1, e2], axis=0).astype(BF16), ka[...])


def post_d_kernel(fused, cap, orders, g, recv, e, s, ka, base, ro, ri, states, gw, upstream, reset, update, gate_update,
                  gate_reset, z1, z2, direct, pay):
    n = e.shape[1]
    hid = base.shape[0]
    block = states.shape[0] // orders
    scaled_grad = add_halo(fused, g, recv, ka, base)
    held = states[:hid, :].astype(F32)
    gate = reset[...]
    grad = (scaled_grad * held * gate * (1.0 - gate)).astype(BF16)
    gate_reset[...] = grad
    weights = hidden_weights(gw[...], hid, block, orders)
    back = tn(weights, jnp.concatenate([grad, gate_update[...]], axis=0))
    rest = back_and_send(cap, hid, back, e[:n, :], e[n:, :], s[...], ro[...], ri[...], z1, z2, pay)
    direct[...] = rest + upstream[0].astype(F32) * update[...] + scaled_grad * gate


def mid_e_kernel(orders, fin, rows, e, z1, z2, direct, gate_reset, states, part, base, grads):
    n = e.shape[1]
    a = e[:n, :]
    hid = z1.shape[0]
    base[...] = direct[...] + nn(z1[...], a) + nt(z2[...], a)
    first = weight_part(gate_reset[...], states[...], orders, hid + fin, hid, fin)
    both = jnp.concatenate([first, part[...].astype(F32)], axis=0)
    for k in range(grads.shape[0]):
        if k * rows < both.shape[0]:
            grads[k] = both[k * rows : (k + 1) * rows, :].astype(BF16)
        else:
            grads[k] = jnp.zeros(grads.shape[1:], BF16)


def post_e_kernel(fused, g, recv, ka, base, out):
    out[0] = add_halo(fused, g, recv, ka, base).astype(BF16)


def add_kernel(recv, out):
    total = recv[0].astype(F32)
    for k in range(1, recv.shape[0]):
        total = total + recv[k].astype(F32)
    for k in range(out.shape[0]):
        out[k] = total.astype(BF16)


def finish_kernel(hid, factor, recv, gw, gb, cw, cb):
    rows = recv.shape[1]
    features = gw.shape[1]
    total = gw.shape[0] + cw.shape[0]
    for k in range(total // rows):
        part = recv[k].astype(F32)[:, :features] * factor
        at = k * rows
        if at < 2 * hid:
            gw[at : at + rows, :] = part
        else:
            cw[at - 2 * hid : at - 2 * hid + rows, :] = part
    flat = jnp.concatenate([recv[k].astype(F32) for k in range(total // rows)], axis=0)
    pick = jnp.where(iota((8, flat.shape[1]), 1) == features, 1.0, 0.0).astype(BF16)
    bias = nt(pick, flat.astype(BF16))[:1] * factor
    gb[...] = bias[:, : 2 * hid]
    cb[...] = bias[:, 2 * hid :]


def spread_body(
    readings,
    previous,
    upstream,
    gate_weight,
    gate_bias,
    cand_weight,
    cand_bias,
    neighbours,
    edge_weight,
    send_rows,
):
    fin, hid = readings.shape[1], previous.shape[1]
    chans = fin + hid
    orders = gate_weight.shape[1] // chans
    n = readings.shape[2]
    nd = lax.axis_size("dom")
    devices = nd * lax.axis_size("snap")
    nh = send_rows.shape[1]
    cap = nh // nd
    block = hid + 16 * (-(-(fin + 1) // 16))
    one = hid + fin
    per = nh + 2 * cap
    fused = 3 * nh * nd * per <= 1 << 18
    move = functools.partial(lax.all_to_all, axis_name="dom", split_axis=0, concat_axis=0, tiled=True)

    e, s, b, pay = run(
        functools.partial(prep_kernel, cap), "prep",
        [((n + nh, n), BF16), ((nh, n), BF16), ((block, n), BF16), ((nd, cap, 2 * LANES), F32)],
        neighbours, edge_weight, send_rows, readings, previous,
    )
    recv = move(pay)
    fa, ra, gw, cw = run(
        functools.partial(mid_a_kernel, hid, fin, orders), "mid_a",
        [((block, n), F32), ((block, n), F32), ((2 * hid, orders * block), BF16), ((hid, orders * block), BF16)],
        e, b, gate_weight, cand_weight,
    )
    wide = 2 * LANES + 4 * nh
    f1, r1, ro, ri, pay = run(
        functools.partial(post_a_kernel, one, cap), "post_a",
        [((block, n), BF16), ((block, n), BF16), ((1, n), F32), ((1, n), F32), ((nd, cap, wide), F32)],
        recv, e, s, fa, ra, scratch=[pltpu.VMEM((nh, 2 * LANES), F32)],
    )
    recv_b = move(pay)
    f2l, r2l, kc, ke, ka = run(
        mid_b_kernel, "mid_b",
        [((block, n), F32), ((block, n), F32), ((2 * nh, n), BF16), ((2 * nh, n), BF16), ((4 * nh, n), BF16)],
        e, s, f1, r1, ro, ri,
    )
    pay_kind = ((nd, per, 2 * hid), BF16)
    field, field16 = ((hid, n), F32), ((hid, n), BF16)
    states, reset, update, y, f1l, r1l, pay = run(
        functools.partial(post_b_kernel, cap, one), "post_b",
        [((orders * block, n), BF16), field, field, field16, field, field, pay_kind],
        recv_b, e, s, b, f1, r1, f2l, r2l, ro, ri, gw, gate_bias[None, :],
        scratch=[pltpu.VMEM((nh, 2 * LANES), F32)],
    )
    recv = move(pay)
    table = ((3 * nh, nd * per), BF16)
    f2l, r2l, *tables = run(
        functools.partial(mid_c_kernel, nd, cap, per, fused), "mid_c",
        [field, field] + [table] * (2 if fused else 0),
        recv_b, e, f1l, r1l, scratch=[pltpu.VMEM((nh, 4 * nh), F32)] if fused else [],
    )
    if fused:
        inward, outward = tables
        halo_of = lambda got, first, factor: got
    else:
        inward = outward = jnp.zeros((8, LANES), BF16)
        coefs = recv_b[:, :, 2 * LANES :].reshape(nd, cap, 4, nd, cap)

        def halo_of(got, first, factor):
            rows = got[:, :nh].reshape(nd, nd, cap, 2, hid).astype(F32)
            two = jnp.einsum("psgrt,rptgk->psgk", coefs[:, :, first : first + 2], rows)
            two = factor * two.reshape(nh, 2 * hid) + got[:, nh + cap :].reshape(nh, 2 * hid).astype(F32)
            return jnp.concatenate([got[:, nh : nh + cap].reshape(nh, 2 * hid).astype(F32), two], axis=0)

    mixed, cand_grad, gate_update, z1, z2, direct, pay = run(
        functools.partial(post_c_kernel, fused, cap, orders), "post_c",
        [((orders * block, n), BF16), field16, field16, field16, field16, field, pay_kind],
        inward, halo_of(recv, 0, 1.0), e, s, kc, ke, y, f1l, r1l, f2l, r2l, ro, ri, states, cw, cand_bias[None, :], upstream, update,
    )
    recv = move(pay)
    width = -(-(orders * chans + 1) // LANES) * LANES
    base, part = run(
        functools.partial(mid_d_kernel, orders, fin), "mid_d", [field, ((2 * hid, width), BF16)],
        e, z1, z2, direct, cand_grad, mixed, gate_update, states,
    )
    gate_reset, z1, z2, direct, pay = run(
        functools.partial(post_d_kernel, fused, cap, orders), "post_d",
        [field16, field16, field16, field, pay_kind],
        outward, halo_of(recv, 2, 2.0), e, s, ka, base, ro, ri, states, gw, upstream, reset, update, gate_update,
    )
    recv = move(pay)
    rows = 8 * (-(-3 * hid // (8 * devices)))
    base, grads = run(
        functools.partial(mid_e_kernel, orders, fin, rows), "mid_e", [field, ((devices, rows, width), BF16)],
        e, z1, z2, direct, gate_reset, states, part,
    )
    (state_grad,) = run(
        functools.partial(post_e_kernel, fused), "post_e", [((1, hid, n), BF16)],
        outward, halo_of(recv, 2, 2.0), ka, base,
    )
    both = ("snap", "dom")
    grads = lax.all_to_all(grads, both, 0, 0, tiled=True)
    (grads,) = run(add_kernel, "add", [((devices, rows, width), BF16)], grads)
    grads = lax.all_to_all(grads, both, 0, 0, tiled=True)
    factor = 1.0 / math.sqrt(readings.shape[0] * lax.axis_size("snap") * n * nd)
    feats = orders * chans
    grad_gw, grad_gb, grad_cw, grad_cb = run(
        functools.partial(finish_kernel, hid, factor), "finish",
        [((2 * hid, feats), F32), ((1, 2 * hid), F32), ((hid, feats), F32), ((1, hid), F32)],
        grads,
    )
    return state_grad, grad_gw, grad_gb[0], grad_cw, grad_cb[0]


def pack_kernel(nb, w, rows, readings, previous, upstream, own, both, tail):
    degree = nb.shape[0]
    nh = rows.shape[1]
    hid = previous.shape[1]
    fin = readings.shape[1]
    block = own.shape[0]
    tail[...] = jnp.zeros_like(tail)
    tail[:fin, :] = readings[0].astype(F32)
    high = lax.shift_right_logical(nb[...], 5)
    tail[fin : fin + degree, :] = high.astype(F32)
    tail[fin + degree : fin + 2 * degree, :] = (nb[...] - high * 32).astype(F32)
    tail[fin + 2 * degree : fin + 3 * degree, :] = w[...]
    at = fin + 3 * degree
    high = lax.shift_right_logical(rows[...], 5)
    tail[at : at + 1, :nh] = high.astype(F32)
    tail[at + 1 : at + 2, :nh] = (rows[...] - high * 32).astype(F32)
    for to in (own, both):
        to[:hid, :] = previous[0]
        to[hid:block, :] = tail[...].astype(BF16)
    both[block:, :] = upstream[0]


def exchange(first, second, hc, sc, pay):
    count = first[0].shape[0]
    parts = len(first)
    pay[:count, :] = jnp.concatenate([nt(first[p], sc[p]).astype(BF16) for p in range(parts)], axis=1)
    pay[count:, :] = jnp.concatenate([nt(second[p], hc[p]).astype(BF16) for p in range(parts)], axis=1)


def merged(parts, mine, got):
    step = mine.shape[1] // (2 * parts)
    here = lax.rem(lax.div(iota(mine.shape, 1), jnp.int32(step)), jnp.int32(2)) == 0
    value = jnp.where(here, mine[...].astype(F32), got[...].astype(F32)).astype(BF16)
    count = mine.shape[0] // 2
    return value[:count, :], value[count:, :]


def build_part(cap, hid, fin, degree, parts, p, block, a, at, hc, hx, sc, sx, b):
    n = a.shape[1]
    slots = sx.shape[0]
    nh = 2 * parts * cap
    half = parts * cap
    core = lax.rem(lax.axis_index("dom"), 2)
    line = iota((nh, 1), 0)
    rel = lax.div(line, jnp.int32(half))
    k = lax.div(line - rel * half, jnp.int32(cap))
    t = line - rel * half - k * cap
    spot = (k * 2 + lax.bitwise_xor(rel, core)) * cap + t
    node = (n + spot).astype(F32)
    width = -(-nh // LANES) * LANES
    slot = iota((slots, nh), 0)
    outer = lax.div(slot, jnp.int32(nh))
    rest = slot - outer * nh
    slot_rel = lax.div(rest, jnp.int32(half))
    rest = rest - slot_rel * half
    inner = lax.div(rest, jnp.int32(cap))
    filled = iota((slots, nh), 1) == slot_rel * half + outer * cap + rest - inner * cap
    row = iota((32, n), 0).astype(F32)
    edges = hid + fin + 3 * degree + 2
    tail = block[hid : hid + 16 * (-(-(edges - hid) // 16)), :].astype(F32)
    high, low = tail[fin : fin + degree], tail[fin + degree : fin + 2 * degree]
    w = tail[fin + 2 * degree : fin + 3 * degree]
    start = fin + 3 * degree
    sent = tail[start : start + 1] * 32.0 + tail[start + 1 : start + 2]
    low_is = [jnp.where(low[d : d + 1] == row, 1.0, 0.0).astype(BF16) for d in range(degree)]
    for chunk in range(n // 32):
        total = None
        for d in range(degree):
            term = low_is[d] * jnp.where(high[d : d + 1] == float(chunk), w[d : d + 1], 0.0).astype(BF16)
            total = term if total is None else total + term
        a[chunk * 32 : (chunk + 1) * 32, :] = total
    at[...] = a[...].T
    names = high * 32.0 + low
    total = jnp.zeros((nh, n), F32)
    for d in range(degree):
        total = total + jnp.where(names[d : d + 1] == node, w[d : d + 1], 0.0)
    halo = total.astype(BF16)
    hc[...] = halo
    named = jnp.where(iota((nh, width), 1) == spot, sent[:, :width], 0.0)
    target = jnp.sum(named, axis=1, keepdims=True).astype(jnp.int32)
    picked = jnp.where(iota((nh, n), 1) == target, 1.0, 0.0).astype(BF16)
    sc[...] = picked
    place = jnp.where(filled & (inner == p), 1.0, 0.0).astype(BF16)
    hx[...] = nn(place, halo).astype(BF16)
    sx[...] = nn(place, picked).astype(BF16)
    b[:hid, :] = block[:hid, :]
    line = iota(tail.shape, 0)
    b[hid:, :] = jnp.where(line < fin, tail, jnp.where(line == fin, 1.0, 0.0)).astype(BF16)


def build_early_kernel(cap, hid, fin, degree, parts, *refs):
    count = parts - 1
    z = lax.shift_right_logical(lax.axis_index("dom"), 1)
    for k in range(count):
        p = lax.bitwise_xor(z, jnp.int32(k))
        build_part(cap, hid, fin, degree, parts, p, refs[k], *(ref.at[k] for ref in refs[count:]))


def build_late_kernel(cap, hid, fin, degree, parts, last, *refs):
    early, outs, pay = refs[:5], refs[5:12], refs[12]
    z = lax.shift_right_logical(lax.axis_index("dom"), 1)
    for k in range(parts - 1):
        p = lax.bitwise_xor(z, jnp.int32(k))
        for source, to in zip(early, outs[2:]):
            to[p] = source[k]
    p = lax.bitwise_xor(z, jnp.int32(parts - 1))
    build_part(cap, hid, fin, degree, parts, p, last, outs[0].at[0], outs[1].at[0], *(ref.at[p] for ref in outs[2:]))
    hc, sc, b = outs[2], outs[4], outs[6]
    base = [b[p] for p in range(parts)]
    exchange(base, base, hc, sc, pay)


def chip_source(col, chans, hid, fin, block):
    m = lax.div(col, jnp.int32(block))
    c = col - m * block
    m = jnp.where(m == 2, 3, jnp.where(m == 3, 2, m))
    return m, c, jnp.where(c < hid, m * chans + fin + c, jnp.where(c < hid + fin, m * chans + c - hid, -1))


def order_kernel(hid, fin, orders, block, gw, cw, gw_o, cw_o, gw_b, cw_b, order):
    chans = hid + fin
    feats = cw.shape[1]
    shape = (feats, orders * block)
    source = chip_source(iota(shape, 1), chans, hid, fin, block)[2]
    pick = jnp.where(iota(shape, 0) == source, 1.0, 0.0).astype(BF16)
    gw_o[...] = tn(gw[...], pick).astype(BF16)
    cw_o[...] = nn(cw[...], pick).astype(BF16)
    shape = (orders * hid, feats)
    line = iota(shape, 0)
    m = lax.div(line, jnp.int32(hid))
    pick = jnp.where(iota(shape, 1) == m * chans + fin + line - m * hid, 1.0, 0.0).astype(BF16)
    gw_b[...] = nn(pick, gw[...]).astype(BF16)
    cw_b[...] = nt(pick, cw[...]).astype(BF16)
    m, c, source = chip_source(iota(order.shape, 0), chans, hid, fin, block)
    source = jnp.where((m == 0) & (c == hid + fin), feats, source)
    order[...] = jnp.where(iota(order.shape, 1) == source, 1.0, 0.0).astype(BF16)


def here(early, late, k):
    z = lax.shift_right_logical(lax.axis_index("dom"), 1)
    count = early.shape[0]
    return lax.bitwise_xor(z, jnp.int32(k)), early[k] if k < count else late[k - count]


def local_kernel(a0, at0, a1, at1, x1, x2, l1, l2):
    for k in range(x1.shape[0]):
        p, a = here(a0, a1, k)
        l1[p] = nn(x1[p], a)
    for k in range(x1.shape[0]):
        p, at = here(at0, at1, k)
        l2[p] = nn(x2[p], at)


def arrive(sx, hx, mine, got, l1, l2):
    parts = range(sx.shape[0])
    top, low = merged(sx.shape[0], mine, got)
    pulled = [l1[p] + nn(top, hx[p]) for p in parts]
    pushed = [l2[p] + nn(low, sx[p]) for p in parts]
    return parts, pulled, pushed


def chip_a_kernel(one, mine, got, hc, hx, sc, sx, b, l1, l2, sa, ro, ri, pay):
    chans = b.shape[1]
    parts, pulled, pushed = arrive(sx, hx, mine, got, l1, l2)
    inv_o = [1.0 / pushed[p][one : one + 1, :] for p in parts]
    inv_i = [1.0 / pulled[p][one : one + 1, :] for p in parts]
    outs = [(pushed[p] * inv_o[p]).astype(BF16) for p in parts]
    ins = [(pulled[p] * inv_i[p]).astype(BF16) for p in parts]
    for p in parts:
        ro[p] = inv_o[p]
        ri[p] = inv_i[p]
        sa[p, :chans, :] = b[p]
        sa[p, chans : 2 * chans, :] = outs[p]
        sa[p, 2 * chans :, :] = ins[p]
    exchange(ins, outs, hc, sc, pay)


def local_b_kernel(a0, at0, a1, at1, sa, gw, l1, l2, gp):
    chans = l1.shape[1]
    weights = gw[:, : 3 * chans]
    for k in range(sa.shape[0]):
        p, a = here(a0, a1, k)
        l1[p] = nn(sa[p, 2 * chans :, :], a)
    for k in range(sa.shape[0]):
        p, at = here(at0, at1, k)
        l2[p] = nn(sa[p, chans : 2 * chans, :], at)
    for p in range(sa.shape[0]):
        gp[p] = nn(weights, sa[p])


def chip_b_kernel(mine, got, hc, hx, sc, sx, sa, l1, l2, ro, ri, gw, gb, gp, sb, reset, update, y, pay):
    hid = y.shape[1]
    chans = l1.shape[1]
    bias = column(gb[...])
    weights = gw[:, 3 * chans :]
    parts, pulled, pushed = arrive(sx, hx, mine, got, l1, l2)
    base = [sa[p, :chans, :].astype(F32) for p in parts]
    r2 = [(pulled[p] * (2.0 * ri[p]) - base[p]).astype(BF16) for p in parts]
    f2 = [(pushed[p] * (2.0 * ro[p]) - base[p]).astype(BF16) for p in parts]
    second = [jnp.concatenate([f2[p], r2[p]], axis=0) for p in parts]
    gates = [jax.nn.sigmoid(gp[p] + nn(weights, second[p]) + bias) for p in parts]
    now = [(gates[p][:hid] * base[p][:hid]).astype(BF16) for p in parts]
    for p in parts:
        sb[p] = second[p]
        reset[p] = gates[p][:hid]
        update[p] = gates[p][hid:]
        y[p] = now[p]
    exchange(now, now, hc, sc, pay)


def chip_c1_kernel(mine, got, hc, hx, sc, sx, y, sa, l1, l2, ro, ri, ma, pay):
    hid = y.shape[1]
    chans = ma.shape[1] // 3
    parts, pulled, pushed = arrive(sx, hx, mine, got, l1, l2)
    ins = [(pulled[p] * ri[p]).astype(BF16) for p in parts]
    outs = [(pushed[p] * ro[p]).astype(BF16) for p in parts]
    exchange(ins, outs, hc, sc, pay)
    for p in parts:
        for m, value in enumerate((y[p], outs[p], ins[p])):
            ma[p, m * chans : m * chans + hid, :] = value
            ma[p, m * chans + hid : (m + 1) * chans, :] = sa[p, m * chans + hid : (m + 1) * chans, :]


def local_c2_kernel(a0, at0, a1, at1, ma, cw, l1, l2, cp):
    hid = l1.shape[1]
    chans = ma.shape[1] // 3
    weights = cw[:, : 3 * chans]
    for k in range(ma.shape[0]):
        p, a = here(a0, a1, k)
        l1[p] = nn(ma[p, 2 * chans : 2 * chans + hid, :], a)
    for k in range(ma.shape[0]):
        p, at = here(at0, at1, k)
        l2[p] = nn(ma[p, chans : chans + hid, :], at)
    for p in range(ma.shape[0]):
        cp[p] = nn(weights, ma[p])


def split_back(back, hid, ro, ri, y1, y2, g1, g3, direct):
    parts = range(len(back))
    blocks = [[back[p][m * hid : (m + 1) * hid, :] for m in range(5)] for p in parts]
    one = [(blocks[p][2] * (2.0 * ro[p])).astype(BF16) for p in parts]
    two = [(blocks[p][4] * (2.0 * ri[p])).astype(BF16) for p in parts]
    for p in parts:
        y1[p] = one[p]
        y2[p] = two[p]
        g1[p] = blocks[p][1].astype(BF16)
        g3[p] = blocks[p][3].astype(BF16)
        direct[p] = blocks[p][0] - blocks[p][2] - blocks[p][4]
    return one, two


def chip_c2_kernel(parts, *refs):
    ups, refs = refs[:parts], refs[parts:]
    mine, got, hc, hx, sc, sx, ma, sa, sb, l1, l2, ro, ri, cw, cw_b, cb, cp, update = refs[:18]
    mb, cand_grad, gate_update, y1, y2, g1, g3, upstream, direct, pay = refs[18:]
    hid = l1.shape[1]
    chans = ma.shape[1] // 3
    z = lax.shift_right_logical(lax.axis_index("dom"), 1)
    for k in range(parts):
        upstream[lax.bitwise_xor(z, jnp.int32(k))] = ups[k][0] if len(ups[k].shape) == 3 else ups[k][ups[k].shape[0] - hid :, :]
    bias = column(cb[...])
    weights = cw[:, 3 * chans :]
    parts, pulled, pushed = arrive(sx, hx, mine, got, l1, l2)
    base = [ma[p, :hid, :].astype(F32) for p in parts]
    r2 = [(pulled[p] * (2.0 * ri[p]) - base[p]).astype(BF16) for p in parts]
    f2 = [(pushed[p] * (2.0 * ro[p]) - base[p]).astype(BF16) for p in parts]
    second = [
        jnp.concatenate([f2[p], sb[p, hid:chans, :], r2[p], sb[p, chans + hid :, :]], axis=0) for p in parts
    ]
    cand = [jnp.tanh(cp[p] + nn(weights, second[p]) + bias) for p in parts]
    rest = [upstream[p].astype(F32) * (1.0 - update[p]) for p in parts]
    grad = [(rest[p] - rest[p] * cand[p] * cand[p]).astype(BF16) for p in parts]
    back = [nn(cw_b[...], grad[p]) for p in parts]
    for p in parts:
        mb[p] = second[p]
        cand_grad[p] = grad[p]
        gate_update[p] = ((sa[p, :hid, :].astype(F32) - cand[p]) * (rest[p] * update[p])).astype(BF16)
    one, two = split_back(back, hid, ro, ri, y1, y2, g1, g3, direct)
    exchange(one, two, hc, sc, pay)


def chip_part(grads, first, second, order):
    parts = range(first.shape[0])
    split = first.shape[1]
    one = sum(nt(grads[p], first[p]) for p in parts).astype(BF16)
    two = sum(nt(grads[p], second[p]) for p in parts).astype(BF16)
    return nn(one, order[:split, :]) + nn(two, order[split:, :])


def local_d_kernel(a0, at0, a1, at1, y1, y2, cand_grad, ma, mb, order, l1, l2, part):
    local_kernel(a0, at0, a1, at1, y1, y2, l1, l2)
    part[...] = chip_part(cand_grad, ma, mb, order).astype(BF16)


def chip_d1_kernel(mine, got, hc, hx, sc, sx, l1, l2, g1, g3, ro, ri, z1, z2, pay):
    parts, pulled, pushed = arrive(sx, hx, mine, got, l1, l2)
    one = [((g1[p].astype(F32) + pulled[p]) * ro[p]).astype(BF16) for p in parts]
    two = [((g3[p].astype(F32) + pushed[p]) * ri[p]).astype(BF16) for p in parts]
    exchange(one, two, hc, sc, pay)
    for p in parts:
        z1[p] = one[p]
        z2[p] = two[p]


def local_d2_kernel(a0, at0, a1, at1, z1, z2, direct, base):
    for k in range(z1.shape[0]):
        p, a = here(a0, a1, k)
        _, at = here(at0, at1, k)
        base[p] = direct[p] + nn(z1[p], a) + nn(z2[p], at)


def chip_d2_kernel(mine, got, hc, hx, sc, sx, base, ro, ri, sa, gw_b, upstream, reset, update, gate_update,
                   gate_grad, y1, y2, g1, g3, direct, pay):
    hid = base.shape[1]
    parts = range(sx.shape[0])
    top, low = merged(sx.shape[0], mine, got)
    scaled_grad = [base[p] + nn(top, hx[p]) + nn(low, sx[p]) for p in parts]
    kept = [scaled_grad[p] * reset[p] for p in parts]
    grad = [
        jnp.concatenate([(sa[p, :hid, :].astype(F32) * (kept[p] - kept[p] * reset[p])).astype(BF16), gate_update[p]], axis=0)
        for p in parts
    ]
    back = [nn(gw_b[...], grad[p]) for p in parts]
    one, two = split_back(back, hid, ro, ri, y1, y2, g1, g3, direct)
    for p in parts:
        gate_grad[p] = grad[p]
        direct[p] = direct[p] + upstream[p].astype(F32) * update[p] + kept[p]
    exchange(one, two, hc, sc, pay)


def grads_kernel(gate_grad, sa, sb, order, part, keep, give, flat):
    both = gate_grad.shape[1]
    half = keep.shape[0]
    core = lax.rem(lax.axis_index("dom"), 2)
    flat[:both, :] = chip_part(gate_grad, sa, sb, order)
    flat[both:, :] = part[...].astype(F32)
    keep[...] = flat[pl.ds(pl.multiple_of(core * half, 8), half), :].astype(BF16)
    give[...] = flat[pl.ds(pl.multiple_of((1 - core) * half, 8), half), :].astype(BF16)


def local_e_kernel(a, at, z1, z2, direct, base):
    z = lax.shift_right_logical(lax.axis_index("dom"), 1)
    base[...] = direct[z] + nn(z1[z], a[0]) + nn(z2[z], at[0])


def chip_e_kernel(mine, got, hc, hx, sc, sx, base, out, done):
    done[...] = jnp.zeros_like(done)
    z = lax.shift_right_logical(lax.axis_index("dom"), 1)
    top, low = merged(sx.shape[0], mine, got)
    out[0] = (base[...] + nn(top, hx[z]) + nn(low, sx[z])).astype(BF16)


def sum_kernel(*refs):
    values = [ref[...].astype(F32) for ref in refs[:-2]]
    while len(values) > 1:
        values = [values[k] + values[k + 1] for k in range(0, len(values), 2)]
    refs[-1][...] = values[0].astype(BF16)
    refs[-2][...] = values[0].astype(BF16)


def end_kernel(factor, mine, got, gw, gb, cw, cb, flat):
    half = mine.shape[0]
    core = lax.rem(lax.axis_index("dom"), 2)
    flat[pl.ds(pl.multiple_of(core * half, 8), half), :] = mine[...].astype(F32)
    flat[pl.ds(pl.multiple_of((1 - core) * half, 8), half), :] = got[...].astype(F32)
    features, rows = gw.shape
    same = jnp.where(iota((features, flat.shape[1]), 0) == iota((features, flat.shape[1]), 1), 1.0, 0.0).astype(BF16)
    gw[...] = nt(same, flat[:rows, :].astype(BF16)) * factor
    cw[...] = flat[rows:, :features] * factor
    pick = jnp.where(iota((8, flat.shape[1]), 1) == features, 1.0, 0.0).astype(BF16)
    bias = nt(pick, flat[...].astype(BF16))[:1] * factor
    gb[...] = bias[:, :rows]
    cb[...] = bias[:, rows:]


def chip_body(
    readings,
    previous,
    upstream,
    gate_weight,
    gate_bias,
    cand_weight,
    cand_bias,
    neighbours,
    edge_weight,
    send_rows,
):
    fin, hid = readings.shape[1], previous.shape[1]
    chans = fin + hid
    orders = gate_weight.shape[1] // chans
    degree = neighbours.shape[0]
    n = readings.shape[2]
    nd = lax.axis_size("dom")
    snaps = lax.axis_size("snap")
    parts = nd // 2
    cap = send_rows.shape[1] // nd
    block = hid + 16 * (-(-(fin + 3 * degree + 2) // 16))
    slots = 2 * parts * parts * cap

    def swap(array, k, axis="dom", size=nd):
        return lax.ppermute(array, axis, [(i, i ^ k) for i in range(size)])

    own, both = run(
        pack_kernel, "pack", [((block, n), BF16), ((block + hid, n), BF16)],
        neighbours, edge_weight, send_rows, readings, previous, upstream,
        scratch=[pltpu.VMEM((block - hid, n), F32)], vmem=56,
    )
    near = swap(both, 2)
    blocks = [own] + [near if k == 1 else swap(own, 2 * k) for k in range(1, parts - 1)]
    relay = blocks[-1]
    ups = [upstream] + [near if k == 1 else swap(upstream, 2 * k) for k in range(1, parts - 1)]
    ups.append(swap(ups[-1], 2))
    width = -(-(orders * chans + 1) // LANES) * LANES
    gw, cw, gw_b, cw_b, order = run(
        functools.partial(order_kernel, hid, fin, orders, block), "order",
        [((2 * hid, orders * block), BF16), ((hid, orders * block), BF16), ((orders * hid, 2 * hid), BF16), ((orders * hid, hid), BF16),
         ((orders * block, width), BF16)],
        gate_weight.T, cand_weight, after=[own],
    )
    relay, gw = lax.optimization_barrier((relay, gw))
    wide, wide16, wide_pay = ((parts, block, n), F32), ((parts, block, n), BF16), ((2 * block, slots), BF16)
    field, field16, pay_kind = ((parts, hid, n), F32), ((parts, hid, n), BF16), ((2 * hid, slots), BF16)
    first, second = ((parts, 3 * block, n), BF16), ((parts, 2 * block, n), BF16)
    line = ((parts, 1, n), F32)
    built = [((n, n), BF16)] * 2 + [((rows, n), BF16) for rows in (2 * parts * cap, slots)] * 2 + [((block, n), BF16)]
    early = run(
        functools.partial(build_early_kernel, cap, hid, fin, degree, parts), "build_early",
        [((parts - 1, *shape), kind) for shape, kind in built], *blocks[:-1], relay,
    )
    a, at, hc, hx, sc, sx, b, pay = run(
        functools.partial(build_late_kernel, cap, hid, fin, degree, parts), "build_late",
        [((1 if shape == (n, n) else parts, *shape), kind) for shape, kind in built] + [wide_pay],
        swap(relay, 2), *early[2:],
    )
    local = (early[0], early[1], a, at)
    edges = (hc, hx, sc, sx)
    got = swap(pay, 1)
    l1, l2 = run(local_kernel, "local_a", [wide, wide], *local, b, b)
    sa, ro, ri, pay = run(
        functools.partial(chip_a_kernel, hid + fin), "chip_a", [first, line, line, wide_pay],
        pay, got, *edges, b, l1, l2, after=ups[2:],
    )
    got = swap(pay, 1)
    l1, l2, gp = run(local_b_kernel, "local_b", [wide, wide, ((parts, 2 * hid, n), F32)], *local, sa, gw)
    sb, reset, update, y, pay = run(
        chip_b_kernel, "chip_b", [second, field, field, field16, pay_kind],
        pay, got, *edges, sa, l1, l2, ro, ri, gw, gate_bias[None, :], gp,
    )
    got = swap(pay, 1)
    l1, l2 = run(local_kernel, "local_c1", [field, field], *local, y, y)
    ma, pay = run(chip_c1_kernel, "chip_c1", [first, pay_kind], pay, got, *edges, y, sa, l1, l2, ro, ri)
    got = swap(pay, 1)
    l1, l2, cp = run(local_c2_kernel, "local_c2", [field, field, field], *local, ma, cw)
    mb, cand_grad, gate_update, y1, y2, g1, g3, up, direct, pay = run(
        functools.partial(chip_c2_kernel, parts), "chip_c2", [second] + [field16] * 7 + [field, pay_kind],
        *ups, pay, got, *edges, ma, sa, sb, l1, l2, ro, ri, cw, cw_b, cand_bias[None, :], cp, update,
    )
    got = swap(pay, 1)
    l1, l2, part = run(
        local_d_kernel, "local_d1", [field, field, ((hid, width), BF16)], *local, y1, y2, cand_grad, ma, mb, order
    )
    z1, z2, pay = run(
        chip_d1_kernel, "chip_d1", [field16, field16, pay_kind], pay, got, *edges, l1, l2, g1, g3, ro, ri
    )
    got = swap(pay, 1)
    (base,) = run(local_d2_kernel, "local_d2", [field], *local, z1, z2, direct)
    gate_grad, y1, y2, g1, g3, direct, pay = run(
        chip_d2_kernel, "chip_d2", [((parts, 2 * hid, n), BF16)] + [field16] * 4 + [field, pay_kind],
        pay, got, *edges, base, ro, ri, sa, gw_b, up, reset, update, gate_update,
    )
    got = swap(pay, 1)
    half = ((3 * hid // 2, width), BF16)
    keep, give = run(
        grads_kernel, "grads", [half, half], gate_grad, sa, sb, order, part, scratch=[pltpu.VMEM((3 * hid, width), F32)]
    )
    l1, l2 = run(local_kernel, "local_e1", [field, field], *local, y1, y2)
    mine, sent = run(sum_kernel, "sum_core", [half] * 2, keep, swap(give, 1), after=[l1, got])
    every = [mine] + [swap(sent, k, "snap", snaps) for k in range(1, snaps)]
    z1, z2, pay = run(
        chip_d1_kernel, "chip_e1", [field16, field16, pay_kind], pay, got, *edges, l1, l2, g1, g3, ro, ri, after=[mine],
    )
    got = swap(pay, 1)
    (base,) = run(local_e_kernel, "local_e2", [((hid, n), F32)], early[0], early[1], z1, z2, direct)
    state_grad, done = run(
        chip_e_kernel, "chip_e2", [((1, hid, n), BF16), ((8, LANES), F32)], pay, got, *edges, base
    )
    mine, sent = run(sum_kernel, "sum_snap", [half] * 2, *every, after=[done])
    factor = 1.0 / math.sqrt(readings.shape[0] * snaps * n * nd)
    feats = orders * chans
    grad_gw, grad_gb, grad_cw, grad_cb = run(
        functools.partial(end_kernel, factor), "end",
        [((feats, 2 * hid), F32), ((1, 2 * hid), F32), ((hid, feats), F32), ((1, hid), F32)],
        mine, swap(sent, 1), scratch=[pltpu.VMEM((3 * hid, width), F32)],
    )
    return state_grad, grad_gw.T, grad_gb[0], grad_cw, grad_cb[0]


def body(*args):
    neighbours, send_rows = args[7], args[9]
    n = neighbours.shape[1]
    nd, snaps = lax.axis_size("dom"), lax.axis_size("snap")
    parts = nd // 2
    slots = 2 * parts * parts * (send_rows.shape[1] // nd)
    powers = nd & (nd - 1) == 0 and snaps & (snaps - 1) == 0 and nd > 2
    if powers and parts * (n + slots) * n * 2 <= 4 << 20:
        return chip_body(*args)
    return spread_body(*args)


def solution(mesh):
    in_specs = (
        P("snap", None, "dom"),
        P("snap", None, "dom"),
        P("snap", None, "dom"),
        P(),
        P(),
        P(),
        P(),
        P(None, "dom"),
        P(None, "dom"),
        P("dom", None),
    )
    out_specs = (P("snap", None, "dom"), P(), P(), P(), P())
    return jax.shard_map(body, mesh=mesh, in_specs=in_specs, out_specs=out_specs, check_vma=False)
```

```python
import functools
import math

import jax
import jax.numpy as jnp
from jax import lax
from jax.experimental import pallas as pl
from jax.experimental.pallas import tpu as pltpu
from jax.sharding import PartitionSpec as P

F32 = jnp.float32
BF16 = jnp.bfloat16
LANES = 128


def nn(a, b):
    return lax.dot_general(a, b, (((1,), (0,)), ((), ())), preferred_element_type=F32)


def nt(a, b):
    return lax.dot_general(a, b, (((1,), (1,)), ((), ())), preferred_element_type=F32)


def tn(a, b):
    return lax.dot_general(a, b, (((0,), (0,)), ((), ())), preferred_element_type=F32)


def iota(shape, axis):
    return lax.broadcasted_iota(jnp.int32, shape, axis)


def column(row):
    k = row.shape[1]
    spread = jnp.broadcast_to(row.astype(F32), (k, k))
    return jnp.sum(jnp.where(iota((k, k), 0) == iota((k, k), 1), spread, 0.0), axis=1, keepdims=True)


def run(kernel, name, outs, *args, scratch=(), flops=20_000_000, vmem=24, after=()):
    return pl.pallas_call(
        lambda *refs: kernel(*refs[len(after) :]),
        name=name,
        out_shape=[jax.ShapeDtypeStruct(shape, kind) for shape, kind in outs],
        in_specs=[pl.BlockSpec(memory_space=pl.ANY)] * len(after) + [pl.BlockSpec(memory_space=pltpu.VMEM)] * len(args),
        out_specs=[pl.BlockSpec(memory_space=pltpu.VMEM)] * len(outs),
        scratch_shapes=list(scratch),
        compiler_params=pltpu.CompilerParams(vmem_limit_bytes=vmem * 1024 * 1024),
        cost_estimate=pl.CostEstimate(flops=flops, bytes_accessed=2_000_000, transcendentals=0),
    )(*after, *args)


def prep_kernel(cap, nb, w, rows, readings, previous, e, s, b, pay):
    degree, n = nb.shape
    nh = s.shape[0]
    hid = previous.shape[1]
    fin = readings.shape[1]
    step = 32
    for at in range(0, n + nh, step):
        node = iota((step, n), 0) + at
        total = jnp.zeros((step, n), F32)
        for d in range(degree):
            total = total + jnp.where(node == nb[d : d + 1, :], w[d : d + 1, :], 0.0)
        e[at : at + step, :] = total.astype(BF16)
    sent = column(rows[...]).astype(jnp.int32)
    s[...] = jnp.where(iota((nh, n), 1) == sent, 1.0, 0.0).astype(BF16)
    b[:hid, :] = previous[0]
    rest = b.shape[0] - hid
    row = iota((rest, n), 0)
    tail = jnp.where(row == fin, 1.0, 0.0)
    for f in range(fin):
        tail = jnp.where(row == f, readings[0, f : f + 1, :].astype(F32), tail)
    b[hid:, :] = tail.astype(BF16)
    base = b[...]
    chans = base.shape[0]
    bound = nt(s[...], base)
    halo = nt(e[n:, :], base)
    for p in range(nh // cap):
        pay[p, :, :chans] = bound[p * cap : (p + 1) * cap, :]
        pay[p, :, LANES : LANES + chans] = halo[p * cap : (p + 1) * cap, :]


def order_matrix(shape, chans, hid, fin, block):
    k = iota(shape, 0)
    col = iota(shape, 1)
    m = lax.div(col, jnp.int32(block))
    c = col - m * block
    source = jnp.where(c < hid, m * chans + fin + c, jnp.where(c < hid + fin, m * chans + c - hid, -1))
    return jnp.where(k == source, 1.0, 0.0).astype(BF16)


def mid_a_kernel(hid, fin, orders, e, b, gw, cw, fa, ra, gw_o, cw_o):
    n = e.shape[1]
    a = e[:n, :]
    base = b[...]
    fa[...] = nt(base, a)
    ra[...] = nn(base, a)
    block = base.shape[0]
    order = order_matrix((gw.shape[1], orders * block), hid + fin, hid, fin, block)
    gw_o[...] = nn(gw[...], order).astype(BF16)
    cw_o[...] = nn(cw[...], order).astype(BF16)


def post_a_kernel(one, cap, recv, e, s, fa, ra, f1, r1, ro, ri, pay, flat):
    n = e.shape[1]
    nh = s.shape[0]
    chans = fa.shape[0]
    for p in range(nh // cap):
        flat[p * cap : (p + 1) * cap, :] = recv[p]
    h = e[n:, :]
    sel = s[...]
    seen = flat[:, :chans].astype(BF16)
    back = flat[:, LANES : LANES + chans]
    back_degree = flat[:, LANES + one : LANES + one + 1]
    out_degree = fa[one : one + 1, :] + jnp.sum(sel.astype(F32) * back_degree, axis=0, keepdims=True)
    pulled = ra[...] + tn(seen, h)
    inv_o = 1.0 / out_degree
    inv_i = 1.0 / pulled[one : one + 1, :]
    ro[...] = inv_o
    ri[...] = inv_i
    first_out = ((fa[...] + tn(back.astype(BF16), sel)) * inv_o).astype(BF16)
    first_in = (pulled * inv_i).astype(BF16)
    f1[...] = first_out
    r1[...] = first_in
    bound = nt(sel, first_in)
    halo = nt(h, first_out)
    hi, ho = scaled(h, inv_i), scaled(h, inv_o)
    si, so = scaled(sel, inv_i), scaled(sel, inv_o)
    coefs = (nt(sel, hi), nt(h, so), nt(sel, ho), nt(h, si))
    for p in range(nh // cap):
        at = slice(p * cap, (p + 1) * cap)
        pay[p, :, :chans] = bound[at, :]
        pay[p, :, LANES : LANES + chans] = halo[at, :]
        for k, coef in enumerate(coefs):
            pay[p, :, 2 * LANES + k * nh : 2 * LANES + (k + 1) * nh] = coef[at, :]


def scaled(rows, factor):
    return (rows.astype(F32) * factor).astype(BF16)


def mid_b_kernel(e, s, f1, r1, ro, ri, f2l, r2l, kc, ke, ka):
    n = e.shape[1]
    a = e[:n, :]
    h = e[n:, :]
    sel = s[...]
    nh = sel.shape[0]
    chans = f1.shape[0]
    inv_o, inv_i = ro[...], ri[...]
    outs = nt(jnp.concatenate([f1[...], scaled(sel, inv_o), scaled(sel, inv_i)], axis=0), a)
    ins = nn(jnp.concatenate([r1[...], scaled(h, inv_i), scaled(h, inv_o)], axis=0), a)
    f2l[...] = outs[:chans]
    r2l[...] = ins[:chans]
    kc[:nh, :] = ins[chans : chans + nh].astype(BF16)
    kc[nh:, :] = h
    ke[:nh, :] = outs[chans : chans + nh].astype(BF16)
    ke[nh:, :] = sel
    ka[:nh, :] = (2.0 * ins[chans + nh :]).astype(BF16)
    ka[nh : 2 * nh, :] = h
    ka[2 * nh : 3 * nh, :] = (2.0 * outs[chans + nh :]).astype(BF16)
    ka[3 * nh :, :] = sel


def send(pay, cap, left, right, left_two, right_two):
    nh = left.shape[0]
    rows = jnp.concatenate([left, right], axis=1)
    rows_two = jnp.concatenate([left_two, right_two], axis=1)
    both = jnp.concatenate([rows, rows_two], axis=0).astype(BF16)
    k = iota((2 * nh, 2 * nh), 0)
    part = lax.div(k, jnp.int32(2 * cap))
    spot = k - part * (2 * cap)
    source = jnp.where(spot < cap, part * cap + spot, nh + part * cap + spot - cap)
    mine = nn(jnp.where(iota((2 * nh, 2 * nh), 1) == source, 1.0, 0.0).astype(BF16), both)
    for p in range(nh // cap):
        own = mine[p * 2 * cap : (p + 1) * 2 * cap, :]
        pay[p] = jnp.concatenate([rows, own], axis=0).astype(BF16)


def post_b_kernel(cap, one, recv, e, s, b, f1, r1, f2l, r2l, ro, ri, gw, gb, states, reset, update, y, f1l, r1l, pay, flat):
    n = e.shape[1]
    nh = s.shape[0]
    hid = y.shape[0]
    chans = b.shape[0]
    for p in range(nh // cap):
        flat[p * cap : (p + 1) * cap, :] = recv[p, :, : 2 * LANES]
    a = e[:n, :]
    h = e[n:, :]
    sel = s[...]
    inv_o, inv_i = ro[...], ri[...]
    base = b[...].astype(F32)
    seen = flat[:, :chans].astype(BF16)
    back = flat[:, LANES : LANES + chans].astype(BF16)
    f2 = 2.0 * (f2l[...] + tn(back, sel)) * inv_o - base
    r2 = 2.0 * (r2l[...] + tn(seen, h)) * inv_i - base
    states[:chans, :] = b[...]
    states[chans : 2 * chans, :] = f1[...]
    states[2 * chans : 3 * chans, :] = f2.astype(BF16)
    states[3 * chans : 4 * chans, :] = r1[...]
    states[4 * chans :, :] = r2.astype(BF16)
    gates = jax.nn.sigmoid(nn(gw[...], states[...]) + column(gb[...]))
    reset[...] = gates[:hid]
    update[...] = gates[hid:]
    now = (gates[:hid] * base[:hid]).astype(BF16)
    y[...] = now
    local_out = nt(now, a) * inv_o
    local_in = nn(now, a) * inv_i
    f1l[...] = local_out
    r1l[...] = local_in
    bound = nt(sel, jnp.concatenate([now, local_in.astype(BF16)], axis=0))
    halo = nt(h, jnp.concatenate([now, local_out.astype(BF16)], axis=0))
    send(pay, cap, bound[:, :hid], halo[:, :hid], bound[:, hid:], halo[:, hid:])


def gather_matrix(coef, out, nd, cap, per, first, factor):
    nh = nd * cap
    width = nd * per
    k = iota((nh, width), 0)
    col = iota((nh, width), 1)
    r = lax.div(col, jnp.int32(per))
    u = col - r * per
    p = lax.div(u, jnp.int32(cap))
    spot = u - p * cap
    here = lax.div(k, jnp.int32(cap))
    slot = k - here * cap
    inside = u < nh
    place = jnp.where((k == r * cap + spot) & inside, 1.0, 0.0).astype(BF16)
    keep = (here == p) & inside
    for i in range(2):
        wide = nn(coef[:, (first + i) * nh : (first + i + 1) * nh].astype(BF16), place)
        own = (r == here) & (u == nh + cap + slot)
        out[(i + 1) * nh : (i + 2) * nh, :] = jnp.where(keep, factor * wide, jnp.where(own, 1.0, 0.0)).astype(BF16)
    out[:nh, :] = jnp.where((r == here) & (u == nh + slot), 1.0, 0.0).astype(BF16)


def mid_c_kernel(nd, cap, per, fused, recv, e, f1l, r1l, f2l, r2l, *rest):
    n = e.shape[1]
    a = e[:n, :]
    f2l[...] = nt(f1l[...].astype(BF16), a)
    r2l[...] = nn(r1l[...].astype(BF16), a)
    if fused:
        gd, ga, flat = rest
        for p in range(nd):
            flat[p * cap : (p + 1) * cap, :] = recv[p, :, 2 * LANES :]
        gather_matrix(flat, gd, nd, cap, per, 0, 1.0)
        gather_matrix(flat, ga, nd, cap, per, 2, 2.0)


def arrived(fused, hid, nh, g, recv):
    if fused:
        halo = nn(g[...], recv[...].reshape(recv.shape[0] * recv.shape[1], recv.shape[2]))
        two = halo[nh : 2 * nh, :hid], halo[2 * nh :, hid:]
    else:
        halo = recv[...]
        two = halo[nh:, :hid], halo[nh:, hid:]
    one = halo[:nh]
    return one[:, :hid], one[:, hid:], two[0], two[1]


def back_and_send(cap, hid, g, a, h, sel, inv_o, inv_i, z1, z2, pay):
    g0, g1, g2, g3, g4 = (g[m * hid : (m + 1) * hid, :].astype(BF16).astype(F32) for m in range(5))
    y1 = (g2 * inv_o).astype(BF16)
    y2 = (g4 * inv_i).astype(BF16)
    now1 = ((g1 + 2.0 * nn(y1, a)) * inv_o).astype(BF16)
    now2 = ((g3 + 2.0 * nt(y2, a)) * inv_i).astype(BF16)
    z1[...] = now1
    z2[...] = now2
    bound = nt(sel, jnp.concatenate([y1, now1], axis=0))
    halo = nt(h, jnp.concatenate([y2, now2], axis=0))
    send(pay, cap, bound[:, :hid], halo[:, :hid], bound[:, hid:], halo[:, hid:])
    return g0 - g2 - g4


def hidden_weights(w, hid, block, orders):
    return jnp.concatenate([w[:, m * block : m * block + hid] for m in range(orders)], axis=1)


def post_c_kernel(fused, cap, orders, g, recv, e, s, kc, ke, y, f1l, r1l, f2l, r2l, ro, ri, states, cw, cb, upstream, update,
                  mixed, cand_grad, gate_update, z1, z2, direct, pay):
    n = e.shape[1]
    nh = s.shape[0]
    hid = y.shape[0]
    block = states.shape[0] // orders
    a = e[:n, :]
    h = e[n:, :]
    sel = s[...]
    inv_o, inv_i = ro[...], ri[...]
    c1, e1, c2, e2 = arrived(fused, hid, nh, g, recv)
    base = y[...].astype(F32)
    c1, e1 = c1.astype(BF16), e1.astype(BF16)
    cc = jnp.concatenate([c1, c2.astype(BF16)], axis=0)
    ee = jnp.concatenate([e1, e2.astype(BF16)], axis=0)
    f1 = f1l[...] + tn(e1, sel) * inv_o
    f2 = 2.0 * (f2l[...] + tn(ee, ke[...])) * inv_o - base
    r1 = r1l[...] + tn(c1, h) * inv_i
    r2 = 2.0 * (r2l[...] + tn(cc, kc[...])) * inv_i - base
    for m, value in enumerate((y[...], f1, f2, r1, r2)):
        mixed[m * block : m * block + hid, :] = value.astype(BF16)
        mixed[m * block + hid : (m + 1) * block, :] = states[m * block + hid : (m + 1) * block, :]
    weights = cw[...]
    cand = jnp.tanh(nn(weights, mixed[...]) + column(cb[...]))
    up = upstream[0].astype(F32)
    gate = update[...]
    grad = (up * (1.0 - gate) * (1.0 - cand * cand)).astype(BF16)
    cand_grad[...] = grad
    held = states[:hid, :].astype(F32)
    gate_update[...] = (up * (held - cand) * gate * (1.0 - gate)).astype(BF16)
    back = tn(hidden_weights(weights, hid, block, orders), grad)
    direct[...] = back_and_send(cap, hid, back, a, h, sel, inv_o, inv_i, z1, z2, pay)


def weight_part(grad, features, orders, chans, hid, fin):
    block = features.shape[0] // orders
    width = -(-(orders * chans + 1) // LANES) * LANES
    shape = (width, orders * block)
    k = iota(shape, 0)
    col = iota(shape, 1)
    m = lax.div(col, jnp.int32(block))
    c = col - m * block
    source = jnp.where(c < hid, m * chans + fin + c, jnp.where(c < hid + fin, m * chans + c - hid, -1))
    source = jnp.where(col == hid + fin, orders * chans, source)
    order = jnp.where(k == source, 1.0, 0.0).astype(BF16)
    return nt(nt(grad, features).astype(BF16), order)


def mid_d_kernel(orders, fin, e, z1, z2, direct, cand_grad, mixed, gate_update, states, base, part):
    n = e.shape[1]
    a = e[:n, :]
    hid = z1.shape[0]
    base[...] = direct[...] + nn(z1[...], a) + nt(z2[...], a)
    part[:hid, :] = weight_part(gate_update[...], states[...], orders, hid + fin, hid, fin).astype(BF16)
    part[hid:, :] = weight_part(cand_grad[...], mixed[...], orders, hid + fin, hid, fin).astype(BF16)


def add_halo(fused, g, recv, ka, base):
    hid = base.shape[0]
    nh = ka.shape[0] // 4
    c1, e1, c2, e2 = arrived(fused, hid, nh, g, recv)
    return base[...] + tn(jnp.concatenate([c1, c2, e1, e2], axis=0).astype(BF16), ka[...])


def post_d_kernel(fused, cap, orders, g, recv, e, s, ka, base, ro, ri, states, gw, upstream, reset, update, gate_update,
                  gate_reset, z1, z2, direct, pay):
    n = e.shape[1]
    hid = base.shape[0]
    block = states.shape[0] // orders
    scaled_grad = add_halo(fused, g, recv, ka, base)
    held = states[:hid, :].astype(F32)
    gate = reset[...]
    grad = (scaled_grad * held * gate * (1.0 - gate)).astype(BF16)
    gate_reset[...] = grad
    weights = hidden_weights(gw[...], hid, block, orders)
    back = tn(weights, jnp.concatenate([grad, gate_update[...]], axis=0))
    rest = back_and_send(cap, hid, back, e[:n, :], e[n:, :], s[...], ro[...], ri[...], z1, z2, pay)
    direct[...] = rest + upstream[0].astype(F32) * update[...] + scaled_grad * gate


def mid_e_kernel(orders, fin, rows, e, z1, z2, direct, gate_reset, states, part, base, grads):
    n = e.shape[1]
    a = e[:n, :]
    hid = z1.shape[0]
    base[...] = direct[...] + nn(z1[...], a) + nt(z2[...], a)
    first = weight_part(gate_reset[...], states[...], orders, hid + fin, hid, fin)
    both = jnp.concatenate([first, part[...].astype(F32)], axis=0)
    for k in range(grads.shape[0]):
        if k * rows < both.shape[0]:
            grads[k] = both[k * rows : (k + 1) * rows, :].astype(BF16)
        else:
            grads[k] = jnp.zeros(grads.shape[1:], BF16)


def post_e_kernel(fused, g, recv, ka, base, out):
    out[0] = add_halo(fused, g, recv, ka, base).astype(BF16)


def add_kernel(recv, out):
    total = recv[0].astype(F32)
    for k in range(1, recv.shape[0]):
        total = total + recv[k].astype(F32)
    for k in range(out.shape[0]):
        out[k] = total.astype(BF16)


def finish_kernel(hid, factor, recv, gw, gb, cw, cb):
    rows = recv.shape[1]
    features = gw.shape[1]
    total = gw.shape[0] + cw.shape[0]
    for k in range(total // rows):
        part = recv[k].astype(F32)[:, :features] * factor
        at = k * rows
        if at < 2 * hid:
            gw[at : at + rows, :] = part
        else:
            cw[at - 2 * hid : at - 2 * hid + rows, :] = part
    flat = jnp.concatenate([recv[k].astype(F32) for k in range(total // rows)], axis=0)
    pick = jnp.where(iota((8, flat.shape[1]), 1) == features, 1.0, 0.0).astype(BF16)
    bias = nt(pick, flat.astype(BF16))[:1] * factor
    gb[...] = bias[:, : 2 * hid]
    cb[...] = bias[:, 2 * hid :]


def spread_body(
    readings,
    previous,
    upstream,
    gate_weight,
    gate_bias,
    cand_weight,
    cand_bias,
    neighbours,
    edge_weight,
    send_rows,
):
    fin, hid = readings.shape[1], previous.shape[1]
    chans = fin + hid
    orders = gate_weight.shape[1] // chans
    n = readings.shape[2]
    nd = lax.axis_size("dom")
    devices = nd * lax.axis_size("snap")
    nh = send_rows.shape[1]
    cap = nh // nd
    block = hid + 16 * (-(-(fin + 1) // 16))
    one = hid + fin
    per = nh + 2 * cap
    fused = 3 * nh * nd * per <= 1 << 18
    move = functools.partial(lax.all_to_all, axis_name="dom", split_axis=0, concat_axis=0, tiled=True)

    e, s, b, pay = run(
        functools.partial(prep_kernel, cap), "prep",
        [((n + nh, n), BF16), ((nh, n), BF16), ((block, n), BF16), ((nd, cap, 2 * LANES), F32)],
        neighbours, edge_weight, send_rows, readings, previous,
    )
    recv = move(pay)
    fa, ra, gw, cw = run(
        functools.partial(mid_a_kernel, hid, fin, orders), "mid_a",
        [((block, n), F32), ((block, n), F32), ((2 * hid, orders * block), BF16), ((hid, orders * block), BF16)],
        e, b, gate_weight, cand_weight,
    )
    wide = 2 * LANES + 4 * nh
    f1, r1, ro, ri, pay = run(
        functools.partial(post_a_kernel, one, cap), "post_a",
        [((block, n), BF16), ((block, n), BF16), ((1, n), F32), ((1, n), F32), ((nd, cap, wide), F32)],
        recv, e, s, fa, ra, scratch=[pltpu.VMEM((nh, 2 * LANES), F32)],
    )
    recv_b = move(pay)
    f2l, r2l, kc, ke, ka = run(
        mid_b_kernel, "mid_b",
        [((block, n), F32), ((block, n), F32), ((2 * nh, n), BF16), ((2 * nh, n), BF16), ((4 * nh, n), BF16)],
        e, s, f1, r1, ro, ri,
    )
    pay_kind = ((nd, per, 2 * hid), BF16)
    field, field16 = ((hid, n), F32), ((hid, n), BF16)
    states, reset, update, y, f1l, r1l, pay = run(
        functools.partial(post_b_kernel, cap, one), "post_b",
        [((orders * block, n), BF16), field, field, field16, field, field, pay_kind],
        recv_b, e, s, b, f1, r1, f2l, r2l, ro, ri, gw, gate_bias[None, :],
        scratch=[pltpu.VMEM((nh, 2 * LANES), F32)],
    )
    recv = move(pay)
    table = ((3 * nh, nd * per), BF16)
    f2l, r2l, *tables = run(
        functools.partial(mid_c_kernel, nd, cap, per, fused), "mid_c",
        [field, field] + [table] * (2 if fused else 0),
        recv_b, e, f1l, r1l, scratch=[pltpu.VMEM((nh, 4 * nh), F32)] if fused else [],
    )
    if fused:
        inward, outward = tables
        halo_of = lambda got, first, factor: got
    else:
        inward = outward = jnp.zeros((8, LANES), BF16)
        coefs = recv_b[:, :, 2 * LANES :].reshape(nd, cap, 4, nd, cap)

        def halo_of(got, first, factor):
            rows = got[:, :nh].reshape(nd, nd, cap, 2, hid).astype(F32)
            two = jnp.einsum("psgrt,rptgk->psgk", coefs[:, :, first : first + 2], rows)
            two = factor * two.reshape(nh, 2 * hid) + got[:, nh + cap :].reshape(nh, 2 * hid).astype(F32)
            return jnp.concatenate([got[:, nh : nh + cap].reshape(nh, 2 * hid).astype(F32), two], axis=0)

    mixed, cand_grad, gate_update, z1, z2, direct, pay = run(
        functools.partial(post_c_kernel, fused, cap, orders), "post_c",
        [((orders * block, n), BF16), field16, field16, field16, field16, field, pay_kind],
        inward, halo_of(recv, 0, 1.0), e, s, kc, ke, y, f1l, r1l, f2l, r2l, ro, ri, states, cw, cand_bias[None, :], upstream, update,
    )
    recv = move(pay)
    width = -(-(orders * chans + 1) // LANES) * LANES
    base, part = run(
        functools.partial(mid_d_kernel, orders, fin), "mid_d", [field, ((2 * hid, width), BF16)],
        e, z1, z2, direct, cand_grad, mixed, gate_update, states,
    )
    gate_reset, z1, z2, direct, pay = run(
        functools.partial(post_d_kernel, fused, cap, orders), "post_d",
        [field16, field16, field16, field, pay_kind],
        outward, halo_of(recv, 2, 2.0), e, s, ka, base, ro, ri, states, gw, upstream, reset, update, gate_update,
    )
    recv = move(pay)
    rows = 8 * (-(-3 * hid // (8 * devices)))
    base, grads = run(
        functools.partial(mid_e_kernel, orders, fin, rows), "mid_e", [field, ((devices, rows, width), BF16)],
        e, z1, z2, direct, gate_reset, states, part,
    )
    (state_grad,) = run(
        functools.partial(post_e_kernel, fused), "post_e", [((1, hid, n), BF16)],
        outward, halo_of(recv, 2, 2.0), ka, base,
    )
    both = ("snap", "dom")
    grads = lax.all_to_all(grads, both, 0, 0, tiled=True)
    (grads,) = run(add_kernel, "add", [((devices, rows, width), BF16)], grads)
    grads = lax.all_to_all(grads, both, 0, 0, tiled=True)
    factor = 1.0 / math.sqrt(readings.shape[0] * lax.axis_size("snap") * n * nd)
    feats = orders * chans
    grad_gw, grad_gb, grad_cw, grad_cb = run(
        functools.partial(finish_kernel, hid, factor), "finish",
        [((2 * hid, feats), F32), ((1, 2 * hid), F32), ((hid, feats), F32), ((1, hid), F32)],
        grads,
    )
    return state_grad, grad_gw, grad_gb[0], grad_cw, grad_cb[0]


def pack_kernel(nb, w, rows, readings, previous, upstream, own, both, tail):
    degree = nb.shape[0]
    nh = rows.shape[1]
    hid = previous.shape[1]
    fin = readings.shape[1]
    block = own.shape[0]
    tail[...] = jnp.zeros_like(tail)
    tail[:fin, :] = readings[0].astype(F32)
    high = lax.shift_right_logical(nb[...], 5)
    tail[fin : fin + degree, :] = high.astype(F32)
    tail[fin + degree : fin + 2 * degree, :] = (nb[...] - high * 32).astype(F32)
    tail[fin + 2 * degree : fin + 3 * degree, :] = w[...]
    at = fin + 3 * degree
    high = lax.shift_right_logical(rows[...], 5)
    tail[at : at + 1, :nh] = high.astype(F32)
    tail[at + 1 : at + 2, :nh] = (rows[...] - high * 32).astype(F32)
    for to in (own, both):
        to[:hid, :] = previous[0]
        to[hid:block, :] = tail[...].astype(BF16)
    both[block:, :] = upstream[0]


def exchange(first, second, hc, sc, pay):
    count = first[0].shape[0]
    parts = len(first)
    pay[:count, :] = jnp.concatenate([nt(first[p], sc[p]).astype(BF16) for p in range(parts)], axis=1)
    pay[count:, :] = jnp.concatenate([nt(second[p], hc[p]).astype(BF16) for p in range(parts)], axis=1)


def merged(parts, mine, got):
    step = mine.shape[1] // (2 * parts)
    here = lax.rem(lax.div(iota(mine.shape, 1), jnp.int32(step)), jnp.int32(2)) == 0
    value = jnp.where(here, mine[...].astype(F32), got[...].astype(F32)).astype(BF16)
    count = mine.shape[0] // 2
    return value[:count, :], value[count:, :]


def build_part(cap, hid, fin, degree, parts, p, block, a, at, hc, hx, sc, sx, b):
    n = a.shape[1]
    slots = sx.shape[0]
    nh = 2 * parts * cap
    half = parts * cap
    core = lax.rem(lax.axis_index("dom"), 2)
    line = iota((nh, 1), 0)
    rel = lax.div(line, jnp.int32(half))
    k = lax.div(line - rel * half, jnp.int32(cap))
    t = line - rel * half - k * cap
    spot = (k * 2 + lax.bitwise_xor(rel, core)) * cap + t
    node = (n + spot).astype(F32)
    width = -(-nh // LANES) * LANES
    slot = iota((slots, nh), 0)
    outer = lax.div(slot, jnp.int32(nh))
    rest = slot - outer * nh
    slot_rel = lax.div(rest, jnp.int32(half))
    rest = rest - slot_rel * half
    inner = lax.div(rest, jnp.int32(cap))
    filled = iota((slots, nh), 1) == slot_rel * half + outer * cap + rest - inner * cap
    row = iota((32, n), 0).astype(F32)
    edges = hid + fin + 3 * degree + 2
    tail = block[hid : hid + 16 * (-(-(edges - hid) // 16)), :].astype(F32)
    high, low = tail[fin : fin + degree], tail[fin + degree : fin + 2 * degree]
    w = tail[fin + 2 * degree : fin + 3 * degree]
    start = fin + 3 * degree
    sent = tail[start : start + 1] * 32.0 + tail[start + 1 : start + 2]
    low_is = [jnp.where(low[d : d + 1] == row, 1.0, 0.0).astype(BF16) for d in range(degree)]
    for chunk in range(n // 32):
        total = None
        for d in range(degree):
            term = low_is[d] * jnp.where(high[d : d + 1] == float(chunk), w[d : d + 1], 0.0).astype(BF16)
            total = term if total is None else total + term
        a[chunk * 32 : (chunk + 1) * 32, :] = total
    at[...] = a[...].T
    names = high * 32.0 + low
    total = jnp.zeros((nh, n), F32)
    for d in range(degree):
        total = total + jnp.where(names[d : d + 1] == node, w[d : d + 1], 0.0)
    halo = total.astype(BF16)
    hc[...] = halo
    named = jnp.where(iota((nh, width), 1) == spot, sent[:, :width], 0.0)
    target = jnp.sum(named, axis=1, keepdims=True).astype(jnp.int32)
    picked = jnp.where(iota((nh, n), 1) == target, 1.0, 0.0).astype(BF16)
    sc[...] = picked
    place = jnp.where(filled & (inner == p), 1.0, 0.0).astype(BF16)
    hx[...] = nn(place, halo).astype(BF16)
    sx[...] = nn(place, picked).astype(BF16)
    b[:hid, :] = block[:hid, :]
    line = iota(tail.shape, 0)
    b[hid:, :] = jnp.where(line < fin, tail, jnp.where(line == fin, 1.0, 0.0)).astype(BF16)


def build_early_kernel(cap, hid, fin, degree, parts, *refs):
    count = parts - 1
    z = lax.shift_right_logical(lax.axis_index("dom"), 1)
    for k in range(count):
        p = lax.bitwise_xor(z, jnp.int32(k))
        build_part(cap, hid, fin, degree, parts, p, refs[k], *(ref.at[k] for ref in refs[count:]))


def build_late_kernel(cap, hid, fin, degree, parts, last, *refs):
    early, outs, pay = refs[:5], refs[5:12], refs[12]
    z = lax.shift_right_logical(lax.axis_index("dom"), 1)
    for k in range(parts - 1):
        p = lax.bitwise_xor(z, jnp.int32(k))
        for source, to in zip(early, outs[2:]):
            to[p] = source[k]
    p = lax.bitwise_xor(z, jnp.int32(parts - 1))
    build_part(cap, hid, fin, degree, parts, p, last, outs[0].at[0], outs[1].at[0], *(ref.at[p] for ref in outs[2:]))
    hc, sc, b = outs[2], outs[4], outs[6]
    base = [b[p] for p in range(parts)]
    exchange(base, base, hc, sc, pay)


def chip_source(col, chans, hid, fin, block):
    m = lax.div(col, jnp.int32(block))
    c = col - m * block
    m = jnp.where(m == 2, 3, jnp.where(m == 3, 2, m))
    return m, c, jnp.where(c < hid, m * chans + fin + c, jnp.where(c < hid + fin, m * chans + c - hid, -1))


def order_kernel(hid, fin, orders, block, gw, cw, gw_o, cw_o, gw_b, cw_b, order):
    chans = hid + fin
    feats = cw.shape[1]
    shape = (feats, orders * block)
    source = chip_source(iota(shape, 1), chans, hid, fin, block)[2]
    pick = jnp.where(iota(shape, 0) == source, 1.0, 0.0).astype(BF16)
    gw_o[...] = tn(gw[...], pick).astype(BF16)
    cw_o[...] = nn(cw[...], pick).astype(BF16)
    shape = (orders * hid, feats)
    line = iota(shape, 0)
    m = lax.div(line, jnp.int32(hid))
    pick = jnp.where(iota(shape, 1) == m * chans + fin + line - m * hid, 1.0, 0.0).astype(BF16)
    gw_b[...] = nn(pick, gw[...]).astype(BF16)
    cw_b[...] = nt(pick, cw[...]).astype(BF16)
    m, c, source = chip_source(iota(order.shape, 0), chans, hid, fin, block)
    source = jnp.where((m == 0) & (c == hid + fin), feats, source)
    order[...] = jnp.where(iota(order.shape, 1) == source, 1.0, 0.0).astype(BF16)


def here(early, late, k):
    z = lax.shift_right_logical(lax.axis_index("dom"), 1)
    count = early.shape[0]
    return lax.bitwise_xor(z, jnp.int32(k)), early[k] if k < count else late[k - count]


def local_kernel(a0, at0, a1, at1, x1, x2, l1, l2):
    for k in range(x1.shape[0]):
        p, a = here(a0, a1, k)
        l1[p] = nn(x1[p], a)
    for k in range(x1.shape[0]):
        p, at = here(at0, at1, k)
        l2[p] = nn(x2[p], at)


def arrive(sx, hx, mine, got, l1, l2):
    parts = range(sx.shape[0])
    top, low = merged(sx.shape[0], mine, got)
    pulled = [l1[p] + nn(top, hx[p]) for p in parts]
    pushed = [l2[p] + nn(low, sx[p]) for p in parts]
    return parts, pulled, pushed


def chip_a_kernel(one, mine, got, hc, hx, sc, sx, b, l1, l2, sa, ro, ri, pay):
    chans = b.shape[1]
    parts, pulled, pushed = arrive(sx, hx, mine, got, l1, l2)
    inv_o = [1.0 / pushed[p][one : one + 1, :] for p in parts]
    inv_i = [1.0 / pulled[p][one : one + 1, :] for p in parts]
    outs = [(pushed[p] * inv_o[p]).astype(BF16) for p in parts]
    ins = [(pulled[p] * inv_i[p]).astype(BF16) for p in parts]
    for p in parts:
        ro[p] = inv_o[p]
        ri[p] = inv_i[p]
        sa[p, :chans, :] = b[p]
        sa[p, chans : 2 * chans, :] = outs[p]
        sa[p, 2 * chans :, :] = ins[p]
    exchange(ins, outs, hc, sc, pay)


def local_b_kernel(a0, at0, a1, at1, sa, gw, l1, l2, gp):
    chans = l1.shape[1]
    weights = gw[:, : 3 * chans]
    for k in range(sa.shape[0]):
        p, a = here(a0, a1, k)
        l1[p] = nn(sa[p, 2 * chans :, :], a)
    for k in range(sa.shape[0]):
        p, at = here(at0, at1, k)
        l2[p] = nn(sa[p, chans : 2 * chans, :], at)
    for p in range(sa.shape[0]):
        gp[p] = nn(weights, sa[p])


def chip_b_kernel(mine, got, hc, hx, sc, sx, sa, l1, l2, ro, ri, gw, gb, gp, sb, reset, update, y, pay):
    hid = y.shape[1]
    chans = l1.shape[1]
    bias = column(gb[...])
    weights = gw[:, 3 * chans :]
    parts, pulled, pushed = arrive(sx, hx, mine, got, l1, l2)
    base = [sa[p, :chans, :].astype(F32) for p in parts]
    r2 = [(pulled[p] * (2.0 * ri[p]) - base[p]).astype(BF16) for p in parts]
    f2 = [(pushed[p] * (2.0 * ro[p]) - base[p]).astype(BF16) for p in parts]
    second = [jnp.concatenate([f2[p], r2[p]], axis=0) for p in parts]
    gates = [jax.nn.sigmoid(gp[p] + nn(weights, second[p]) + bias) for p in parts]
    now = [(gates[p][:hid] * base[p][:hid]).astype(BF16) for p in parts]
    for p in parts:
        sb[p] = second[p]
        reset[p] = gates[p][:hid]
        update[p] = gates[p][hid:]
        y[p] = now[p]
    exchange(now, now, hc, sc, pay)


def chip_c1_kernel(mine, got, hc, hx, sc, sx, y, sa, l1, l2, ro, ri, ma, pay):
    hid = y.shape[1]
    chans = ma.shape[1] // 3
    parts, pulled, pushed = arrive(sx, hx, mine, got, l1, l2)
    ins = [(pulled[p] * ri[p]).astype(BF16) for p in parts]
    outs = [(pushed[p] * ro[p]).astype(BF16) for p in parts]
    exchange(ins, outs, hc, sc, pay)
    for p in parts:
        for m, value in enumerate((y[p], outs[p], ins[p])):
            ma[p, m * chans : m * chans + hid, :] = value
            ma[p, m * chans + hid : (m + 1) * chans, :] = sa[p, m * chans + hid : (m + 1) * chans, :]


def local_c2_kernel(a0, at0, a1, at1, ma, cw, l1, l2, cp):
    hid = l1.shape[1]
    chans = ma.shape[1] // 3
    weights = cw[:, : 3 * chans]
    for k in range(ma.shape[0]):
        p, a = here(a0, a1, k)
        l1[p] = nn(ma[p, 2 * chans : 2 * chans + hid, :], a)
    for k in range(ma.shape[0]):
        p, at = here(at0, at1, k)
        l2[p] = nn(ma[p, chans : chans + hid, :], at)
    for p in range(ma.shape[0]):
        cp[p] = nn(weights, ma[p])


def split_back(back, hid, ro, ri, y1, y2, g1, g3, direct):
    parts = range(len(back))
    blocks = [[back[p][m * hid : (m + 1) * hid, :] for m in range(5)] for p in parts]
    one = [(blocks[p][2] * (2.0 * ro[p])).astype(BF16) for p in parts]
    two = [(blocks[p][4] * (2.0 * ri[p])).astype(BF16) for p in parts]
    for p in parts:
        y1[p] = one[p]
        y2[p] = two[p]
        g1[p] = blocks[p][1].astype(BF16)
        g3[p] = blocks[p][3].astype(BF16)
        direct[p] = blocks[p][0] - blocks[p][2] - blocks[p][4]
    return one, two


def chip_c2_kernel(parts, *refs):
    ups, refs = refs[:parts], refs[parts:]
    mine, got, hc, hx, sc, sx, ma, sa, sb, l1, l2, ro, ri, cw, cw_b, cb, cp, update = refs[:18]
    mb, cand_grad, gate_update, y1, y2, g1, g3, upstream, direct, pay = refs[18:]
    hid = l1.shape[1]
    chans = ma.shape[1] // 3
    z = lax.shift_right_logical(lax.axis_index("dom"), 1)
    for k in range(parts):
        upstream[lax.bitwise_xor(z, jnp.int32(k))] = ups[k][0] if len(ups[k].shape) == 3 else ups[k][ups[k].shape[0] - hid :, :]
    bias = column(cb[...])
    weights = cw[:, 3 * chans :]
    parts, pulled, pushed = arrive(sx, hx, mine, got, l1, l2)
    base = [ma[p, :hid, :].astype(F32) for p in parts]
    r2 = [(pulled[p] * (2.0 * ri[p]) - base[p]).astype(BF16) for p in parts]
    f2 = [(pushed[p] * (2.0 * ro[p]) - base[p]).astype(BF16) for p in parts]
    second = [
        jnp.concatenate([f2[p], sb[p, hid:chans, :], r2[p], sb[p, chans + hid :, :]], axis=0) for p in parts
    ]
    cand = [jnp.tanh(cp[p] + nn(weights, second[p]) + bias) for p in parts]
    rest = [upstream[p].astype(F32) * (1.0 - update[p]) for p in parts]
    grad = [(rest[p] - rest[p] * cand[p] * cand[p]).astype(BF16) for p in parts]
    back = [nn(cw_b[...], grad[p]) for p in parts]
    for p in parts:
        mb[p] = second[p]
        cand_grad[p] = grad[p]
        gate_update[p] = ((sa[p, :hid, :].astype(F32) - cand[p]) * (rest[p] * update[p])).astype(BF16)
    one, two = split_back(back, hid, ro, ri, y1, y2, g1, g3, direct)
    exchange(one, two, hc, sc, pay)


def chip_part(grads, first, second, order):
    parts = range(first.shape[0])
    split = first.shape[1]
    one = sum(nt(grads[p], first[p]) for p in parts).astype(BF16)
    two = sum(nt(grads[p], second[p]) for p in parts).astype(BF16)
    return nn(one, order[:split, :]) + nn(two, order[split:, :])


def local_d_kernel(a0, at0, a1, at1, y1, y2, cand_grad, ma, mb, order, l1, l2, part):
    local_kernel(a0, at0, a1, at1, y1, y2, l1, l2)
    part[...] = chip_part(cand_grad, ma, mb, order).astype(BF16)


def chip_d1_kernel(mine, got, hc, hx, sc, sx, l1, l2, g1, g3, ro, ri, z1, z2, pay):
    parts, pulled, pushed = arrive(sx, hx, mine, got, l1, l2)
    one = [((g1[p].astype(F32) + pulled[p]) * ro[p]).astype(BF16) for p in parts]
    two = [((g3[p].astype(F32) + pushed[p]) * ri[p]).astype(BF16) for p in parts]
    exchange(one, two, hc, sc, pay)
    for p in parts:
        z1[p] = one[p]
        z2[p] = two[p]


def local_d2_kernel(a0, at0, a1, at1, z1, z2, direct, base):
    for k in range(z1.shape[0]):
        p, a = here(a0, a1, k)
        _, at = here(at0, at1, k)
        base[p] = direct[p] + nn(z1[p], a) + nn(z2[p], at)


def chip_d2_kernel(mine, got, hx, sx, base, sa, sb, reset, gate_update, order, part, gate_grad, kept, keep, give, flat):
    hid = base.shape[1]
    both = 2 * hid
    half = keep.shape[0]
    core = lax.rem(lax.axis_index("dom"), 2)
    parts = range(sx.shape[0])
    top, low = merged(sx.shape[0], mine, got)
    scaled_grad = [base[p] + nn(top, hx[p]) + nn(low, sx[p]) for p in parts]
    through = [scaled_grad[p] * reset[p] for p in parts]
    grad = [
        jnp.concatenate([(sa[p, :hid, :].astype(F32) * (through[p] - through[p] * reset[p])).astype(BF16), gate_update[p]], axis=0)
        for p in parts
    ]
    for p in parts:
        gate_grad[p] = grad[p]
        kept[p] = through[p]
    flat[:both, :] = chip_part(grad, sa, sb, order)
    flat[both:, :] = part[...].astype(F32)
    keep[...] = flat[pl.ds(pl.multiple_of(core * half, 8), half), :].astype(BF16)
    give[...] = flat[pl.ds(pl.multiple_of((1 - core) * half, 8), half), :].astype(BF16)


def back_e_kernel(hc, sc, gate_grad, kept, ro, ri, gw_b, upstream, update, y1, y2, g1, g3, direct, pay):
    hid = kept.shape[1]
    parts = range(sc.shape[0])
    back = [nn(gw_b[...], gate_grad[p]) for p in parts]
    one, two = split_back(back, hid, ro, ri, y1, y2, g1, g3, direct)
    for p in parts:
        direct[p] = direct[p] + upstream[p].astype(F32) * update[p] + kept[p]
    exchange(one, two, hc, sc, pay)


def local_e_kernel(a, at, z1, z2, direct, base):
    z = lax.shift_right_logical(lax.axis_index("dom"), 1)
    base[...] = direct[z] + nn(z1[z], a[0]) + nn(z2[z], at[0])


def chip_e_kernel(mine, got, hc, hx, sc, sx, base, out, done):
    done[...] = jnp.zeros_like(done)
    z = lax.shift_right_logical(lax.axis_index("dom"), 1)
    top, low = merged(sx.shape[0], mine, got)
    out[0] = (base[...] + nn(top, hx[z]) + nn(low, sx[z])).astype(BF16)


def sum_kernel(*refs):
    values = [ref[...].astype(F32) for ref in refs[:-2]]
    while len(values) > 1:
        values = [values[k] + values[k + 1] for k in range(0, len(values), 2)]
    refs[-1][...] = values[0].astype(BF16)
    refs[-2][...] = values[0].astype(BF16)


def end_kernel(factor, mine, got, gw, gb, cw, cb, flat):
    half = mine.shape[0]
    core = lax.rem(lax.axis_index("dom"), 2)
    flat[pl.ds(pl.multiple_of(core * half, 8), half), :] = mine[...].astype(F32)
    flat[pl.ds(pl.multiple_of((1 - core) * half, 8), half), :] = got[...].astype(F32)
    features, rows = gw.shape
    same = jnp.where(iota((features, flat.shape[1]), 0) == iota((features, flat.shape[1]), 1), 1.0, 0.0).astype(BF16)
    gw[...] = nt(same, flat[:rows, :].astype(BF16)) * factor
    cw[...] = flat[rows:, :features] * factor
    pick = jnp.where(iota((8, flat.shape[1]), 1) == features, 1.0, 0.0).astype(BF16)
    bias = nt(pick, flat[...].astype(BF16))[:1] * factor
    gb[...] = bias[:, :rows]
    cb[...] = bias[:, rows:]


def chip_body(
    readings,
    previous,
    upstream,
    gate_weight,
    gate_bias,
    cand_weight,
    cand_bias,
    neighbours,
    edge_weight,
    send_rows,
):
    fin, hid = readings.shape[1], previous.shape[1]
    chans = fin + hid
    orders = gate_weight.shape[1] // chans
    degree = neighbours.shape[0]
    n = readings.shape[2]
    nd = lax.axis_size("dom")
    snaps = lax.axis_size("snap")
    parts = nd // 2
    cap = send_rows.shape[1] // nd
    block = hid + 16 * (-(-(fin + 3 * degree + 2) // 16))
    slots = 2 * parts * parts * cap

    def swap(array, k, axis="dom", size=nd):
        return lax.ppermute(array, axis, [(i, i ^ k) for i in range(size)])

    own, both = run(
        pack_kernel, "pack", [((block, n), BF16), ((block + hid, n), BF16)],
        neighbours, edge_weight, send_rows, readings, previous, upstream,
        scratch=[pltpu.VMEM((block - hid, n), F32)], vmem=56,
    )
    near = swap(both, 2)
    blocks = [own] + [near if k == 1 else swap(own, 2 * k) for k in range(1, parts - 1)]
    relay = blocks[-1]
    ups = [upstream] + [near if k == 1 else swap(upstream, 2 * k) for k in range(1, parts - 1)]
    ups.append(swap(ups[-1], 2))
    width = -(-(orders * chans + 1) // LANES) * LANES
    gw, cw, gw_b, cw_b, order = run(
        functools.partial(order_kernel, hid, fin, orders, block), "order",
        [((2 * hid, orders * block), BF16), ((hid, orders * block), BF16), ((orders * hid, 2 * hid), BF16), ((orders * hid, hid), BF16),
         ((orders * block, width), BF16)],
        gate_weight.T, cand_weight, after=[own],
    )
    relay, gw = lax.optimization_barrier((relay, gw))
    wide, wide16, wide_pay = ((parts, block, n), F32), ((parts, block, n), BF16), ((2 * block, slots), BF16)
    field, field16, pay_kind = ((parts, hid, n), F32), ((parts, hid, n), BF16), ((2 * hid, slots), BF16)
    first, second = ((parts, 3 * block, n), BF16), ((parts, 2 * block, n), BF16)
    line = ((parts, 1, n), F32)
    built = [((n, n), BF16)] * 2 + [((rows, n), BF16) for rows in (2 * parts * cap, slots)] * 2 + [((block, n), BF16)]
    early = run(
        functools.partial(build_early_kernel, cap, hid, fin, degree, parts), "build_early",
        [((parts - 1, *shape), kind) for shape, kind in built], *blocks[:-1], relay,
    )
    a, at, hc, hx, sc, sx, b, pay = run(
        functools.partial(build_late_kernel, cap, hid, fin, degree, parts), "build_late",
        [((1 if shape == (n, n) else parts, *shape), kind) for shape, kind in built] + [wide_pay],
        swap(relay, 2), *early[2:],
    )
    local = (early[0], early[1], a, at)
    edges = (hc, hx, sc, sx)
    got = swap(pay, 1)
    l1, l2 = run(local_kernel, "local_a", [wide, wide], *local, b, b)
    sa, ro, ri, pay = run(
        functools.partial(chip_a_kernel, hid + fin), "chip_a", [first, line, line, wide_pay],
        pay, got, *edges, b, l1, l2, after=ups[2:],
    )
    got = swap(pay, 1)
    l1, l2, gp = run(local_b_kernel, "local_b", [wide, wide, ((parts, 2 * hid, n), F32)], *local, sa, gw)
    sb, reset, update, y, pay = run(
        chip_b_kernel, "chip_b", [second, field, field, field16, pay_kind],
        pay, got, *edges, sa, l1, l2, ro, ri, gw, gate_bias[None, :], gp,
    )
    got = swap(pay, 1)
    l1, l2 = run(local_kernel, "local_c1", [field, field], *local, y, y)
    ma, pay = run(chip_c1_kernel, "chip_c1", [first, pay_kind], pay, got, *edges, y, sa, l1, l2, ro, ri)
    got = swap(pay, 1)
    l1, l2, cp = run(local_c2_kernel, "local_c2", [field, field, field], *local, ma, cw)
    mb, cand_grad, gate_update, y1, y2, g1, g3, up, direct, pay = run(
        functools.partial(chip_c2_kernel, parts), "chip_c2", [second] + [field16] * 7 + [field, pay_kind],
        *ups, pay, got, *edges, ma, sa, sb, l1, l2, ro, ri, cw, cw_b, cand_bias[None, :], cp, update,
    )
    got = swap(pay, 1)
    l1, l2, part = run(
        local_d_kernel, "local_d1", [field, field, ((hid, width), BF16)], *local, y1, y2, cand_grad, ma, mb, order
    )
    z1, z2, pay = run(
        chip_d1_kernel, "chip_d1", [field16, field16, pay_kind], pay, got, *edges, l1, l2, g1, g3, ro, ri
    )
    got = swap(pay, 1)
    (base,) = run(local_d2_kernel, "local_d2", [field], *local, z1, z2, direct)
    half = ((3 * hid // 2, width), BF16)
    gate_grad, kept, keep, give = run(
        chip_d2_kernel, "chip_d2", [((parts, 2 * hid, n), BF16), field, half, half],
        pay, got, hx, sx, base, sa, sb, reset, gate_update, order, part, scratch=[pltpu.VMEM((3 * hid, width), F32)],
    )
    y1, y2, g1, g3, direct, pay = run(
        back_e_kernel, "back_e", [field16] * 4 + [field, pay_kind], hc, sc, gate_grad, kept, ro, ri, gw_b, up, update
    )
    got = swap(pay, 1)
    l1, l2 = run(local_kernel, "local_e1", [field, field], *local, y1, y2)
    mine, sent = run(sum_kernel, "sum_core", [half] * 2, keep, swap(give, 1), after=[direct])
    every = [mine] + [swap(sent, k, "snap", snaps) for k in range(1, snaps)]
    z1, z2, pay = run(
        chip_d1_kernel, "chip_e1", [field16, field16, pay_kind], pay, got, *edges, l1, l2, g1, g3, ro, ri, after=[mine],
    )
    got = swap(pay, 1)
    (base,) = run(local_e_kernel, "local_e2", [((hid, n), F32)], early[0], early[1], z1, z2, direct)
    state_grad, done = run(
        chip_e_kernel, "chip_e2", [((1, hid, n), BF16), ((8, LANES), F32)], pay, got, *edges, base
    )
    mine, sent = run(sum_kernel, "sum_snap", [half] * 2, *every, after=[done])
    factor = 1.0 / math.sqrt(readings.shape[0] * snaps * n * nd)
    feats = orders * chans
    grad_gw, grad_gb, grad_cw, grad_cb = run(
        functools.partial(end_kernel, factor), "end",
        [((feats, 2 * hid), F32), ((1, 2 * hid), F32), ((hid, feats), F32), ((1, hid), F32)],
        mine, swap(sent, 1), scratch=[pltpu.VMEM((3 * hid, width), F32)],
    )
    return state_grad, grad_gw.T, grad_gb[0], grad_cw, grad_cb[0]


def body(*args):
    neighbours, send_rows = args[7], args[9]
    n = neighbours.shape[1]
    nd, snaps = lax.axis_size("dom"), lax.axis_size("snap")
    parts = nd // 2
    slots = 2 * parts * parts * (send_rows.shape[1] // nd)
    powers = nd & (nd - 1) == 0 and snaps & (snaps - 1) == 0 and nd > 2
    if powers and parts * (n + slots) * n * 2 <= 4 << 20:
        return chip_body(*args)
    return spread_body(*args)


def solution(mesh):
    in_specs = (
        P("snap", None, "dom"),
        P("snap", None, "dom"),
        P("snap", None, "dom"),
        P(),
        P(),
        P(),
        P(),
        P(None, "dom"),
        P(None, "dom"),
        P("dom", None),
    )
    out_specs = (P("snap", None, "dom"), P(), P(), P(), P())
    return jax.shard_map(body, mesh=mesh, in_specs=in_specs, out_specs=out_specs, check_vma=False)
```

```python
import functools
import math

import jax
import jax.numpy as jnp
from jax import lax
from jax.experimental import pallas as pl
from jax.experimental.pallas import tpu as pltpu
from jax.sharding import PartitionSpec as P

F32 = jnp.float32
BF16 = jnp.bfloat16
LANES = 128


def nn(a, b):
    return lax.dot_general(a, b, (((1,), (0,)), ((), ())), preferred_element_type=F32)


def nt(a, b):
    return lax.dot_general(a, b, (((1,), (1,)), ((), ())), preferred_element_type=F32)


def tn(a, b):
    return lax.dot_general(a, b, (((0,), (0,)), ((), ())), preferred_element_type=F32)


def iota(shape, axis):
    return lax.broadcasted_iota(jnp.int32, shape, axis)


def column(row):
    k = row.shape[1]
    spread = jnp.broadcast_to(row.astype(F32), (k, k))
    return jnp.sum(jnp.where(iota((k, k), 0) == iota((k, k), 1), spread, 0.0), axis=1, keepdims=True)


def run(kernel, name, outs, *args, scratch=(), flops=20_000_000, vmem=24, after=()):
    return pl.pallas_call(
        lambda *refs: kernel(*refs[len(after) :]),
        name=name,
        out_shape=[jax.ShapeDtypeStruct(shape, kind) for shape, kind in outs],
        in_specs=[pl.BlockSpec(memory_space=pl.ANY)] * len(after) + [pl.BlockSpec(memory_space=pltpu.VMEM)] * len(args),
        out_specs=[pl.BlockSpec(memory_space=pltpu.VMEM)] * len(outs),
        scratch_shapes=list(scratch),
        compiler_params=pltpu.CompilerParams(vmem_limit_bytes=vmem * 1024 * 1024),
        cost_estimate=pl.CostEstimate(flops=flops, bytes_accessed=2_000_000, transcendentals=0),
    )(*after, *args)


def prep_kernel(cap, nb, w, rows, readings, previous, e, s, b, pay):
    degree, n = nb.shape
    nh = s.shape[0]
    hid = previous.shape[1]
    fin = readings.shape[1]
    step = 32
    for at in range(0, n + nh, step):
        node = iota((step, n), 0) + at
        total = jnp.zeros((step, n), F32)
        for d in range(degree):
            total = total + jnp.where(node == nb[d : d + 1, :], w[d : d + 1, :], 0.0)
        e[at : at + step, :] = total.astype(BF16)
    sent = column(rows[...]).astype(jnp.int32)
    s[...] = jnp.where(iota((nh, n), 1) == sent, 1.0, 0.0).astype(BF16)
    b[:hid, :] = previous[0]
    rest = b.shape[0] - hid
    row = iota((rest, n), 0)
    tail = jnp.where(row == fin, 1.0, 0.0)
    for f in range(fin):
        tail = jnp.where(row == f, readings[0, f : f + 1, :].astype(F32), tail)
    b[hid:, :] = tail.astype(BF16)
    base = b[...]
    chans = base.shape[0]
    bound = nt(s[...], base)
    halo = nt(e[n:, :], base)
    for p in range(nh // cap):
        pay[p, :, :chans] = bound[p * cap : (p + 1) * cap, :]
        pay[p, :, LANES : LANES + chans] = halo[p * cap : (p + 1) * cap, :]


def order_matrix(shape, chans, hid, fin, block):
    k = iota(shape, 0)
    col = iota(shape, 1)
    m = lax.div(col, jnp.int32(block))
    c = col - m * block
    source = jnp.where(c < hid, m * chans + fin + c, jnp.where(c < hid + fin, m * chans + c - hid, -1))
    return jnp.where(k == source, 1.0, 0.0).astype(BF16)


def mid_a_kernel(hid, fin, orders, e, b, gw, cw, fa, ra, gw_o, cw_o):
    n = e.shape[1]
    a = e[:n, :]
    base = b[...]
    fa[...] = nt(base, a)
    ra[...] = nn(base, a)
    block = base.shape[0]
    order = order_matrix((gw.shape[1], orders * block), hid + fin, hid, fin, block)
    gw_o[...] = nn(gw[...], order).astype(BF16)
    cw_o[...] = nn(cw[...], order).astype(BF16)


def post_a_kernel(one, cap, recv, e, s, fa, ra, f1, r1, ro, ri, pay, flat):
    n = e.shape[1]
    nh = s.shape[0]
    chans = fa.shape[0]
    for p in range(nh // cap):
        flat[p * cap : (p + 1) * cap, :] = recv[p]
    h = e[n:, :]
    sel = s[...]
    seen = flat[:, :chans].astype(BF16)
    back = flat[:, LANES : LANES + chans]
    back_degree = flat[:, LANES + one : LANES + one + 1]
    out_degree = fa[one : one + 1, :] + jnp.sum(sel.astype(F32) * back_degree, axis=0, keepdims=True)
    pulled = ra[...] + tn(seen, h)
    inv_o = 1.0 / out_degree
    inv_i = 1.0 / pulled[one : one + 1, :]
    ro[...] = inv_o
    ri[...] = inv_i
    first_out = ((fa[...] + tn(back.astype(BF16), sel)) * inv_o).astype(BF16)
    first_in = (pulled * inv_i).astype(BF16)
    f1[...] = first_out
    r1[...] = first_in
    bound = nt(sel, first_in)
    halo = nt(h, first_out)
    hi, ho = scaled(h, inv_i), scaled(h, inv_o)
    si, so = scaled(sel, inv_i), scaled(sel, inv_o)
    coefs = (nt(sel, hi), nt(h, so), nt(sel, ho), nt(h, si))
    for p in range(nh // cap):
        at = slice(p * cap, (p + 1) * cap)
        pay[p, :, :chans] = bound[at, :]
        pay[p, :, LANES : LANES + chans] = halo[at, :]
        for k, coef in enumerate(coefs):
            pay[p, :, 2 * LANES + k * nh : 2 * LANES + (k + 1) * nh] = coef[at, :]


def scaled(rows, factor):
    return (rows.astype(F32) * factor).astype(BF16)


def mid_b_kernel(e, s, f1, r1, ro, ri, f2l, r2l, kc, ke, ka):
    n = e.shape[1]
    a = e[:n, :]
    h = e[n:, :]
    sel = s[...]
    nh = sel.shape[0]
    chans = f1.shape[0]
    inv_o, inv_i = ro[...], ri[...]
    outs = nt(jnp.concatenate([f1[...], scaled(sel, inv_o), scaled(sel, inv_i)], axis=0), a)
    ins = nn(jnp.concatenate([r1[...], scaled(h, inv_i), scaled(h, inv_o)], axis=0), a)
    f2l[...] = outs[:chans]
    r2l[...] = ins[:chans]
    kc[:nh, :] = ins[chans : chans + nh].astype(BF16)
    kc[nh:, :] = h
    ke[:nh, :] = outs[chans : chans + nh].astype(BF16)
    ke[nh:, :] = sel
    ka[:nh, :] = (2.0 * ins[chans + nh :]).astype(BF16)
    ka[nh : 2 * nh, :] = h
    ka[2 * nh : 3 * nh, :] = (2.0 * outs[chans + nh :]).astype(BF16)
    ka[3 * nh :, :] = sel


def send(pay, cap, left, right, left_two, right_two):
    nh = left.shape[0]
    rows = jnp.concatenate([left, right], axis=1)
    rows_two = jnp.concatenate([left_two, right_two], axis=1)
    both = jnp.concatenate([rows, rows_two], axis=0).astype(BF16)
    k = iota((2 * nh, 2 * nh), 0)
    part = lax.div(k, jnp.int32(2 * cap))
    spot = k - part * (2 * cap)
    source = jnp.where(spot < cap, part * cap + spot, nh + part * cap + spot - cap)
    mine = nn(jnp.where(iota((2 * nh, 2 * nh), 1) == source, 1.0, 0.0).astype(BF16), both)
    for p in range(nh // cap):
        own = mine[p * 2 * cap : (p + 1) * 2 * cap, :]
        pay[p] = jnp.concatenate([rows, own], axis=0).astype(BF16)


def post_b_kernel(cap, one, recv, e, s, b, f1, r1, f2l, r2l, ro, ri, gw, gb, states, reset, update, y, f1l, r1l, pay, flat):
    n = e.shape[1]
    nh = s.shape[0]
    hid = y.shape[0]
    chans = b.shape[0]
    for p in range(nh // cap):
        flat[p * cap : (p + 1) * cap, :] = recv[p, :, : 2 * LANES]
    a = e[:n, :]
    h = e[n:, :]
    sel = s[...]
    inv_o, inv_i = ro[...], ri[...]
    base = b[...].astype(F32)
    seen = flat[:, :chans].astype(BF16)
    back = flat[:, LANES : LANES + chans].astype(BF16)
    f2 = 2.0 * (f2l[...] + tn(back, sel)) * inv_o - base
    r2 = 2.0 * (r2l[...] + tn(seen, h)) * inv_i - base
    states[:chans, :] = b[...]
    states[chans : 2 * chans, :] = f1[...]
    states[2 * chans : 3 * chans, :] = f2.astype(BF16)
    states[3 * chans : 4 * chans, :] = r1[...]
    states[4 * chans :, :] = r2.astype(BF16)
    gates = jax.nn.sigmoid(nn(gw[...], states[...]) + column(gb[...]))
    reset[...] = gates[:hid]
    update[...] = gates[hid:]
    now = (gates[:hid] * base[:hid]).astype(BF16)
    y[...] = now
    local_out = nt(now, a) * inv_o
    local_in = nn(now, a) * inv_i
    f1l[...] = local_out
    r1l[...] = local_in
    bound = nt(sel, jnp.concatenate([now, local_in.astype(BF16)], axis=0))
    halo = nt(h, jnp.concatenate([now, local_out.astype(BF16)], axis=0))
    send(pay, cap, bound[:, :hid], halo[:, :hid], bound[:, hid:], halo[:, hid:])


def gather_matrix(coef, out, nd, cap, per, first, factor):
    nh = nd * cap
    width = nd * per
    k = iota((nh, width), 0)
    col = iota((nh, width), 1)
    r = lax.div(col, jnp.int32(per))
    u = col - r * per
    p = lax.div(u, jnp.int32(cap))
    spot = u - p * cap
    here = lax.div(k, jnp.int32(cap))
    slot = k - here * cap
    inside = u < nh
    place = jnp.where((k == r * cap + spot) & inside, 1.0, 0.0).astype(BF16)
    keep = (here == p) & inside
    for i in range(2):
        wide = nn(coef[:, (first + i) * nh : (first + i + 1) * nh].astype(BF16), place)
        own = (r == here) & (u == nh + cap + slot)
        out[(i + 1) * nh : (i + 2) * nh, :] = jnp.where(keep, factor * wide, jnp.where(own, 1.0, 0.0)).astype(BF16)
    out[:nh, :] = jnp.where((r == here) & (u == nh + slot), 1.0, 0.0).astype(BF16)


def mid_c_kernel(nd, cap, per, fused, recv, e, f1l, r1l, f2l, r2l, *rest):
    n = e.shape[1]
    a = e[:n, :]
    f2l[...] = nt(f1l[...].astype(BF16), a)
    r2l[...] = nn(r1l[...].astype(BF16), a)
    if fused:
        gd, ga, flat = rest
        for p in range(nd):
            flat[p * cap : (p + 1) * cap, :] = recv[p, :, 2 * LANES :]
        gather_matrix(flat, gd, nd, cap, per, 0, 1.0)
        gather_matrix(flat, ga, nd, cap, per, 2, 2.0)


def arrived(fused, hid, nh, g, recv):
    if fused:
        halo = nn(g[...], recv[...].reshape(recv.shape[0] * recv.shape[1], recv.shape[2]))
        two = halo[nh : 2 * nh, :hid], halo[2 * nh :, hid:]
    else:
        halo = recv[...]
        two = halo[nh:, :hid], halo[nh:, hid:]
    one = halo[:nh]
    return one[:, :hid], one[:, hid:], two[0], two[1]


def back_and_send(cap, hid, g, a, h, sel, inv_o, inv_i, z1, z2, pay):
    g0, g1, g2, g3, g4 = (g[m * hid : (m + 1) * hid, :].astype(BF16).astype(F32) for m in range(5))
    y1 = (g2 * inv_o).astype(BF16)
    y2 = (g4 * inv_i).astype(BF16)
    now1 = ((g1 + 2.0 * nn(y1, a)) * inv_o).astype(BF16)
    now2 = ((g3 + 2.0 * nt(y2, a)) * inv_i).astype(BF16)
    z1[...] = now1
    z2[...] = now2
    bound = nt(sel, jnp.concatenate([y1, now1], axis=0))
    halo = nt(h, jnp.concatenate([y2, now2], axis=0))
    send(pay, cap, bound[:, :hid], halo[:, :hid], bound[:, hid:], halo[:, hid:])
    return g0 - g2 - g4


def hidden_weights(w, hid, block, orders):
    return jnp.concatenate([w[:, m * block : m * block + hid] for m in range(orders)], axis=1)


def post_c_kernel(fused, cap, orders, g, recv, e, s, kc, ke, y, f1l, r1l, f2l, r2l, ro, ri, states, cw, cb, upstream, update,
                  mixed, cand_grad, gate_update, z1, z2, direct, pay):
    n = e.shape[1]
    nh = s.shape[0]
    hid = y.shape[0]
    block = states.shape[0] // orders
    a = e[:n, :]
    h = e[n:, :]
    sel = s[...]
    inv_o, inv_i = ro[...], ri[...]
    c1, e1, c2, e2 = arrived(fused, hid, nh, g, recv)
    base = y[...].astype(F32)
    c1, e1 = c1.astype(BF16), e1.astype(BF16)
    cc = jnp.concatenate([c1, c2.astype(BF16)], axis=0)
    ee = jnp.concatenate([e1, e2.astype(BF16)], axis=0)
    f1 = f1l[...] + tn(e1, sel) * inv_o
    f2 = 2.0 * (f2l[...] + tn(ee, ke[...])) * inv_o - base
    r1 = r1l[...] + tn(c1, h) * inv_i
    r2 = 2.0 * (r2l[...] + tn(cc, kc[...])) * inv_i - base
    for m, value in enumerate((y[...], f1, f2, r1, r2)):
        mixed[m * block : m * block + hid, :] = value.astype(BF16)
        mixed[m * block + hid : (m + 1) * block, :] = states[m * block + hid : (m + 1) * block, :]
    weights = cw[...]
    cand = jnp.tanh(nn(weights, mixed[...]) + column(cb[...]))
    up = upstream[0].astype(F32)
    gate = update[...]
    grad = (up * (1.0 - gate) * (1.0 - cand * cand)).astype(BF16)
    cand_grad[...] = grad
    held = states[:hid, :].astype(F32)
    gate_update[...] = (up * (held - cand) * gate * (1.0 - gate)).astype(BF16)
    back = tn(hidden_weights(weights, hid, block, orders), grad)
    direct[...] = back_and_send(cap, hid, back, a, h, sel, inv_o, inv_i, z1, z2, pay)


def weight_part(grad, features, orders, chans, hid, fin):
    block = features.shape[0] // orders
    width = -(-(orders * chans + 1) // LANES) * LANES
    shape = (width, orders * block)
    k = iota(shape, 0)
    col = iota(shape, 1)
    m = lax.div(col, jnp.int32(block))
    c = col - m * block
    source = jnp.where(c < hid, m * chans + fin + c, jnp.where(c < hid + fin, m * chans + c - hid, -1))
    source = jnp.where(col == hid + fin, orders * chans, source)
    order = jnp.where(k == source, 1.0, 0.0).astype(BF16)
    return nt(nt(grad, features).astype(BF16), order)


def mid_d_kernel(orders, fin, e, z1, z2, direct, cand_grad, mixed, gate_update, states, base, part):
    n = e.shape[1]
    a = e[:n, :]
    hid = z1.shape[0]
    base[...] = direct[...] + nn(z1[...], a) + nt(z2[...], a)
    part[:hid, :] = weight_part(gate_update[...], states[...], orders, hid + fin, hid, fin).astype(BF16)
    part[hid:, :] = weight_part(cand_grad[...], mixed[...], orders, hid + fin, hid, fin).astype(BF16)


def add_halo(fused, g, recv, ka, base):
    hid = base.shape[0]
    nh = ka.shape[0] // 4
    c1, e1, c2, e2 = arrived(fused, hid, nh, g, recv)
    return base[...] + tn(jnp.concatenate([c1, c2, e1, e2], axis=0).astype(BF16), ka[...])


def post_d_kernel(fused, cap, orders, g, recv, e, s, ka, base, ro, ri, states, gw, upstream, reset, update, gate_update,
                  gate_reset, z1, z2, direct, pay):
    n = e.shape[1]
    hid = base.shape[0]
    block = states.shape[0] // orders
    scaled_grad = add_halo(fused, g, recv, ka, base)
    held = states[:hid, :].astype(F32)
    gate = reset[...]
    grad = (scaled_grad * held * gate * (1.0 - gate)).astype(BF16)
    gate_reset[...] = grad
    weights = hidden_weights(gw[...], hid, block, orders)
    back = tn(weights, jnp.concatenate([grad, gate_update[...]], axis=0))
    rest = back_and_send(cap, hid, back, e[:n, :], e[n:, :], s[...], ro[...], ri[...], z1, z2, pay)
    direct[...] = rest + upstream[0].astype(F32) * update[...] + scaled_grad * gate


def mid_e_kernel(orders, fin, rows, e, z1, z2, direct, gate_reset, states, part, base, grads):
    n = e.shape[1]
    a = e[:n, :]
    hid = z1.shape[0]
    base[...] = direct[...] + nn(z1[...], a) + nt(z2[...], a)
    first = weight_part(gate_reset[...], states[...], orders, hid + fin, hid, fin)
    both = jnp.concatenate([first, part[...].astype(F32)], axis=0)
    for k in range(grads.shape[0]):
        if k * rows < both.shape[0]:
            grads[k] = both[k * rows : (k + 1) * rows, :].astype(BF16)
        else:
            grads[k] = jnp.zeros(grads.shape[1:], BF16)


def post_e_kernel(fused, g, recv, ka, base, out):
    out[0] = add_halo(fused, g, recv, ka, base).astype(BF16)


def add_kernel(recv, out):
    total = recv[0].astype(F32)
    for k in range(1, recv.shape[0]):
        total = total + recv[k].astype(F32)
    for k in range(out.shape[0]):
        out[k] = total.astype(BF16)


def finish_kernel(hid, factor, recv, gw, gb, cw, cb):
    rows = recv.shape[1]
    features = gw.shape[1]
    total = gw.shape[0] + cw.shape[0]
    for k in range(total // rows):
        part = recv[k].astype(F32)[:, :features] * factor
        at = k * rows
        if at < 2 * hid:
            gw[at : at + rows, :] = part
        else:
            cw[at - 2 * hid : at - 2 * hid + rows, :] = part
    flat = jnp.concatenate([recv[k].astype(F32) for k in range(total // rows)], axis=0)
    pick = jnp.where(iota((8, flat.shape[1]), 1) == features, 1.0, 0.0).astype(BF16)
    bias = nt(pick, flat.astype(BF16))[:1] * factor
    gb[...] = bias[:, : 2 * hid]
    cb[...] = bias[:, 2 * hid :]


def spread_body(
    readings,
    previous,
    upstream,
    gate_weight,
    gate_bias,
    cand_weight,
    cand_bias,
    neighbours,
    edge_weight,
    send_rows,
):
    fin, hid = readings.shape[1], previous.shape[1]
    chans = fin + hid
    orders = gate_weight.shape[1] // chans
    n = readings.shape[2]
    nd = lax.axis_size("dom")
    devices = nd * lax.axis_size("snap")
    nh = send_rows.shape[1]
    cap = nh // nd
    block = hid + 16 * (-(-(fin + 1) // 16))
    one = hid + fin
    per = nh + 2 * cap
    fused = 3 * nh * nd * per <= 1 << 18
    move = functools.partial(lax.all_to_all, axis_name="dom", split_axis=0, concat_axis=0, tiled=True)

    e, s, b, pay = run(
        functools.partial(prep_kernel, cap), "prep",
        [((n + nh, n), BF16), ((nh, n), BF16), ((block, n), BF16), ((nd, cap, 2 * LANES), F32)],
        neighbours, edge_weight, send_rows, readings, previous,
    )
    recv = move(pay)
    fa, ra, gw, cw = run(
        functools.partial(mid_a_kernel, hid, fin, orders), "mid_a",
        [((block, n), F32), ((block, n), F32), ((2 * hid, orders * block), BF16), ((hid, orders * block), BF16)],
        e, b, gate_weight, cand_weight,
    )
    wide = 2 * LANES + 4 * nh
    f1, r1, ro, ri, pay = run(
        functools.partial(post_a_kernel, one, cap), "post_a",
        [((block, n), BF16), ((block, n), BF16), ((1, n), F32), ((1, n), F32), ((nd, cap, wide), F32)],
        recv, e, s, fa, ra, scratch=[pltpu.VMEM((nh, 2 * LANES), F32)],
    )
    recv_b = move(pay)
    f2l, r2l, kc, ke, ka = run(
        mid_b_kernel, "mid_b",
        [((block, n), F32), ((block, n), F32), ((2 * nh, n), BF16), ((2 * nh, n), BF16), ((4 * nh, n), BF16)],
        e, s, f1, r1, ro, ri,
    )
    pay_kind = ((nd, per, 2 * hid), BF16)
    field, field16 = ((hid, n), F32), ((hid, n), BF16)
    states, reset, update, y, f1l, r1l, pay = run(
        functools.partial(post_b_kernel, cap, one), "post_b",
        [((orders * block, n), BF16), field, field, field16, field, field, pay_kind],
        recv_b, e, s, b, f1, r1, f2l, r2l, ro, ri, gw, gate_bias[None, :],
        scratch=[pltpu.VMEM((nh, 2 * LANES), F32)],
    )
    recv = move(pay)
    table = ((3 * nh, nd * per), BF16)
    f2l, r2l, *tables = run(
        functools.partial(mid_c_kernel, nd, cap, per, fused), "mid_c",
        [field, field] + [table] * (2 if fused else 0),
        recv_b, e, f1l, r1l, scratch=[pltpu.VMEM((nh, 4 * nh), F32)] if fused else [],
    )
    if fused:
        inward, outward = tables
        halo_of = lambda got, first, factor: got
    else:
        inward = outward = jnp.zeros((8, LANES), BF16)
        coefs = recv_b[:, :, 2 * LANES :].reshape(nd, cap, 4, nd, cap)

        def halo_of(got, first, factor):
            rows = got[:, :nh].reshape(nd, nd, cap, 2, hid).astype(F32)
            two = jnp.einsum("psgrt,rptgk->psgk", coefs[:, :, first : first + 2], rows)
            two = factor * two.reshape(nh, 2 * hid) + got[:, nh + cap :].reshape(nh, 2 * hid).astype(F32)
            return jnp.concatenate([got[:, nh : nh + cap].reshape(nh, 2 * hid).astype(F32), two], axis=0)

    mixed, cand_grad, gate_update, z1, z2, direct, pay = run(
        functools.partial(post_c_kernel, fused, cap, orders), "post_c",
        [((orders * block, n), BF16), field16, field16, field16, field16, field, pay_kind],
        inward, halo_of(recv, 0, 1.0), e, s, kc, ke, y, f1l, r1l, f2l, r2l, ro, ri, states, cw, cand_bias[None, :], upstream, update,
    )
    recv = move(pay)
    width = -(-(orders * chans + 1) // LANES) * LANES
    base, part = run(
        functools.partial(mid_d_kernel, orders, fin), "mid_d", [field, ((2 * hid, width), BF16)],
        e, z1, z2, direct, cand_grad, mixed, gate_update, states,
    )
    gate_reset, z1, z2, direct, pay = run(
        functools.partial(post_d_kernel, fused, cap, orders), "post_d",
        [field16, field16, field16, field, pay_kind],
        outward, halo_of(recv, 2, 2.0), e, s, ka, base, ro, ri, states, gw, upstream, reset, update, gate_update,
    )
    recv = move(pay)
    rows = 8 * (-(-3 * hid // (8 * devices)))
    base, grads = run(
        functools.partial(mid_e_kernel, orders, fin, rows), "mid_e", [field, ((devices, rows, width), BF16)],
        e, z1, z2, direct, gate_reset, states, part,
    )
    (state_grad,) = run(
        functools.partial(post_e_kernel, fused), "post_e", [((1, hid, n), BF16)],
        outward, halo_of(recv, 2, 2.0), ka, base,
    )
    both = ("snap", "dom")
    grads = lax.all_to_all(grads, both, 0, 0, tiled=True)
    (grads,) = run(add_kernel, "add", [((devices, rows, width), BF16)], grads)
    grads = lax.all_to_all(grads, both, 0, 0, tiled=True)
    factor = 1.0 / math.sqrt(readings.shape[0] * lax.axis_size("snap") * n * nd)
    feats = orders * chans
    grad_gw, grad_gb, grad_cw, grad_cb = run(
        functools.partial(finish_kernel, hid, factor), "finish",
        [((2 * hid, feats), F32), ((1, 2 * hid), F32), ((hid, feats), F32), ((1, hid), F32)],
        grads,
    )
    return state_grad, grad_gw, grad_gb[0], grad_cw, grad_cb[0]


def pack_kernel(nb, w, rows, readings, previous, upstream, own, both, tail):
    degree = nb.shape[0]
    nh = rows.shape[1]
    hid = previous.shape[1]
    fin = readings.shape[1]
    block = own.shape[0]
    tail[...] = jnp.zeros_like(tail)
    tail[:fin, :] = readings[0].astype(F32)
    high = lax.shift_right_logical(nb[...], 5)
    tail[fin : fin + degree, :] = high.astype(F32)
    tail[fin + degree : fin + 2 * degree, :] = (nb[...] - high * 32).astype(F32)
    tail[fin + 2 * degree : fin + 3 * degree, :] = w[...]
    at = fin + 3 * degree
    high = lax.shift_right_logical(rows[...], 5)
    tail[at : at + 1, :nh] = high.astype(F32)
    tail[at + 1 : at + 2, :nh] = (rows[...] - high * 32).astype(F32)
    for to in (own, both):
        to[:hid, :] = previous[0]
        to[hid:block, :] = tail[...].astype(BF16)
    both[block:, :] = upstream[0]


def exchange(first, second, hc, sc, pay):
    count = first[0].shape[0]
    parts = len(first)
    pay[:count, :] = jnp.concatenate([nt(first[p], sc[p]).astype(BF16) for p in range(parts)], axis=1)
    pay[count:, :] = jnp.concatenate([nt(second[p], hc[p]).astype(BF16) for p in range(parts)], axis=1)


def merged(parts, mine, got):
    step = mine.shape[1] // (2 * parts)
    here = lax.rem(lax.div(iota(mine.shape, 1), jnp.int32(step)), jnp.int32(2)) == 0
    value = jnp.where(here, mine[...].astype(F32), got[...].astype(F32)).astype(BF16)
    count = mine.shape[0] // 2
    return value[:count, :], value[count:, :]


def build_part(cap, hid, fin, degree, parts, p, block, a, at, hc, hx, sc, sx, b):
    n = a.shape[1]
    slots = sx.shape[0]
    nh = 2 * parts * cap
    half = parts * cap
    core = lax.rem(lax.axis_index("dom"), 2)
    line = iota((nh, 1), 0)
    rel = lax.div(line, jnp.int32(half))
    k = lax.div(line - rel * half, jnp.int32(cap))
    t = line - rel * half - k * cap
    spot = (k * 2 + lax.bitwise_xor(rel, core)) * cap + t
    node = (n + spot).astype(F32)
    width = -(-nh // LANES) * LANES
    slot = iota((slots, nh), 0)
    outer = lax.div(slot, jnp.int32(nh))
    rest = slot - outer * nh
    slot_rel = lax.div(rest, jnp.int32(half))
    rest = rest - slot_rel * half
    inner = lax.div(rest, jnp.int32(cap))
    filled = iota((slots, nh), 1) == slot_rel * half + outer * cap + rest - inner * cap
    row = iota((32, n), 0).astype(F32)
    edges = hid + fin + 3 * degree + 2
    tail = block[hid : hid + 16 * (-(-(edges - hid) // 16)), :].astype(F32)
    high, low = tail[fin : fin + degree], tail[fin + degree : fin + 2 * degree]
    w = tail[fin + 2 * degree : fin + 3 * degree]
    start = fin + 3 * degree
    sent = tail[start : start + 1] * 32.0 + tail[start + 1 : start + 2]
    low_is = [jnp.where(low[d : d + 1] == row, 1.0, 0.0).astype(BF16) for d in range(degree)]
    for chunk in range(n // 32):
        total = None
        for d in range(degree):
            term = low_is[d] * jnp.where(high[d : d + 1] == float(chunk), w[d : d + 1], 0.0).astype(BF16)
            total = term if total is None else total + term
        a[chunk * 32 : (chunk + 1) * 32, :] = total
    at[...] = a[...].T
    names = high * 32.0 + low
    total = jnp.zeros((nh, n), F32)
    for d in range(degree):
        total = total + jnp.where(names[d : d + 1] == node, w[d : d + 1], 0.0)
    halo = total.astype(BF16)
    hc[...] = halo
    named = jnp.where(iota((nh, width), 1) == spot, sent[:, :width], 0.0)
    target = jnp.sum(named, axis=1, keepdims=True).astype(jnp.int32)
    picked = jnp.where(iota((nh, n), 1) == target, 1.0, 0.0).astype(BF16)
    sc[...] = picked
    place = jnp.where(filled & (inner == p), 1.0, 0.0).astype(BF16)
    hx[...] = nn(place, halo).astype(BF16)
    sx[...] = nn(place, picked).astype(BF16)
    b[:hid, :] = block[:hid, :]
    line = iota(tail.shape, 0)
    b[hid:, :] = jnp.where(line < fin, tail, jnp.where(line == fin, 1.0, 0.0)).astype(BF16)


def build_early_kernel(cap, hid, fin, degree, parts, *refs):
    count = parts - 1
    z = lax.shift_right_logical(lax.axis_index("dom"), 1)
    for k in range(count):
        p = lax.bitwise_xor(z, jnp.int32(k))
        build_part(cap, hid, fin, degree, parts, p, refs[k], *(ref.at[k] for ref in refs[count:]))


def build_late_kernel(cap, hid, fin, degree, parts, last, *refs):
    early, outs, pay = refs[:5], refs[5:12], refs[12]
    z = lax.shift_right_logical(lax.axis_index("dom"), 1)
    for k in range(parts - 1):
        p = lax.bitwise_xor(z, jnp.int32(k))
        for source, to in zip(early, outs[2:]):
            to[p] = source[k]
    p = lax.bitwise_xor(z, jnp.int32(parts - 1))
    build_part(cap, hid, fin, degree, parts, p, last, outs[0].at[0], outs[1].at[0], *(ref.at[p] for ref in outs[2:]))
    hc, sc, b = outs[2], outs[4], outs[6]
    base = [b[p] for p in range(parts)]
    exchange(base, base, hc, sc, pay)


def chip_source(col, chans, hid, fin, block):
    m = lax.div(col, jnp.int32(block))
    c = col - m * block
    m = jnp.where(m == 2, 3, jnp.where(m == 3, 2, m))
    return m, c, jnp.where(c < hid, m * chans + fin + c, jnp.where(c < hid + fin, m * chans + c - hid, -1))


def order_kernel(hid, fin, orders, block, gw, cw, gw_o, cw_o, gw_b, cw_b, order):
    chans = hid + fin
    feats = cw.shape[1]
    shape = (feats, orders * block)
    source = chip_source(iota(shape, 1), chans, hid, fin, block)[2]
    pick = jnp.where(iota(shape, 0) == source, 1.0, 0.0).astype(BF16)
    gw_o[...] = tn(gw[...], pick).astype(BF16)
    cw_o[...] = nn(cw[...], pick).astype(BF16)
    shape = (orders * hid, feats)
    line = iota(shape, 0)
    m = lax.div(line, jnp.int32(hid))
    pick = jnp.where(iota(shape, 1) == m * chans + fin + line - m * hid, 1.0, 0.0).astype(BF16)
    gw_b[...] = nn(pick, gw[...]).astype(BF16)
    cw_b[...] = nt(pick, cw[...]).astype(BF16)
    m, c, source = chip_source(iota(order.shape, 0), chans, hid, fin, block)
    source = jnp.where((m == 0) & (c == hid + fin), feats, source)
    order[...] = jnp.where(iota(order.shape, 1) == source, 1.0, 0.0).astype(BF16)


def here(early, late, k):
    z = lax.shift_right_logical(lax.axis_index("dom"), 1)
    count = early.shape[0]
    return lax.bitwise_xor(z, jnp.int32(k)), early[k] if k < count else late[k - count]


def local_kernel(a0, at0, a1, at1, x1, x2, l1, l2):
    for k in range(x1.shape[0]):
        p, a = here(a0, a1, k)
        l1[p] = nn(x1[p], a)
    for k in range(x1.shape[0]):
        p, at = here(at0, at1, k)
        l2[p] = nn(x2[p], at)


def arrive(sx, hx, mine, got, l1, l2):
    parts = range(sx.shape[0])
    top, low = merged(sx.shape[0], mine, got)
    pulled = [l1[p] + nn(top, hx[p]) for p in parts]
    pushed = [l2[p] + nn(low, sx[p]) for p in parts]
    return parts, pulled, pushed


def chip_a_kernel(one, mine, got, hc, hx, sc, sx, b, l1, l2, sa, ro, ri, pay):
    chans = b.shape[1]
    parts, pulled, pushed = arrive(sx, hx, mine, got, l1, l2)
    inv_o = [1.0 / pushed[p][one : one + 1, :] for p in parts]
    inv_i = [1.0 / pulled[p][one : one + 1, :] for p in parts]
    outs = [(pushed[p] * inv_o[p]).astype(BF16) for p in parts]
    ins = [(pulled[p] * inv_i[p]).astype(BF16) for p in parts]
    for p in parts:
        ro[p] = inv_o[p]
        ri[p] = inv_i[p]
        sa[p, :chans, :] = b[p]
        sa[p, chans : 2 * chans, :] = outs[p]
        sa[p, 2 * chans :, :] = ins[p]
    exchange(ins, outs, hc, sc, pay)


def local_b_kernel(a0, at0, a1, at1, sa, gw, l1, l2, gp):
    chans = l1.shape[1]
    weights = gw[:, : 3 * chans]
    for k in range(sa.shape[0]):
        p, a = here(a0, a1, k)
        l1[p] = nn(sa[p, 2 * chans :, :], a)
    for k in range(sa.shape[0]):
        p, at = here(at0, at1, k)
        l2[p] = nn(sa[p, chans : 2 * chans, :], at)
    for p in range(sa.shape[0]):
        gp[p] = nn(weights, sa[p])


def chip_b_kernel(mine, got, hc, hx, sc, sx, sa, l1, l2, ro, ri, gw, gb, gp, sb, reset, update, y, pay):
    hid = y.shape[1]
    chans = l1.shape[1]
    bias = column(gb[...])
    weights = gw[:, 3 * chans :]
    parts, pulled, pushed = arrive(sx, hx, mine, got, l1, l2)
    base = [sa[p, :chans, :].astype(F32) for p in parts]
    r2 = [(pulled[p] * (2.0 * ri[p]) - base[p]).astype(BF16) for p in parts]
    f2 = [(pushed[p] * (2.0 * ro[p]) - base[p]).astype(BF16) for p in parts]
    second = [jnp.concatenate([f2[p], r2[p]], axis=0) for p in parts]
    gates = [jax.nn.sigmoid(gp[p] + nn(weights, second[p]) + bias) for p in parts]
    now = [(gates[p][:hid] * base[p][:hid]).astype(BF16) for p in parts]
    for p in parts:
        sb[p] = second[p]
        reset[p] = gates[p][:hid]
        update[p] = gates[p][hid:]
        y[p] = now[p]
    exchange(now, now, hc, sc, pay)


def chip_c1_kernel(mine, got, hc, hx, sc, sx, y, sa, l1, l2, ro, ri, ma, pay):
    hid = y.shape[1]
    chans = ma.shape[1] // 3
    parts, pulled, pushed = arrive(sx, hx, mine, got, l1, l2)
    ins = [(pulled[p] * ri[p]).astype(BF16) for p in parts]
    outs = [(pushed[p] * ro[p]).astype(BF16) for p in parts]
    exchange(ins, outs, hc, sc, pay)
    for p in parts:
        for m, value in enumerate((y[p], outs[p], ins[p])):
            ma[p, m * chans : m * chans + hid, :] = value
            ma[p, m * chans + hid : (m + 1) * chans, :] = sa[p, m * chans + hid : (m + 1) * chans, :]


def local_c2_kernel(a0, at0, a1, at1, ma, cw, l1, l2, cp):
    hid = l1.shape[1]
    chans = ma.shape[1] // 3
    weights = cw[:, : 3 * chans]
    for k in range(ma.shape[0]):
        p, a = here(a0, a1, k)
        l1[p] = nn(ma[p, 2 * chans : 2 * chans + hid, :], a)
    for k in range(ma.shape[0]):
        p, at = here(at0, at1, k)
        l2[p] = nn(ma[p, chans : chans + hid, :], at)
    for p in range(ma.shape[0]):
        cp[p] = nn(weights, ma[p])


def split_back(back, hid, ro, ri, y1, y2, g1, g3, direct):
    parts = range(len(back))
    blocks = [[back[p][m * hid : (m + 1) * hid, :] for m in range(5)] for p in parts]
    one = [(blocks[p][2] * (2.0 * ro[p])).astype(BF16) for p in parts]
    two = [(blocks[p][4] * (2.0 * ri[p])).astype(BF16) for p in parts]
    for p in parts:
        y1[p] = one[p]
        y2[p] = two[p]
        g1[p] = blocks[p][1].astype(BF16)
        g3[p] = blocks[p][3].astype(BF16)
        direct[p] = blocks[p][0] - blocks[p][2] - blocks[p][4]
    return one, two


def chip_c2_kernel(parts, *refs):
    ups, refs = refs[:parts], refs[parts:]
    mine, got, hc, hx, sc, sx, ma, sa, sb, l1, l2, ro, ri, cw, cw_b, cb, cp, update = refs[:18]
    mb, cand_grad, gate_update, y1, y2, g1, g3, upstream, direct, pay = refs[18:]
    hid = l1.shape[1]
    chans = ma.shape[1] // 3
    z = lax.shift_right_logical(lax.axis_index("dom"), 1)
    for k in range(parts):
        upstream[lax.bitwise_xor(z, jnp.int32(k))] = ups[k][0] if len(ups[k].shape) == 3 else ups[k][ups[k].shape[0] - hid :, :]
    bias = column(cb[...])
    weights = cw[:, 3 * chans :]
    parts, pulled, pushed = arrive(sx, hx, mine, got, l1, l2)
    base = [ma[p, :hid, :].astype(F32) for p in parts]
    r2 = [(pulled[p] * (2.0 * ri[p]) - base[p]).astype(BF16) for p in parts]
    f2 = [(pushed[p] * (2.0 * ro[p]) - base[p]).astype(BF16) for p in parts]
    second = [
        jnp.concatenate([f2[p], sb[p, hid:chans, :], r2[p], sb[p, chans + hid :, :]], axis=0) for p in parts
    ]
    cand = [jnp.tanh(cp[p] + nn(weights, second[p]) + bias) for p in parts]
    rest = [upstream[p].astype(F32) * (1.0 - update[p]) for p in parts]
    grad = [(rest[p] - rest[p] * cand[p] * cand[p]).astype(BF16) for p in parts]
    back = [nn(cw_b[...], grad[p]) for p in parts]
    for p in parts:
        mb[p] = second[p]
        cand_grad[p] = grad[p]
        gate_update[p] = ((sa[p, :hid, :].astype(F32) - cand[p]) * (rest[p] * update[p])).astype(BF16)
    one, two = split_back(back, hid, ro, ri, y1, y2, g1, g3, direct)
    exchange(one, two, hc, sc, pay)


def chip_part(grads, first, second, order):
    parts = range(first.shape[0])
    split = first.shape[1]
    one = sum(nt(grads[p], first[p]) for p in parts).astype(BF16)
    two = sum(nt(grads[p], second[p]) for p in parts).astype(BF16)
    return nn(one, order[:split, :]) + nn(two, order[split:, :])


def local_d_kernel(a0, at0, a1, at1, y1, y2, cand_grad, ma, mb, order, l1, l2, part):
    local_kernel(a0, at0, a1, at1, y1, y2, l1, l2)
    part[...] = chip_part(cand_grad, ma, mb, order).astype(BF16)


def chip_d1_kernel(mine, got, hc, hx, sc, sx, l1, l2, g1, g3, ro, ri, z1, z2, pay):
    parts, pulled, pushed = arrive(sx, hx, mine, got, l1, l2)
    one = [((g1[p].astype(F32) + pulled[p]) * ro[p]).astype(BF16) for p in parts]
    two = [((g3[p].astype(F32) + pushed[p]) * ri[p]).astype(BF16) for p in parts]
    exchange(one, two, hc, sc, pay)
    for p in parts:
        z1[p] = one[p]
        z2[p] = two[p]


def local_d2_kernel(a0, at0, a1, at1, z1, z2, direct, base):
    for k in range(z1.shape[0]):
        p, a = here(a0, a1, k)
        _, at = here(at0, at1, k)
        base[p] = direct[p] + nn(z1[p], a) + nn(z2[p], at)


def chip_d2_kernel(mine, got, hx, sx, base, sa, sb, reset, gate_update, order, part, gate_grad, kept, keep, give, flat):
    hid = base.shape[1]
    both = 2 * hid
    half = keep.shape[0]
    core = lax.rem(lax.axis_index("dom"), 2)
    parts = range(sx.shape[0])
    top, low = merged(sx.shape[0], mine, got)
    scaled_grad = [base[p] + nn(top, hx[p]) + nn(low, sx[p]) for p in parts]
    through = [scaled_grad[p] * reset[p] for p in parts]
    grad = [
        jnp.concatenate([(sa[p, :hid, :].astype(F32) * (through[p] - through[p] * reset[p])).astype(BF16), gate_update[p]], axis=0)
        for p in parts
    ]
    for p in parts:
        gate_grad[p] = grad[p]
        kept[p] = through[p]
    flat[:both, :] = chip_part(grad, sa, sb, order)
    flat[both:, :] = part[...].astype(F32)
    keep[...] = flat[pl.ds(pl.multiple_of(core * half, 8), half), :].astype(BF16)
    give[...] = flat[pl.ds(pl.multiple_of((1 - core) * half, 8), half), :].astype(BF16)


def back_e_kernel(hc, sc, gate_grad, kept, ro, ri, gw_b, upstream, update, y1, y2, g1, g3, direct, pay):
    hid = kept.shape[1]
    parts = range(sc.shape[0])
    back = [nn(gw_b[...], gate_grad[p]) for p in parts]
    one, two = split_back(back, hid, ro, ri, y1, y2, g1, g3, direct)
    for p in parts:
        direct[p] = direct[p] + upstream[p].astype(F32) * update[p] + kept[p]
    exchange(one, two, hc, sc, pay)


def local_e_kernel(a, at, z1, z2, direct, base):
    z = lax.shift_right_logical(lax.axis_index("dom"), 1)
    base[...] = direct[z] + nn(z1[z], a[0]) + nn(z2[z], at[0])


def chip_e_kernel(mine, got, hc, hx, sc, sx, base, out, done):
    done[...] = jnp.zeros_like(done)
    z = lax.shift_right_logical(lax.axis_index("dom"), 1)
    top, low = merged(sx.shape[0], mine, got)
    out[0] = (base[...] + nn(top, hx[z]) + nn(low, sx[z])).astype(BF16)


def sum_kernel(*refs):
    values = [ref[...].astype(F32) for ref in refs[:-2]]
    while len(values) > 1:
        values = [values[k] + values[k + 1] for k in range(0, len(values), 2)]
    refs[-1][...] = values[0].astype(refs[-1].dtype)
    refs[-2][...] = values[0].astype(refs[-2].dtype)


def end_kernel(factor, mine, got, gw, gb, cw, cb, flat):
    half = mine.shape[0]
    core = lax.rem(lax.axis_index("dom"), 2)
    flat[pl.ds(pl.multiple_of(core * half, 8), half), :] = mine[...] * factor
    flat[pl.ds(pl.multiple_of((1 - core) * half, 8), half), :] = got[...] * factor
    features, rows = gw.shape
    gates = flat[:rows, :].T
    gw[...] = gates[:features, :]
    gb[...] = gates[features : features + 1, :]
    cw[...] = flat[rows:, :features]
    last = (features // LANES) * LANES
    cb[...] = flat[rows:, last : last + LANES].T[features - last : features - last + 1, :]


def chip_body(
    readings,
    previous,
    upstream,
    gate_weight,
    gate_bias,
    cand_weight,
    cand_bias,
    neighbours,
    edge_weight,
    send_rows,
):
    fin, hid = readings.shape[1], previous.shape[1]
    chans = fin + hid
    orders = gate_weight.shape[1] // chans
    degree = neighbours.shape[0]
    n = readings.shape[2]
    nd = lax.axis_size("dom")
    snaps = lax.axis_size("snap")
    parts = nd // 2
    cap = send_rows.shape[1] // nd
    block = hid + 16 * (-(-(fin + 3 * degree + 2) // 16))
    slots = 2 * parts * parts * cap

    def swap(array, k, axis="dom", size=nd):
        return lax.ppermute(array, axis, [(i, i ^ k) for i in range(size)])

    own, both = run(
        pack_kernel, "pack", [((block, n), BF16), ((block + hid, n), BF16)],
        neighbours, edge_weight, send_rows, readings, previous, upstream,
        scratch=[pltpu.VMEM((block - hid, n), F32)], vmem=56,
    )
    near = swap(both, 2)
    blocks = [own] + [near if k == 1 else swap(own, 2 * k) for k in range(1, parts - 1)]
    relay = blocks[-1]
    ups = [upstream] + [near if k == 1 else swap(upstream, 2 * k) for k in range(1, parts - 1)]
    ups.append(swap(ups[-1], 2))
    width = -(-(orders * chans + 1) // LANES) * LANES
    gw, cw, gw_b, cw_b, order = run(
        functools.partial(order_kernel, hid, fin, orders, block), "order",
        [((2 * hid, orders * block), BF16), ((hid, orders * block), BF16), ((orders * hid, 2 * hid), BF16), ((orders * hid, hid), BF16),
         ((orders * block, width), BF16)],
        gate_weight.T, cand_weight, after=[own],
    )
    relay, gw = lax.optimization_barrier((relay, gw))
    wide, wide16, wide_pay = ((parts, block, n), F32), ((parts, block, n), BF16), ((2 * block, slots), BF16)
    field, field16, pay_kind = ((parts, hid, n), F32), ((parts, hid, n), BF16), ((2 * hid, slots), BF16)
    first, second = ((parts, 3 * block, n), BF16), ((parts, 2 * block, n), BF16)
    line = ((parts, 1, n), F32)
    built = [((n, n), BF16)] * 2 + [((rows, n), BF16) for rows in (2 * parts * cap, slots)] * 2 + [((block, n), BF16)]
    early = run(
        functools.partial(build_early_kernel, cap, hid, fin, degree, parts), "build_early",
        [((parts - 1, *shape), kind) for shape, kind in built], *blocks[:-1], relay,
    )
    a, at, hc, hx, sc, sx, b, pay = run(
        functools.partial(build_late_kernel, cap, hid, fin, degree, parts), "build_late",
        [((1 if shape == (n, n) else parts, *shape), kind) for shape, kind in built] + [wide_pay],
        swap(relay, 2), *early[2:],
    )
    local = (early[0], early[1], a, at)
    edges = (hc, hx, sc, sx)
    got = swap(pay, 1)
    l1, l2 = run(local_kernel, "local_a", [wide, wide], *local, b, b)
    sa, ro, ri, pay = run(
        functools.partial(chip_a_kernel, hid + fin), "chip_a", [first, line, line, wide_pay],
        pay, got, *edges, b, l1, l2, after=ups[2:],
    )
    got = swap(pay, 1)
    l1, l2, gp = run(local_b_kernel, "local_b", [wide, wide, ((parts, 2 * hid, n), F32)], *local, sa, gw)
    sb, reset, update, y, pay = run(
        chip_b_kernel, "chip_b", [second, field, field, field16, pay_kind],
        pay, got, *edges, sa, l1, l2, ro, ri, gw, gate_bias[None, :], gp,
    )
    got = swap(pay, 1)
    l1, l2 = run(local_kernel, "local_c1", [field, field], *local, y, y)
    ma, pay = run(chip_c1_kernel, "chip_c1", [first, pay_kind], pay, got, *edges, y, sa, l1, l2, ro, ri)
    got = swap(pay, 1)
    l1, l2, cp = run(local_c2_kernel, "local_c2", [field, field, field], *local, ma, cw)
    mb, cand_grad, gate_update, y1, y2, g1, g3, up, direct, pay = run(
        functools.partial(chip_c2_kernel, parts), "chip_c2", [second] + [field16] * 7 + [field, pay_kind],
        *ups, pay, got, *edges, ma, sa, sb, l1, l2, ro, ri, cw, cw_b, cand_bias[None, :], cp, update,
    )
    got = swap(pay, 1)
    l1, l2, part = run(
        local_d_kernel, "local_d1", [field, field, ((hid, width), BF16)], *local, y1, y2, cand_grad, ma, mb, order
    )
    z1, z2, pay = run(
        chip_d1_kernel, "chip_d1", [field16, field16, pay_kind], pay, got, *edges, l1, l2, g1, g3, ro, ri
    )
    got = swap(pay, 1)
    (base,) = run(local_d2_kernel, "local_d2", [field], *local, z1, z2, direct)
    half = ((3 * hid // 2, width), BF16)
    gate_grad, kept, keep, give = run(
        chip_d2_kernel, "chip_d2", [((parts, 2 * hid, n), BF16), field, half, half],
        pay, got, hx, sx, base, sa, sb, reset, gate_update, order, part, scratch=[pltpu.VMEM((3 * hid, width), F32)],
    )
    y1, y2, g1, g3, direct, pay = run(
        back_e_kernel, "back_e", [field16] * 4 + [field, pay_kind], hc, sc, gate_grad, kept, ro, ri, gw_b, up, update
    )
    got = swap(pay, 1)
    l1, l2 = run(local_kernel, "local_e1", [field, field], *local, y1, y2)
    mine, sent = run(sum_kernel, "sum_core", [half] * 2, keep, swap(give, 1), after=[direct])
    every = [mine] + [swap(sent, k, "snap", snaps) for k in range(1, snaps)]
    z1, z2, pay = run(
        chip_d1_kernel, "chip_e1", [field16, field16, pay_kind], pay, got, *edges, l1, l2, g1, g3, ro, ri, after=[mine],
    )
    got = swap(pay, 1)
    (base,) = run(local_e_kernel, "local_e2", [((hid, n), F32)], early[0], early[1], z1, z2, direct)
    state_grad, done = run(
        chip_e_kernel, "chip_e2", [((1, hid, n), BF16), ((8, LANES), F32)], pay, got, *edges, base
    )
    mine, sent = run(sum_kernel, "sum_snap", [(half[0], F32)] * 2, *every, after=[done])
    factor = 1.0 / math.sqrt(readings.shape[0] * snaps * n * nd)
    feats = orders * chans
    grad_gw, grad_gb, grad_cw, grad_cb = run(
        functools.partial(end_kernel, factor), "end",
        [((feats, 2 * hid), F32), ((1, 2 * hid), F32), ((hid, feats), F32), ((1, hid), F32)],
        mine, swap(sent, 1), scratch=[pltpu.VMEM((3 * hid, width), F32)],
    )
    return state_grad, grad_gw.T, grad_gb[0], grad_cw, grad_cb[0]


def body(*args):
    neighbours, send_rows = args[7], args[9]
    n = neighbours.shape[1]
    nd, snaps = lax.axis_size("dom"), lax.axis_size("snap")
    parts = nd // 2
    slots = 2 * parts * parts * (send_rows.shape[1] // nd)
    powers = nd & (nd - 1) == 0 and snaps & (snaps - 1) == 0 and nd > 2
    if powers and parts * (n + slots) * n * 2 <= 4 << 20:
        return chip_body(*args)
    return spread_body(*args)


def solution(mesh):
    in_specs = (
        P("snap", None, "dom"),
        P("snap", None, "dom"),
        P("snap", None, "dom"),
        P(),
        P(),
        P(),
        P(),
        P(None, "dom"),
        P(None, "dom"),
        P("dom", None),
    )
    out_specs = (P("snap", None, "dom"), P(), P(), P(), P())
    return jax.shard_map(body, mesh=mesh, in_specs=in_specs, out_specs=out_specs, check_vma=False)
```

```python
import functools
import math

import jax
import jax.numpy as jnp
from jax import lax
from jax.experimental import pallas as pl
from jax.experimental.pallas import tpu as pltpu
from jax.sharding import PartitionSpec as P

F32 = jnp.float32
BF16 = jnp.bfloat16
LANES = 128


def nn(a, b):
    return lax.dot_general(a, b, (((1,), (0,)), ((), ())), preferred_element_type=F32)


def nt(a, b):
    return lax.dot_general(a, b, (((1,), (1,)), ((), ())), preferred_element_type=F32)


def tn(a, b):
    return lax.dot_general(a, b, (((0,), (0,)), ((), ())), preferred_element_type=F32)


def iota(shape, axis):
    return lax.broadcasted_iota(jnp.int32, shape, axis)


def column(row):
    k = row.shape[1]
    spread = jnp.broadcast_to(row.astype(F32), (k, k))
    return jnp.sum(jnp.where(iota((k, k), 0) == iota((k, k), 1), spread, 0.0), axis=1, keepdims=True)


def run(kernel, name, outs, *args, scratch=(), flops=20_000_000, vmem=24, after=()):
    return pl.pallas_call(
        lambda *refs: kernel(*refs[len(after) :]),
        name=name,
        out_shape=[jax.ShapeDtypeStruct(shape, kind) for shape, kind in outs],
        in_specs=[pl.BlockSpec(memory_space=pl.ANY)] * len(after) + [pl.BlockSpec(memory_space=pltpu.VMEM)] * len(args),
        out_specs=[pl.BlockSpec(memory_space=pltpu.VMEM)] * len(outs),
        scratch_shapes=list(scratch),
        compiler_params=pltpu.CompilerParams(vmem_limit_bytes=vmem * 1024 * 1024),
        cost_estimate=pl.CostEstimate(flops=flops, bytes_accessed=2_000_000, transcendentals=0),
    )(*after, *args)


def prep_kernel(cap, nb, w, rows, readings, previous, e, s, b, pay):
    degree, n = nb.shape
    nh = s.shape[0]
    hid = previous.shape[1]
    fin = readings.shape[1]
    step = 32
    for at in range(0, n + nh, step):
        node = iota((step, n), 0) + at
        total = jnp.zeros((step, n), F32)
        for d in range(degree):
            total = total + jnp.where(node == nb[d : d + 1, :], w[d : d + 1, :], 0.0)
        e[at : at + step, :] = total.astype(BF16)
    sent = column(rows[...]).astype(jnp.int32)
    s[...] = jnp.where(iota((nh, n), 1) == sent, 1.0, 0.0).astype(BF16)
    b[:hid, :] = previous[0]
    rest = b.shape[0] - hid
    row = iota((rest, n), 0)
    tail = jnp.where(row == fin, 1.0, 0.0)
    for f in range(fin):
        tail = jnp.where(row == f, readings[0, f : f + 1, :].astype(F32), tail)
    b[hid:, :] = tail.astype(BF16)
    base = b[...]
    chans = base.shape[0]
    bound = nt(s[...], base)
    halo = nt(e[n:, :], base)
    for p in range(nh // cap):
        pay[p, :, :chans] = bound[p * cap : (p + 1) * cap, :]
        pay[p, :, LANES : LANES + chans] = halo[p * cap : (p + 1) * cap, :]


def order_matrix(shape, chans, hid, fin, block):
    k = iota(shape, 0)
    col = iota(shape, 1)
    m = lax.div(col, jnp.int32(block))
    c = col - m * block
    source = jnp.where(c < hid, m * chans + fin + c, jnp.where(c < hid + fin, m * chans + c - hid, -1))
    return jnp.where(k == source, 1.0, 0.0).astype(BF16)


def mid_a_kernel(hid, fin, orders, e, b, gw, cw, fa, ra, gw_o, cw_o):
    n = e.shape[1]
    a = e[:n, :]
    base = b[...]
    fa[...] = nt(base, a)
    ra[...] = nn(base, a)
    block = base.shape[0]
    order = order_matrix((gw.shape[1], orders * block), hid + fin, hid, fin, block)
    gw_o[...] = nn(gw[...], order).astype(BF16)
    cw_o[...] = nn(cw[...], order).astype(BF16)


def post_a_kernel(one, cap, recv, e, s, fa, ra, f1, r1, ro, ri, pay, flat):
    n = e.shape[1]
    nh = s.shape[0]
    chans = fa.shape[0]
    for p in range(nh // cap):
        flat[p * cap : (p + 1) * cap, :] = recv[p]
    h = e[n:, :]
    sel = s[...]
    seen = flat[:, :chans].astype(BF16)
    back = flat[:, LANES : LANES + chans]
    back_degree = flat[:, LANES + one : LANES + one + 1]
    out_degree = fa[one : one + 1, :] + jnp.sum(sel.astype(F32) * back_degree, axis=0, keepdims=True)
    pulled = ra[...] + tn(seen, h)
    inv_o = 1.0 / out_degree
    inv_i = 1.0 / pulled[one : one + 1, :]
    ro[...] = inv_o
    ri[...] = inv_i
    first_out = ((fa[...] + tn(back.astype(BF16), sel)) * inv_o).astype(BF16)
    first_in = (pulled * inv_i).astype(BF16)
    f1[...] = first_out
    r1[...] = first_in
    bound = nt(sel, first_in)
    halo = nt(h, first_out)
    hi, ho = scaled(h, inv_i), scaled(h, inv_o)
    si, so = scaled(sel, inv_i), scaled(sel, inv_o)
    coefs = (nt(sel, hi), nt(h, so), nt(sel, ho), nt(h, si))
    for p in range(nh // cap):
        at = slice(p * cap, (p + 1) * cap)
        pay[p, :, :chans] = bound[at, :]
        pay[p, :, LANES : LANES + chans] = halo[at, :]
        for k, coef in enumerate(coefs):
            pay[p, :, 2 * LANES + k * nh : 2 * LANES + (k + 1) * nh] = coef[at, :]


def scaled(rows, factor):
    return (rows.astype(F32) * factor).astype(BF16)


def mid_b_kernel(e, s, f1, r1, ro, ri, f2l, r2l, kc, ke, ka):
    n = e.shape[1]
    a = e[:n, :]
    h = e[n:, :]
    sel = s[...]
    nh = sel.shape[0]
    chans = f1.shape[0]
    inv_o, inv_i = ro[...], ri[...]
    outs = nt(jnp.concatenate([f1[...], scaled(sel, inv_o), scaled(sel, inv_i)], axis=0), a)
    ins = nn(jnp.concatenate([r1[...], scaled(h, inv_i), scaled(h, inv_o)], axis=0), a)
    f2l[...] = outs[:chans]
    r2l[...] = ins[:chans]
    kc[:nh, :] = ins[chans : chans + nh].astype(BF16)
    kc[nh:, :] = h
    ke[:nh, :] = outs[chans : chans + nh].astype(BF16)
    ke[nh:, :] = sel
    ka[:nh, :] = (2.0 * ins[chans + nh :]).astype(BF16)
    ka[nh : 2 * nh, :] = h
    ka[2 * nh : 3 * nh, :] = (2.0 * outs[chans + nh :]).astype(BF16)
    ka[3 * nh :, :] = sel


def send(pay, cap, left, right, left_two, right_two):
    nh = left.shape[0]
    rows = jnp.concatenate([left, right], axis=1)
    rows_two = jnp.concatenate([left_two, right_two], axis=1)
    both = jnp.concatenate([rows, rows_two], axis=0).astype(BF16)
    k = iota((2 * nh, 2 * nh), 0)
    part = lax.div(k, jnp.int32(2 * cap))
    spot = k - part * (2 * cap)
    source = jnp.where(spot < cap, part * cap + spot, nh + part * cap + spot - cap)
    mine = nn(jnp.where(iota((2 * nh, 2 * nh), 1) == source, 1.0, 0.0).astype(BF16), both)
    for p in range(nh // cap):
        own = mine[p * 2 * cap : (p + 1) * 2 * cap, :]
        pay[p] = jnp.concatenate([rows, own], axis=0).astype(BF16)


def post_b_kernel(cap, one, recv, e, s, b, f1, r1, f2l, r2l, ro, ri, gw, gb, states, reset, update, y, f1l, r1l, pay, flat):
    n = e.shape[1]
    nh = s.shape[0]
    hid = y.shape[0]
    chans = b.shape[0]
    for p in range(nh // cap):
        flat[p * cap : (p + 1) * cap, :] = recv[p, :, : 2 * LANES]
    a = e[:n, :]
    h = e[n:, :]
    sel = s[...]
    inv_o, inv_i = ro[...], ri[...]
    base = b[...].astype(F32)
    seen = flat[:, :chans].astype(BF16)
    back = flat[:, LANES : LANES + chans].astype(BF16)
    f2 = 2.0 * (f2l[...] + tn(back, sel)) * inv_o - base
    r2 = 2.0 * (r2l[...] + tn(seen, h)) * inv_i - base
    states[:chans, :] = b[...]
    states[chans : 2 * chans, :] = f1[...]
    states[2 * chans : 3 * chans, :] = f2.astype(BF16)
    states[3 * chans : 4 * chans, :] = r1[...]
    states[4 * chans :, :] = r2.astype(BF16)
    gates = jax.nn.sigmoid(nn(gw[...], states[...]) + column(gb[...]))
    reset[...] = gates[:hid]
    update[...] = gates[hid:]
    now = (gates[:hid] * base[:hid]).astype(BF16)
    y[...] = now
    local_out = nt(now, a) * inv_o
    local_in = nn(now, a) * inv_i
    f1l[...] = local_out
    r1l[...] = local_in
    bound = nt(sel, jnp.concatenate([now, local_in.astype(BF16)], axis=0))
    halo = nt(h, jnp.concatenate([now, local_out.astype(BF16)], axis=0))
    send(pay, cap, bound[:, :hid], halo[:, :hid], bound[:, hid:], halo[:, hid:])


def gather_matrix(coef, out, nd, cap, per, first, factor):
    nh = nd * cap
    width = nd * per
    k = iota((nh, width), 0)
    col = iota((nh, width), 1)
    r = lax.div(col, jnp.int32(per))
    u = col - r * per
    p = lax.div(u, jnp.int32(cap))
    spot = u - p * cap
    here = lax.div(k, jnp.int32(cap))
    slot = k - here * cap
    inside = u < nh
    place = jnp.where((k == r * cap + spot) & inside, 1.0, 0.0).astype(BF16)
    keep = (here == p) & inside
    for i in range(2):
        wide = nn(coef[:, (first + i) * nh : (first + i + 1) * nh].astype(BF16), place)
        own = (r == here) & (u == nh + cap + slot)
        out[(i + 1) * nh : (i + 2) * nh, :] = jnp.where(keep, factor * wide, jnp.where(own, 1.0, 0.0)).astype(BF16)
    out[:nh, :] = jnp.where((r == here) & (u == nh + slot), 1.0, 0.0).astype(BF16)


def mid_c_kernel(nd, cap, per, fused, recv, e, f1l, r1l, f2l, r2l, *rest):
    n = e.shape[1]
    a = e[:n, :]
    f2l[...] = nt(f1l[...].astype(BF16), a)
    r2l[...] = nn(r1l[...].astype(BF16), a)
    if fused:
        gd, ga, flat = rest
        for p in range(nd):
            flat[p * cap : (p + 1) * cap, :] = recv[p, :, 2 * LANES :]
        gather_matrix(flat, gd, nd, cap, per, 0, 1.0)
        gather_matrix(flat, ga, nd, cap, per, 2, 2.0)


def arrived(fused, hid, nh, g, recv):
    if fused:
        halo = nn(g[...], recv[...].reshape(recv.shape[0] * recv.shape[1], recv.shape[2]))
        two = halo[nh : 2 * nh, :hid], halo[2 * nh :, hid:]
    else:
        halo = recv[...]
        two = halo[nh:, :hid], halo[nh:, hid:]
    one = halo[:nh]
    return one[:, :hid], one[:, hid:], two[0], two[1]


def back_and_send(cap, hid, g, a, h, sel, inv_o, inv_i, z1, z2, pay):
    g0, g1, g2, g3, g4 = (g[m * hid : (m + 1) * hid, :].astype(BF16).astype(F32) for m in range(5))
    y1 = (g2 * inv_o).astype(BF16)
    y2 = (g4 * inv_i).astype(BF16)
    now1 = ((g1 + 2.0 * nn(y1, a)) * inv_o).astype(BF16)
    now2 = ((g3 + 2.0 * nt(y2, a)) * inv_i).astype(BF16)
    z1[...] = now1
    z2[...] = now2
    bound = nt(sel, jnp.concatenate([y1, now1], axis=0))
    halo = nt(h, jnp.concatenate([y2, now2], axis=0))
    send(pay, cap, bound[:, :hid], halo[:, :hid], bound[:, hid:], halo[:, hid:])
    return g0 - g2 - g4


def hidden_weights(w, hid, block, orders):
    return jnp.concatenate([w[:, m * block : m * block + hid] for m in range(orders)], axis=1)


def post_c_kernel(fused, cap, orders, g, recv, e, s, kc, ke, y, f1l, r1l, f2l, r2l, ro, ri, states, cw, cb, upstream, update,
                  mixed, cand_grad, gate_update, z1, z2, direct, pay):
    n = e.shape[1]
    nh = s.shape[0]
    hid = y.shape[0]
    block = states.shape[0] // orders
    a = e[:n, :]
    h = e[n:, :]
    sel = s[...]
    inv_o, inv_i = ro[...], ri[...]
    c1, e1, c2, e2 = arrived(fused, hid, nh, g, recv)
    base = y[...].astype(F32)
    c1, e1 = c1.astype(BF16), e1.astype(BF16)
    cc = jnp.concatenate([c1, c2.astype(BF16)], axis=0)
    ee = jnp.concatenate([e1, e2.astype(BF16)], axis=0)
    f1 = f1l[...] + tn(e1, sel) * inv_o
    f2 = 2.0 * (f2l[...] + tn(ee, ke[...])) * inv_o - base
    r1 = r1l[...] + tn(c1, h) * inv_i
    r2 = 2.0 * (r2l[...] + tn(cc, kc[...])) * inv_i - base
    for m, value in enumerate((y[...], f1, f2, r1, r2)):
        mixed[m * block : m * block + hid, :] = value.astype(BF16)
        mixed[m * block + hid : (m + 1) * block, :] = states[m * block + hid : (m + 1) * block, :]
    weights = cw[...]
    cand = jnp.tanh(nn(weights, mixed[...]) + column(cb[...]))
    up = upstream[0].astype(F32)
    gate = update[...]
    grad = (up * (1.0 - gate) * (1.0 - cand * cand)).astype(BF16)
    cand_grad[...] = grad
    held = states[:hid, :].astype(F32)
    gate_update[...] = (up * (held - cand) * gate * (1.0 - gate)).astype(BF16)
    back = tn(hidden_weights(weights, hid, block, orders), grad)
    direct[...] = back_and_send(cap, hid, back, a, h, sel, inv_o, inv_i, z1, z2, pay)


def weight_part(grad, features, orders, chans, hid, fin):
    block = features.shape[0] // orders
    width = -(-(orders * chans + 1) // LANES) * LANES
    shape = (width, orders * block)
    k = iota(shape, 0)
    col = iota(shape, 1)
    m = lax.div(col, jnp.int32(block))
    c = col - m * block
    source = jnp.where(c < hid, m * chans + fin + c, jnp.where(c < hid + fin, m * chans + c - hid, -1))
    source = jnp.where(col == hid + fin, orders * chans, source)
    order = jnp.where(k == source, 1.0, 0.0).astype(BF16)
    return nt(nt(grad, features).astype(BF16), order)


def mid_d_kernel(orders, fin, e, z1, z2, direct, cand_grad, mixed, gate_update, states, base, part):
    n = e.shape[1]
    a = e[:n, :]
    hid = z1.shape[0]
    base[...] = direct[...] + nn(z1[...], a) + nt(z2[...], a)
    part[:hid, :] = weight_part(gate_update[...], states[...], orders, hid + fin, hid, fin).astype(BF16)
    part[hid:, :] = weight_part(cand_grad[...], mixed[...], orders, hid + fin, hid, fin).astype(BF16)


def add_halo(fused, g, recv, ka, base):
    hid = base.shape[0]
    nh = ka.shape[0] // 4
    c1, e1, c2, e2 = arrived(fused, hid, nh, g, recv)
    return base[...] + tn(jnp.concatenate([c1, c2, e1, e2], axis=0).astype(BF16), ka[...])


def post_d_kernel(fused, cap, orders, g, recv, e, s, ka, base, ro, ri, states, gw, upstream, reset, update, gate_update,
                  gate_reset, z1, z2, direct, pay):
    n = e.shape[1]
    hid = base.shape[0]
    block = states.shape[0] // orders
    scaled_grad = add_halo(fused, g, recv, ka, base)
    held = states[:hid, :].astype(F32)
    gate = reset[...]
    grad = (scaled_grad * held * gate * (1.0 - gate)).astype(BF16)
    gate_reset[...] = grad
    weights = hidden_weights(gw[...], hid, block, orders)
    back = tn(weights, jnp.concatenate([grad, gate_update[...]], axis=0))
    rest = back_and_send(cap, hid, back, e[:n, :], e[n:, :], s[...], ro[...], ri[...], z1, z2, pay)
    direct[...] = rest + upstream[0].astype(F32) * update[...] + scaled_grad * gate


def mid_e_kernel(orders, fin, rows, e, z1, z2, direct, gate_reset, states, part, base, grads):
    n = e.shape[1]
    a = e[:n, :]
    hid = z1.shape[0]
    base[...] = direct[...] + nn(z1[...], a) + nt(z2[...], a)
    first = weight_part(gate_reset[...], states[...], orders, hid + fin, hid, fin)
    both = jnp.concatenate([first, part[...].astype(F32)], axis=0)
    for k in range(grads.shape[0]):
        if k * rows < both.shape[0]:
            grads[k] = both[k * rows : (k + 1) * rows, :].astype(BF16)
        else:
            grads[k] = jnp.zeros(grads.shape[1:], BF16)


def post_e_kernel(fused, g, recv, ka, base, out):
    out[0] = add_halo(fused, g, recv, ka, base).astype(BF16)


def add_kernel(recv, out):
    total = recv[0].astype(F32)
    for k in range(1, recv.shape[0]):
        total = total + recv[k].astype(F32)
    for k in range(out.shape[0]):
        out[k] = total.astype(BF16)


def finish_kernel(hid, factor, recv, gw, gb, cw, cb):
    rows = recv.shape[1]
    features = gw.shape[1]
    total = gw.shape[0] + cw.shape[0]
    for k in range(total // rows):
        part = recv[k].astype(F32)[:, :features] * factor
        at = k * rows
        if at < 2 * hid:
            gw[at : at + rows, :] = part
        else:
            cw[at - 2 * hid : at - 2 * hid + rows, :] = part
    flat = jnp.concatenate([recv[k].astype(F32) for k in range(total // rows)], axis=0)
    pick = jnp.where(iota((8, flat.shape[1]), 1) == features, 1.0, 0.0).astype(BF16)
    bias = nt(pick, flat.astype(BF16))[:1] * factor
    gb[...] = bias[:, : 2 * hid]
    cb[...] = bias[:, 2 * hid :]


def spread_body(
    readings,
    previous,
    upstream,
    gate_weight,
    gate_bias,
    cand_weight,
    cand_bias,
    neighbours,
    edge_weight,
    send_rows,
):
    fin, hid = readings.shape[1], previous.shape[1]
    chans = fin + hid
    orders = gate_weight.shape[1] // chans
    n = readings.shape[2]
    nd = lax.axis_size("dom")
    devices = nd * lax.axis_size("snap")
    nh = send_rows.shape[1]
    cap = nh // nd
    block = hid + 16 * (-(-(fin + 1) // 16))
    one = hid + fin
    per = nh + 2 * cap
    fused = 3 * nh * nd * per <= 1 << 18
    move = functools.partial(lax.all_to_all, axis_name="dom", split_axis=0, concat_axis=0, tiled=True)

    e, s, b, pay = run(
        functools.partial(prep_kernel, cap), "prep",
        [((n + nh, n), BF16), ((nh, n), BF16), ((block, n), BF16), ((nd, cap, 2 * LANES), F32)],
        neighbours, edge_weight, send_rows, readings, previous,
    )
    recv = move(pay)
    fa, ra, gw, cw = run(
        functools.partial(mid_a_kernel, hid, fin, orders), "mid_a",
        [((block, n), F32), ((block, n), F32), ((2 * hid, orders * block), BF16), ((hid, orders * block), BF16)],
        e, b, gate_weight, cand_weight,
    )
    wide = 2 * LANES + 4 * nh
    f1, r1, ro, ri, pay = run(
        functools.partial(post_a_kernel, one, cap), "post_a",
        [((block, n), BF16), ((block, n), BF16), ((1, n), F32), ((1, n), F32), ((nd, cap, wide), F32)],
        recv, e, s, fa, ra, scratch=[pltpu.VMEM((nh, 2 * LANES), F32)],
    )
    recv_b = move(pay)
    f2l, r2l, kc, ke, ka = run(
        mid_b_kernel, "mid_b",
        [((block, n), F32), ((block, n), F32), ((2 * nh, n), BF16), ((2 * nh, n), BF16), ((4 * nh, n), BF16)],
        e, s, f1, r1, ro, ri,
    )
    pay_kind = ((nd, per, 2 * hid), BF16)
    field, field16 = ((hid, n), F32), ((hid, n), BF16)
    states, reset, update, y, f1l, r1l, pay = run(
        functools.partial(post_b_kernel, cap, one), "post_b",
        [((orders * block, n), BF16), field, field, field16, field, field, pay_kind],
        recv_b, e, s, b, f1, r1, f2l, r2l, ro, ri, gw, gate_bias[None, :],
        scratch=[pltpu.VMEM((nh, 2 * LANES), F32)],
    )
    recv = move(pay)
    table = ((3 * nh, nd * per), BF16)
    f2l, r2l, *tables = run(
        functools.partial(mid_c_kernel, nd, cap, per, fused), "mid_c",
        [field, field] + [table] * (2 if fused else 0),
        recv_b, e, f1l, r1l, scratch=[pltpu.VMEM((nh, 4 * nh), F32)] if fused else [],
    )
    if fused:
        inward, outward = tables
        halo_of = lambda got, first, factor: got
    else:
        inward = outward = jnp.zeros((8, LANES), BF16)
        coefs = recv_b[:, :, 2 * LANES :].reshape(nd, cap, 4, nd, cap)

        def halo_of(got, first, factor):
            rows = got[:, :nh].reshape(nd, nd, cap, 2, hid).astype(F32)
            two = jnp.einsum("psgrt,rptgk->psgk", coefs[:, :, first : first + 2], rows)
            two = factor * two.reshape(nh, 2 * hid) + got[:, nh + cap :].reshape(nh, 2 * hid).astype(F32)
            return jnp.concatenate([got[:, nh : nh + cap].reshape(nh, 2 * hid).astype(F32), two], axis=0)

    mixed, cand_grad, gate_update, z1, z2, direct, pay = run(
        functools.partial(post_c_kernel, fused, cap, orders), "post_c",
        [((orders * block, n), BF16), field16, field16, field16, field16, field, pay_kind],
        inward, halo_of(recv, 0, 1.0), e, s, kc, ke, y, f1l, r1l, f2l, r2l, ro, ri, states, cw, cand_bias[None, :], upstream, update,
    )
    recv = move(pay)
    width = -(-(orders * chans + 1) // LANES) * LANES
    base, part = run(
        functools.partial(mid_d_kernel, orders, fin), "mid_d", [field, ((2 * hid, width), BF16)],
        e, z1, z2, direct, cand_grad, mixed, gate_update, states,
    )
    gate_reset, z1, z2, direct, pay = run(
        functools.partial(post_d_kernel, fused, cap, orders), "post_d",
        [field16, field16, field16, field, pay_kind],
        outward, halo_of(recv, 2, 2.0), e, s, ka, base, ro, ri, states, gw, upstream, reset, update, gate_update,
    )
    recv = move(pay)
    rows = 8 * (-(-3 * hid // (8 * devices)))
    base, grads = run(
        functools.partial(mid_e_kernel, orders, fin, rows), "mid_e", [field, ((devices, rows, width), BF16)],
        e, z1, z2, direct, gate_reset, states, part,
    )
    (state_grad,) = run(
        functools.partial(post_e_kernel, fused), "post_e", [((1, hid, n), BF16)],
        outward, halo_of(recv, 2, 2.0), ka, base,
    )
    both = ("snap", "dom")
    grads = lax.all_to_all(grads, both, 0, 0, tiled=True)
    (grads,) = run(add_kernel, "add", [((devices, rows, width), BF16)], grads)
    grads = lax.all_to_all(grads, both, 0, 0, tiled=True)
    factor = 1.0 / math.sqrt(readings.shape[0] * lax.axis_size("snap") * n * nd)
    feats = orders * chans
    grad_gw, grad_gb, grad_cw, grad_cb = run(
        functools.partial(finish_kernel, hid, factor), "finish",
        [((2 * hid, feats), F32), ((1, 2 * hid), F32), ((hid, feats), F32), ((1, hid), F32)],
        grads,
    )
    return state_grad, grad_gw, grad_gb[0], grad_cw, grad_cb[0]


def pack_kernel(nb, w, rows, readings, previous, upstream, own, both, tail):
    degree = nb.shape[0]
    nh = rows.shape[1]
    hid = previous.shape[1]
    fin = readings.shape[1]
    block = own.shape[0]
    tail[...] = jnp.zeros_like(tail)
    tail[:fin, :] = readings[0].astype(F32)
    high = lax.shift_right_logical(nb[...], 5)
    tail[fin : fin + degree, :] = high.astype(F32)
    tail[fin + degree : fin + 2 * degree, :] = (nb[...] - high * 32).astype(F32)
    tail[fin + 2 * degree : fin + 3 * degree, :] = w[...]
    at = fin + 3 * degree
    high = lax.shift_right_logical(rows[...], 5)
    tail[at : at + 1, :nh] = high.astype(F32)
    tail[at + 1 : at + 2, :nh] = (rows[...] - high * 32).astype(F32)
    for to in (own, both):
        to[:hid, :] = previous[0]
        to[hid:block, :] = tail[...].astype(BF16)
    both[block:, :] = upstream[0]


def exchange(first, second, hc, sc, pay):
    count = first[0].shape[0]
    parts = len(first)
    pay[:count, :] = jnp.concatenate([nt(first[p], sc[p]).astype(BF16) for p in range(parts)], axis=1)
    pay[count:, :] = jnp.concatenate([nt(second[p], hc[p]).astype(BF16) for p in range(parts)], axis=1)


def merged(parts, mine, got):
    step = mine.shape[1] // (2 * parts)
    here = lax.rem(lax.div(iota(mine.shape, 1), jnp.int32(step)), jnp.int32(2)) == 0
    value = jnp.where(here, mine[...].astype(F32), got[...].astype(F32)).astype(BF16)
    count = mine.shape[0] // 2
    return value[:count, :], value[count:, :]


def build_part(cap, hid, fin, degree, parts, p, block, a, at, hc, hx, sc, sx, b):
    n = a.shape[1]
    slots = sx.shape[0]
    nh = 2 * parts * cap
    half = parts * cap
    core = lax.rem(lax.axis_index("dom"), 2)
    line = iota((nh, 1), 0)
    rel = lax.div(line, jnp.int32(half))
    k = lax.div(line - rel * half, jnp.int32(cap))
    t = line - rel * half - k * cap
    spot = (k * 2 + lax.bitwise_xor(rel, core)) * cap + t
    node = (n + spot).astype(F32)
    width = -(-nh // LANES) * LANES
    slot = iota((slots, nh), 0)
    outer = lax.div(slot, jnp.int32(nh))
    rest = slot - outer * nh
    slot_rel = lax.div(rest, jnp.int32(half))
    rest = rest - slot_rel * half
    inner = lax.div(rest, jnp.int32(cap))
    filled = iota((slots, nh), 1) == slot_rel * half + outer * cap + rest - inner * cap
    row = iota((32, n), 0).astype(F32)
    edges = hid + fin + 3 * degree + 2
    tail = block[hid : hid + 16 * (-(-(edges - hid) // 16)), :].astype(F32)
    high, low = tail[fin : fin + degree], tail[fin + degree : fin + 2 * degree]
    w = tail[fin + 2 * degree : fin + 3 * degree]
    start = fin + 3 * degree
    sent = tail[start : start + 1] * 32.0 + tail[start + 1 : start + 2]
    low_is = [jnp.where(low[d : d + 1] == row, 1.0, 0.0).astype(BF16) for d in range(degree)]
    for chunk in range(n // 32):
        total = None
        for d in range(degree):
            term = low_is[d] * jnp.where(high[d : d + 1] == float(chunk), w[d : d + 1], 0.0).astype(BF16)
            total = term if total is None else total + term
        a[chunk * 32 : (chunk + 1) * 32, :] = total
    at[...] = a[...].T
    names = high * 32.0 + low
    total = jnp.zeros((nh, n), F32)
    for d in range(degree):
        total = total + jnp.where(names[d : d + 1] == node, w[d : d + 1], 0.0)
    halo = total.astype(BF16)
    hc[...] = halo
    named = jnp.where(iota((nh, width), 1) == spot, sent[:, :width], 0.0)
    target = jnp.sum(named, axis=1, keepdims=True).astype(jnp.int32)
    picked = jnp.where(iota((nh, n), 1) == target, 1.0, 0.0).astype(BF16)
    sc[...] = picked
    place = jnp.where(filled & (inner == p), 1.0, 0.0).astype(BF16)
    hx[...] = nn(place, halo).astype(BF16)
    sx[...] = nn(place, picked).astype(BF16)
    b[:hid, :] = block[:hid, :]
    line = iota(tail.shape, 0)
    b[hid:, :] = jnp.where(line < fin, tail, jnp.where(line == fin, 1.0, 0.0)).astype(BF16)


def build_early_kernel(cap, hid, fin, degree, parts, *refs):
    count = parts - 1
    z = lax.shift_right_logical(lax.axis_index("dom"), 1)
    for k in range(count):
        p = lax.bitwise_xor(z, jnp.int32(k))
        build_part(cap, hid, fin, degree, parts, p, refs[k], *(ref.at[k] for ref in refs[count:]))


def build_late_kernel(cap, hid, fin, degree, parts, last, *refs):
    early, outs, pay = refs[:5], refs[5:12], refs[12]
    z = lax.shift_right_logical(lax.axis_index("dom"), 1)
    for k in range(parts - 1):
        p = lax.bitwise_xor(z, jnp.int32(k))
        for source, to in zip(early, outs[2:]):
            to[p] = source[k]
    p = lax.bitwise_xor(z, jnp.int32(parts - 1))
    build_part(cap, hid, fin, degree, parts, p, last, outs[0].at[0], outs[1].at[0], *(ref.at[p] for ref in outs[2:]))
    hc, sc, b = outs[2], outs[4], outs[6]
    base = [b[p] for p in range(parts)]
    exchange(base, base, hc, sc, pay)


def chip_source(col, chans, hid, fin, block):
    m = lax.div(col, jnp.int32(block))
    c = col - m * block
    m = jnp.where(m == 2, 3, jnp.where(m == 3, 2, m))
    return m, c, jnp.where(c < hid, m * chans + fin + c, jnp.where(c < hid + fin, m * chans + c - hid, -1))


def order_kernel(hid, fin, orders, block, gw, cw, gw_o, cw_o, gw_b, cw_b, order):
    chans = hid + fin
    feats = cw.shape[1]
    shape = (feats, orders * block)
    source = chip_source(iota(shape, 1), chans, hid, fin, block)[2]
    pick = jnp.where(iota(shape, 0) == source, 1.0, 0.0).astype(BF16)
    gw_o[...] = tn(gw[...], pick).astype(BF16)
    cw_o[...] = nn(cw[...], pick).astype(BF16)
    shape = (orders * hid, feats)
    line = iota(shape, 0)
    m = lax.div(line, jnp.int32(hid))
    pick = jnp.where(iota(shape, 1) == m * chans + fin + line - m * hid, 1.0, 0.0).astype(BF16)
    gw_b[...] = nn(pick, gw[...]).astype(BF16)
    cw_b[...] = nt(pick, cw[...]).astype(BF16)
    m, c, source = chip_source(iota(order.shape, 0), chans, hid, fin, block)
    source = jnp.where((m == 0) & (c == hid + fin), feats, source)
    order[...] = jnp.where(iota(order.shape, 1) == source, 1.0, 0.0).astype(BF16)


def here(early, late, k):
    z = lax.shift_right_logical(lax.axis_index("dom"), 1)
    count = early.shape[0]
    return lax.bitwise_xor(z, jnp.int32(k)), early[k] if k < count else late[k - count]


def local_kernel(a0, at0, a1, at1, x1, x2, l1, l2):
    for k in range(x1.shape[0]):
        p, a = here(a0, a1, k)
        l1[p] = nn(x1[p], a)
    for k in range(x1.shape[0]):
        p, at = here(at0, at1, k)
        l2[p] = nn(x2[p], at)


def arrive(sx, hx, mine, got, l1, l2):
    parts = range(sx.shape[0])
    top, low = merged(sx.shape[0], mine, got)
    pulled = [l1[p] + nn(top, hx[p]) for p in parts]
    pushed = [l2[p] + nn(low, sx[p]) for p in parts]
    return parts, pulled, pushed


def chip_a_kernel(one, mine, got, hc, hx, sc, sx, b, l1, l2, sa, ro, ri, pay):
    chans = b.shape[1]
    parts, pulled, pushed = arrive(sx, hx, mine, got, l1, l2)
    inv_o = [1.0 / pushed[p][one : one + 1, :] for p in parts]
    inv_i = [1.0 / pulled[p][one : one + 1, :] for p in parts]
    outs = [(pushed[p] * inv_o[p]).astype(BF16) for p in parts]
    ins = [(pulled[p] * inv_i[p]).astype(BF16) for p in parts]
    for p in parts:
        ro[p] = inv_o[p]
        ri[p] = inv_i[p]
        sa[p, :chans, :] = b[p]
        sa[p, chans : 2 * chans, :] = outs[p]
        sa[p, 2 * chans :, :] = ins[p]
    exchange(ins, outs, hc, sc, pay)


def local_b_kernel(a0, at0, a1, at1, sa, gw, l1, l2, gp):
    chans = l1.shape[1]
    weights = gw[:, : 3 * chans]
    for k in range(sa.shape[0]):
        p, a = here(a0, a1, k)
        l1[p] = nn(sa[p, 2 * chans :, :], a)
    for k in range(sa.shape[0]):
        p, at = here(at0, at1, k)
        l2[p] = nn(sa[p, chans : 2 * chans, :], at)
    for p in range(sa.shape[0]):
        gp[p] = nn(weights, sa[p])


def chip_b_kernel(mine, got, hc, hx, sc, sx, sa, l1, l2, ro, ri, gw, gb, gp, sb, reset, update, y, pay):
    hid = y.shape[1]
    chans = l1.shape[1]
    bias = column(gb[...])
    weights = gw[:, 3 * chans :]
    parts, pulled, pushed = arrive(sx, hx, mine, got, l1, l2)
    base = [sa[p, :chans, :].astype(F32) for p in parts]
    r2 = [(pulled[p] * (2.0 * ri[p]) - base[p]).astype(BF16) for p in parts]
    f2 = [(pushed[p] * (2.0 * ro[p]) - base[p]).astype(BF16) for p in parts]
    second = [jnp.concatenate([f2[p], r2[p]], axis=0) for p in parts]
    gates = [jax.nn.sigmoid(gp[p] + nn(weights, second[p]) + bias) for p in parts]
    now = [(gates[p][:hid] * base[p][:hid]).astype(BF16) for p in parts]
    for p in parts:
        sb[p] = second[p]
        reset[p] = gates[p][:hid]
        update[p] = gates[p][hid:]
        y[p] = now[p]
    exchange(now, now, hc, sc, pay)


def chip_c1_kernel(mine, got, hc, hx, sc, sx, y, sa, l1, l2, ro, ri, ma, pay):
    hid = y.shape[1]
    chans = ma.shape[1] // 3
    parts, pulled, pushed = arrive(sx, hx, mine, got, l1, l2)
    ins = [(pulled[p] * ri[p]).astype(BF16) for p in parts]
    outs = [(pushed[p] * ro[p]).astype(BF16) for p in parts]
    exchange(ins, outs, hc, sc, pay)
    for p in parts:
        for m, value in enumerate((y[p], outs[p], ins[p])):
            ma[p, m * chans : m * chans + hid, :] = value
            ma[p, m * chans + hid : (m + 1) * chans, :] = sa[p, m * chans + hid : (m + 1) * chans, :]


def local_c2_kernel(a0, at0, a1, at1, ma, cw, l1, l2, cp):
    hid = l1.shape[1]
    chans = ma.shape[1] // 3
    weights = cw[:, : 3 * chans]
    for k in range(ma.shape[0]):
        p, a = here(a0, a1, k)
        l1[p] = nn(ma[p, 2 * chans : 2 * chans + hid, :], a)
    for k in range(ma.shape[0]):
        p, at = here(at0, at1, k)
        l2[p] = nn(ma[p, chans : chans + hid, :], at)
    for p in range(ma.shape[0]):
        cp[p] = nn(weights, ma[p])


def split_back(back, hid, ro, ri, y1, y2, g1, g3, direct):
    parts = range(len(back))
    blocks = [[back[p][m * hid : (m + 1) * hid, :] for m in range(5)] for p in parts]
    one = [(blocks[p][2] * (2.0 * ro[p])).astype(BF16) for p in parts]
    two = [(blocks[p][4] * (2.0 * ri[p])).astype(BF16) for p in parts]
    for p in parts:
        y1[p] = one[p]
        y2[p] = two[p]
        g1[p] = blocks[p][1].astype(BF16)
        g3[p] = blocks[p][3].astype(BF16)
        direct[p] = blocks[p][0] - blocks[p][2] - blocks[p][4]
    return one, two


def chip_c2_kernel(parts, *refs):
    ups, refs = refs[:parts], refs[parts:]
    mine, got, hc, hx, sc, sx, ma, sa, sb, l1, l2, ro, ri, cw, cw_b, cb, cp, update = refs[:18]
    mb, cand_grad, gate_update, y1, y2, g1, g3, upstream, direct, pay = refs[18:]
    hid = l1.shape[1]
    chans = ma.shape[1] // 3
    z = lax.shift_right_logical(lax.axis_index("dom"), 1)
    for k in range(parts):
        upstream[lax.bitwise_xor(z, jnp.int32(k))] = ups[k][0] if len(ups[k].shape) == 3 else ups[k][ups[k].shape[0] - hid :, :]
    bias = column(cb[...])
    weights = cw[:, 3 * chans :]
    parts, pulled, pushed = arrive(sx, hx, mine, got, l1, l2)
    base = [ma[p, :hid, :].astype(F32) for p in parts]
    r2 = [(pulled[p] * (2.0 * ri[p]) - base[p]).astype(BF16) for p in parts]
    f2 = [(pushed[p] * (2.0 * ro[p]) - base[p]).astype(BF16) for p in parts]
    second = [
        jnp.concatenate([f2[p], sb[p, hid:chans, :], r2[p], sb[p, chans + hid :, :]], axis=0) for p in parts
    ]
    cand = [jnp.tanh(cp[p] + nn(weights, second[p]) + bias) for p in parts]
    rest = [upstream[p].astype(F32) * (1.0 - update[p]) for p in parts]
    grad = [(rest[p] - rest[p] * cand[p] * cand[p]).astype(BF16) for p in parts]
    back = [nn(cw_b[...], grad[p]) for p in parts]
    for p in parts:
        mb[p] = second[p]
        cand_grad[p] = grad[p]
        gate_update[p] = ((sa[p, :hid, :].astype(F32) - cand[p]) * (rest[p] * update[p])).astype(BF16)
    one, two = split_back(back, hid, ro, ri, y1, y2, g1, g3, direct)
    exchange(one, two, hc, sc, pay)


def chip_part(grads, first, second, order):
    parts = range(first.shape[0])
    split = first.shape[1]
    one = sum(nt(grads[p], first[p]) for p in parts).astype(BF16)
    two = sum(nt(grads[p], second[p]) for p in parts).astype(BF16)
    return nn(one, order[:split, :]) + nn(two, order[split:, :])


def cand_sums(cand_grad, features, parts):
    return sum(nt(cand_grad[p], features[p]) for p in parts)


def local_d_kernel(count, a0, at0, a1, at1, y1, y2, cand_grad, ma, mb, l1, l2, one, two):
    local_kernel(a0, at0, a1, at1, y1, y2, l1, l2)
    one[...] = cand_sums(cand_grad, ma, range(count))
    two[...] = cand_sums(cand_grad, mb, range(count))


def chip_d1_kernel(mine, got, hc, hx, sc, sx, l1, l2, g1, g3, ro, ri, z1, z2, pay):
    parts, pulled, pushed = arrive(sx, hx, mine, got, l1, l2)
    one = [((g1[p].astype(F32) + pulled[p]) * ro[p]).astype(BF16) for p in parts]
    two = [((g3[p].astype(F32) + pushed[p]) * ri[p]).astype(BF16) for p in parts]
    exchange(one, two, hc, sc, pay)
    for p in parts:
        z1[p] = one[p]
        z2[p] = two[p]


def local_d2_kernel(count, a0, at0, a1, at1, z1, z2, direct, cand_grad, ma, mb, one, two, order, base, part):
    rest = range(count, z1.shape[0])
    split = one.shape[1]
    first = (one[...] + cand_sums(cand_grad, ma, rest)).astype(BF16)
    second = (two[...] + cand_sums(cand_grad, mb, rest)).astype(BF16)
    part[...] = (nn(first, order[:split, :]) + nn(second, order[split:, :])).astype(BF16)
    for k in range(z1.shape[0]):
        p, a = here(a0, a1, k)
        _, at = here(at0, at1, k)
        base[p] = direct[p] + nn(z1[p], a) + nn(z2[p], at)


def chip_d2_kernel(mine, got, hx, sx, base, sa, sb, reset, gate_update, order, part, gate_grad, kept, keep, give, flat):
    hid = base.shape[1]
    both = 2 * hid
    half = keep.shape[0]
    core = lax.rem(lax.axis_index("dom"), 2)
    parts = range(sx.shape[0])
    top, low = merged(sx.shape[0], mine, got)
    scaled_grad = [base[p] + nn(top, hx[p]) + nn(low, sx[p]) for p in parts]
    through = [scaled_grad[p] * reset[p] for p in parts]
    grad = [
        jnp.concatenate([(sa[p, :hid, :].astype(F32) * (through[p] - through[p] * reset[p])).astype(BF16), gate_update[p]], axis=0)
        for p in parts
    ]
    for p in parts:
        gate_grad[p] = grad[p]
        kept[p] = through[p]
    flat[:both, :] = chip_part(grad, sa, sb, order)
    flat[both:, :] = part[...].astype(F32)
    keep[...] = flat[pl.ds(pl.multiple_of(core * half, 8), half), :].astype(BF16)
    give[...] = flat[pl.ds(pl.multiple_of((1 - core) * half, 8), half), :].astype(BF16)


def back_e_kernel(hc, sc, gate_grad, kept, ro, ri, gw_b, upstream, update, y1, y2, g1, g3, direct, pay):
    hid = kept.shape[1]
    parts = range(sc.shape[0])
    back = [nn(gw_b[...], gate_grad[p]) for p in parts]
    one, two = split_back(back, hid, ro, ri, y1, y2, g1, g3, direct)
    for p in parts:
        direct[p] = direct[p] + upstream[p].astype(F32) * update[p] + kept[p]
    exchange(one, two, hc, sc, pay)


def local_e_kernel(a, at, z1, z2, direct, base):
    z = lax.shift_right_logical(lax.axis_index("dom"), 1)
    base[...] = direct[z] + nn(z1[z], a[0]) + nn(z2[z], at[0])


def chip_e_kernel(mine, got, hc, hx, sc, sx, base, out, done):
    done[...] = jnp.zeros_like(done)
    z = lax.shift_right_logical(lax.axis_index("dom"), 1)
    top, low = merged(sx.shape[0], mine, got)
    out[0] = (base[...] + nn(top, hx[z]) + nn(low, sx[z])).astype(BF16)


def sum_kernel(*refs):
    values = [ref[...].astype(F32) for ref in refs[:-2]]
    while len(values) > 1:
        values = [values[k] + values[k + 1] for k in range(0, len(values), 2)]
    refs[-1][...] = values[0].astype(refs[-1].dtype)
    refs[-2][...] = values[0].astype(refs[-2].dtype)


def end_kernel(factor, mine, got, gw, gb, cw, cb, flat):
    half = mine.shape[0]
    core = lax.rem(lax.axis_index("dom"), 2)
    flat[pl.ds(pl.multiple_of(core * half, 8), half), :] = mine[...] * factor
    flat[pl.ds(pl.multiple_of((1 - core) * half, 8), half), :] = got[...] * factor
    features, rows = gw.shape
    gates = flat[:rows, :].T
    gw[...] = gates[:features, :]
    gb[...] = gates[features : features + 1, :]
    cw[...] = flat[rows:, :features]
    last = (features // LANES) * LANES
    cb[...] = flat[rows:, last : last + LANES].T[features - last : features - last + 1, :]


def chip_body(
    readings,
    previous,
    upstream,
    gate_weight,
    gate_bias,
    cand_weight,
    cand_bias,
    neighbours,
    edge_weight,
    send_rows,
):
    fin, hid = readings.shape[1], previous.shape[1]
    chans = fin + hid
    orders = gate_weight.shape[1] // chans
    degree = neighbours.shape[0]
    n = readings.shape[2]
    nd = lax.axis_size("dom")
    snaps = lax.axis_size("snap")
    parts = nd // 2
    cap = send_rows.shape[1] // nd
    block = hid + 16 * (-(-(fin + 3 * degree + 2) // 16))
    slots = 2 * parts * parts * cap

    def swap(array, k, axis="dom", size=nd):
        return lax.ppermute(array, axis, [(i, i ^ k) for i in range(size)])

    own, both = run(
        pack_kernel, "pack", [((block, n), BF16), ((block + hid, n), BF16)],
        neighbours, edge_weight, send_rows, readings, previous, upstream,
        scratch=[pltpu.VMEM((block - hid, n), F32)], vmem=56,
    )
    near = swap(both, 2)
    blocks = [own] + [near if k == 1 else swap(own, 2 * k) for k in range(1, parts - 1)]
    relay = blocks[-1]
    ups = [upstream] + [near if k == 1 else swap(upstream, 2 * k) for k in range(1, parts - 1)]
    ups.append(swap(ups[-1], 2))
    width = -(-(orders * chans + 1) // LANES) * LANES
    gw, cw, gw_b, cw_b, order = run(
        functools.partial(order_kernel, hid, fin, orders, block), "order",
        [((2 * hid, orders * block), BF16), ((hid, orders * block), BF16), ((orders * hid, 2 * hid), BF16), ((orders * hid, hid), BF16),
         ((orders * block, width), BF16)],
        gate_weight.T, cand_weight, after=[own],
    )
    relay, gw = lax.optimization_barrier((relay, gw))
    wide, wide16, wide_pay = ((parts, block, n), F32), ((parts, block, n), BF16), ((2 * block, slots), BF16)
    field, field16, pay_kind = ((parts, hid, n), F32), ((parts, hid, n), BF16), ((2 * hid, slots), BF16)
    first, second = ((parts, 3 * block, n), BF16), ((parts, 2 * block, n), BF16)
    line = ((parts, 1, n), F32)
    built = [((n, n), BF16)] * 2 + [((rows, n), BF16) for rows in (2 * parts * cap, slots)] * 2 + [((block, n), BF16)]
    early = run(
        functools.partial(build_early_kernel, cap, hid, fin, degree, parts), "build_early",
        [((parts - 1, *shape), kind) for shape, kind in built], *blocks[:-1], relay,
    )
    a, at, hc, hx, sc, sx, b, pay = run(
        functools.partial(build_late_kernel, cap, hid, fin, degree, parts), "build_late",
        [((1 if shape == (n, n) else parts, *shape), kind) for shape, kind in built] + [wide_pay],
        swap(relay, 2), *early[2:],
    )
    local = (early[0], early[1], a, at)
    edges = (hc, hx, sc, sx)
    got = swap(pay, 1)
    l1, l2 = run(local_kernel, "local_a", [wide, wide], *local, b, b)
    sa, ro, ri, pay = run(
        functools.partial(chip_a_kernel, hid + fin), "chip_a", [first, line, line, wide_pay],
        pay, got, *edges, b, l1, l2, after=ups[2:],
    )
    got = swap(pay, 1)
    l1, l2, gp = run(local_b_kernel, "local_b", [wide, wide, ((parts, 2 * hid, n), F32)], *local, sa, gw)
    sb, reset, update, y, pay = run(
        chip_b_kernel, "chip_b", [second, field, field, field16, pay_kind],
        pay, got, *edges, sa, l1, l2, ro, ri, gw, gate_bias[None, :], gp,
    )
    got = swap(pay, 1)
    l1, l2 = run(local_kernel, "local_c1", [field, field], *local, y, y)
    ma, pay = run(chip_c1_kernel, "chip_c1", [first, pay_kind], pay, got, *edges, y, sa, l1, l2, ro, ri)
    got = swap(pay, 1)
    l1, l2, cp = run(local_c2_kernel, "local_c2", [field, field, field], *local, ma, cw)
    mb, cand_grad, gate_update, y1, y2, g1, g3, up, direct, pay = run(
        functools.partial(chip_c2_kernel, parts), "chip_c2", [second] + [field16] * 7 + [field, pay_kind],
        *ups, pay, got, *edges, ma, sa, sb, l1, l2, ro, ri, cw, cw_b, cand_bias[None, :], cp, update,
    )
    got = swap(pay, 1)
    count = parts // 2
    l1, l2, one, two = run(
        functools.partial(local_d_kernel, count), "local_d1",
        [field, field, ((hid, 3 * block), F32), ((hid, (orders - 3) * block), F32)], *local, y1, y2, cand_grad, ma, mb
    )
    z1, z2, pay = run(
        chip_d1_kernel, "chip_d1", [field16, field16, pay_kind], pay, got, *edges, l1, l2, g1, g3, ro, ri
    )
    got = swap(pay, 1)
    base, part = run(
        functools.partial(local_d2_kernel, count), "local_d2", [field, ((hid, width), BF16)],
        *local, z1, z2, direct, cand_grad, ma, mb, one, two, order,
    )
    half = ((3 * hid // 2, width), BF16)
    gate_grad, kept, keep, give = run(
        chip_d2_kernel, "chip_d2", [((parts, 2 * hid, n), BF16), field, half, half],
        pay, got, hx, sx, base, sa, sb, reset, gate_update, order, part, scratch=[pltpu.VMEM((3 * hid, width), F32)],
    )
    y1, y2, g1, g3, direct, pay = run(
        back_e_kernel, "back_e", [field16] * 4 + [field, pay_kind], hc, sc, gate_grad, kept, ro, ri, gw_b, up, update
    )
    got = swap(pay, 1)
    l1, l2 = run(local_kernel, "local_e1", [field, field], *local, y1, y2)
    mine, sent = run(sum_kernel, "sum_core", [half] * 2, keep, swap(give, 1), after=[direct])
    every = [mine] + [swap(sent, k, "snap", snaps) for k in range(1, snaps)]
    z1, z2, pay = run(
        chip_d1_kernel, "chip_e1", [field16, field16, pay_kind], pay, got, *edges, l1, l2, g1, g3, ro, ri, after=[mine],
    )
    got = swap(pay, 1)
    (base,) = run(local_e_kernel, "local_e2", [((hid, n), F32)], early[0], early[1], z1, z2, direct)
    state_grad, done = run(
        chip_e_kernel, "chip_e2", [((1, hid, n), BF16), ((8, LANES), F32)], pay, got, *edges, base
    )
    mine, sent = run(sum_kernel, "sum_snap", [(half[0], F32)] * 2, *every, after=[done])
    factor = 1.0 / math.sqrt(readings.shape[0] * snaps * n * nd)
    feats = orders * chans
    grad_gw, grad_gb, grad_cw, grad_cb = run(
        functools.partial(end_kernel, factor), "end",
        [((feats, 2 * hid), F32), ((1, 2 * hid), F32), ((hid, feats), F32), ((1, hid), F32)],
        mine, swap(sent, 1), scratch=[pltpu.VMEM((3 * hid, width), F32)],
    )
    return state_grad, grad_gw.T, grad_gb[0], grad_cw, grad_cb[0]


def body(*args):
    neighbours, send_rows = args[7], args[9]
    n = neighbours.shape[1]
    nd, snaps = lax.axis_size("dom"), lax.axis_size("snap")
    parts = nd // 2
    slots = 2 * parts * parts * (send_rows.shape[1] // nd)
    powers = nd & (nd - 1) == 0 and snaps & (snaps - 1) == 0 and nd > 2
    if powers and parts * (n + slots) * n * 2 <= 4 << 20:
        return chip_body(*args)
    return spread_body(*args)


def solution(mesh):
    in_specs = (
        P("snap", None, "dom"),
        P("snap", None, "dom"),
        P("snap", None, "dom"),
        P(),
        P(),
        P(),
        P(),
        P(None, "dom"),
        P(None, "dom"),
        P("dom", None),
    )
    out_specs = (P("snap", None, "dom"), P(), P(), P(), P())
    return jax.shard_map(body, mesh=mesh, in_specs=in_specs, out_specs=out_specs, check_vma=False)
```

```python
import functools
import math

import jax
import jax.numpy as jnp
from jax import lax
from jax.experimental import pallas as pl
from jax.experimental.pallas import tpu as pltpu
from jax.sharding import PartitionSpec as P

F32 = jnp.float32
BF16 = jnp.bfloat16
LANES = 128


def nn(a, b):
    return lax.dot_general(a, b, (((1,), (0,)), ((), ())), preferred_element_type=F32)


def nt(a, b):
    return lax.dot_general(a, b, (((1,), (1,)), ((), ())), preferred_element_type=F32)


def tn(a, b):
    return lax.dot_general(a, b, (((0,), (0,)), ((), ())), preferred_element_type=F32)


def iota(shape, axis):
    return lax.broadcasted_iota(jnp.int32, shape, axis)


def column(row):
    k = row.shape[1]
    spread = jnp.broadcast_to(row.astype(F32), (k, k))
    return jnp.sum(jnp.where(iota((k, k), 0) == iota((k, k), 1), spread, 0.0), axis=1, keepdims=True)


def run(kernel, name, outs, *args, scratch=(), flops=20_000_000, vmem=24, after=()):
    return pl.pallas_call(
        lambda *refs: kernel(*refs[len(after) :]),
        name=name,
        out_shape=[jax.ShapeDtypeStruct(shape, kind) for shape, kind in outs],
        in_specs=[pl.BlockSpec(memory_space=pl.ANY)] * len(after) + [pl.BlockSpec(memory_space=pltpu.VMEM)] * len(args),
        out_specs=[pl.BlockSpec(memory_space=pltpu.VMEM)] * len(outs),
        scratch_shapes=list(scratch),
        compiler_params=pltpu.CompilerParams(vmem_limit_bytes=vmem * 1024 * 1024),
        cost_estimate=pl.CostEstimate(flops=flops, bytes_accessed=2_000_000, transcendentals=0),
    )(*after, *args)


def prep_kernel(cap, nb, w, rows, readings, previous, e, s, b, pay):
    degree, n = nb.shape
    nh = s.shape[0]
    hid = previous.shape[1]
    fin = readings.shape[1]
    step = 32
    for at in range(0, n + nh, step):
        node = iota((step, n), 0) + at
        total = jnp.zeros((step, n), F32)
        for d in range(degree):
            total = total + jnp.where(node == nb[d : d + 1, :], w[d : d + 1, :], 0.0)
        e[at : at + step, :] = total.astype(BF16)
    sent = column(rows[...]).astype(jnp.int32)
    s[...] = jnp.where(iota((nh, n), 1) == sent, 1.0, 0.0).astype(BF16)
    b[:hid, :] = previous[0]
    rest = b.shape[0] - hid
    row = iota((rest, n), 0)
    tail = jnp.where(row == fin, 1.0, 0.0)
    for f in range(fin):
        tail = jnp.where(row == f, readings[0, f : f + 1, :].astype(F32), tail)
    b[hid:, :] = tail.astype(BF16)
    base = b[...]
    chans = base.shape[0]
    bound = nt(s[...], base)
    halo = nt(e[n:, :], base)
    for p in range(nh // cap):
        pay[p, :, :chans] = bound[p * cap : (p + 1) * cap, :]
        pay[p, :, LANES : LANES + chans] = halo[p * cap : (p + 1) * cap, :]


def order_matrix(shape, chans, hid, fin, block):
    k = iota(shape, 0)
    col = iota(shape, 1)
    m = lax.div(col, jnp.int32(block))
    c = col - m * block
    source = jnp.where(c < hid, m * chans + fin + c, jnp.where(c < hid + fin, m * chans + c - hid, -1))
    return jnp.where(k == source, 1.0, 0.0).astype(BF16)


def mid_a_kernel(hid, fin, orders, e, b, gw, cw, fa, ra, gw_o, cw_o):
    n = e.shape[1]
    a = e[:n, :]
    base = b[...]
    fa[...] = nt(base, a)
    ra[...] = nn(base, a)
    block = base.shape[0]
    order = order_matrix((gw.shape[1], orders * block), hid + fin, hid, fin, block)
    gw_o[...] = nn(gw[...], order).astype(BF16)
    cw_o[...] = nn(cw[...], order).astype(BF16)


def post_a_kernel(one, cap, recv, e, s, fa, ra, f1, r1, ro, ri, pay, flat):
    n = e.shape[1]
    nh = s.shape[0]
    chans = fa.shape[0]
    for p in range(nh // cap):
        flat[p * cap : (p + 1) * cap, :] = recv[p]
    h = e[n:, :]
    sel = s[...]
    seen = flat[:, :chans].astype(BF16)
    back = flat[:, LANES : LANES + chans]
    back_degree = flat[:, LANES + one : LANES + one + 1]
    out_degree = fa[one : one + 1, :] + jnp.sum(sel.astype(F32) * back_degree, axis=0, keepdims=True)
    pulled = ra[...] + tn(seen, h)
    inv_o = 1.0 / out_degree
    inv_i = 1.0 / pulled[one : one + 1, :]
    ro[...] = inv_o
    ri[...] = inv_i
    first_out = ((fa[...] + tn(back.astype(BF16), sel)) * inv_o).astype(BF16)
    first_in = (pulled * inv_i).astype(BF16)
    f1[...] = first_out
    r1[...] = first_in
    bound = nt(sel, first_in)
    halo = nt(h, first_out)
    hi, ho = scaled(h, inv_i), scaled(h, inv_o)
    si, so = scaled(sel, inv_i), scaled(sel, inv_o)
    coefs = (nt(sel, hi), nt(h, so), nt(sel, ho), nt(h, si))
    for p in range(nh // cap):
        at = slice(p * cap, (p + 1) * cap)
        pay[p, :, :chans] = bound[at, :]
        pay[p, :, LANES : LANES + chans] = halo[at, :]
        for k, coef in enumerate(coefs):
            pay[p, :, 2 * LANES + k * nh : 2 * LANES + (k + 1) * nh] = coef[at, :]


def scaled(rows, factor):
    return (rows.astype(F32) * factor).astype(BF16)


def mid_b_kernel(e, s, f1, r1, ro, ri, f2l, r2l, kc, ke, ka):
    n = e.shape[1]
    a = e[:n, :]
    h = e[n:, :]
    sel = s[...]
    nh = sel.shape[0]
    chans = f1.shape[0]
    inv_o, inv_i = ro[...], ri[...]
    outs = nt(jnp.concatenate([f1[...], scaled(sel, inv_o), scaled(sel, inv_i)], axis=0), a)
    ins = nn(jnp.concatenate([r1[...], scaled(h, inv_i), scaled(h, inv_o)], axis=0), a)
    f2l[...] = outs[:chans]
    r2l[...] = ins[:chans]
    kc[:nh, :] = ins[chans : chans + nh].astype(BF16)
    kc[nh:, :] = h
    ke[:nh, :] = outs[chans : chans + nh].astype(BF16)
    ke[nh:, :] = sel
    ka[:nh, :] = (2.0 * ins[chans + nh :]).astype(BF16)
    ka[nh : 2 * nh, :] = h
    ka[2 * nh : 3 * nh, :] = (2.0 * outs[chans + nh :]).astype(BF16)
    ka[3 * nh :, :] = sel


def send(pay, cap, left, right, left_two, right_two):
    nh = left.shape[0]
    rows = jnp.concatenate([left, right], axis=1)
    rows_two = jnp.concatenate([left_two, right_two], axis=1)
    both = jnp.concatenate([rows, rows_two], axis=0).astype(BF16)
    k = iota((2 * nh, 2 * nh), 0)
    part = lax.div(k, jnp.int32(2 * cap))
    spot = k - part * (2 * cap)
    source = jnp.where(spot < cap, part * cap + spot, nh + part * cap + spot - cap)
    mine = nn(jnp.where(iota((2 * nh, 2 * nh), 1) == source, 1.0, 0.0).astype(BF16), both)
    for p in range(nh // cap):
        own = mine[p * 2 * cap : (p + 1) * 2 * cap, :]
        pay[p] = jnp.concatenate([rows, own], axis=0).astype(BF16)


def post_b_kernel(cap, one, recv, e, s, b, f1, r1, f2l, r2l, ro, ri, gw, gb, states, reset, update, y, f1l, r1l, pay, flat):
    n = e.shape[1]
    nh = s.shape[0]
    hid = y.shape[0]
    chans = b.shape[0]
    for p in range(nh // cap):
        flat[p * cap : (p + 1) * cap, :] = recv[p, :, : 2 * LANES]
    a = e[:n, :]
    h = e[n:, :]
    sel = s[...]
    inv_o, inv_i = ro[...], ri[...]
    base = b[...].astype(F32)
    seen = flat[:, :chans].astype(BF16)
    back = flat[:, LANES : LANES + chans].astype(BF16)
    f2 = 2.0 * (f2l[...] + tn(back, sel)) * inv_o - base
    r2 = 2.0 * (r2l[...] + tn(seen, h)) * inv_i - base
    states[:chans, :] = b[...]
    states[chans : 2 * chans, :] = f1[...]
    states[2 * chans : 3 * chans, :] = f2.astype(BF16)
    states[3 * chans : 4 * chans, :] = r1[...]
    states[4 * chans :, :] = r2.astype(BF16)
    gates = jax.nn.sigmoid(nn(gw[...], states[...]) + column(gb[...]))
    reset[...] = gates[:hid]
    update[...] = gates[hid:]
    now = (gates[:hid] * base[:hid]).astype(BF16)
    y[...] = now
    local_out = nt(now, a) * inv_o
    local_in = nn(now, a) * inv_i
    f1l[...] = local_out
    r1l[...] = local_in
    bound = nt(sel, jnp.concatenate([now, local_in.astype(BF16)], axis=0))
    halo = nt(h, jnp.concatenate([now, local_out.astype(BF16)], axis=0))
    send(pay, cap, bound[:, :hid], halo[:, :hid], bound[:, hid:], halo[:, hid:])


def gather_matrix(coef, out, nd, cap, per, first, factor):
    nh = nd * cap
    width = nd * per
    k = iota((nh, width), 0)
    col = iota((nh, width), 1)
    r = lax.div(col, jnp.int32(per))
    u = col - r * per
    p = lax.div(u, jnp.int32(cap))
    spot = u - p * cap
    here = lax.div(k, jnp.int32(cap))
    slot = k - here * cap
    inside = u < nh
    place = jnp.where((k == r * cap + spot) & inside, 1.0, 0.0).astype(BF16)
    keep = (here == p) & inside
    for i in range(2):
        wide = nn(coef[:, (first + i) * nh : (first + i + 1) * nh].astype(BF16), place)
        own = (r == here) & (u == nh + cap + slot)
        out[(i + 1) * nh : (i + 2) * nh, :] = jnp.where(keep, factor * wide, jnp.where(own, 1.0, 0.0)).astype(BF16)
    out[:nh, :] = jnp.where((r == here) & (u == nh + slot), 1.0, 0.0).astype(BF16)


def mid_c_kernel(nd, cap, per, fused, recv, e, f1l, r1l, f2l, r2l, *rest):
    n = e.shape[1]
    a = e[:n, :]
    f2l[...] = nt(f1l[...].astype(BF16), a)
    r2l[...] = nn(r1l[...].astype(BF16), a)
    if fused:
        gd, ga, flat = rest
        for p in range(nd):
            flat[p * cap : (p + 1) * cap, :] = recv[p, :, 2 * LANES :]
        gather_matrix(flat, gd, nd, cap, per, 0, 1.0)
        gather_matrix(flat, ga, nd, cap, per, 2, 2.0)


def arrived(fused, hid, nh, g, recv):
    if fused:
        halo = nn(g[...], recv[...].reshape(recv.shape[0] * recv.shape[1], recv.shape[2]))
        two = halo[nh : 2 * nh, :hid], halo[2 * nh :, hid:]
    else:
        halo = recv[...]
        two = halo[nh:, :hid], halo[nh:, hid:]
    one = halo[:nh]
    return one[:, :hid], one[:, hid:], two[0], two[1]


def back_and_send(cap, hid, g, a, h, sel, inv_o, inv_i, z1, z2, pay):
    g0, g1, g2, g3, g4 = (g[m * hid : (m + 1) * hid, :].astype(BF16).astype(F32) for m in range(5))
    y1 = (g2 * inv_o).astype(BF16)
    y2 = (g4 * inv_i).astype(BF16)
    now1 = ((g1 + 2.0 * nn(y1, a)) * inv_o).astype(BF16)
    now2 = ((g3 + 2.0 * nt(y2, a)) * inv_i).astype(BF16)
    z1[...] = now1
    z2[...] = now2
    bound = nt(sel, jnp.concatenate([y1, now1], axis=0))
    halo = nt(h, jnp.concatenate([y2, now2], axis=0))
    send(pay, cap, bound[:, :hid], halo[:, :hid], bound[:, hid:], halo[:, hid:])
    return g0 - g2 - g4


def hidden_weights(w, hid, block, orders):
    return jnp.concatenate([w[:, m * block : m * block + hid] for m in range(orders)], axis=1)


def post_c_kernel(fused, cap, orders, g, recv, e, s, kc, ke, y, f1l, r1l, f2l, r2l, ro, ri, states, cw, cb, upstream, update,
                  mixed, cand_grad, gate_update, z1, z2, direct, pay):
    n = e.shape[1]
    nh = s.shape[0]
    hid = y.shape[0]
    block = states.shape[0] // orders
    a = e[:n, :]
    h = e[n:, :]
    sel = s[...]
    inv_o, inv_i = ro[...], ri[...]
    c1, e1, c2, e2 = arrived(fused, hid, nh, g, recv)
    base = y[...].astype(F32)
    c1, e1 = c1.astype(BF16), e1.astype(BF16)
    cc = jnp.concatenate([c1, c2.astype(BF16)], axis=0)
    ee = jnp.concatenate([e1, e2.astype(BF16)], axis=0)
    f1 = f1l[...] + tn(e1, sel) * inv_o
    f2 = 2.0 * (f2l[...] + tn(ee, ke[...])) * inv_o - base
    r1 = r1l[...] + tn(c1, h) * inv_i
    r2 = 2.0 * (r2l[...] + tn(cc, kc[...])) * inv_i - base
    for m, value in enumerate((y[...], f1, f2, r1, r2)):
        mixed[m * block : m * block + hid, :] = value.astype(BF16)
        mixed[m * block + hid : (m + 1) * block, :] = states[m * block + hid : (m + 1) * block, :]
    weights = cw[...]
    cand = jnp.tanh(nn(weights, mixed[...]) + column(cb[...]))
    up = upstream[0].astype(F32)
    gate = update[...]
    grad = (up * (1.0 - gate) * (1.0 - cand * cand)).astype(BF16)
    cand_grad[...] = grad
    held = states[:hid, :].astype(F32)
    gate_update[...] = (up * (held - cand) * gate * (1.0 - gate)).astype(BF16)
    back = tn(hidden_weights(weights, hid, block, orders), grad)
    direct[...] = back_and_send(cap, hid, back, a, h, sel, inv_o, inv_i, z1, z2, pay)


def weight_part(grad, features, orders, chans, hid, fin):
    block = features.shape[0] // orders
    width = -(-(orders * chans + 1) // LANES) * LANES
    shape = (width, orders * block)
    k = iota(shape, 0)
    col = iota(shape, 1)
    m = lax.div(col, jnp.int32(block))
    c = col - m * block
    source = jnp.where(c < hid, m * chans + fin + c, jnp.where(c < hid + fin, m * chans + c - hid, -1))
    source = jnp.where(col == hid + fin, orders * chans, source)
    order = jnp.where(k == source, 1.0, 0.0).astype(BF16)
    return nt(nt(grad, features).astype(BF16), order)


def mid_d_kernel(orders, fin, e, z1, z2, direct, cand_grad, mixed, gate_update, states, base, part):
    n = e.shape[1]
    a = e[:n, :]
    hid = z1.shape[0]
    base[...] = direct[...] + nn(z1[...], a) + nt(z2[...], a)
    part[:hid, :] = weight_part(gate_update[...], states[...], orders, hid + fin, hid, fin).astype(BF16)
    part[hid:, :] = weight_part(cand_grad[...], mixed[...], orders, hid + fin, hid, fin).astype(BF16)


def add_halo(fused, g, recv, ka, base):
    hid = base.shape[0]
    nh = ka.shape[0] // 4
    c1, e1, c2, e2 = arrived(fused, hid, nh, g, recv)
    return base[...] + tn(jnp.concatenate([c1, c2, e1, e2], axis=0).astype(BF16), ka[...])


def post_d_kernel(fused, cap, orders, g, recv, e, s, ka, base, ro, ri, states, gw, upstream, reset, update, gate_update,
                  gate_reset, z1, z2, direct, pay):
    n = e.shape[1]
    hid = base.shape[0]
    block = states.shape[0] // orders
    scaled_grad = add_halo(fused, g, recv, ka, base)
    held = states[:hid, :].astype(F32)
    gate = reset[...]
    grad = (scaled_grad * held * gate * (1.0 - gate)).astype(BF16)
    gate_reset[...] = grad
    weights = hidden_weights(gw[...], hid, block, orders)
    back = tn(weights, jnp.concatenate([grad, gate_update[...]], axis=0))
    rest = back_and_send(cap, hid, back, e[:n, :], e[n:, :], s[...], ro[...], ri[...], z1, z2, pay)
    direct[...] = rest + upstream[0].astype(F32) * update[...] + scaled_grad * gate


def mid_e_kernel(orders, fin, rows, e, z1, z2, direct, gate_reset, states, part, base, grads):
    n = e.shape[1]
    a = e[:n, :]
    hid = z1.shape[0]
    base[...] = direct[...] + nn(z1[...], a) + nt(z2[...], a)
    first = weight_part(gate_reset[...], states[...], orders, hid + fin, hid, fin)
    both = jnp.concatenate([first, part[...].astype(F32)], axis=0)
    for k in range(grads.shape[0]):
        if k * rows < both.shape[0]:
            grads[k] = both[k * rows : (k + 1) * rows, :].astype(BF16)
        else:
            grads[k] = jnp.zeros(grads.shape[1:], BF16)


def post_e_kernel(fused, g, recv, ka, base, out):
    out[0] = add_halo(fused, g, recv, ka, base).astype(BF16)


def add_kernel(recv, out):
    total = recv[0].astype(F32)
    for k in range(1, recv.shape[0]):
        total = total + recv[k].astype(F32)
    for k in range(out.shape[0]):
        out[k] = total.astype(BF16)


def finish_kernel(hid, factor, recv, gw, gb, cw, cb):
    rows = recv.shape[1]
    features = gw.shape[1]
    total = gw.shape[0] + cw.shape[0]
    for k in range(total // rows):
        part = recv[k].astype(F32)[:, :features] * factor
        at = k * rows
        if at < 2 * hid:
            gw[at : at + rows, :] = part
        else:
            cw[at - 2 * hid : at - 2 * hid + rows, :] = part
    flat = jnp.concatenate([recv[k].astype(F32) for k in range(total // rows)], axis=0)
    pick = jnp.where(iota((8, flat.shape[1]), 1) == features, 1.0, 0.0).astype(BF16)
    bias = nt(pick, flat.astype(BF16))[:1] * factor
    gb[...] = bias[:, : 2 * hid]
    cb[...] = bias[:, 2 * hid :]


def spread_body(
    readings,
    previous,
    upstream,
    gate_weight,
    gate_bias,
    cand_weight,
    cand_bias,
    neighbours,
    edge_weight,
    send_rows,
):
    fin, hid = readings.shape[1], previous.shape[1]
    chans = fin + hid
    orders = gate_weight.shape[1] // chans
    n = readings.shape[2]
    nd = lax.axis_size("dom")
    devices = nd * lax.axis_size("snap")
    nh = send_rows.shape[1]
    cap = nh // nd
    block = hid + 16 * (-(-(fin + 1) // 16))
    one = hid + fin
    per = nh + 2 * cap
    fused = 3 * nh * nd * per <= 1 << 18
    move = functools.partial(lax.all_to_all, axis_name="dom", split_axis=0, concat_axis=0, tiled=True)

    e, s, b, pay = run(
        functools.partial(prep_kernel, cap), "prep",
        [((n + nh, n), BF16), ((nh, n), BF16), ((block, n), BF16), ((nd, cap, 2 * LANES), F32)],
        neighbours, edge_weight, send_rows, readings, previous,
    )
    recv = move(pay)
    fa, ra, gw, cw = run(
        functools.partial(mid_a_kernel, hid, fin, orders), "mid_a",
        [((block, n), F32), ((block, n), F32), ((2 * hid, orders * block), BF16), ((hid, orders * block), BF16)],
        e, b, gate_weight, cand_weight,
    )
    wide = 2 * LANES + 4 * nh
    f1, r1, ro, ri, pay = run(
        functools.partial(post_a_kernel, one, cap), "post_a",
        [((block, n), BF16), ((block, n), BF16), ((1, n), F32), ((1, n), F32), ((nd, cap, wide), F32)],
        recv, e, s, fa, ra, scratch=[pltpu.VMEM((nh, 2 * LANES), F32)],
    )
    recv_b = move(pay)
    f2l, r2l, kc, ke, ka = run(
        mid_b_kernel, "mid_b",
        [((block, n), F32), ((block, n), F32), ((2 * nh, n), BF16), ((2 * nh, n), BF16), ((4 * nh, n), BF16)],
        e, s, f1, r1, ro, ri,
    )
    pay_kind = ((nd, per, 2 * hid), BF16)
    field, field16 = ((hid, n), F32), ((hid, n), BF16)
    states, reset, update, y, f1l, r1l, pay = run(
        functools.partial(post_b_kernel, cap, one), "post_b",
        [((orders * block, n), BF16), field, field, field16, field, field, pay_kind],
        recv_b, e, s, b, f1, r1, f2l, r2l, ro, ri, gw, gate_bias[None, :],
        scratch=[pltpu.VMEM((nh, 2 * LANES), F32)],
    )
    recv = move(pay)
    table = ((3 * nh, nd * per), BF16)
    f2l, r2l, *tables = run(
        functools.partial(mid_c_kernel, nd, cap, per, fused), "mid_c",
        [field, field] + [table] * (2 if fused else 0),
        recv_b, e, f1l, r1l, scratch=[pltpu.VMEM((nh, 4 * nh), F32)] if fused else [],
    )
    if fused:
        inward, outward = tables
        halo_of = lambda got, first, factor: got
    else:
        inward = outward = jnp.zeros((8, LANES), BF16)
        coefs = recv_b[:, :, 2 * LANES :].reshape(nd, cap, 4, nd, cap)

        def halo_of(got, first, factor):
            rows = got[:, :nh].reshape(nd, nd, cap, 2, hid).astype(F32)
            two = jnp.einsum("psgrt,rptgk->psgk", coefs[:, :, first : first + 2], rows)
            two = factor * two.reshape(nh, 2 * hid) + got[:, nh + cap :].reshape(nh, 2 * hid).astype(F32)
            return jnp.concatenate([got[:, nh : nh + cap].reshape(nh, 2 * hid).astype(F32), two], axis=0)

    mixed, cand_grad, gate_update, z1, z2, direct, pay = run(
        functools.partial(post_c_kernel, fused, cap, orders), "post_c",
        [((orders * block, n), BF16), field16, field16, field16, field16, field, pay_kind],
        inward, halo_of(recv, 0, 1.0), e, s, kc, ke, y, f1l, r1l, f2l, r2l, ro, ri, states, cw, cand_bias[None, :], upstream, update,
    )
    recv = move(pay)
    width = -(-(orders * chans + 1) // LANES) * LANES
    base, part = run(
        functools.partial(mid_d_kernel, orders, fin), "mid_d", [field, ((2 * hid, width), BF16)],
        e, z1, z2, direct, cand_grad, mixed, gate_update, states,
    )
    gate_reset, z1, z2, direct, pay = run(
        functools.partial(post_d_kernel, fused, cap, orders), "post_d",
        [field16, field16, field16, field, pay_kind],
        outward, halo_of(recv, 2, 2.0), e, s, ka, base, ro, ri, states, gw, upstream, reset, update, gate_update,
    )
    recv = move(pay)
    rows = 8 * (-(-3 * hid // (8 * devices)))
    base, grads = run(
        functools.partial(mid_e_kernel, orders, fin, rows), "mid_e", [field, ((devices, rows, width), BF16)],
        e, z1, z2, direct, gate_reset, states, part,
    )
    (state_grad,) = run(
        functools.partial(post_e_kernel, fused), "post_e", [((1, hid, n), BF16)],
        outward, halo_of(recv, 2, 2.0), ka, base,
    )
    both = ("snap", "dom")
    grads = lax.all_to_all(grads, both, 0, 0, tiled=True)
    (grads,) = run(add_kernel, "add", [((devices, rows, width), BF16)], grads)
    grads = lax.all_to_all(grads, both, 0, 0, tiled=True)
    factor = 1.0 / math.sqrt(readings.shape[0] * lax.axis_size("snap") * n * nd)
    feats = orders * chans
    grad_gw, grad_gb, grad_cw, grad_cb = run(
        functools.partial(finish_kernel, hid, factor), "finish",
        [((2 * hid, feats), F32), ((1, 2 * hid), F32), ((hid, feats), F32), ((1, hid), F32)],
        grads,
    )
    return state_grad, grad_gw, grad_gb[0], grad_cw, grad_cb[0]


def pack_kernel(nb, w, rows, readings, previous, upstream, own, both, tail):
    degree = nb.shape[0]
    nh = rows.shape[1]
    hid = previous.shape[1]
    fin = readings.shape[1]
    block = own.shape[0]
    tail[...] = jnp.zeros_like(tail)
    tail[:fin, :] = readings[0].astype(F32)
    high = lax.shift_right_logical(nb[...], 5)
    tail[fin : fin + degree, :] = high.astype(F32)
    tail[fin + degree : fin + 2 * degree, :] = (nb[...] - high * 32).astype(F32)
    tail[fin + 2 * degree : fin + 3 * degree, :] = w[...]
    at = fin + 3 * degree
    high = lax.shift_right_logical(rows[...], 5)
    tail[at : at + 1, :nh] = high.astype(F32)
    tail[at + 1 : at + 2, :nh] = (rows[...] - high * 32).astype(F32)
    for to in (own, both):
        to[:hid, :] = previous[0]
        to[hid:block, :] = tail[...].astype(BF16)
    both[block:, :] = upstream[0]


def exchange(first, second, hc, sc, pay):
    count = first[0].shape[0]
    parts = len(first)
    pay[:count, :] = jnp.concatenate([nt(first[p], sc[p]).astype(BF16) for p in range(parts)], axis=1)
    pay[count:, :] = jnp.concatenate([nt(second[p], hc[p]).astype(BF16) for p in range(parts)], axis=1)


def merged(parts, mine, got):
    step = mine.shape[1] // (2 * parts)
    here = lax.rem(lax.div(iota(mine.shape, 1), jnp.int32(step)), jnp.int32(2)) == 0
    value = jnp.where(here, mine[...].astype(F32), got[...].astype(F32)).astype(BF16)
    count = mine.shape[0] // 2
    return value[:count, :], value[count:, :]


def build_square(hid, fin, degree, block, a, at):
    n = a.shape[1]
    row = iota((32, n), 0).astype(F32)
    tail = block[hid : hid + 16 * (-(-(fin + 3 * degree + 2) // 16)), :].astype(F32)
    high, low = tail[fin : fin + degree], tail[fin + degree : fin + 2 * degree]
    w = tail[fin + 2 * degree : fin + 3 * degree]
    low_is = [jnp.where(low[d : d + 1] == row, 1.0, 0.0).astype(BF16) for d in range(degree)]
    for chunk in range(n // 32):
        total = None
        for d in range(degree):
            term = low_is[d] * jnp.where(high[d : d + 1] == float(chunk), w[d : d + 1], 0.0).astype(BF16)
            total = term if total is None else total + term
        a[chunk * 32 : (chunk + 1) * 32, :] = total
    at[...] = a[...].T


def build_edge(cap, hid, fin, degree, parts, p, block, hc, hx, sc, sx, b):
    n = b.shape[1]
    slots = sx.shape[0]
    nh = 2 * parts * cap
    half = parts * cap
    core = lax.rem(lax.axis_index("dom"), 2)
    line = iota((nh, 1), 0)
    rel = lax.div(line, jnp.int32(half))
    k = lax.div(line - rel * half, jnp.int32(cap))
    t = line - rel * half - k * cap
    spot = (k * 2 + lax.bitwise_xor(rel, core)) * cap + t
    node = (n + spot).astype(F32)
    width = -(-nh // LANES) * LANES
    slot = iota((slots, nh), 0)
    outer = lax.div(slot, jnp.int32(nh))
    rest = slot - outer * nh
    slot_rel = lax.div(rest, jnp.int32(half))
    rest = rest - slot_rel * half
    inner = lax.div(rest, jnp.int32(cap))
    filled = iota((slots, nh), 1) == slot_rel * half + outer * cap + rest - inner * cap
    tail = block[hid : hid + 16 * (-(-(fin + 3 * degree + 2) // 16)), :].astype(F32)
    w = tail[fin + 2 * degree : fin + 3 * degree]
    start = fin + 3 * degree
    sent = tail[start : start + 1] * 32.0 + tail[start + 1 : start + 2]
    names = tail[fin : fin + degree] * 32.0 + tail[fin + degree : fin + 2 * degree]
    total = jnp.zeros((nh, n), F32)
    for d in range(degree):
        total = total + jnp.where(names[d : d + 1] == node, w[d : d + 1], 0.0)
    halo = total.astype(BF16)
    hc[...] = halo
    named = jnp.where(iota((nh, width), 1) == spot, sent[:, :width], 0.0)
    target = jnp.sum(named, axis=1, keepdims=True).astype(jnp.int32)
    picked = jnp.where(iota((nh, n), 1) == target, 1.0, 0.0).astype(BF16)
    sc[...] = picked
    place = jnp.where(filled & (inner == p), 1.0, 0.0).astype(BF16)
    hx[...] = nn(place, halo).astype(BF16)
    sx[...] = nn(place, picked).astype(BF16)
    b[:hid, :] = block[:hid, :]
    line = iota(tail.shape, 0)
    b[hid:, :] = jnp.where(line < fin, tail, jnp.where(line == fin, 1.0, 0.0)).astype(BF16)


def build_early_kernel(cap, hid, fin, degree, parts, *refs):
    count = parts - 1
    z = lax.shift_right_logical(lax.axis_index("dom"), 1)
    for k in range(count):
        p = lax.bitwise_xor(z, jnp.int32(k))
        build_edge(cap, hid, fin, degree, parts, p, refs[k], *(ref.at[k] for ref in refs[count + 2 :]))
        build_square(hid, fin, degree, refs[k], refs[count].at[k], refs[count + 1].at[k])


def build_late_kernel(cap, hid, fin, degree, parts, last, *refs):
    early, outs, pay = refs[:5], refs[5:10], refs[10]
    z = lax.shift_right_logical(lax.axis_index("dom"), 1)
    for k in range(parts - 1):
        p = lax.bitwise_xor(z, jnp.int32(k))
        for source, to in zip(early, outs):
            to[p] = source[k]
    p = lax.bitwise_xor(z, jnp.int32(parts - 1))
    build_edge(cap, hid, fin, degree, parts, p, last, *(ref.at[p] for ref in outs))
    hc, sc, b = outs[0], outs[2], outs[4]
    base = [b[p] for p in range(parts)]
    exchange(base, base, hc, sc, pay)


def chip_source(col, chans, hid, fin, block):
    m = lax.div(col, jnp.int32(block))
    c = col - m * block
    m = jnp.where(m == 2, 3, jnp.where(m == 3, 2, m))
    return m, c, jnp.where(c < hid, m * chans + fin + c, jnp.where(c < hid + fin, m * chans + c - hid, -1))


def order_kernel(hid, fin, orders, block, gw, cw, gw_o, cw_o, gw_b, cw_b, order):
    chans = hid + fin
    feats = cw.shape[1]
    shape = (feats, orders * block)
    source = chip_source(iota(shape, 1), chans, hid, fin, block)[2]
    pick = jnp.where(iota(shape, 0) == source, 1.0, 0.0).astype(BF16)
    gw_o[...] = tn(gw[...], pick).astype(BF16)
    cw_o[...] = nn(cw[...], pick).astype(BF16)
    shape = (orders * hid, feats)
    line = iota(shape, 0)
    m = lax.div(line, jnp.int32(hid))
    pick = jnp.where(iota(shape, 1) == m * chans + fin + line - m * hid, 1.0, 0.0).astype(BF16)
    gw_b[...] = nn(pick, gw[...]).astype(BF16)
    cw_b[...] = nt(pick, cw[...]).astype(BF16)
    m, c, source = chip_source(iota(order.shape, 0), chans, hid, fin, block)
    source = jnp.where((m == 0) & (c == hid + fin), feats, source)
    order[...] = jnp.where(iota(order.shape, 1) == source, 1.0, 0.0).astype(BF16)


def here(early, late, k):
    z = lax.shift_right_logical(lax.axis_index("dom"), 1)
    count = early.shape[0]
    return lax.bitwise_xor(z, jnp.int32(k)), early[k] if k < count else late[k - count]


def local_kernel(a0, at0, a1, at1, x1, x2, l1, l2):
    for k in range(x1.shape[0]):
        p, a = here(a0, a1, k)
        l1[p] = nn(x1[p], a)
    for k in range(x1.shape[0]):
        p, at = here(at0, at1, k)
        l2[p] = nn(x2[p], at)


def arrive(sx, hx, mine, got, l1, l2):
    parts = range(sx.shape[0])
    top, low = merged(sx.shape[0], mine, got)
    pulled = [l1[p] + nn(top, hx[p]) for p in parts]
    pushed = [l2[p] + nn(low, sx[p]) for p in parts]
    return parts, pulled, pushed


def chip_a_kernel(one, mine, got, hc, hx, sc, sx, b, l1, l2, sa, ro, ri, pay):
    chans = b.shape[1]
    parts, pulled, pushed = arrive(sx, hx, mine, got, l1, l2)
    inv_o = [1.0 / pushed[p][one : one + 1, :] for p in parts]
    inv_i = [1.0 / pulled[p][one : one + 1, :] for p in parts]
    outs = [(pushed[p] * inv_o[p]).astype(BF16) for p in parts]
    ins = [(pulled[p] * inv_i[p]).astype(BF16) for p in parts]
    for p in parts:
        ro[p] = inv_o[p]
        ri[p] = inv_i[p]
        sa[p, :chans, :] = b[p]
        sa[p, chans : 2 * chans, :] = outs[p]
        sa[p, 2 * chans :, :] = ins[p]
    exchange(ins, outs, hc, sc, pay)


def local_a_kernel(hid, fin, degree, a0, at0, last, b, a1, at1, l1, l2):
    build_square(hid, fin, degree, last, a1.at[0], at1.at[0])
    local_kernel(a0, at0, a1, at1, b, b, l1, l2)


def local_b_kernel(a0, at0, a1, at1, sa, gw, l1, l2, gp):
    chans = l1.shape[1]
    weights = gw[:, : 3 * chans]
    for k in range(sa.shape[0]):
        p, a = here(a0, a1, k)
        l1[p] = nn(sa[p, 2 * chans :, :], a)
    for k in range(sa.shape[0]):
        p, at = here(at0, at1, k)
        l2[p] = nn(sa[p, chans : 2 * chans, :], at)
    for p in range(sa.shape[0]):
        gp[p] = nn(weights, sa[p])


def chip_b_kernel(mine, got, hc, hx, sc, sx, sa, l1, l2, ro, ri, gw, gb, gp, sb, reset, y, pay):
    hid = y.shape[1]
    chans = l1.shape[1]
    bias = column(gb[:, :hid])
    weights = gw[:hid, 3 * chans :]
    parts, pulled, pushed = arrive(sx, hx, mine, got, l1, l2)
    base = [sa[p, :chans, :].astype(F32) for p in parts]
    r2 = [(pulled[p] * (2.0 * ri[p]) - base[p]).astype(BF16) for p in parts]
    f2 = [(pushed[p] * (2.0 * ro[p]) - base[p]).astype(BF16) for p in parts]
    second = [jnp.concatenate([f2[p], r2[p]], axis=0) for p in parts]
    gates = [jax.nn.sigmoid(gp[p, :hid, :] + nn(weights, second[p]) + bias) for p in parts]
    now = [(gates[p] * base[p][:hid]).astype(BF16) for p in parts]
    for p in parts:
        sb[p] = second[p]
        reset[p] = gates[p]
        y[p] = now[p]
    exchange(now, now, hc, sc, pay)


def local_c1_kernel(a0, at0, a1, at1, y, sb, gw, gb, gp, l1, l2, update):
    hid = y.shape[1]
    local_kernel(a0, at0, a1, at1, y, y, l1, l2)
    bias = column(gb[:, hid:])
    weights = gw[hid:, gw.shape[1] - sb.shape[1] :]
    parts = range(y.shape[0])
    gates = [gp[p, hid:, :] + nn(weights, sb[p]) + bias for p in parts]
    for p in parts:
        update[p] = jax.nn.sigmoid(gates[p])


def chip_c1_kernel(mine, got, hc, hx, sc, sx, y, sa, l1, l2, ro, ri, ma, pay):
    hid = y.shape[1]
    chans = ma.shape[1] // 3
    parts, pulled, pushed = arrive(sx, hx, mine, got, l1, l2)
    ins = [(pulled[p] * ri[p]).astype(BF16) for p in parts]
    outs = [(pushed[p] * ro[p]).astype(BF16) for p in parts]
    exchange(ins, outs, hc, sc, pay)
    for p in parts:
        for m, value in enumerate((y[p], outs[p], ins[p])):
            ma[p, m * chans : m * chans + hid, :] = value
            ma[p, m * chans + hid : (m + 1) * chans, :] = sa[p, m * chans + hid : (m + 1) * chans, :]


def local_c2_kernel(a0, at0, a1, at1, ma, cw, l1, l2, cp):
    hid = l1.shape[1]
    chans = ma.shape[1] // 3
    weights = cw[:, : 3 * chans]
    for k in range(ma.shape[0]):
        p, a = here(a0, a1, k)
        l1[p] = nn(ma[p, 2 * chans : 2 * chans + hid, :], a)
    for k in range(ma.shape[0]):
        p, at = here(at0, at1, k)
        l2[p] = nn(ma[p, chans : chans + hid, :], at)
    for p in range(ma.shape[0]):
        cp[p] = nn(weights, ma[p])


def split_back(back, hid, ro, ri, y1, y2, g1, g3, direct):
    parts = range(len(back))
    blocks = [[back[p][m * hid : (m + 1) * hid, :] for m in range(5)] for p in parts]
    one = [(blocks[p][2] * (2.0 * ro[p])).astype(BF16) for p in parts]
    two = [(blocks[p][4] * (2.0 * ri[p])).astype(BF16) for p in parts]
    for p in parts:
        y1[p] = one[p]
        y2[p] = two[p]
        g1[p] = blocks[p][1].astype(BF16)
        g3[p] = blocks[p][3].astype(BF16)
        direct[p] = blocks[p][0] - blocks[p][2] - blocks[p][4]
    return one, two


def chip_c2_kernel(parts, *refs):
    ups, refs = refs[:parts], refs[parts:]
    mine, got, hc, hx, sc, sx, ma, sa, sb, l1, l2, ro, ri, cw, cw_b, cb, cp, update = refs[:18]
    mb, cand_grad, gate_update, y1, y2, g1, g3, upstream, direct, pay = refs[18:]
    hid = l1.shape[1]
    chans = ma.shape[1] // 3
    z = lax.shift_right_logical(lax.axis_index("dom"), 1)
    for k in range(parts):
        upstream[lax.bitwise_xor(z, jnp.int32(k))] = ups[k][0] if len(ups[k].shape) == 3 else ups[k][ups[k].shape[0] - hid :, :]
    bias = column(cb[...])
    weights = cw[:, 3 * chans :]
    parts, pulled, pushed = arrive(sx, hx, mine, got, l1, l2)
    base = [ma[p, :hid, :].astype(F32) for p in parts]
    r2 = [(pulled[p] * (2.0 * ri[p]) - base[p]).astype(BF16) for p in parts]
    f2 = [(pushed[p] * (2.0 * ro[p]) - base[p]).astype(BF16) for p in parts]
    second = [
        jnp.concatenate([f2[p], sb[p, hid:chans, :], r2[p], sb[p, chans + hid :, :]], axis=0) for p in parts
    ]
    cand = [jnp.tanh(cp[p] + nn(weights, second[p]) + bias) for p in parts]
    rest = [upstream[p].astype(F32) * (1.0 - update[p]) for p in parts]
    grad = [(rest[p] - rest[p] * cand[p] * cand[p]).astype(BF16) for p in parts]
    back = [nn(cw_b[...], grad[p]) for p in parts]
    for p in parts:
        mb[p] = second[p]
        cand_grad[p] = grad[p]
        gate_update[p] = ((sa[p, :hid, :].astype(F32) - cand[p]) * (rest[p] * update[p])).astype(BF16)
    one, two = split_back(back, hid, ro, ri, y1, y2, g1, g3, direct)
    exchange(one, two, hc, sc, pay)


def chip_part(grads, first, second, order):
    parts = range(first.shape[0])
    split = first.shape[1]
    one = sum(nt(grads[p], first[p]) for p in parts).astype(BF16)
    two = sum(nt(grads[p], second[p]) for p in parts).astype(BF16)
    return nn(one, order[:split, :]) + nn(two, order[split:, :])


def cand_sums(cand_grad, features, parts):
    return sum(nt(cand_grad[p], features[p]) for p in parts)


def local_d_kernel(count, a0, at0, a1, at1, y1, y2, cand_grad, ma, mb, l1, l2, one, two):
    local_kernel(a0, at0, a1, at1, y1, y2, l1, l2)
    one[...] = cand_sums(cand_grad, ma, range(count))
    two[...] = cand_sums(cand_grad, mb, range(count))


def chip_d1_kernel(mine, got, hc, hx, sc, sx, l1, l2, g1, g3, ro, ri, z1, z2, pay):
    parts, pulled, pushed = arrive(sx, hx, mine, got, l1, l2)
    one = [((g1[p].astype(F32) + pulled[p]) * ro[p]).astype(BF16) for p in parts]
    two = [((g3[p].astype(F32) + pushed[p]) * ri[p]).astype(BF16) for p in parts]
    exchange(one, two, hc, sc, pay)
    for p in parts:
        z1[p] = one[p]
        z2[p] = two[p]


def local_d2_kernel(count, a0, at0, a1, at1, z1, z2, direct, cand_grad, ma, mb, one, two, order, base, part):
    rest = range(count, z1.shape[0])
    split = one.shape[1]
    first = (one[...] + cand_sums(cand_grad, ma, rest)).astype(BF16)
    second = (two[...] + cand_sums(cand_grad, mb, rest)).astype(BF16)
    part[...] = (nn(first, order[:split, :]) + nn(second, order[split:, :])).astype(BF16)
    for k in range(z1.shape[0]):
        p, a = here(a0, a1, k)
        _, at = here(at0, at1, k)
        base[p] = direct[p] + nn(z1[p], a) + nn(z2[p], at)


def chip_d2_kernel(mine, got, hx, sx, base, sa, sb, reset, gate_update, order, part, gate_grad, kept, keep, give, flat):
    hid = base.shape[1]
    both = 2 * hid
    half = keep.shape[0]
    core = lax.rem(lax.axis_index("dom"), 2)
    parts = range(sx.shape[0])
    top, low = merged(sx.shape[0], mine, got)
    scaled_grad = [base[p] + nn(top, hx[p]) + nn(low, sx[p]) for p in parts]
    through = [scaled_grad[p] * reset[p] for p in parts]
    grad = [
        jnp.concatenate([(sa[p, :hid, :].astype(F32) * (through[p] - through[p] * reset[p])).astype(BF16), gate_update[p]], axis=0)
        for p in parts
    ]
    for p in parts:
        gate_grad[p] = grad[p]
        kept[p] = through[p]
    flat[:both, :] = chip_part(grad, sa, sb, order)
    flat[both:, :] = part[...].astype(F32)
    keep[...] = flat[pl.ds(pl.multiple_of(core * half, 8), half), :].astype(BF16)
    give[...] = flat[pl.ds(pl.multiple_of((1 - core) * half, 8), half), :].astype(BF16)


def back_e_kernel(hc, sc, gate_grad, kept, ro, ri, gw_b, upstream, update, y1, y2, g1, g3, direct, pay):
    hid = kept.shape[1]
    parts = range(sc.shape[0])
    back = [nn(gw_b[...], gate_grad[p]) for p in parts]
    one, two = split_back(back, hid, ro, ri, y1, y2, g1, g3, direct)
    for p in parts:
        direct[p] = direct[p] + upstream[p].astype(F32) * update[p] + kept[p]
    exchange(one, two, hc, sc, pay)


def local_e_kernel(a, at, z1, z2, direct, base):
    z = lax.shift_right_logical(lax.axis_index("dom"), 1)
    base[...] = direct[z] + nn(z1[z], a[0]) + nn(z2[z], at[0])


def chip_e_kernel(mine, got, hc, hx, sc, sx, base, out, done):
    done[...] = jnp.zeros_like(done)
    z = lax.shift_right_logical(lax.axis_index("dom"), 1)
    top, low = merged(sx.shape[0], mine, got)
    out[0] = (base[...] + nn(top, hx[z]) + nn(low, sx[z])).astype(BF16)


def sum_kernel(*refs):
    values = [ref[...].astype(F32) for ref in refs[:-2]]
    while len(values) > 1:
        values = [values[k] + values[k + 1] for k in range(0, len(values), 2)]
    refs[-1][...] = values[0].astype(refs[-1].dtype)
    refs[-2][...] = values[0].astype(refs[-2].dtype)


def end_kernel(factor, mine, got, gw, gb, cw, cb, flat):
    half = mine.shape[0]
    core = lax.rem(lax.axis_index("dom"), 2)
    flat[pl.ds(pl.multiple_of(core * half, 8), half), :] = mine[...] * factor
    flat[pl.ds(pl.multiple_of((1 - core) * half, 8), half), :] = got[...] * factor
    features, rows = gw.shape
    gates = flat[:rows, :].T
    gw[...] = gates[:features, :]
    gb[...] = gates[features : features + 1, :]
    cw[...] = flat[rows:, :features]
    last = (features // LANES) * LANES
    cb[...] = flat[rows:, last : last + LANES].T[features - last : features - last + 1, :]


def chip_body(
    readings,
    previous,
    upstream,
    gate_weight,
    gate_bias,
    cand_weight,
    cand_bias,
    neighbours,
    edge_weight,
    send_rows,
):
    fin, hid = readings.shape[1], previous.shape[1]
    chans = fin + hid
    orders = gate_weight.shape[1] // chans
    degree = neighbours.shape[0]
    n = readings.shape[2]
    nd = lax.axis_size("dom")
    snaps = lax.axis_size("snap")
    parts = nd // 2
    cap = send_rows.shape[1] // nd
    block = hid + 16 * (-(-(fin + 3 * degree + 2) // 16))
    slots = 2 * parts * parts * cap

    def swap(array, k, axis="dom", size=nd):
        return lax.ppermute(array, axis, [(i, i ^ k) for i in range(size)])

    own, both = run(
        pack_kernel, "pack", [((block, n), BF16), ((block + hid, n), BF16)],
        neighbours, edge_weight, send_rows, readings, previous, upstream,
        scratch=[pltpu.VMEM((block - hid, n), F32)], vmem=56,
    )
    near = swap(both, 2)
    blocks = [own] + [near if k == 1 else swap(own, 2 * k) for k in range(1, parts - 1)]
    relay = blocks[-1]
    ups = [upstream] + [near if k == 1 else swap(upstream, 2 * k) for k in range(1, parts - 1)]
    ups.append(swap(ups[-1], 2))
    width = -(-(orders * chans + 1) // LANES) * LANES
    gw, cw, gw_b, cw_b, order = run(
        functools.partial(order_kernel, hid, fin, orders, block), "order",
        [((2 * hid, orders * block), BF16), ((hid, orders * block), BF16), ((orders * hid, 2 * hid), BF16), ((orders * hid, hid), BF16),
         ((orders * block, width), BF16)],
        gate_weight.T, cand_weight, after=[own],
    )
    relay, gw = lax.optimization_barrier((relay, gw))
    wide, wide16, wide_pay = ((parts, block, n), F32), ((parts, block, n), BF16), ((2 * block, slots), BF16)
    field, field16, pay_kind = ((parts, hid, n), F32), ((parts, hid, n), BF16), ((2 * hid, slots), BF16)
    first, second = ((parts, 3 * block, n), BF16), ((parts, 2 * block, n), BF16)
    line = ((parts, 1, n), F32)
    built = [((n, n), BF16)] * 2 + [((rows, n), BF16) for rows in (2 * parts * cap, slots)] * 2 + [((block, n), BF16)]
    early = run(
        functools.partial(build_early_kernel, cap, hid, fin, degree, parts), "build_early",
        [((parts - 1, *shape), kind) for shape, kind in built], *blocks[:-1], relay,
    )
    last = swap(relay, 2)
    hc, hx, sc, sx, b, pay = run(
        functools.partial(build_late_kernel, cap, hid, fin, degree, parts), "build_late",
        [((parts, *shape), kind) for shape, kind in built[2:]] + [wide_pay], last, *early[2:],
    )
    edges = (hc, hx, sc, sx)
    got = swap(pay, 1)
    a, at, l1, l2 = run(
        functools.partial(local_a_kernel, hid, fin, degree), "local_a", [((1, n, n), BF16)] * 2 + [wide, wide], *early[:2], last, b
    )
    local = (early[0], early[1], a, at)
    sa, ro, ri, pay = run(
        functools.partial(chip_a_kernel, hid + fin), "chip_a", [first, line, line, wide_pay],
        pay, got, *edges, b, l1, l2, after=ups[2:],
    )
    got = swap(pay, 1)
    l1, l2, gp = run(local_b_kernel, "local_b", [wide, wide, ((parts, 2 * hid, n), F32)], *local, sa, gw)
    sb, reset, y, pay = run(
        chip_b_kernel, "chip_b", [second, field, field16, pay_kind],
        pay, got, *edges, sa, l1, l2, ro, ri, gw, gate_bias[None, :], gp,
    )
    got = swap(pay, 1)
    l1, l2, update = run(
        local_c1_kernel, "local_c1", [field, field, field], *local, y, sb, gw, gate_bias[None, :], gp
    )
    ma, pay = run(chip_c1_kernel, "chip_c1", [first, pay_kind], pay, got, *edges, y, sa, l1, l2, ro, ri)
    got = swap(pay, 1)
    l1, l2, cp = run(local_c2_kernel, "local_c2", [field, field, field], *local, ma, cw)
    mb, cand_grad, gate_update, y1, y2, g1, g3, up, direct, pay = run(
        functools.partial(chip_c2_kernel, parts), "chip_c2", [second] + [field16] * 7 + [field, pay_kind],
        *ups, pay, got, *edges, ma, sa, sb, l1, l2, ro, ri, cw, cw_b, cand_bias[None, :], cp, update,
    )
    got = swap(pay, 1)
    count = parts // 2
    l1, l2, one, two = run(
        functools.partial(local_d_kernel, count), "local_d1",
        [field, field, ((hid, 3 * block), F32), ((hid, (orders - 3) * block), F32)], *local, y1, y2, cand_grad, ma, mb
    )
    z1, z2, pay = run(
        chip_d1_kernel, "chip_d1", [field16, field16, pay_kind], pay, got, *edges, l1, l2, g1, g3, ro, ri
    )
    got = swap(pay, 1)
    base, part = run(
        functools.partial(local_d2_kernel, count), "local_d2", [field, ((hid, width), BF16)],
        *local, z1, z2, direct, cand_grad, ma, mb, one, two, order,
    )
    half = ((3 * hid // 2, width), BF16)
    gate_grad, kept, keep, give = run(
        chip_d2_kernel, "chip_d2", [((parts, 2 * hid, n), BF16), field, half, half],
        pay, got, hx, sx, base, sa, sb, reset, gate_update, order, part, scratch=[pltpu.VMEM((3 * hid, width), F32)],
    )
    y1, y2, g1, g3, direct, pay = run(
        back_e_kernel, "back_e", [field16] * 4 + [field, pay_kind], hc, sc, gate_grad, kept, ro, ri, gw_b, up, update
    )
    got = swap(pay, 1)
    l1, l2 = run(local_kernel, "local_e1", [field, field], *local, y1, y2)
    mine, sent = run(sum_kernel, "sum_core", [half] * 2, keep, swap(give, 1), after=[direct])
    every = [mine] + [swap(sent, k, "snap", snaps) for k in range(1, snaps)]
    z1, z2, pay = run(
        chip_d1_kernel, "chip_e1", [field16, field16, pay_kind], pay, got, *edges, l1, l2, g1, g3, ro, ri, after=[mine],
    )
    got = swap(pay, 1)
    (base,) = run(local_e_kernel, "local_e2", [((hid, n), F32)], early[0], early[1], z1, z2, direct)
    state_grad, done = run(
        chip_e_kernel, "chip_e2", [((1, hid, n), BF16), ((8, LANES), F32)], pay, got, *edges, base
    )
    mine, sent = run(sum_kernel, "sum_snap", [(half[0], F32)] * 2, *every, after=[done])
    factor = 1.0 / math.sqrt(readings.shape[0] * snaps * n * nd)
    feats = orders * chans
    grad_gw, grad_gb, grad_cw, grad_cb = run(
        functools.partial(end_kernel, factor), "end",
        [((feats, 2 * hid), F32), ((1, 2 * hid), F32), ((hid, feats), F32), ((1, hid), F32)],
        mine, swap(sent, 1), scratch=[pltpu.VMEM((3 * hid, width), F32)],
    )
    return state_grad, grad_gw.T, grad_gb[0], grad_cw, grad_cb[0]


def body(*args):
    neighbours, send_rows = args[7], args[9]
    n = neighbours.shape[1]
    nd, snaps = lax.axis_size("dom"), lax.axis_size("snap")
    parts = nd // 2
    slots = 2 * parts * parts * (send_rows.shape[1] // nd)
    powers = nd & (nd - 1) == 0 and snaps & (snaps - 1) == 0 and nd > 2
    if powers and parts * (n + slots) * n * 2 <= 4 << 20:
        return chip_body(*args)
    return spread_body(*args)


def solution(mesh):
    in_specs = (
        P("snap", None, "dom"),
        P("snap", None, "dom"),
        P("snap", None, "dom"),
        P(),
        P(),
        P(),
        P(),
        P(None, "dom"),
        P(None, "dom"),
        P("dom", None),
    )
    out_specs = (P("snap", None, "dom"), P(), P(), P(), P())
    return jax.shard_map(body, mesh=mesh, in_specs=in_specs, out_specs=out_specs, check_vma=False)
```
